32 devices in a mesh: groups: 2 (over x), frame: 8 (over z, y), space: 2 (over core).
Axes of the slice: x: 2, y: 2, z: 4, core: 2. Of those that a mesh axis runs over, the one named last changes fastest.
Arguments:
- queries: bfloat16 [16, 12, 80, 2240], P(('groups', 'frame'), 'space'), parts along dimension 0, may hold values from -6 to 6
- keys: bfloat16 [16, 12, 80, 2240], P(('groups', 'frame'), 'space'), parts along dimension 0, may hold values from -6 to 6
- values: bfloat16 [16, 12, 80, 2240], P(('groups', 'frame'), 'space'), parts along dimension 0, may hold values from -6 to 6
- residual: bfloat16 [16, 12, 80, 2240], P(('groups', 'frame'), 'space'), parts along dimension 0, may hold values from -6 to 6
- attn_gain: float32 [2240], replicated, may hold values from 0.5 to 1.5
- value_taps: float32 [9, 2240], replicated, may hold values from -2 to 2
- gate_taps: float32 [9, 2240], replicated, may hold values from -2 to 2
Outputs:
- block_out: bfloat16 [16, 12, 80, 2240], P(('groups', 'frame'), 'space'), parts along dimension 0
The draws below stay inside these ranges and needn't reach their ends.
There are 2 independent parts, one for each index of `groups`. The reference program is written for one: setup_inputs(seed, part) draws one part's arguments, and reference() takes and returns one part's arrays. A program takes and returns all parts, laid end to end along the dimension named above; an argument that names none is the same for every part. Nothing has to cross between parts.
All inputs are finite; a program needn't handle non-finite values.
Results may differ from the reference program's by a relative error of at most 0.008.
Values may be sent and summed in bfloat16 or wider, within the bound.
No kernel may reach another device: no remote copies, remote signals or barrier semaphores. Data moves between devices by JAX's collectives and lax.ppermute only.
A program may use at most 128 MiB of HBM per device.

```python
import jax
import jax.numpy as jnp
from jax import lax

D = 2240
HEADS = 20
HEAD_DIM = 112
WID = 80
HGT = 12
FRAMES = 8


def block_scale(rng, shape, cuts, smallest, top_value):
    level, own = 1.0, jax.random.fold_in(rng, 6)
    for position, blocks in cuts:
        draws = jnp.exp(jax.random.uniform(jax.random.fold_in(own, position), (blocks,), jnp.float32, smallest / len(cuts), top_value / len(cuts)))
        level = level * jnp.repeat(draws, shape[position] // blocks).reshape([-1 if axis == position else 1 for axis in range(len(shape))])
    return level


def normal_values(rng, dims, deviation, limit, split=(), held_as=jnp.bfloat16):
    loudness = block_scale(rng, dims, split, -0.22, 0.18) if split else 1.0
    array = jax.random.normal(rng, dims, jnp.float32) * deviation * loudness
    return jnp.minimum(jnp.maximum(array, -limit), limit).astype(held_as)


def setup_inputs(seed: int = 0, part: int = 0) -> dict:
    key_list = jax.random.split(jax.random.key(seed), 8)
    own_keys = jax.random.split(jax.random.fold_in(key_list[7], part), 8)
    queries = normal_values(own_keys[0], (FRAMES, HGT, WID, D), 1.0, 6.0, ((0, 8), (1, 2)))
    keys = normal_values(own_keys[1], (FRAMES, HGT, WID, D), 1.0, 6.0, ((0, 8), (1, 2)))
    values = normal_values(own_keys[2], (FRAMES, HGT, WID, D), 1.0, 6.0, ((0, 8), (1, 2)))
    residual = normal_values(own_keys[3], (FRAMES, HGT, WID, D), 1.0, 6.0, ((0, 8), (1, 2)))
    attn_gain = jnp.clip(1.0 + 0.1 * jax.random.normal(key_list[4], (D,), jnp.float32), 0.5, 1.5)
    value_taps = normal_values(key_list[5], (9, D), 9 ** -0.5, 2.0, (), jnp.float32)
    gate_taps = normal_values(key_list[6], (9, D), 9 ** -0.5, 2.0, (), jnp.float32)
    return {"queries": queries, "keys": keys, "values": values, "residual": residual, "attn_gain": attn_gain, "value_taps": value_taps, "gate_taps": gate_taps}


def reference(queries, keys, values, residual, attn_gain, value_taps, gate_taps):
    tokens = HGT * WID
    feature_keys = jnp.maximum(keys, 0).reshape(FRAMES, tokens, HEADS, HEAD_DIM).astype(jnp.float32)
    value_rows = values.reshape(FRAMES, tokens, HEADS, HEAD_DIM).astype(jnp.float32)
    own_state = jnp.einsum('fthk,fthv->fhkv', feature_keys, value_rows, precision=lax.Precision.HIGHEST)
    running = jnp.cumsum(own_state, axis=0)
    prev_state = jnp.concatenate([jnp.zeros_like(own_state[:1]), running[:-1] - 0.0 * own_state[:-1]], axis=0)
    prev_state = jnp.concatenate([jnp.zeros_like(own_state[:1]), jnp.cumsum(own_state, axis=0)[:-1]], axis=0)
    previous_frame_pass = prev_state.astype(jnp.bfloat16).astype(jnp.float32)
    local_frame_pass = own_state.astype(jnp.bfloat16).astype(jnp.float32)
    feature_queries = jnp.maximum(queries, 0).reshape(FRAMES, tokens, HEADS, HEAD_DIM).astype(jnp.float32)
    numerator_sum = jnp.einsum('fthk,fhkv->fthv', feature_queries, previous_frame_pass, precision=lax.Precision.HIGHEST)
    numerator_sum = numerator_sum + jnp.einsum('fthk,fhkv->fthv', feature_queries, local_frame_pass, precision=lax.Precision.HIGHEST)
    scale = lax.rsqrt(lax.optimization_barrier(jnp.mean(numerator_sum * numerator_sum, axis=-1, keepdims=True)) + 1e-06)
    normed = (numerator_sum * scale).reshape(FRAMES, HGT, WID, D)
    mixed = (residual.astype(jnp.float32) + normed * attn_gain).astype(jnp.bfloat16)
    padded = jnp.pad(mixed.astype(jnp.float32), ((0, 0), (1, 1), (1, 1), (0, 0)))
    conv_v = jnp.zeros((FRAMES, HGT, WID, D), jnp.float32)
    conv_g = jnp.zeros((FRAMES, HGT, WID, D), jnp.float32)
    for tap_row in range(3):
        for tap_col in range(3):
            window = padded[:, tap_row:tap_row + HGT, tap_col:tap_col + WID, :]
            conv_v = conv_v + value_taps[3 * tap_row + tap_col] * window
            conv_g = conv_g + gate_taps[3 * tap_row + tap_col] * window
    block_out = mixed.astype(jnp.float32) + conv_v * jax.nn.silu(conv_g)
    return block_out.astype(jnp.bfloat16)
```

```python
import functools
import math

import jax
import jax.numpy as jnp
from jax import lax
from jax.experimental import pallas as pl
from jax.experimental.pallas import tpu as pltpu
from jax.sharding import PartitionSpec as P

HEAD_DIM = 112
LANES = 128
GROUP = math.lcm(HEAD_DIM, LANES)
TILES = GROUP // LANES
VMEM_LIMIT = 48 * 2**20


def cdiv(a, b):
    return -(-a // b)


def lane_iota(shape):
    return lax.broadcasted_iota(jnp.int32, shape, len(shape) - 1)


def tile_heads(j):
    lo, hi = j * LANES, (j + 1) * LANES
    heads = range(lo // HEAD_DIM, cdiv(hi, HEAD_DIM))
    return [(h, max(h * HEAD_DIM - lo, 0), min((h + 1) * HEAD_DIM - lo, LANES)) for h in heads]


def spans():
    result = []
    for j in range(0, TILES, 2):
        tiles = list(range(j, min(j + 2, TILES)))
        first = tile_heads(tiles[0])[0][0] * HEAD_DIM // LANES
        last = cdiv((tile_heads(tiles[-1])[-1][0] + 1) * HEAD_DIM, LANES)
        result.append((tiles, first, last))
    return result


def state_kernel(dim, keys_ref, values_ref, state_ref, turned):
    g = pl.program_id(0)
    left = dim - g * GROUP
    turned[...] = jnp.maximum(keys_ref[...], 0).T
    for j in range(TILES):

        def tile(j=j):
            heads = tile_heads(j)
            start = heads[0][0] * HEAD_DIM
            stop = (heads[-1][0] + 1) * HEAD_DIM
            product = jnp.dot(
                turned[start:stop, :],
                values_ref[:, j * LANES : (j + 1) * LANES],
                preferred_element_type=jnp.float32,
            )
            lane = lane_iota((HEAD_DIM, LANES))
            total = jnp.zeros((HEAD_DIM, LANES), jnp.float32)
            for place, (_, lo, hi) in enumerate(heads):
                part = product[place * HEAD_DIM : (place + 1) * HEAD_DIM]
                total = jnp.where((lane >= lo) & (lane < hi), part, total)
            total = jnp.where(lane + j * LANES < left, total, 0.0)
            state_ref[j * HEAD_DIM : (j + 1) * HEAD_DIM, :] = total.astype(jnp.bfloat16)

        pl.when(j * LANES < left)(tile)

        @pl.when(j * LANES >= left)
        def _(j=j):
            state_ref[j * HEAD_DIM : (j + 1) * HEAD_DIM, :] = jnp.zeros(
                (HEAD_DIM, LANES), jnp.bfloat16
            )


def frame_states(keys, values, rows):
    tokens, dim = keys.shape
    return pl.pallas_call(
        functools.partial(state_kernel, dim),
        out_shape=jax.ShapeDtypeStruct((rows, LANES), jnp.bfloat16),
        grid=(cdiv(dim, GROUP),),
        in_specs=[pl.BlockSpec((tokens, GROUP), lambda g: (0, g))] * 2,
        out_specs=pl.BlockSpec((TILES * HEAD_DIM, LANES), lambda g: (g, 0)),
        scratch_shapes=[pltpu.VMEM((GROUP, tokens), jnp.bfloat16)],
        compiler_params=pltpu.CompilerParams(vmem_limit_bytes=VMEM_LIMIT),
        cost_estimate=pl.CostEstimate(
            flops=2 * tokens * dim * HEAD_DIM, bytes_accessed=4 * tokens * dim, transcendentals=0
        ),
        name="frame_states",
    )(keys, values)


def mix_kernel(
    dim, rows, width, edges,
    place_ref, queries_ref, residual_ref, edge_ref, state_ref, gain_ref, vtaps_ref, gtaps_ref,
    out_ref,
    features, weights, same, numer, shifted,
):
    g = pl.program_id(0)
    left = dim - g * GROUP
    tokens = rows * width
    total = tokens + edges * width

    @pl.when(g == 0)
    def _():
        weights[...] = jnp.zeros_like(weights)
        same[...] = jnp.zeros_like(same)
        ones = jnp.ones((HEAD_DIM, LANES), jnp.float32)
        lane = lane_iota((HEAD_DIM, LANES))
        for number, (tiles, first, _) in enumerate(spans()):
            for side, j in enumerate(tiles):
                for h, lo, hi in tile_heads(j):
                    start = h * HEAD_DIM - first * LANES
                    block = jnp.where((lane >= lo) & (lane < hi), ones, 0.0)
                    same[
                        number, start : start + HEAD_DIM, side * LANES : (side + 1) * LANES
                    ] = block.astype(jnp.bfloat16)
        for row in range(rows + 2):
            if edges == 2 and row in (0, rows + 1):
                continue
            shifted[:, row] = jnp.zeros((3, width, LANES), jnp.float32)

    inside = lane_iota((1, GROUP)) < left
    zero = jnp.zeros((), jnp.bfloat16)
    features[:tokens] = jnp.where(inside, jnp.maximum(queries_ref[...], zero), zero)
    for e in range(edges):
        features[tokens + e * width : tokens + (e + 1) * width] = jnp.where(
            inside, jnp.maximum(edge_ref[0, e], zero), zero
        )

    for number, (tiles, first, last) in enumerate(spans()):

        def numerators(number=number, tiles=tiles, first=first, last=last):
            for side, j in enumerate(tiles):
                state = state_ref[j * HEAD_DIM : (j + 1) * HEAD_DIM, :].astype(jnp.float32)
                lane = lane_iota((HEAD_DIM, LANES))
                for h, lo, hi in tile_heads(j):
                    start = h * HEAD_DIM - first * LANES
                    block = jnp.where((lane >= lo) & (lane < hi), state, 0.0)
                    weights[
                        number, start : start + HEAD_DIM, side * LANES : (side + 1) * LANES
                    ] = block.astype(jnp.bfloat16)
            depth, wide = (last - first) * LANES, len(tiles) * LANES
            numer[:, tiles[0] * LANES : tiles[0] * LANES + wide] = jnp.dot(
                features[:, first * LANES : last * LANES],
                weights[number, :depth, :wide],
                preferred_element_type=jnp.float32,
            )

        pl.when(tiles[0] * LANES < left)(numerators)

        @pl.when(tiles[0] * LANES >= left)
        def _(tiles=tiles):
            numer[:, tiles[0] * LANES : (tiles[-1] + 1) * LANES] = jnp.zeros(
                (total, len(tiles) * LANES), jnp.float32
            )

    column = lax.broadcasted_iota(jnp.int32, (width, LANES), 0)
    for number, (tiles, first, last) in enumerate(spans()):
        for side, j in enumerate(tiles):

            def tile(number=number, side=side, first=first, last=last, j=j):
                lanes = slice(j * LANES, (j + 1) * LANES)
                gain = gain_ref[:, lanes]

                def mixed_row(source, residual, row):
                    here = numer[pl.ds(source, width), first * LANES : last * LANES]
                    squares = (here * here).astype(jnp.bfloat16)
                    mean = jnp.dot(
                        squares,
                        same[
                            number, : (last - first) * LANES, side * LANES : (side + 1) * LANES
                        ],
                        preferred_element_type=jnp.float32,
                    ) * (1.0 / HEAD_DIM)
                    value = numer[pl.ds(source, width), lanes] * lax.rsqrt(mean + 1e-06)
                    mixed = residual.astype(jnp.float32) + value * gain
                    mixed = mixed.astype(jnp.bfloat16).astype(jnp.float32)
                    shifted[1, row] = mixed
                    shifted[0, row] = jnp.where(column == 0, 0.0, pltpu.roll(mixed, 1, 0))
                    shifted[2, row] = jnp.where(
                        column == width - 1, 0.0, pltpu.roll(mixed, width - 1, 0)
                    )

                def mix(row, carry):
                    source = pl.multiple_of(row * width, width)
                    mixed_row(source, residual_ref[pl.ds(source, width), lanes], row + 1)
                    return carry

                lax.fori_loop(0, rows, mix, 0)
                for e in range(edges):
                    mixed_row(tokens + e * width, edge_ref[1, e, :, lanes], place_ref[e])

                def convolve(row, carry):
                    conv_v = jnp.zeros((width, LANES), jnp.float32)
                    conv_g = jnp.zeros((width, LANES), jnp.float32)
                    for tap_row in range(3):
                        for tap_col in range(3):
                            window = shifted[tap_col, row + tap_row]
                            tap = 3 * tap_row + tap_col
                            conv_v = conv_v + vtaps_ref[tap : tap + 1, lanes] * window
                            conv_g = conv_g + gtaps_ref[tap : tap + 1, lanes] * window
                    gate = conv_g / (1.0 + jnp.exp(-conv_g))
                    result = shifted[1, row + 1] + conv_v * gate
                    out_ref[pl.ds(pl.multiple_of(row * width, width), width), lanes] = (
                        result.astype(jnp.bfloat16)
                    )
                    return carry

                lax.fori_loop(0, rows, convolve, 0)

            pl.when(j * LANES < left)(tile)


def mix(place, queries, residual, edge, state, gain, value_taps, gate_taps, rows, width):
    tokens, dim = queries.shape
    edges = edge.shape[1]
    total = tokens + edges * width
    depth = max(last - first for _, first, last in spans()) * LANES
    block = pl.BlockSpec((tokens, GROUP), lambda g: (0, g))
    taps = pl.BlockSpec((value_taps.shape[0], GROUP), lambda g: (0, g))
    return pl.pallas_call(
        functools.partial(mix_kernel, dim, rows, width, edges),
        out_shape=jax.ShapeDtypeStruct((tokens, dim), jnp.bfloat16),
        grid=(cdiv(dim, GROUP),),
        in_specs=[
            pl.BlockSpec(memory_space=pltpu.SMEM),
            block,
            block,
            pl.BlockSpec((2, edges, width, GROUP), lambda g: (0, 0, 0, g)),
            pl.BlockSpec((TILES * HEAD_DIM, LANES), lambda g: (g, 0)),
            pl.BlockSpec((1, GROUP), lambda g: (0, g)),
            taps,
            taps,
        ],
        out_specs=block,
        scratch_shapes=[
            pltpu.VMEM((total, GROUP), jnp.bfloat16),
            pltpu.VMEM((len(spans()), depth, 2 * LANES), jnp.bfloat16),
            pltpu.VMEM((len(spans()), depth, 2 * LANES), jnp.bfloat16),
            pltpu.VMEM((total, GROUP), jnp.float32),
            pltpu.VMEM((3, rows + 2, width, LANES), jnp.float32),
        ],
        compiler_params=pltpu.CompilerParams(vmem_limit_bytes=VMEM_LIMIT),
        cost_estimate=pl.CostEstimate(
            flops=60 * tokens * dim, bytes_accessed=6 * tokens * dim, transcendentals=2 * tokens * dim
        ),
        name="mix",
    )(place, queries, residual, edge, state, gain, value_taps, gate_taps)


def edge_rows(queries, residual, rows, width):
    devices, here = lax.axis_size("space"), lax.axis_index("space")
    dim = queries.shape[-1]
    both = [a.reshape(rows, width, dim) for a in (queries, residual)]
    if devices == 2:
        mine = jnp.stack([jnp.where(here == 0, a[rows - 1 :], a[:1]) for a in both])
        edge = lax.ppermute(mine, "space", [(0, 1), (1, 0)])
        place = jnp.where(here == 0, rows + 1, 0).astype(jnp.int32)[None]
        return edge, place
    up = [(i, i + 1) for i in range(devices - 1)]
    down = [(j, i) for i, j in up]
    before = lax.ppermute(jnp.stack([a[rows - 1 :] for a in both]), "space", up)
    after = lax.ppermute(jnp.stack([a[:1] for a in both]), "space", down)
    return jnp.concatenate([before, after], axis=1), jnp.array([0, rows + 1], jnp.int32)


def share_of_sum(state):
    devices, here = lax.axis_size("space"), lax.axis_index("space")
    if devices != 2:
        return lax.psum_scatter(state, "space", scatter_dimension=0, tiled=True)
    half = state.shape[0] // 2
    halves = state.reshape(2, half, LANES)
    sent = jnp.where(here == 0, halves[1], halves[0])
    kept = jnp.where(here == 0, halves[0], halves[1])
    got = lax.ppermute(sent, "space", [(0, 1), (1, 0)])
    return (kept.astype(jnp.float32) + got.astype(jnp.float32)).astype(jnp.bfloat16)


def prefix_sum(share):
    frames = lax.axis_size("frame")
    pieces = share.reshape(frames, share.shape[0] // frames, LANES)
    pieces = lax.all_to_all(pieces, "frame", split_axis=0, concat_axis=0, tiled=True)
    running = [pieces[0].astype(jnp.float32)]
    for f in range(1, frames):
        running.append(running[-1] + pieces[f].astype(jnp.float32))
    sums = jnp.stack(running).astype(jnp.bfloat16)
    sums = lax.all_to_all(sums, "frame", split_axis=0, concat_axis=0, tiled=True)
    return sums.reshape(share.shape)


def on_device(queries, keys, values, residual, attn_gain, value_taps, gate_taps):
    frames, rows, width, dim = queries.shape
    tokens = frames * rows * width
    flat = lambda a: a.reshape(tokens, dim)
    unit = 16 * lax.axis_size("space") * lax.axis_size("frame")
    state_rows = cdiv(cdiv(dim, LANES) * HEAD_DIM, unit) * unit
    edge, place = edge_rows(queries, residual, rows, width)
    state = frame_states(flat(keys), flat(values), state_rows)
    share = prefix_sum(share_of_sum(state))
    state = lax.all_gather(share, "space", axis=0, tiled=True)
    out = mix(
        place, flat(queries), flat(residual), edge, state, attn_gain[None], value_taps, gate_taps,
        rows, width,
    )
    return out.reshape(frames, rows, width, dim)


def solution(mesh):
    placed = P(("groups", "frame"), "space", None, None)
    return jax.shard_map(
        on_device,
        mesh=mesh,
        in_specs=(placed, placed, placed, placed, P(), P(), P()),
        out_specs=placed,
        check_vma=False,
    )
```

```python
import functools
import math

import jax
import jax.numpy as jnp
from jax import lax
from jax.experimental import pallas as pl
from jax.experimental.pallas import tpu as pltpu
from jax.sharding import PartitionSpec as P

HEAD_DIM = 112
LANES = 128
GROUP = math.lcm(HEAD_DIM, LANES)
TILES = GROUP // LANES
VMEM_LIMIT = 60 * 2**20


def cdiv(a, b):
    return -(-a // b)


def lane_iota(shape):
    return lax.broadcasted_iota(jnp.int32, shape, len(shape) - 1)


def tile_heads(j, lanes):
    lo, hi = j * LANES, min((j + 1) * LANES, lanes)
    heads = range(lo // HEAD_DIM, cdiv(hi, HEAD_DIM))
    return [(h, max(h * HEAD_DIM - lo, 0), min((h + 1) * HEAD_DIM - lo, LANES)) for h in heads]


def spans(lanes):
    count = cdiv(lanes, LANES)
    result = []
    for j in range(0, count, 2):
        tiles = list(range(j, min(j + 2, count)))
        first = tile_heads(tiles[0], lanes)[0][0] * HEAD_DIM // LANES
        last = cdiv((tile_heads(tiles[-1], lanes)[-1][0] + 1) * HEAD_DIM, LANES)
        result.append((tiles, first, last))
    return result


def by_group(dim, body):
    full, rest = divmod(dim, GROUP)
    if full:
        pl.when(pl.program_id(0) < full)(lambda: body(GROUP))
    if rest:
        pl.when(pl.program_id(0) >= full)(lambda: body(rest))


def state_kernel(dim, keys_ref, values_ref, state_ref, turned):
    def body(lanes):
        turned[...] = jnp.maximum(keys_ref[...], 0).T
        lane = lane_iota((HEAD_DIM, LANES))
        for tiles, _, _ in spans(lanes):
            begin = tile_heads(tiles[0], lanes)[0][0]
            end = tile_heads(tiles[-1], lanes)[-1][0] + 1
            product = jnp.dot(
                turned[begin * HEAD_DIM : end * HEAD_DIM, :],
                values_ref[:, tiles[0] * LANES : (tiles[-1] + 1) * LANES],
                preferred_element_type=jnp.float32,
            )
            for side, j in enumerate(tiles):
                total = jnp.zeros((HEAD_DIM, LANES), jnp.float32)
                for h, lo, hi in tile_heads(j, lanes):
                    part = product[
                        (h - begin) * HEAD_DIM : (h - begin + 1) * HEAD_DIM,
                        side * LANES : (side + 1) * LANES,
                    ]
                    total = jnp.where((lane >= lo) & (lane < hi), part, total)
                state_ref[j * HEAD_DIM : (j + 1) * HEAD_DIM, :] = total.astype(jnp.bfloat16)
        unused = (TILES - cdiv(lanes, LANES)) * HEAD_DIM
        if unused:
            state_ref[TILES * HEAD_DIM - unused :, :] = jnp.zeros((unused, LANES), jnp.bfloat16)

    by_group(dim, body)


def frame_states(keys, values, rows):
    tokens, dim = keys.shape
    return pl.pallas_call(
        functools.partial(state_kernel, dim),
        out_shape=jax.ShapeDtypeStruct((rows, LANES), jnp.bfloat16),
        grid=(cdiv(dim, GROUP),),
        in_specs=[pl.BlockSpec((tokens, GROUP), lambda g: (0, g))] * 2,
        out_specs=pl.BlockSpec((TILES * HEAD_DIM, LANES), lambda g: (g, 0)),
        scratch_shapes=[pltpu.VMEM((GROUP, tokens), jnp.bfloat16)],
        compiler_params=pltpu.CompilerParams(vmem_limit_bytes=VMEM_LIMIT),
        cost_estimate=pl.CostEstimate(
            flops=2 * tokens * dim * HEAD_DIM, bytes_accessed=4 * tokens * dim, transcendentals=0
        ),
        name="frame_states",
    )(keys, values)


def mix_kernel(
    dim, rows, width, edges,
    place_ref, queries_ref, residual_ref, edge_ref, state_ref, gain_ref, vtaps_ref, gtaps_ref,
    out_ref,
    features, weights, same, numer, squares, shifted,
):
    tokens = rows * width
    total = tokens + edges * width

    @pl.when(pl.program_id(0) == 0)
    def _():
        weights[...] = jnp.zeros_like(weights)
        same[...] = jnp.zeros_like(same)
        lane = lane_iota((HEAD_DIM, LANES))
        for number, (tiles, first, _) in enumerate(spans(min(GROUP, dim))):
            for side, j in enumerate(tiles):
                for h, lo, hi in tile_heads(j, GROUP):
                    start = h * HEAD_DIM - first * LANES
                    block = jnp.where((lane >= lo) & (lane < hi), 1.0, 0.0)
                    same[
                        number, start : start + HEAD_DIM, side * LANES : (side + 1) * LANES
                    ] = block.astype(jnp.bfloat16)
        for row in (0, rows + 1):
            shifted[:, row] = jnp.zeros((3, width, LANES), jnp.float32)

    zero = jnp.zeros((), jnp.bfloat16)
    column = lax.broadcasted_iota(jnp.int32, (width, LANES), 0)
    lane = lane_iota((HEAD_DIM, LANES))

    def store_shifted(mixed, row):
        mixed = mixed.astype(jnp.bfloat16).astype(jnp.float32)
        shifted[1, row] = mixed
        shifted[0, row] = jnp.where(column == 0, 0.0, pltpu.roll(mixed, 1, 0))
        shifted[2, row] = jnp.where(column == width - 1, 0.0, pltpu.roll(mixed, width - 1, 0))

    def body(lanes):
        count = cdiv(lanes, LANES)
        end = count * LANES
        inside = lane_iota((1, end)) < lanes

        def feature(queries):
            queries = jnp.maximum(queries, zero)
            return queries if lanes == end else jnp.where(inside, queries, zero)

        features[:tokens, :end] = feature(queries_ref[:, :end])
        for e in range(edges):
            features[tokens + e * width : tokens + (e + 1) * width, :end] = feature(
                edge_ref[0, e, :, :end]
            )
        for number, (tiles, first, last) in enumerate(spans(lanes)):
            for side, j in enumerate(tiles):
                state = state_ref[j * HEAD_DIM : (j + 1) * HEAD_DIM, :].astype(jnp.float32)
                for h, lo, hi in tile_heads(j, lanes):
                    start = h * HEAD_DIM - first * LANES
                    block = jnp.where((lane >= lo) & (lane < hi), state, 0.0)
                    weights[
                        number, start : start + HEAD_DIM, side * LANES : (side + 1) * LANES
                    ] = block.astype(jnp.bfloat16)
            depth, wide = (last - first) * LANES, len(tiles) * LANES
            product = jnp.dot(
                features[:, first * LANES : last * LANES],
                weights[number, :depth, :wide],
                preferred_element_type=jnp.float32,
            )
            here = slice(tiles[0] * LANES, tiles[0] * LANES + wide)
            numer[:, here] = product
            squares[:, here] = (product * product).astype(jnp.bfloat16)

        for number, (tiles, first, last) in enumerate(spans(lanes)):
            depth, wide = (last - first) * LANES, len(tiles) * LANES
            sums = jnp.dot(
                squares[:, first * LANES : last * LANES],
                same[number, :depth, :wide],
                preferred_element_type=jnp.float32,
            )
            here = slice(tiles[0] * LANES, tiles[0] * LANES + wide)
            scale = lax.rsqrt(sums * (1.0 / HEAD_DIM) + 1e-06)
            numer[:, here] = numer[:, here] * scale * gain_ref[:, here]

        for j in range(count):
            here = slice(j * LANES, (j + 1) * LANES)
            for row in range(rows):
                source = slice(row * width, (row + 1) * width)
                store_shifted(
                    residual_ref[source, here].astype(jnp.float32) + numer[source, here], row + 1
                )
            for e in range(edges):
                source = slice(tokens + e * width, tokens + (e + 1) * width)
                store_shifted(
                    edge_ref[1, e, :, here].astype(jnp.float32) + numer[source, here], place_ref[e]
                )

            def convolve(row, carry, here=here):
                conv_v = jnp.zeros((width, LANES), jnp.float32)
                half_g = jnp.zeros((width, LANES), jnp.float32)
                for tap_row in range(3):
                    for tap_col in range(3):
                        window = shifted[tap_col, row + tap_row]
                        tap = 3 * tap_row + tap_col
                        conv_v = conv_v + vtaps_ref[tap : tap + 1, here] * window
                        half_g = half_g + (0.5 * gtaps_ref[tap : tap + 1, here]) * window
                gate = half_g + half_g * jnp.tanh(half_g)
                result = shifted[1, row + 1] + conv_v * gate
                out_ref[pl.ds(pl.multiple_of(row * width, width), width), here] = result.astype(
                    jnp.bfloat16
                )
                return carry

            lax.fori_loop(0, rows, convolve, 0)

    by_group(dim, body)


def mix(place, queries, residual, edge, state, gain, value_taps, gate_taps, rows, width):
    tokens, dim = queries.shape
    edges = edge.shape[1]
    total = tokens + edges * width
    pairs = spans(min(GROUP, dim))
    depth = max(last - first for _, first, last in pairs) * LANES
    block = pl.BlockSpec((tokens, GROUP), lambda g: (0, g))
    taps = pl.BlockSpec((value_taps.shape[0], GROUP), lambda g: (0, g))
    return pl.pallas_call(
        functools.partial(mix_kernel, dim, rows, width, edges),
        out_shape=jax.ShapeDtypeStruct((tokens, dim), jnp.bfloat16),
        grid=(cdiv(dim, GROUP),),
        in_specs=[
            pl.BlockSpec(memory_space=pltpu.SMEM),
            block,
            block,
            pl.BlockSpec((2, edges, width, GROUP), lambda g: (0, 0, 0, g)),
            pl.BlockSpec((TILES * HEAD_DIM, LANES), lambda g: (g, 0)),
            pl.BlockSpec((1, GROUP), lambda g: (0, g)),
            taps,
            taps,
        ],
        out_specs=block,
        scratch_shapes=[
            pltpu.VMEM((total, GROUP), jnp.bfloat16),
            pltpu.VMEM((len(pairs), depth, 2 * LANES), jnp.bfloat16),
            pltpu.VMEM((len(pairs), depth, 2 * LANES), jnp.bfloat16),
            pltpu.VMEM((total, GROUP), jnp.float32),
            pltpu.VMEM((total, GROUP), jnp.bfloat16),
            pltpu.VMEM((3, rows + 2, width, LANES), jnp.float32),
        ],
        compiler_params=pltpu.CompilerParams(vmem_limit_bytes=VMEM_LIMIT),
        cost_estimate=pl.CostEstimate(
            flops=60 * tokens * dim, bytes_accessed=6 * tokens * dim, transcendentals=2 * tokens * dim
        ),
        name="mix",
    )(place, queries, residual, edge, state, gain, value_taps, gate_taps)


def edge_rows(queries, residual, rows, width):
    devices, here = lax.axis_size("space"), lax.axis_index("space")
    dim = queries.shape[-1]
    both = [a.reshape(rows, width, dim) for a in (queries, residual)]
    if devices == 2:
        mine = jnp.stack([jnp.where(here == 0, a[rows - 1 :], a[:1]) for a in both])
        edge = lax.ppermute(mine, "space", [(0, 1), (1, 0)])
        place = jnp.where(here == 0, rows + 1, 0).astype(jnp.int32)[None]
        return edge, place
    up = [(i, i + 1) for i in range(devices - 1)]
    down = [(j, i) for i, j in up]
    before = lax.ppermute(jnp.stack([a[rows - 1 :] for a in both]), "space", up)
    after = lax.ppermute(jnp.stack([a[:1] for a in both]), "space", down)
    return jnp.concatenate([before, after], axis=1), jnp.array([0, rows + 1], jnp.int32)


def share_of_sum(state):
    devices, here = lax.axis_size("space"), lax.axis_index("space")
    if devices != 2:
        return lax.psum_scatter(state, "space", scatter_dimension=0, tiled=True)
    half = state.shape[0] // 2
    halves = state.reshape(2, half, LANES)
    sent = jnp.where(here == 0, halves[1], halves[0])
    kept = jnp.where(here == 0, halves[0], halves[1])
    got = lax.ppermute(sent, "space", [(0, 1), (1, 0)])
    return (kept.astype(jnp.float32) + got.astype(jnp.float32)).astype(jnp.bfloat16)


def running_sum_kernel(pieces_ref, sums_ref):
    running = jnp.zeros(pieces_ref.shape[1:], jnp.float32)
    for f in range(pieces_ref.shape[0]):
        running = running + pieces_ref[f].astype(jnp.float32)
        sums_ref[f] = running.astype(jnp.bfloat16)


def prefix_sum(share):
    frames = lax.axis_size("frame")
    pieces = share.reshape(frames, share.shape[0] // frames, LANES)
    pieces = lax.all_to_all(pieces, "frame", split_axis=0, concat_axis=0, tiled=True)
    sums = pl.pallas_call(
        running_sum_kernel,
        out_shape=jax.ShapeDtypeStruct(pieces.shape, jnp.bfloat16),
        name="running_sum",
    )(pieces)
    sums = lax.all_to_all(sums, "frame", split_axis=0, concat_axis=0, tiled=True)
    return sums.reshape(share.shape)


def on_device(queries, keys, values, residual, attn_gain, value_taps, gate_taps):
    frames, rows, width, dim = queries.shape
    tokens = frames * rows * width
    flat = lambda a: a.reshape(tokens, dim)
    unit = 16 * lax.axis_size("space") * lax.axis_size("frame")
    state_rows = cdiv(cdiv(dim, LANES) * HEAD_DIM, unit) * unit
    edge, place = edge_rows(queries, residual, rows, width)
    state = frame_states(flat(keys), flat(values), state_rows)
    share = prefix_sum(share_of_sum(state))
    state = lax.all_gather(share, "space", axis=0, tiled=True)
    out = mix(
        place, flat(queries), flat(residual), edge, state, attn_gain[None], value_taps, gate_taps,
        rows, width,
    )
    return out.reshape(frames, rows, width, dim)


def solution(mesh):
    placed = P(("groups", "frame"), "space", None, None)
    return jax.shard_map(
        on_device,
        mesh=mesh,
        in_specs=(placed, placed, placed, placed, P(), P(), P()),
        out_specs=placed,
        check_vma=False,
    )
```

```python
import functools
import math

import jax
import jax.numpy as jnp
from jax import lax
from jax.experimental import pallas as pl
from jax.experimental.pallas import tpu as pltpu
from jax.sharding import PartitionSpec as P

HEAD_DIM = 112
LANES = 128
GROUP = math.lcm(HEAD_DIM, LANES)
TILES = GROUP // LANES


def cdiv(a, b):
    return -(-a // b)


def lane_iota(shape):
    return lax.broadcasted_iota(jnp.int32, shape, len(shape) - 1)


def tile_heads(j, lanes):
    lo, hi = j * LANES, min((j + 1) * LANES, lanes)
    heads = range(lo // HEAD_DIM, cdiv(hi, HEAD_DIM))
    return [(h, max(h * HEAD_DIM - lo, 0), min((h + 1) * HEAD_DIM - lo, LANES)) for h in heads]


def spans(lanes):
    count = cdiv(lanes, LANES)
    result = []
    for j in range(0, count, 2):
        tiles = list(range(j, min(j + 2, count)))
        first = tile_heads(tiles[0], lanes)[0][0] * HEAD_DIM // LANES
        last = cdiv((tile_heads(tiles[-1], lanes)[-1][0] + 1) * HEAD_DIM, LANES)
        result.append((tiles, first, last))
    return result


def by_group(dim, body):
    full, rest = divmod(dim, GROUP)
    if full:
        pl.when(pl.program_id(0) < full)(lambda: body(GROUP))
    if rest:
        pl.when(pl.program_id(0) >= full)(lambda: body(rest))


def state_kernel(dim, spot_ref, keys_ref, values_ref, *refs):
    *parts, turned, whole = refs
    step = pl.program_id(0)

    def body(lanes):
        turned[...] = jnp.maximum(keys_ref[...], 0).T
        lane = lane_iota((HEAD_DIM, LANES))
        for tiles, _, _ in spans(lanes):
            begin = tile_heads(tiles[0], lanes)[0][0]
            end = tile_heads(tiles[-1], lanes)[-1][0] + 1
            product = jnp.dot(
                turned[begin * HEAD_DIM : end * HEAD_DIM, :],
                values_ref[:, tiles[0] * LANES : (tiles[-1] + 1) * LANES],
                preferred_element_type=jnp.float32,
            )
            for side, j in enumerate(tiles):
                total = jnp.zeros((HEAD_DIM, LANES), jnp.float32)
                for h, lo, hi in tile_heads(j, lanes):
                    part = product[
                        (h - begin) * HEAD_DIM : (h - begin + 1) * HEAD_DIM,
                        side * LANES : (side + 1) * LANES,
                    ]
                    total = jnp.where((lane >= lo) & (lane < hi), part, total)
                row = pl.multiple_of((step * TILES + j) * HEAD_DIM, 16)
                whole[pl.ds(row, HEAD_DIM), :] = total.astype(jnp.bfloat16)

    by_group(dim, body)

    @pl.when(step == pl.num_programs(0) - 1)
    def _():
        used = cdiv(dim, LANES) * HEAD_DIM
        if used < whole.shape[0]:
            whole[used:, :] = jnp.zeros((whole.shape[0] - used, LANES), jnp.bfloat16)
        for k, part in enumerate(parts):
            size = part.shape[0]
            row = pl.multiple_of(lax.rem(spot_ref[0] + k, len(parts)) * size, 16)
            part[...] = whole[pl.ds(row, size), :]


def frame_states(spot, keys, values, rows, parts):
    tokens, dim = keys.shape
    part = (rows // parts, LANES)
    block = pl.BlockSpec((tokens, GROUP), lambda g: (0, g))
    return pl.pallas_call(
        functools.partial(state_kernel, dim),
        out_shape=[jax.ShapeDtypeStruct(part, jnp.bfloat16)] * parts,
        grid=(cdiv(dim, GROUP),),
        in_specs=[pl.BlockSpec(memory_space=pltpu.SMEM), block, block],
        out_specs=[pl.BlockSpec(part, lambda g: (0, 0))] * parts,
        scratch_shapes=[
            pltpu.VMEM((GROUP, tokens), jnp.bfloat16),
            pltpu.VMEM((rows, LANES), jnp.bfloat16),
        ],
        compiler_params=pltpu.CompilerParams(vmem_limit_bytes=60 * 2**20),
        cost_estimate=pl.CostEstimate(
            flops=2 * tokens * dim * HEAD_DIM, bytes_accessed=4 * tokens * dim, transcendentals=0
        ),
        name="frame_states",
    )(spot, keys, values)


def mix_kernel(
    dim, rows, width, edges,
    place_ref, spots_ref, queries_ref, residual_ref, edge_ref, gain_ref, vtaps_ref, gtaps_ref, *refs,
):
    *pieces, out_ref, states, features, weights, same, numer, squares, shifted = refs
    step = pl.program_id(0)
    tokens = rows * width
    total = tokens + edges * width

    @pl.when(pl.program_id(0) == 0)
    def _():
        weights[...] = jnp.zeros_like(weights)
        same[...] = jnp.zeros_like(same)
        lane = lane_iota((HEAD_DIM, LANES))
        for number, (tiles, first, _) in enumerate(spans(min(GROUP, dim))):
            for side, j in enumerate(tiles):
                for h, lo, hi in tile_heads(j, GROUP):
                    start = h * HEAD_DIM - first * LANES
                    block = jnp.where((lane >= lo) & (lane < hi), 1.0, 0.0)
                    same[
                        number, start : start + HEAD_DIM, side * LANES : (side + 1) * LANES
                    ] = block.astype(jnp.bfloat16)
        for row in (0, rows + 1):
            shifted[:, row] = jnp.zeros((3, width, LANES), jnp.float32)
        for k, piece in enumerate(pieces):
            size = piece.shape[0]
            states[pl.ds(pl.multiple_of(spots_ref[k] * size, 16), size), :] = piece[...]

    zero = jnp.zeros((), jnp.bfloat16)
    column = lax.broadcasted_iota(jnp.int32, (width, LANES), 0)
    lane = lane_iota((HEAD_DIM, LANES))

    def store_shifted(mixed, row):
        mixed = mixed.astype(jnp.bfloat16).astype(jnp.float32)
        shifted[1, row] = mixed
        shifted[0, row] = jnp.where(column == 0, 0.0, pltpu.roll(mixed, 1, 0))
        shifted[2, row] = jnp.where(column == width - 1, 0.0, pltpu.roll(mixed, width - 1, 0))

    def body(lanes):
        count = cdiv(lanes, LANES)
        end = count * LANES
        inside = lane_iota((1, end)) < lanes

        def feature(queries):
            queries = jnp.maximum(queries, zero)
            return queries if lanes == end else jnp.where(inside, queries, zero)

        features[:tokens, :end] = feature(queries_ref[:, :end])
        for e in range(edges):
            features[tokens + e * width : tokens + (e + 1) * width, :end] = feature(
                edge_ref[0, e, :, :end]
            )
        for number, (tiles, first, last) in enumerate(spans(lanes)):
            for side, j in enumerate(tiles):
                row = pl.multiple_of((step * TILES + j) * HEAD_DIM, 16)
                state = states[pl.ds(row, HEAD_DIM), :].astype(jnp.float32)
                for h, lo, hi in tile_heads(j, lanes):
                    start = h * HEAD_DIM - first * LANES
                    block = jnp.where((lane >= lo) & (lane < hi), state, 0.0)
                    weights[
                        number, start : start + HEAD_DIM, side * LANES : (side + 1) * LANES
                    ] = block.astype(jnp.bfloat16)
            depth, wide = (last - first) * LANES, len(tiles) * LANES
            product = jnp.dot(
                features[:, first * LANES : last * LANES],
                weights[number, :depth, :wide],
                preferred_element_type=jnp.float32,
            )
            here = slice(tiles[0] * LANES, tiles[0] * LANES + wide)
            numer[:, here] = product
            squares[:, here] = (product * product).astype(jnp.bfloat16)

        for number, (tiles, first, last) in enumerate(spans(lanes)):
            depth, wide = (last - first) * LANES, len(tiles) * LANES
            sums = jnp.dot(
                squares[:, first * LANES : last * LANES],
                same[number, :depth, :wide],
                preferred_element_type=jnp.float32,
            )
            here = slice(tiles[0] * LANES, tiles[0] * LANES + wide)
            scale = lax.rsqrt(sums * (1.0 / HEAD_DIM) + 1e-06)
            numer[:, here] = numer[:, here] * scale * gain_ref[:, here]

        for j in range(count):
            here = slice(j * LANES, (j + 1) * LANES)
            for row in range(rows):
                source = slice(row * width, (row + 1) * width)
                store_shifted(
                    residual_ref[source, here].astype(jnp.float32) + numer[source, here], row + 1
                )
            for e in range(edges):
                source = slice(tokens + e * width, tokens + (e + 1) * width)
                store_shifted(
                    edge_ref[1, e, :, here].astype(jnp.float32) + numer[source, here], place_ref[e]
                )

            def convolve(row, carry, here=here):
                conv_v = jnp.zeros((width, LANES), jnp.float32)
                half_g = jnp.zeros((width, LANES), jnp.float32)
                for tap_row in range(3):
                    for tap_col in range(3):
                        window = shifted[tap_col, row + tap_row]
                        tap = 3 * tap_row + tap_col
                        conv_v = conv_v + vtaps_ref[tap : tap + 1, here] * window
                        half_g = half_g + (0.5 * gtaps_ref[tap : tap + 1, here]) * window
                gate = half_g + half_g * jnp.tanh(half_g)
                result = shifted[1, row + 1] + conv_v * gate
                out_ref[pl.ds(pl.multiple_of(row * width, width), width), here] = result.astype(
                    jnp.bfloat16
                )
                return carry

            lax.fori_loop(0, rows, convolve, 0)

    by_group(dim, body)


def mix(place, spots, queries, residual, edge, gain, value_taps, gate_taps, pieces, rows, width):
    tokens, dim = queries.shape
    edges = edge.shape[1]
    total = tokens + edges * width
    pairs = spans(min(GROUP, dim))
    depth = max(last - first for _, first, last in pairs) * LANES
    block = pl.BlockSpec((tokens, GROUP), lambda g: (0, g))
    taps = pl.BlockSpec((value_taps.shape[0], GROUP), lambda g: (0, g))
    return pl.pallas_call(
        functools.partial(mix_kernel, dim, rows, width, edges),
        out_shape=jax.ShapeDtypeStruct((tokens, dim), jnp.bfloat16),
        grid=(cdiv(dim, GROUP),),
        in_specs=[
            pl.BlockSpec(memory_space=pltpu.SMEM),
            pl.BlockSpec(memory_space=pltpu.SMEM),
            block,
            block,
            pl.BlockSpec((2, edges, width, GROUP), lambda g: (0, 0, 0, g)),
            pl.BlockSpec((1, GROUP), lambda g: (0, g)),
            taps,
            taps,
        ]
        + [pl.BlockSpec(piece.shape, lambda g: (0, 0)) for piece in pieces],
        out_specs=block,
        scratch_shapes=[
            pltpu.VMEM((sum(piece.shape[0] for piece in pieces), LANES), jnp.bfloat16),
            pltpu.VMEM((total, GROUP), jnp.bfloat16),
            pltpu.VMEM((len(pairs), depth, 2 * LANES), jnp.bfloat16),
            pltpu.VMEM((len(pairs), depth, 2 * LANES), jnp.bfloat16),
            pltpu.VMEM((total, GROUP), jnp.float32),
            pltpu.VMEM((total, GROUP), jnp.bfloat16),
            pltpu.VMEM((3, rows + 2, width, LANES), jnp.float32),
        ],
        compiler_params=pltpu.CompilerParams(vmem_limit_bytes=36 * 2**20),
        cost_estimate=pl.CostEstimate(
            flops=60 * tokens * dim, bytes_accessed=6 * tokens * dim, transcendentals=2 * tokens * dim
        ),
        name="mix",
    )(place, spots, queries, residual, edge, gain, value_taps, gate_taps, *pieces)


def edge_rows(queries, residual, rows, width):
    devices, here = lax.axis_size("space"), lax.axis_index("space")
    dim = queries.shape[-1]
    both = [a.reshape(rows, width, dim) for a in (queries, residual)]
    if devices == 2:
        mine = jnp.stack([jnp.where(here == 0, a[rows - 1 :], a[:1]) for a in both])
        edge = lax.ppermute(mine, "space", [(0, 1), (1, 0)])
        place = jnp.where(here == 0, rows + 1, 0).astype(jnp.int32)[None]
        return edge, place
    up = [(i, i + 1) for i in range(devices - 1)]
    down = [(j, i) for i, j in up]
    before = lax.ppermute(jnp.stack([a[rows - 1 :] for a in both]), "space", up)
    after = lax.ppermute(jnp.stack([a[:1] for a in both]), "space", down)
    return jnp.concatenate([before, after], axis=1), jnp.array([0, rows + 1], jnp.int32)


def small_kernel(body, name, outs, scalars, *arrays):
    return pl.pallas_call(
        body,
        out_shape=[jax.ShapeDtypeStruct(shape, jnp.bfloat16) for shape in outs],
        in_specs=[pl.BlockSpec(memory_space=pltpu.SMEM)]
        + [pl.BlockSpec(memory_space=pltpu.VMEM)] * len(arrays),
        out_specs=[pl.BlockSpec(memory_space=pltpu.VMEM)] * len(outs),
        name=name,
    )(scalars, *arrays)


def add(*values):
    total = values[0].astype(jnp.float32)
    for value in values[1:]:
        total = total + value.astype(jnp.float32)
    return total


def split_sum_body(spot_ref, kept_ref, got_ref, mine_ref, theirs_ref):
    size = mine_ref.shape[0]
    for ref, side in ((theirs_ref, 1 - spot_ref[0]), (mine_ref, spot_ref[0])):
        rows = pl.ds(pl.multiple_of(side * size, 16), size)
        ref[...] = add(kept_ref[rows, :], got_ref[rows, :]).astype(jnp.bfloat16)


def sum_body(_, *refs):
    *terms, out_ref = refs
    out_ref[...] = add(*[term[...] for term in terms]).astype(jnp.bfloat16)


def pair_sums_body(spot_ref, own_ref, partner_ref, *refs):
    *earlier, mine_ref, theirs_ref = refs
    before = add(*[ref[...] for ref in earlier])
    own, partner = add(own_ref[...]), add(partner_ref[...])
    first = spot_ref[0] == 0
    both = before + (own + partner)
    mine_ref[...] = jnp.where(first, before + own, both).astype(jnp.bfloat16)
    theirs_ref[...] = jnp.where(first, both, before + partner).astype(jnp.bfloat16)


def running_states(keys, values, rows):
    devices, frames = lax.axis_size("space"), lax.axis_size("frame")
    core, frame = lax.axis_index("space"), lax.axis_index("frame")
    if devices != 2 or frames % 2 or frames < 4:
        (state,) = frame_states(jnp.zeros((1,), jnp.int32), keys, values, rows, 1)
        state = lax.psum(state.astype(jnp.float32), "space").astype(jnp.bfloat16)
        every = lax.all_gather(state, "frame").astype(jnp.float32)
        reached = (jnp.arange(frames) <= frame)[:, None, None]
        total = jnp.sum(jnp.where(reached, every, 0.0), axis=0).astype(jnp.bfloat16)
        return [total], jnp.zeros((1,), jnp.int32)
    parity = lax.rem(frame, 2)
    swap = [(0, 1), (1, 0)]
    partners = [(f, f ^ 1) for f in range(frames)]
    spot = parity.astype(jnp.int32)[None]
    kept, sent = frame_states(core.astype(jnp.int32)[None], keys, values, rows, 2)
    got = lax.ppermute(sent, "space", swap)
    quarter = (rows // 4, LANES)
    own, sent = small_kernel(split_sum_body, "split_sum", [quarter] * 2, spot, kept, got)
    partner = lax.ppermute(sent, "frame", partners)
    (total,) = small_kernel(sum_body, "pair_sum", [quarter], spot, own, partner)
    earlier = []
    stride = 2
    while stride < frames:
        got = lax.ppermute(total, "frame", [(f, f + stride) for f in range(frames - stride)])
        earlier.append(got)
        stride *= 2
        if stride < frames:
            (total,) = small_kernel(sum_body, "stride_sum", [quarter], spot, total, got)
    mine, theirs = small_kernel(
        pair_sums_body, "pair_sums", [quarter] * 2, spot, own, partner, *earlier
    )
    other = lax.ppermute(theirs, "frame", partners)
    pieces = [mine, other, lax.ppermute(mine, "space", swap), lax.ppermute(other, "space", swap)]
    spots = [2 * c + p for c in (core, 1 - core) for p in (parity, 1 - parity)]
    return pieces, jnp.stack(spots).astype(jnp.int32)


def on_device(queries, keys, values, residual, attn_gain, value_taps, gate_taps):
    frames, rows, width, dim = queries.shape
    tokens = frames * rows * width
    flat = lambda a: a.reshape(tokens, dim)
    state_rows = cdiv(cdiv(dim, LANES) * HEAD_DIM, 64) * 64
    edge, place = edge_rows(queries, residual, rows, width)
    pieces, spots = running_states(flat(keys), flat(values), state_rows)
    out = mix(
        place, spots, flat(queries), flat(residual), edge, attn_gain[None], value_taps, gate_taps,
        pieces, rows, width,
    )
    return out.reshape(frames, rows, width, dim)


def solution(mesh):
    placed = P(("groups", "frame"), "space", None, None)
    return jax.shard_map(
        on_device,
        mesh=mesh,
        in_specs=(placed, placed, placed, placed, P(), P(), P()),
        out_specs=placed,
        check_vma=False,
    )
```

```python
import functools
import math

import jax
import jax.numpy as jnp
from jax import lax
from jax.experimental import pallas as pl
from jax.experimental.pallas import tpu as pltpu
from jax.sharding import PartitionSpec as P

HEAD_DIM = 112
LANES = 128
GROUP = math.lcm(HEAD_DIM, LANES)
TILES = GROUP // LANES


def cdiv(a, b):
    return -(-a // b)


def in_hbm(array):
    return pltpu.with_memory_space_constraint(array, pltpu.HBM)


def lane_iota(shape):
    return lax.broadcasted_iota(jnp.int32, shape, len(shape) - 1)


def tile_heads(j, lanes):
    lo, hi = j * LANES, min((j + 1) * LANES, lanes)
    heads = range(lo // HEAD_DIM, cdiv(hi, HEAD_DIM))
    return [(h, max(h * HEAD_DIM - lo, 0), min((h + 1) * HEAD_DIM - lo, LANES)) for h in heads]


def spans(lanes):
    count = cdiv(lanes, LANES)
    result = []
    for j in range(0, count, 2):
        tiles = list(range(j, min(j + 2, count)))
        first = tile_heads(tiles[0], lanes)[0][0] * HEAD_DIM // LANES
        last = cdiv((tile_heads(tiles[-1], lanes)[-1][0] + 1) * HEAD_DIM, LANES)
        result.append((tiles, first, last))
    return result


def by_group(dim, body):
    full, rest = divmod(dim, GROUP)
    if full:
        pl.when(pl.program_id(0) < full)(lambda: body(GROUP))
    if rest:
        pl.when(pl.program_id(0) >= full)(lambda: body(rest))


def state_kernel(dim, with_edge, spot_ref, keys_ref, values_ref, *refs):
    step = pl.program_id(0)
    *refs, turned, whole, semaphores = refs
    if with_edge:
        *sources, edge_ref = refs[:2] + refs[-1:]
        parts = refs[2:-1]
        row = (sources[0].shape[0] - 1) * (1 - lax.axis_index("space"))
        copies = [
            pltpu.make_async_copy(source.at[row], edge_ref.at[k, 0], semaphores.at[k])
            for k, source in enumerate(sources)
        ]

        @pl.when(step == 0)
        def _():
            for copy in copies:
                copy.start()

    else:
        parts = refs

    def body(lanes):
        turned[...] = jnp.maximum(keys_ref[...], 0).T
        lane = lane_iota((HEAD_DIM, LANES))
        for tiles, _, _ in spans(lanes):
            begin = tile_heads(tiles[0], lanes)[0][0]
            end = tile_heads(tiles[-1], lanes)[-1][0] + 1
            product = jnp.dot(
                turned[begin * HEAD_DIM : end * HEAD_DIM, :],
                values_ref[:, tiles[0] * LANES : (tiles[-1] + 1) * LANES],
                preferred_element_type=jnp.float32,
            )
            for side, j in enumerate(tiles):
                total = jnp.zeros((HEAD_DIM, LANES), jnp.float32)
                for h, lo, hi in tile_heads(j, lanes):
                    part = product[
                        (h - begin) * HEAD_DIM : (h - begin + 1) * HEAD_DIM,
                        side * LANES : (side + 1) * LANES,
                    ]
                    total = jnp.where((lane >= lo) & (lane < hi), part, total)
                row = pl.multiple_of((step * TILES + j) * HEAD_DIM, 16)
                whole[pl.ds(row, HEAD_DIM), :] = total.astype(jnp.bfloat16)

    by_group(dim, body)

    @pl.when(step == pl.num_programs(0) - 1)
    def _():
        used = cdiv(dim, LANES) * HEAD_DIM
        if used < whole.shape[0]:
            whole[used:, :] = jnp.zeros((whole.shape[0] - used, LANES), jnp.bfloat16)
        for k, part in enumerate(parts):
            size = part.shape[0]
            row = pl.multiple_of(lax.rem(spot_ref[0] + k, len(parts)) * size, 16)
            part[...] = whole[pl.ds(row, size), :]
        if with_edge:
            for copy in copies:
                copy.wait()


def frame_states(spot, keys, values, rows, parts, edged=()):
    tokens, dim = keys.shape
    part = (rows // parts, LANES)
    block = pl.BlockSpec((tokens, GROUP), lambda g: (0, g))
    return pl.pallas_call(
        functools.partial(state_kernel, dim, bool(edged)),
        out_shape=[pltpu.VMEM(part, jnp.bfloat16)] * parts
        + [pltpu.VMEM((len(edged), 1, *edged[0].shape[1:]), jnp.bfloat16) for _ in edged[:1]],
        grid=(cdiv(dim, GROUP),),
        in_specs=[pl.BlockSpec(memory_space=pltpu.SMEM), block, block]
        + [pl.BlockSpec(memory_space=pl.ANY)] * len(edged),
        out_specs=[pl.BlockSpec(part, lambda g: (0, 0))] * parts
        + [pl.BlockSpec(memory_space=pl.ANY) for _ in edged[:1]],
        scratch_shapes=[
            pltpu.VMEM((GROUP, tokens), jnp.bfloat16),
            pltpu.VMEM((rows, LANES), jnp.bfloat16),
            pltpu.SemaphoreType.DMA((2,)),
        ],
        compiler_params=pltpu.CompilerParams(vmem_limit_bytes=60 * 2**20),
        cost_estimate=pl.CostEstimate(
            flops=2 * tokens * dim * HEAD_DIM, bytes_accessed=4 * tokens * dim, transcendentals=0
        ),
        name="frame_states",
    )(spot, in_hbm(keys), in_hbm(values), *[in_hbm(array) for array in edged])


def mix_kernel(
    dim, rows, width, edges,
    place_ref, spots_ref, queries_ref, residual_ref, edge_ref, gain_ref, vtaps_ref, gtaps_ref, *refs,
):
    *pieces, out_ref, states, features, weights, same, numer, squares, shifted = refs
    step = pl.program_id(0)
    tokens = rows * width
    total = tokens + edges * width

    @pl.when(pl.program_id(0) == 0)
    def _():
        weights[...] = jnp.zeros_like(weights)
        same[...] = jnp.zeros_like(same)
        lane = lane_iota((HEAD_DIM, LANES))
        for number, (tiles, first, _) in enumerate(spans(min(GROUP, dim))):
            for side, j in enumerate(tiles):
                for h, lo, hi in tile_heads(j, GROUP):
                    start = h * HEAD_DIM - first * LANES
                    block = jnp.where((lane >= lo) & (lane < hi), 1.0, 0.0)
                    same[
                        number, start : start + HEAD_DIM, side * LANES : (side + 1) * LANES
                    ] = block.astype(jnp.bfloat16)
        for row in (0, rows + 1):
            shifted[:, row] = jnp.zeros((3, width, LANES), jnp.float32)
        for k, piece in enumerate(pieces):
            size = piece.shape[0]
            states[pl.ds(pl.multiple_of(spots_ref[k] * size, 16), size), :] = piece[...]

    zero = jnp.zeros((), jnp.bfloat16)
    column = lax.broadcasted_iota(jnp.int32, (width, LANES), 0)
    lane = lane_iota((HEAD_DIM, LANES))

    def store_shifted(mixed, row):
        mixed = mixed.astype(jnp.bfloat16).astype(jnp.float32)
        shifted[1, row] = mixed
        shifted[0, row] = jnp.where(column == 0, 0.0, pltpu.roll(mixed, 1, 0))
        shifted[2, row] = jnp.where(column == width - 1, 0.0, pltpu.roll(mixed, width - 1, 0))

    def body(lanes):
        count = cdiv(lanes, LANES)
        end = count * LANES
        inside = lane_iota((1, end)) < lanes

        def feature(queries):
            queries = jnp.maximum(queries, zero)
            return queries if lanes == end else jnp.where(inside, queries, zero)

        features[:tokens, :end] = feature(queries_ref[:, :end])
        for e in range(edges):
            features[tokens + e * width : tokens + (e + 1) * width, :end] = feature(
                edge_ref[0, e, :, :end]
            )
        for number, (tiles, first, last) in enumerate(spans(lanes)):
            for side, j in enumerate(tiles):
                row = pl.multiple_of((step * TILES + j) * HEAD_DIM, 16)
                state = states[pl.ds(row, HEAD_DIM), :].astype(jnp.float32)
                for h, lo, hi in tile_heads(j, lanes):
                    start = h * HEAD_DIM - first * LANES
                    block = jnp.where((lane >= lo) & (lane < hi), state, 0.0)
                    weights[
                        number, start : start + HEAD_DIM, side * LANES : (side + 1) * LANES
                    ] = block.astype(jnp.bfloat16)
            depth, wide = (last - first) * LANES, len(tiles) * LANES
            product = jnp.dot(
                features[:, first * LANES : last * LANES],
                weights[number, :depth, :wide],
                preferred_element_type=jnp.float32,
            )
            here = slice(tiles[0] * LANES, tiles[0] * LANES + wide)
            numer[:, here] = product
            squares[:, here] = (product * product).astype(jnp.bfloat16)

        for number, (tiles, first, last) in enumerate(spans(lanes)):
            depth, wide = (last - first) * LANES, len(tiles) * LANES
            sums = jnp.dot(
                squares[:, first * LANES : last * LANES],
                same[number, :depth, :wide],
                preferred_element_type=jnp.float32,
            )
            here = slice(tiles[0] * LANES, tiles[0] * LANES + wide)
            scale = lax.rsqrt(sums * (1.0 / HEAD_DIM) + 1e-06)
            numer[:, here] = numer[:, here] * scale * gain_ref[:, here]

        for j in range(count):
            here = slice(j * LANES, (j + 1) * LANES)
            for row in range(rows):
                source = slice(row * width, (row + 1) * width)
                store_shifted(
                    residual_ref[source, here].astype(jnp.float32) + numer[source, here], row + 1
                )
            for e in range(edges):
                source = slice(tokens + e * width, tokens + (e + 1) * width)
                store_shifted(
                    edge_ref[1, e, :, here].astype(jnp.float32) + numer[source, here], place_ref[e]
                )

            def convolve(row, carry, here=here):
                conv_v = jnp.zeros((width, LANES), jnp.float32)
                half_g = jnp.zeros((width, LANES), jnp.float32)
                for tap_row in range(3):
                    for tap_col in range(3):
                        window = shifted[tap_col, row + tap_row]
                        tap = 3 * tap_row + tap_col
                        conv_v = conv_v + vtaps_ref[tap : tap + 1, here] * window
                        half_g = half_g + (0.5 * gtaps_ref[tap : tap + 1, here]) * window
                gate = half_g + half_g * jnp.tanh(half_g)
                result = shifted[1, row + 1] + conv_v * gate
                out_ref[pl.ds(pl.multiple_of(row * width, width), width), here] = result.astype(
                    jnp.bfloat16
                )
                return carry

            lax.fori_loop(0, rows, convolve, 0)

    by_group(dim, body)


def mix(place, spots, queries, residual, edge, gain, value_taps, gate_taps, pieces, rows, width):
    tokens, dim = queries.shape
    edges = edge.shape[1]
    total = tokens + edges * width
    pairs = spans(min(GROUP, dim))
    depth = max(last - first for _, first, last in pairs) * LANES
    block = pl.BlockSpec((tokens, GROUP), lambda g: (0, g))
    taps = pl.BlockSpec((value_taps.shape[0], GROUP), lambda g: (0, g))
    return pl.pallas_call(
        functools.partial(mix_kernel, dim, rows, width, edges),
        out_shape=jax.ShapeDtypeStruct((tokens, dim), jnp.bfloat16),
        grid=(cdiv(dim, GROUP),),
        in_specs=[
            pl.BlockSpec(memory_space=pltpu.SMEM),
            pl.BlockSpec(memory_space=pltpu.SMEM),
            block,
            block,
            pl.BlockSpec((2, edges, width, GROUP), lambda g: (0, 0, 0, g)),
            pl.BlockSpec((1, GROUP), lambda g: (0, g)),
            taps,
            taps,
        ]
        + [pl.BlockSpec(piece.shape, lambda g: (0, 0)) for piece in pieces],
        out_specs=block,
        scratch_shapes=[
            pltpu.VMEM((sum(piece.shape[0] for piece in pieces), LANES), jnp.bfloat16),
            pltpu.VMEM((total, GROUP), jnp.bfloat16),
            pltpu.VMEM((len(pairs), depth, 2 * LANES), jnp.bfloat16),
            pltpu.VMEM((len(pairs), depth, 2 * LANES), jnp.bfloat16),
            pltpu.VMEM((total, GROUP), jnp.float32),
            pltpu.VMEM((total, GROUP), jnp.bfloat16),
            pltpu.VMEM((3, rows + 2, width, LANES), jnp.float32),
        ],
        compiler_params=pltpu.CompilerParams(vmem_limit_bytes=36 * 2**20),
        cost_estimate=pl.CostEstimate(
            flops=60 * tokens * dim, bytes_accessed=6 * tokens * dim, transcendentals=2 * tokens * dim
        ),
        name="mix",
    )(place, spots, in_hbm(queries), in_hbm(residual), edge, gain, value_taps, gate_taps, *pieces)


def edge_rows(queries, residual):
    devices, rows = lax.axis_size("space"), queries.shape[0]
    up = [(i, i + 1) for i in range(devices - 1)]
    down = [(j, i) for i, j in up]
    both = jnp.stack([queries, residual])
    before = lax.ppermute(both[:, rows - 1 :], "space", up)
    after = lax.ppermute(both[:, :1], "space", down)
    return jnp.concatenate([before, after], axis=1), jnp.array([0, rows + 1], jnp.int32)


def small_kernel(body, name, outs, scalars, *arrays):
    return pl.pallas_call(
        body,
        out_shape=[pltpu.VMEM(shape, jnp.bfloat16) for shape in outs],
        in_specs=[pl.BlockSpec(memory_space=pltpu.SMEM)]
        + [pl.BlockSpec(memory_space=pltpu.VMEM)] * len(arrays),
        out_specs=[pl.BlockSpec(memory_space=pltpu.VMEM)] * len(outs),
        compiler_params=pltpu.CompilerParams(vmem_limit_bytes=4 * 2**20),
        name=name,
    )(scalars, *arrays)


def add(*values):
    total = values[0].astype(jnp.float32)
    for value in values[1:]:
        total = total + value.astype(jnp.float32)
    return total


def split_sum_body(spot_ref, kept_ref, got_ref, mine_ref, theirs_ref):
    size = mine_ref.shape[0]
    for ref, side in ((theirs_ref, 1 - spot_ref[0]), (mine_ref, spot_ref[0])):
        rows = pl.ds(pl.multiple_of(side * size, 16), size)
        ref[...] = add(kept_ref[rows, :], got_ref[rows, :]).astype(jnp.bfloat16)


def sum_body(_, *refs):
    *terms, out_ref = refs
    out_ref[...] = add(*[term[...] for term in terms]).astype(jnp.bfloat16)


def pair_sums_body(spot_ref, own_ref, partner_ref, *refs):
    *earlier, mine_ref, theirs_ref = refs
    before = jnp.zeros(own_ref.shape, jnp.float32)
    for k, ref in enumerate(earlier):
        from_before = lax.rem(spot_ref[1] // (2 << k), 2) == 1
        before = before + jnp.where(from_before, add(ref[...]), 0.0)
    own, partner = add(own_ref[...]), add(partner_ref[...])
    first = spot_ref[0] == 0
    both = before + (own + partner)
    mine_ref[...] = jnp.where(first, before + own, both).astype(jnp.bfloat16)
    theirs_ref[...] = jnp.where(first, both, before + partner).astype(jnp.bfloat16)


def running_states(keys, values, queries, residual, rows):
    devices, frames = lax.axis_size("space"), lax.axis_size("frame")
    core, frame = lax.axis_index("space"), lax.axis_index("frame")
    if devices != 2 or frames < 2 or frames & (frames - 1):
        (state,) = frame_states(jnp.zeros((1,), jnp.int32), keys, values, rows, 1)
        state = lax.psum(state.astype(jnp.float32), "space").astype(jnp.bfloat16)
        every = lax.all_gather(state, "frame").astype(jnp.float32)
        reached = (jnp.arange(frames) <= frame)[:, None, None]
        total = jnp.sum(jnp.where(reached, every, 0.0), axis=0).astype(jnp.bfloat16)
        return [total], jnp.zeros((1,), jnp.int32), edge_rows(queries, residual)
    swap = [(0, 1), (1, 0)]
    spot = jnp.stack([lax.rem(frame, 2), frame]).astype(jnp.int32)
    kept, sent, edge = frame_states(
        core.astype(jnp.int32)[None], keys, values, rows, 2, (queries, residual)
    )
    got = lax.ppermute(sent, "space", swap)
    quarter = (rows // 4, LANES)
    own, sent = small_kernel(split_sum_body, "split_sum", [quarter] * 2, spot, kept, got)
    edge, sent = lax.optimization_barrier((edge, sent))
    edge = lax.ppermute(edge, "space", swap)
    place = jnp.where(core == 0, queries.shape[0] + 1, 0).astype(jnp.int32)[None]
    partner = lax.ppermute(sent, "frame", [(f, f ^ 1) for f in range(frames)])
    (total,) = small_kernel(sum_body, "pair_sum", [quarter], spot, own, partner)
    earlier = []
    stride = 2
    while stride < frames:
        got = lax.ppermute(total, "frame", [(f, f ^ stride) for f in range(frames)])
        earlier.append(got)
        stride *= 2
        if stride < frames:
            (total,) = small_kernel(sum_body, "stride_sum", [quarter], spot, total, got)
    mine, theirs = small_kernel(
        pair_sums_body, "pair_sums", [quarter] * 2, spot, own, partner, *earlier
    )
    other = lax.ppermute(theirs, "frame", [(f, f ^ 1) for f in range(frames)])
    pieces = [mine, other, lax.ppermute(mine, "space", swap), lax.ppermute(other, "space", swap)]
    spots = [2 * c + p for c in (core, 1 - core) for p in (spot[0], 1 - spot[0])]
    return pieces, jnp.stack(spots).astype(jnp.int32), (edge, place)


def on_device(queries, keys, values, residual, attn_gain, value_taps, gate_taps):
    frames, rows, width, dim = queries.shape
    tokens = frames * rows * width
    flat = lambda a: a.reshape(tokens, dim)
    state_rows = cdiv(cdiv(dim, LANES) * HEAD_DIM, 64) * 64
    pieces, spots, (edge, place) = running_states(
        flat(keys),
        flat(values),
        queries.reshape(rows, width, dim),
        residual.reshape(rows, width, dim),
        state_rows,
    )
    out = mix(
        place, spots, flat(queries), flat(residual), edge, attn_gain[None], value_taps, gate_taps,
        pieces, rows, width,
    )
    return out.reshape(frames, rows, width, dim)


def solution(mesh):
    placed = P(("groups", "frame"), "space", None, None)
    return jax.shard_map(
        on_device,
        mesh=mesh,
        in_specs=(placed, placed, placed, placed, P(), P(), P()),
        out_specs=placed,
        check_vma=False,
    )
```

```python
import functools
import math

import jax
import jax.numpy as jnp
from jax import lax
from jax.experimental import pallas as pl
from jax.experimental.pallas import tpu as pltpu
from jax.sharding import PartitionSpec as P

HEAD_DIM = 112
LANES = 128
PACK = 16
GROUP = math.lcm(HEAD_DIM, LANES)
TILES = GROUP // LANES


def cdiv(a, b):
    return -(-a // b)


def in_hbm(array):
    return pltpu.with_memory_space_constraint(array, pltpu.HBM)


def lane_iota(shape):
    return lax.broadcasted_iota(jnp.int32, shape, len(shape) - 1)


def tile_heads(j, lanes):
    lo, hi = j * LANES, min((j + 1) * LANES, lanes)
    heads = range(lo // HEAD_DIM, cdiv(hi, HEAD_DIM))
    return [(h, max(h * HEAD_DIM - lo, 0), min((h + 1) * HEAD_DIM - lo, LANES)) for h in heads]


def spans(lanes):
    count = cdiv(lanes, LANES)
    result = []
    for j in range(0, count, 2):
        tiles = list(range(j, min(j + 2, count)))
        first = tile_heads(tiles[0], lanes)[0][0] * HEAD_DIM // LANES
        last = cdiv((tile_heads(tiles[-1], lanes)[-1][0] + 1) * HEAD_DIM, LANES)
        result.append((tiles, first, last))
    return result


def by_group(dim, body):
    full, rest = divmod(dim, GROUP)
    if full:
        pl.when(pl.program_id(0) < full)(lambda: body(GROUP))
    if rest:
        pl.when(pl.program_id(0) >= full)(lambda: body(rest))


def state_kernel(dim, with_edge, spot_ref, keys_ref, values_ref, *refs):
    step = pl.program_id(0)
    *refs, turned, whole, semaphores = refs
    if with_edge:
        *sources, edge_ref = refs[:2] + refs[-1:]
        parts = refs[2:-1]
        row = (sources[0].shape[0] - 1) * (1 - lax.axis_index("space"))
        copies = [
            pltpu.make_async_copy(source.at[row], edge_ref.at[k, 0], semaphores.at[k])
            for k, source in enumerate(sources)
        ]

        @pl.when(step == 0)
        def _():
            for copy in copies:
                copy.start()

    else:
        parts = refs

    def body(lanes):
        turned[...] = jnp.maximum(keys_ref[...], 0).T
        lane = lane_iota((HEAD_DIM, LANES))
        for tiles, _, _ in spans(lanes):
            begin = tile_heads(tiles[0], lanes)[0][0]
            end = tile_heads(tiles[-1], lanes)[-1][0] + 1
            product = jnp.dot(
                turned[begin * HEAD_DIM : end * HEAD_DIM, :],
                values_ref[:, tiles[0] * LANES : (tiles[-1] + 1) * LANES],
                preferred_element_type=jnp.float32,
            )
            for side, j in enumerate(tiles):
                total = jnp.zeros((HEAD_DIM, LANES), jnp.float32)
                for h, lo, hi in tile_heads(j, lanes):
                    part = product[
                        (h - begin) * HEAD_DIM : (h - begin + 1) * HEAD_DIM,
                        side * LANES : (side + 1) * LANES,
                    ]
                    total = jnp.where((lane >= lo) & (lane < hi), part, total)
                row = pl.multiple_of((step * TILES + j) * HEAD_DIM, 16)
                whole[pl.ds(row, HEAD_DIM), :] = total.astype(jnp.bfloat16)

    by_group(dim, body)

    @pl.when(step == pl.num_programs(0) - 1)
    def _():
        used = cdiv(dim, LANES) * HEAD_DIM
        if used < whole.shape[0]:
            whole[used:, :] = jnp.zeros((whole.shape[0] - used, LANES), jnp.bfloat16)
        for k, part in enumerate(parts):
            size = part.shape[0]
            row = pl.multiple_of(lax.rem(spot_ref[0] + k, len(parts)) * size, 16)
            part[...] = whole[pl.ds(row, size), :]
        if with_edge:
            for copy in copies:
                copy.wait()


def frame_states(spot, keys, values, rows, parts, edged=()):
    tokens, dim = keys.shape
    part = (rows // parts, LANES)
    block = pl.BlockSpec((tokens, GROUP), lambda g: (0, g))
    return pl.pallas_call(
        functools.partial(state_kernel, dim, bool(edged)),
        out_shape=[pltpu.VMEM(part, jnp.bfloat16)] * parts
        + [pltpu.VMEM((len(edged), 1, *edged[0].shape[1:]), jnp.bfloat16) for _ in edged[:1]],
        grid=(cdiv(dim, GROUP),),
        in_specs=[pl.BlockSpec(memory_space=pltpu.SMEM), block, block]
        + [pl.BlockSpec(memory_space=pl.ANY)] * len(edged),
        out_specs=[pl.BlockSpec(part, lambda g: (0, 0))] * parts
        + [pl.BlockSpec(memory_space=pl.ANY) for _ in edged[:1]],
        scratch_shapes=[
            pltpu.VMEM((GROUP, tokens), jnp.bfloat16),
            pltpu.VMEM((rows, LANES), jnp.bfloat16),
            pltpu.SemaphoreType.DMA((2,)),
        ],
        compiler_params=pltpu.CompilerParams(vmem_limit_bytes=60 * 2**20),
        cost_estimate=pl.CostEstimate(
            flops=2 * tokens * dim * HEAD_DIM, bytes_accessed=4 * tokens * dim, transcendentals=0
        ),
        name="frame_states",
    )(spot, in_hbm(keys), in_hbm(values), *[in_hbm(array) for array in edged])


def mix_kernel(
    dim, rows, width, edges,
    place_ref, spots_ref, queries_ref, residual_ref, edge_ref, gain_ref, vtaps_ref, gtaps_ref, *refs,
):
    *pieces, out_ref, states, features, weights, same, numer, squares, shifted, taps = refs
    step = pl.program_id(0)
    tokens = rows * width
    total = tokens + edges * width

    @pl.when(pl.program_id(0) == 0)
    def _():
        weights[...] = jnp.zeros_like(weights)
        same[...] = jnp.zeros_like(same)
        lane = lane_iota((HEAD_DIM, LANES))
        for number, (tiles, first, _) in enumerate(spans(min(GROUP, dim))):
            for side, j in enumerate(tiles):
                for h, lo, hi in tile_heads(j, GROUP):
                    start = h * HEAD_DIM - first * LANES
                    block = jnp.where((lane >= lo) & (lane < hi), 1.0, 0.0)
                    same[
                        number, start : start + HEAD_DIM, side * LANES : (side + 1) * LANES
                    ] = block.astype(jnp.bfloat16)
        for row in (0, rows + 1):
            shifted[:, row] = jnp.zeros(shifted.shape[:1] + shifted.shape[2:], jnp.bfloat16)
        for k, piece in enumerate(pieces):
            size = piece.shape[0]
            states[pl.ds(pl.multiple_of(spots_ref[k] * size, 16), size), :] = piece[...]

    zero = jnp.zeros((), jnp.bfloat16)
    column = lax.broadcasted_iota(jnp.int32, (width, LANES), 0)
    lane = lane_iota((HEAD_DIM, LANES))

    def store_shifted(mixed, row):
        packed = lambda a: a.astype(jnp.bfloat16).reshape(width // PACK, PACK, LANES)
        shifted[1, row] = packed(mixed)
        shifted[0, row] = packed(jnp.where(column == 0, 0.0, pltpu.roll(mixed, 1, 0)))
        shifted[2, row] = packed(
            jnp.where(column == width - 1, 0.0, pltpu.roll(mixed, width - 1, 0))
        )

    def body(lanes):
        count = cdiv(lanes, LANES)
        end = count * LANES
        inside = lane_iota((1, end)) < lanes

        def feature(queries):
            queries = jnp.maximum(queries, zero)
            return queries if lanes == end else jnp.where(inside, queries, zero)

        features[:tokens, :end] = feature(queries_ref[:, :end])
        for e in range(edges):
            features[tokens + e * width : tokens + (e + 1) * width, :end] = feature(
                edge_ref[0, e, :, :end]
            )
        for number, (tiles, first, last) in enumerate(spans(lanes)):
            for side, j in enumerate(tiles):
                row = pl.multiple_of((step * TILES + j) * HEAD_DIM, 16)
                state = states[pl.ds(row, HEAD_DIM), :].astype(jnp.float32)
                for h, lo, hi in tile_heads(j, lanes):
                    start = h * HEAD_DIM - first * LANES
                    block = jnp.where((lane >= lo) & (lane < hi), state, 0.0)
                    weights[
                        number, start : start + HEAD_DIM, side * LANES : (side + 1) * LANES
                    ] = block.astype(jnp.bfloat16)
            depth, wide = (last - first) * LANES, len(tiles) * LANES
            product = jnp.dot(
                features[:, first * LANES : last * LANES],
                weights[number, :depth, :wide],
                preferred_element_type=jnp.float32,
            )
            here = slice(tiles[0] * LANES, tiles[0] * LANES + wide)
            numer[:, here] = product
            squares[:, here] = (product * product).astype(jnp.bfloat16)

        for number, (tiles, first, last) in enumerate(spans(lanes)):
            depth, wide = (last - first) * LANES, len(tiles) * LANES
            sums = jnp.dot(
                squares[:, first * LANES : last * LANES],
                same[number, :depth, :wide],
                preferred_element_type=jnp.float32,
            )
            scale = lax.rsqrt(sums * (1.0 / HEAD_DIM) + 1e-06)
            for side, j in enumerate(tiles):
                here = slice(j * LANES, (j + 1) * LANES)
                gain = gain_ref[:, here]

                def mixed(source, residual, side=side, here=here, gain=gain):
                    normed = numer[source, here] * scale[source, side * LANES : (side + 1) * LANES]
                    return residual.astype(jnp.float32) + normed * gain

                for row in range(rows):
                    source = slice(row * width, (row + 1) * width)
                    store_shifted(mixed(source, residual_ref[source, here]), row + 1)
                for e in range(edges):
                    source = slice(tokens + e * width, tokens + (e + 1) * width)
                    store_shifted(mixed(source, edge_ref[1, e, :, here]), place_ref[e])
                for tap in range(9):
                    for k, (ref, factor) in enumerate(((vtaps_ref, 1.0), (gtaps_ref, 0.5))):
                        row = ref[tap : tap + 1, here] * factor
                        taps[k, tap] = jnp.broadcast_to(row, (PACK, LANES)).astype(jnp.bfloat16)

                def convolve(row, carry, here=here):
                    sums = []
                    for tap_row in range(3):
                        windows = [shifted[i, row + tap_row] for i in range(3)]
                        for k in range(2):
                            terms = [taps[k, 3 * tap_row + i] * windows[i] for i in range(3)]
                            sums.append(terms[0] + terms[1] + terms[2])
                    conv_v = (sums[0] + sums[2] + sums[4]).astype(jnp.float32)
                    half_g = (sums[1] + sums[3] + sums[5]).astype(jnp.float32)
                    gate = half_g + half_g * jnp.tanh(half_g)
                    result = shifted[1, row + 1].astype(jnp.float32) + conv_v * gate
                    out_ref[pl.ds(pl.multiple_of(row * width, width), width), here] = (
                        result.astype(jnp.bfloat16).reshape(width, LANES)
                    )
                    return carry

                lax.fori_loop(0, rows, convolve, 0)

    by_group(dim, body)


def mix(place, spots, queries, residual, edge, gain, value_taps, gate_taps, pieces, rows, width):
    tokens, dim = queries.shape
    edges = edge.shape[1]
    total = tokens + edges * width
    pairs = spans(min(GROUP, dim))
    depth = max(last - first for _, first, last in pairs) * LANES
    block = pl.BlockSpec((tokens, GROUP), lambda g: (0, g))
    taps = pl.BlockSpec((value_taps.shape[0], GROUP), lambda g: (0, g))
    return pl.pallas_call(
        functools.partial(mix_kernel, dim, rows, width, edges),
        out_shape=jax.ShapeDtypeStruct((tokens, dim), jnp.bfloat16),
        grid=(cdiv(dim, GROUP),),
        in_specs=[
            pl.BlockSpec(memory_space=pltpu.SMEM),
            pl.BlockSpec(memory_space=pltpu.SMEM),
            block,
            block,
            pl.BlockSpec((2, edges, width, GROUP), lambda g: (0, 0, 0, g)),
            pl.BlockSpec((1, GROUP), lambda g: (0, g)),
            taps,
            taps,
        ]
        + [pl.BlockSpec(piece.shape, lambda g: (0, 0)) for piece in pieces],
        out_specs=block,
        scratch_shapes=[
            pltpu.VMEM((sum(piece.shape[0] for piece in pieces), LANES), jnp.bfloat16),
            pltpu.VMEM((total, GROUP), jnp.bfloat16),
            pltpu.VMEM((len(pairs), depth, 2 * LANES), jnp.bfloat16),
            pltpu.VMEM((len(pairs), depth, 2 * LANES), jnp.bfloat16),
            pltpu.VMEM((total, GROUP), jnp.float32),
            pltpu.VMEM((total, GROUP), jnp.bfloat16),
            pltpu.VMEM((3, rows + 2, width // PACK, PACK, LANES), jnp.bfloat16),
            pltpu.VMEM((2, 9, PACK, LANES), jnp.bfloat16),
        ],
        compiler_params=pltpu.CompilerParams(vmem_limit_bytes=36 * 2**20),
        cost_estimate=pl.CostEstimate(
            flops=60 * tokens * dim, bytes_accessed=6 * tokens * dim, transcendentals=2 * tokens * dim
        ),
        name="mix",
    )(place, spots, in_hbm(queries), in_hbm(residual), edge, gain, value_taps, gate_taps, *pieces)


def edge_rows(queries, residual):
    devices, rows = lax.axis_size("space"), queries.shape[0]
    up = [(i, i + 1) for i in range(devices - 1)]
    down = [(j, i) for i, j in up]
    both = jnp.stack([queries, residual])
    before = lax.ppermute(both[:, rows - 1 :], "space", up)
    after = lax.ppermute(both[:, :1], "space", down)
    return jnp.concatenate([before, after], axis=1), jnp.array([0, rows + 1], jnp.int32)


def small_kernel(body, name, outs, scalars, *arrays):
    return pl.pallas_call(
        body,
        out_shape=[pltpu.VMEM(shape, jnp.bfloat16) for shape in outs],
        in_specs=[pl.BlockSpec(memory_space=pltpu.SMEM)]
        + [pl.BlockSpec(memory_space=pltpu.VMEM)] * len(arrays),
        out_specs=[pl.BlockSpec(memory_space=pltpu.VMEM)] * len(outs),
        compiler_params=pltpu.CompilerParams(vmem_limit_bytes=4 * 2**20),
        name=name,
    )(scalars, *arrays)


def add(*values):
    total = values[0].astype(jnp.float32)
    for value in values[1:]:
        total = total + value.astype(jnp.float32)
    return total


def split_sum_body(spot_ref, kept_ref, got_ref, mine_ref, theirs_ref):
    size = mine_ref.shape[0]
    for ref, side in ((theirs_ref, 1 - spot_ref[0]), (mine_ref, spot_ref[0])):
        rows = pl.ds(pl.multiple_of(side * size, 16), size)
        ref[...] = add(kept_ref[rows, :], got_ref[rows, :]).astype(jnp.bfloat16)


def sum_body(_, *refs):
    *terms, out_ref = refs
    out_ref[...] = add(*[term[...] for term in terms]).astype(jnp.bfloat16)


def pair_sums_body(spot_ref, own_ref, partner_ref, *refs):
    *earlier, mine_ref, theirs_ref = refs
    before = jnp.zeros(own_ref.shape, jnp.float32)
    for k, ref in enumerate(earlier):
        from_before = lax.rem(spot_ref[1] // (2 << k), 2) == 1
        before = before + jnp.where(from_before, add(ref[...]), 0.0)
    own, partner = add(own_ref[...]), add(partner_ref[...])
    first = spot_ref[0] == 0
    both = before + (own + partner)
    mine_ref[...] = jnp.where(first, before + own, both).astype(jnp.bfloat16)
    theirs_ref[...] = jnp.where(first, both, before + partner).astype(jnp.bfloat16)


def running_states(keys, values, queries, residual, rows):
    devices, frames = lax.axis_size("space"), lax.axis_size("frame")
    core, frame = lax.axis_index("space"), lax.axis_index("frame")
    if devices != 2 or frames < 2 or frames & (frames - 1):
        (state,) = frame_states(jnp.zeros((1,), jnp.int32), keys, values, rows, 1)
        state = lax.psum(state.astype(jnp.float32), "space").astype(jnp.bfloat16)
        every = lax.all_gather(state, "frame").astype(jnp.float32)
        reached = (jnp.arange(frames) <= frame)[:, None, None]
        total = jnp.sum(jnp.where(reached, every, 0.0), axis=0).astype(jnp.bfloat16)
        return [total], jnp.zeros((1,), jnp.int32), edge_rows(queries, residual)
    swap = [(0, 1), (1, 0)]
    spot = jnp.stack([lax.rem(frame, 2), frame]).astype(jnp.int32)
    kept, sent, edge = frame_states(
        core.astype(jnp.int32)[None], keys, values, rows, 2, (queries, residual)
    )
    got = lax.ppermute(sent, "space", swap)
    quarter = (rows // 4, LANES)
    own, sent = small_kernel(split_sum_body, "split_sum", [quarter] * 2, spot, kept, got)
    edge, sent = lax.optimization_barrier((edge, sent))
    edge = lax.ppermute(edge, "space", swap)
    place = jnp.where(core == 0, queries.shape[0] + 1, 0).astype(jnp.int32)[None]
    partner = lax.ppermute(sent, "frame", [(f, f ^ 1) for f in range(frames)])
    (total,) = small_kernel(sum_body, "pair_sum", [quarter], spot, own, partner)
    earlier = []
    stride = 2
    while stride < frames:
        got = lax.ppermute(total, "frame", [(f, f ^ stride) for f in range(frames)])
        earlier.append(got)
        stride *= 2
        if stride < frames:
            (total,) = small_kernel(sum_body, "stride_sum", [quarter], spot, total, got)
    mine, theirs = small_kernel(
        pair_sums_body, "pair_sums", [quarter] * 2, spot, own, partner, *earlier
    )
    other = lax.ppermute(theirs, "frame", [(f, f ^ 1) for f in range(frames)])
    pieces = [mine, other, lax.ppermute(mine, "space", swap), lax.ppermute(other, "space", swap)]
    spots = [2 * c + p for c in (core, 1 - core) for p in (spot[0], 1 - spot[0])]
    return pieces, jnp.stack(spots).astype(jnp.int32), (edge, place)


def on_device(queries, keys, values, residual, attn_gain, value_taps, gate_taps):
    frames, rows, width, dim = queries.shape
    tokens = frames * rows * width
    flat = lambda a: a.reshape(tokens, dim)
    state_rows = cdiv(cdiv(dim, LANES) * HEAD_DIM, 64) * 64
    pieces, spots, (edge, place) = running_states(
        flat(keys),
        flat(values),
        queries.reshape(rows, width, dim),
        residual.reshape(rows, width, dim),
        state_rows,
    )
    out = mix(
        place, spots, flat(queries), flat(residual), edge, attn_gain[None], value_taps, gate_taps,
        pieces, rows, width,
    )
    return out.reshape(frames, rows, width, dim)


def solution(mesh):
    placed = P(("groups", "frame"), "space", None, None)
    return jax.shard_map(
        on_device,
        mesh=mesh,
        in_specs=(placed, placed, placed, placed, P(), P(), P()),
        out_specs=placed,
        check_vma=False,
    )
```

```python
import functools
import math

import jax
import jax.numpy as jnp
from jax import lax
from jax.experimental import pallas as pl
from jax.experimental.pallas import tpu as pltpu
from jax.sharding import PartitionSpec as P

HEAD_DIM = 112
LANES = 128
GROUP = math.lcm(HEAD_DIM, LANES)
TILES = GROUP // LANES


def cdiv(a, b):
    return -(-a // b)


def in_hbm(array):
    return pltpu.with_memory_space_constraint(array, pltpu.HBM)


def lane_iota(shape):
    return lax.broadcasted_iota(jnp.int32, shape, len(shape) - 1)


def tile_heads(j, lanes):
    lo, hi = j * LANES, min((j + 1) * LANES, lanes)
    heads = range(lo // HEAD_DIM, cdiv(hi, HEAD_DIM))
    return [(h, max(h * HEAD_DIM - lo, 0), min((h + 1) * HEAD_DIM - lo, LANES)) for h in heads]


def spans(lanes):
    count = cdiv(lanes, LANES)
    result = []
    for j in range(0, count, 2):
        tiles = list(range(j, min(j + 2, count)))
        first = tile_heads(tiles[0], lanes)[0][0] * HEAD_DIM // LANES
        last = cdiv((tile_heads(tiles[-1], lanes)[-1][0] + 1) * HEAD_DIM, LANES)
        result.append((tiles, first, last))
    return result


def by_group(dim, body):
    full, rest = divmod(dim, GROUP)
    if full:
        pl.when(pl.program_id(0) < full)(lambda: body(GROUP))
    if rest:
        pl.when(pl.program_id(0) >= full)(lambda: body(rest))


def state_kernel(dim, with_edge, spot_ref, keys_ref, values_ref, *refs):
    step = pl.program_id(0)
    *refs, turned, whole, semaphores = refs
    if with_edge:
        *sources, edge_ref = refs[:2] + refs[-1:]
        parts = refs[2:-1]
        row = (sources[0].shape[0] - 1) * (1 - lax.axis_index("space"))
        copies = [
            pltpu.make_async_copy(source.at[row], edge_ref.at[k, 0], semaphores.at[k])
            for k, source in enumerate(sources)
        ]

        @pl.when(step == 0)
        def _():
            for copy in copies:
                copy.start()

    else:
        parts = refs

    def body(lanes):
        turned[...] = jnp.maximum(keys_ref[...], 0).T
        lane = lane_iota((HEAD_DIM, LANES))
        for tiles, _, _ in spans(lanes):
            begin = tile_heads(tiles[0], lanes)[0][0]
            end = tile_heads(tiles[-1], lanes)[-1][0] + 1
            product = jnp.dot(
                turned[begin * HEAD_DIM : end * HEAD_DIM, :],
                values_ref[:, tiles[0] * LANES : (tiles[-1] + 1) * LANES],
                preferred_element_type=jnp.float32,
            )
            for side, j in enumerate(tiles):
                total = jnp.zeros((HEAD_DIM, LANES), jnp.float32)
                for h, lo, hi in tile_heads(j, lanes):
                    part = product[
                        (h - begin) * HEAD_DIM : (h - begin + 1) * HEAD_DIM,
                        side * LANES : (side + 1) * LANES,
                    ]
                    total = jnp.where((lane >= lo) & (lane < hi), part, total)
                row = pl.multiple_of((step * TILES + j) * HEAD_DIM, 16)
                whole[pl.ds(row, HEAD_DIM), :] = total.astype(jnp.bfloat16)

    by_group(dim, body)

    @pl.when(step == pl.num_programs(0) - 1)
    def _():
        used = cdiv(dim, LANES) * HEAD_DIM
        if used < whole.shape[0]:
            whole[used:, :] = jnp.zeros((whole.shape[0] - used, LANES), jnp.bfloat16)
        for k, part in enumerate(parts):
            size = part.shape[0]
            row = pl.multiple_of(lax.rem(spot_ref[0] + k, len(parts)) * size, 16)
            part[...] = whole[pl.ds(row, size), :]
        if with_edge:
            for copy in copies:
                copy.wait()


def frame_states(spot, keys, values, rows, parts, edged=()):
    tokens, dim = keys.shape
    part = (rows // parts, LANES)
    block = pl.BlockSpec((tokens, GROUP), lambda g: (0, g))
    return pl.pallas_call(
        functools.partial(state_kernel, dim, bool(edged)),
        out_shape=[pltpu.VMEM(part, jnp.bfloat16)] * parts
        + [pltpu.VMEM((len(edged), 1, *edged[0].shape[1:]), jnp.bfloat16) for _ in edged[:1]],
        grid=(cdiv(dim, GROUP),),
        in_specs=[pl.BlockSpec(memory_space=pltpu.SMEM), block, block]
        + [pl.BlockSpec(memory_space=pl.ANY)] * len(edged),
        out_specs=[pl.BlockSpec(part, lambda g: (0, 0))] * parts
        + [pl.BlockSpec(memory_space=pl.ANY) for _ in edged[:1]],
        scratch_shapes=[
            pltpu.VMEM((GROUP, tokens), jnp.bfloat16),
            pltpu.VMEM((rows, LANES), jnp.bfloat16),
            pltpu.SemaphoreType.DMA((2,)),
        ],
        compiler_params=pltpu.CompilerParams(vmem_limit_bytes=60 * 2**20),
        cost_estimate=pl.CostEstimate(
            flops=2 * tokens * dim * HEAD_DIM, bytes_accessed=4 * tokens * dim, transcendentals=0
        ),
        name="frame_states",
    )(spot, in_hbm(keys), in_hbm(values), *[in_hbm(array) for array in edged])


def mix_kernel(
    dim, rows, width, edges,
    place_ref, spots_ref, queries_ref, residual_ref, edge_ref, gain_ref, vtaps_ref, gtaps_ref, *refs,
):
    *pieces, out_ref, states, features, weights, same, numer, squares, windows, diagonals = refs
    step = pl.program_id(0)
    tokens = rows * width
    total = tokens + edges * width

    @pl.when(pl.program_id(0) == 0)
    def _():
        weights[...] = jnp.zeros_like(weights)
        same[...] = jnp.zeros_like(same)
        lane = lane_iota((HEAD_DIM, LANES))
        for number, (tiles, first, _) in enumerate(spans(min(GROUP, dim))):
            for side, j in enumerate(tiles):
                for h, lo, hi in tile_heads(j, GROUP):
                    start = h * HEAD_DIM - first * LANES
                    block = jnp.where((lane >= lo) & (lane < hi), 1.0, 0.0)
                    same[
                        number, start : start + HEAD_DIM, side * LANES : (side + 1) * LANES
                    ] = block.astype(jnp.bfloat16)
        diagonals[...] = jnp.zeros_like(diagonals)
        for k, piece in enumerate(pieces):
            size = piece.shape[0]
            states[pl.ds(pl.multiple_of(spots_ref[k] * size, 16), size), :] = piece[...]

    zero = jnp.zeros((), jnp.bfloat16)
    column = lax.broadcasted_iota(jnp.int32, (width, LANES), 0)
    lane = lane_iota((HEAD_DIM, LANES))

    diagonal = lax.broadcasted_iota(jnp.int32, (LANES, LANES), 0) == lane_iota((LANES, LANES))

    def store_windows(mixed, row, slot):
        here = slice(row * width, (row + 1) * width)
        before = jnp.where(column == 0, 0.0, pltpu.roll(mixed, 1, 0))
        after = jnp.where(column == width - 1, 0.0, pltpu.roll(mixed, width - 1, 0))
        for i, window in enumerate((before, mixed, after)):
            windows[slot, here, i * LANES : (i + 1) * LANES] = window.astype(jnp.bfloat16)

    def body(lanes):
        count = cdiv(lanes, LANES)
        end = count * LANES
        inside = lane_iota((1, end)) < lanes

        def feature(queries):
            queries = jnp.maximum(queries, zero)
            return queries if lanes == end else jnp.where(inside, queries, zero)

        features[:tokens, :end] = feature(queries_ref[:, :end])
        for e in range(edges):
            features[tokens + e * width : tokens + (e + 1) * width, :end] = feature(
                edge_ref[0, e, :, :end]
            )
        for number, (tiles, first, last) in enumerate(spans(lanes)):
            for side, j in enumerate(tiles):
                row = pl.multiple_of((step * TILES + j) * HEAD_DIM, 16)
                state = states[pl.ds(row, HEAD_DIM), :].astype(jnp.float32)
                for h, lo, hi in tile_heads(j, lanes):
                    start = h * HEAD_DIM - first * LANES
                    block = jnp.where((lane >= lo) & (lane < hi), state, 0.0)
                    weights[
                        number, start : start + HEAD_DIM, side * LANES : (side + 1) * LANES
                    ] = block.astype(jnp.bfloat16)
            depth, wide = (last - first) * LANES, len(tiles) * LANES
            product = jnp.dot(
                features[:, first * LANES : last * LANES],
                weights[number, :depth, :wide],
                preferred_element_type=jnp.float32,
            )
            here = slice(tiles[0] * LANES, tiles[0] * LANES + wide)
            numer[:, here] = product
            squares[:, here] = (product * product).astype(jnp.bfloat16)

        for number, (tiles, first, last) in enumerate(spans(lanes)):
            depth, wide = (last - first) * LANES, len(tiles) * LANES
            sums = jnp.dot(
                squares[:, first * LANES : last * LANES],
                same[number, :depth, :wide],
                preferred_element_type=jnp.float32,
            )
            scale = lax.rsqrt(sums * (1.0 / HEAD_DIM) + 1e-06)
            for side, j in enumerate(tiles):
                here = slice(j * LANES, (j + 1) * LANES)
                gain = gain_ref[:, here]

                def mixed(source, residual, side=side, here=here, gain=gain):
                    normed = numer[source, here] * scale[source, side * LANES : (side + 1) * LANES]
                    value = residual.astype(jnp.float32) + normed * gain
                    if lanes < here.stop:
                        value = jnp.where(lane_iota(value.shape) < lanes - here.start, value, 0.0)
                    return value

                slot = j % 2
                for row in range(rows):
                    source = slice(row * width, (row + 1) * width)
                    store_windows(mixed(source, residual_ref[source, here]), row + 1, slot)
                outside = [None, None]
                for e in range(edges):
                    source = slice(tokens + e * width, tokens + (e + 1) * width)
                    value = mixed(source, edge_ref[1, e, :, here])
                    for k, row in enumerate((0, rows + 1)):
                        part = jnp.where(place_ref[e] == row, value, 0.0)
                        outside[k] = part if outside[k] is None else outside[k] + part
                for k, row in enumerate((0, rows + 1)):
                    store_windows(outside[k], row, slot)
                for tap in range(9):
                    for k, (ref, factor) in enumerate(((vtaps_ref, 1.0), (gtaps_ref, 0.5))):
                        block = jnp.where(diagonal, ref[tap : tap + 1, here] * factor, 0.0)
                        diagonals[
                            slot, tap * LANES : (tap + 1) * LANES, k * LANES : (k + 1) * LANES
                        ] = block.astype(jnp.bfloat16)
                conv = jnp.zeros((tokens, 2 * LANES), jnp.float32)
                for i in range(3):
                    conv = conv + jnp.dot(
                        windows[slot, i * width : i * width + tokens, :],
                        diagonals[slot, 3 * i * LANES : 3 * (i + 1) * LANES, :],
                        preferred_element_type=jnp.float32,
                    )
                conv_v, half_g = conv[:, :LANES], conv[:, LANES:]
                gate = half_g + half_g * jnp.tanh(half_g)
                center = windows[slot, width : width + tokens, LANES : 2 * LANES]
                out_ref[:, here] = (center.astype(jnp.float32) + conv_v * gate).astype(jnp.bfloat16)

    by_group(dim, body)


def mix(place, spots, queries, residual, edge, gain, value_taps, gate_taps, pieces, rows, width):
    tokens, dim = queries.shape
    edges = edge.shape[1]
    total = tokens + edges * width
    pairs = spans(min(GROUP, dim))
    depth = max(last - first for _, first, last in pairs) * LANES
    block = pl.BlockSpec((tokens, GROUP), lambda g: (0, g))
    taps = pl.BlockSpec((value_taps.shape[0], GROUP), lambda g: (0, g))
    return pl.pallas_call(
        functools.partial(mix_kernel, dim, rows, width, edges),
        out_shape=jax.ShapeDtypeStruct((tokens, dim), jnp.bfloat16),
        grid=(cdiv(dim, GROUP),),
        in_specs=[
            pl.BlockSpec(memory_space=pltpu.SMEM),
            pl.BlockSpec(memory_space=pltpu.SMEM),
            block,
            block,
            pl.BlockSpec((2, edges, width, GROUP), lambda g: (0, 0, 0, g)),
            pl.BlockSpec((1, GROUP), lambda g: (0, g)),
            taps,
            taps,
        ]
        + [pl.BlockSpec(piece.shape, lambda g: (0, 0)) for piece in pieces],
        out_specs=block,
        scratch_shapes=[
            pltpu.VMEM((sum(piece.shape[0] for piece in pieces), LANES), jnp.bfloat16),
            pltpu.VMEM((total, GROUP), jnp.bfloat16),
            pltpu.VMEM((len(pairs), depth, 2 * LANES), jnp.bfloat16),
            pltpu.VMEM((len(pairs), depth, 2 * LANES), jnp.bfloat16),
            pltpu.VMEM((total, GROUP), jnp.float32),
            pltpu.VMEM((total, GROUP), jnp.bfloat16),
            pltpu.VMEM((2, (rows + 2) * width, 3 * LANES), jnp.bfloat16),
            pltpu.VMEM((2, 9 * LANES, 2 * LANES), jnp.bfloat16),
        ],
        compiler_params=pltpu.CompilerParams(vmem_limit_bytes=36 * 2**20),
        cost_estimate=pl.CostEstimate(
            flops=60 * tokens * dim, bytes_accessed=6 * tokens * dim, transcendentals=2 * tokens * dim
        ),
        name="mix",
    )(place, spots, in_hbm(queries), in_hbm(residual), edge, gain, value_taps, gate_taps, *pieces)


def edge_rows(queries, residual):
    devices, rows = lax.axis_size("space"), queries.shape[0]
    up = [(i, i + 1) for i in range(devices - 1)]
    down = [(j, i) for i, j in up]
    both = jnp.stack([queries, residual])
    before = lax.ppermute(both[:, rows - 1 :], "space", up)
    after = lax.ppermute(both[:, :1], "space", down)
    return jnp.concatenate([before, after], axis=1), jnp.array([0, rows + 1], jnp.int32)


def small_kernel(body, name, outs, scalars, *arrays):
    return pl.pallas_call(
        body,
        out_shape=[pltpu.VMEM(shape, jnp.bfloat16) for shape in outs],
        in_specs=[pl.BlockSpec(memory_space=pltpu.SMEM)]
        + [pl.BlockSpec(memory_space=pltpu.VMEM)] * len(arrays),
        out_specs=[pl.BlockSpec(memory_space=pltpu.VMEM)] * len(outs),
        compiler_params=pltpu.CompilerParams(vmem_limit_bytes=4 * 2**20),
        name=name,
    )(scalars, *arrays)


def add(*values):
    total = values[0].astype(jnp.float32)
    for value in values[1:]:
        total = total + value.astype(jnp.float32)
    return total


def split_sum_body(spot_ref, kept_ref, got_ref, mine_ref, theirs_ref):
    size = mine_ref.shape[0]
    for ref, side in ((theirs_ref, 1 - spot_ref[0]), (mine_ref, spot_ref[0])):
        rows = pl.ds(pl.multiple_of(side * size, 16), size)
        ref[...] = add(kept_ref[rows, :], got_ref[rows, :]).astype(jnp.bfloat16)


def sum_body(_, *refs):
    *terms, out_ref = refs
    out_ref[...] = add(*[term[...] for term in terms]).astype(jnp.bfloat16)


def pair_sums_body(spot_ref, own_ref, partner_ref, *refs):
    *earlier, mine_ref, theirs_ref = refs
    before = jnp.zeros(own_ref.shape, jnp.float32)
    for k, ref in enumerate(earlier):
        from_before = lax.rem(spot_ref[1] // (2 << k), 2) == 1
        before = before + jnp.where(from_before, add(ref[...]), 0.0)
    own, partner = add(own_ref[...]), add(partner_ref[...])
    first = spot_ref[0] == 0
    both = before + (own + partner)
    mine_ref[...] = jnp.where(first, before + own, both).astype(jnp.bfloat16)
    theirs_ref[...] = jnp.where(first, both, before + partner).astype(jnp.bfloat16)


def running_states(keys, values, queries, residual, rows):
    devices, frames = lax.axis_size("space"), lax.axis_size("frame")
    core, frame = lax.axis_index("space"), lax.axis_index("frame")
    if devices != 2 or frames < 2 or frames & (frames - 1):
        (state,) = frame_states(jnp.zeros((1,), jnp.int32), keys, values, rows, 1)
        state = lax.psum(state.astype(jnp.float32), "space").astype(jnp.bfloat16)
        every = lax.all_gather(state, "frame").astype(jnp.float32)
        reached = (jnp.arange(frames) <= frame)[:, None, None]
        total = jnp.sum(jnp.where(reached, every, 0.0), axis=0).astype(jnp.bfloat16)
        return [total], jnp.zeros((1,), jnp.int32), edge_rows(queries, residual)
    swap = [(0, 1), (1, 0)]
    spot = jnp.stack([lax.rem(frame, 2), frame]).astype(jnp.int32)
    kept, sent, edge = frame_states(
        core.astype(jnp.int32)[None], keys, values, rows, 2, (queries, residual)
    )
    got = lax.ppermute(sent, "space", swap)
    quarter = (rows // 4, LANES)
    own, sent = small_kernel(split_sum_body, "split_sum", [quarter] * 2, spot, kept, got)
    edge, sent = lax.optimization_barrier((edge, sent))
    edge = lax.ppermute(edge, "space", swap)
    place = jnp.where(core == 0, queries.shape[0] + 1, 0).astype(jnp.int32)[None]
    partner = lax.ppermute(sent, "frame", [(f, f ^ 1) for f in range(frames)])
    (total,) = small_kernel(sum_body, "pair_sum", [quarter], spot, own, partner)
    earlier = []
    stride = 2
    while stride < frames:
        got = lax.ppermute(total, "frame", [(f, f ^ stride) for f in range(frames)])
        earlier.append(got)
        stride *= 2
        if stride < frames:
            (total,) = small_kernel(sum_body, "stride_sum", [quarter], spot, total, got)
    mine, theirs = small_kernel(
        pair_sums_body, "pair_sums", [quarter] * 2, spot, own, partner, *earlier
    )
    other = lax.ppermute(theirs, "frame", [(f, f ^ 1) for f in range(frames)])
    pieces = [mine, other, lax.ppermute(mine, "space", swap), lax.ppermute(other, "space", swap)]
    spots = [2 * c + p for c in (core, 1 - core) for p in (spot[0], 1 - spot[0])]
    return pieces, jnp.stack(spots).astype(jnp.int32), (edge, place)


def on_device(queries, keys, values, residual, attn_gain, value_taps, gate_taps):
    frames, rows, width, dim = queries.shape
    tokens = frames * rows * width
    flat = lambda a: a.reshape(tokens, dim)
    state_rows = cdiv(cdiv(dim, LANES) * HEAD_DIM, 64) * 64
    pieces, spots, (edge, place) = running_states(
        flat(keys),
        flat(values),
        queries.reshape(rows, width, dim),
        residual.reshape(rows, width, dim),
        state_rows,
    )
    out = mix(
        place, spots, flat(queries), flat(residual), edge, attn_gain[None], value_taps, gate_taps,
        pieces, rows, width,
    )
    return out.reshape(frames, rows, width, dim)


def solution(mesh):
    placed = P(("groups", "frame"), "space", None, None)
    return jax.shard_map(
        on_device,
        mesh=mesh,
        in_specs=(placed, placed, placed, placed, P(), P(), P()),
        out_specs=placed,
        check_vma=False,
    )
```

```python
import functools
import math

import jax
import jax.numpy as jnp
from jax import lax
from jax.experimental import pallas as pl
from jax.experimental.pallas import tpu as pltpu
from jax.sharding import PartitionSpec as P

HEAD_DIM = 112
LANES = 128
GROUP = math.lcm(HEAD_DIM, LANES)
TILES = GROUP // LANES


def cdiv(a, b):
    return -(-a // b)


def in_hbm(array):
    return pltpu.with_memory_space_constraint(array, pltpu.HBM)


def lane_iota(shape):
    return lax.broadcasted_iota(jnp.int32, shape, len(shape) - 1)


def tile_heads(j, lanes):
    lo, hi = j * LANES, min((j + 1) * LANES, lanes)
    heads = range(lo // HEAD_DIM, cdiv(hi, HEAD_DIM))
    return [(h, max(h * HEAD_DIM - lo, 0), min((h + 1) * HEAD_DIM - lo, LANES)) for h in heads]


def spans(lanes):
    count = cdiv(lanes, LANES)
    result = []
    for j in range(0, count, 2):
        tiles = list(range(j, min(j + 2, count)))
        first = tile_heads(tiles[0], lanes)[0][0] * HEAD_DIM // LANES
        last = cdiv((tile_heads(tiles[-1], lanes)[-1][0] + 1) * HEAD_DIM, LANES)
        result.append((tiles, first, last))
    return result


def by_group(dim, groups, body):
    full, rest = divmod(dim, GROUP)
    group = pl.program_id(0) + groups[0]
    if groups[0] < full:
        pl.when(group < full)(lambda: body(GROUP))
    if rest and groups[-1] == full:
        pl.when(group == full)(lambda: body(rest))


def chunks(dim):
    count = cdiv(dim, GROUP)
    return [range(0, 1), range(1, count)] if count > 1 else [range(0, 1)]


def state_rows(dim, groups):
    lanes = min(dim, (groups[-1] + 1) * GROUP) - groups[0] * GROUP
    return cdiv(lanes, LANES) * HEAD_DIM


def state_kernel(dim, groups, with_edge, spot_ref, keys_ref, values_ref, *refs):
    step = pl.program_id(0)
    *refs, turned, whole, semaphores = refs
    if with_edge:
        *sources, edge_ref = refs[:2] + refs[-1:]
        parts = refs[2:-1]
        row = (sources[0].shape[0] - 1) * (1 - lax.axis_index("space"))
        copies = [
            pltpu.make_async_copy(source.at[row], edge_ref.at[k, 0], semaphores.at[k])
            for k, source in enumerate(sources)
        ]

        @pl.when(step == 0)
        def _():
            for copy in copies:
                copy.start()

    else:
        parts = refs

    def body(lanes):
        turned[...] = jnp.maximum(keys_ref[...], 0).T
        lane = lane_iota((HEAD_DIM, LANES))
        for tiles, _, _ in spans(lanes):
            begin = tile_heads(tiles[0], lanes)[0][0]
            end = tile_heads(tiles[-1], lanes)[-1][0] + 1
            product = jnp.dot(
                turned[begin * HEAD_DIM : end * HEAD_DIM, :],
                values_ref[:, tiles[0] * LANES : (tiles[-1] + 1) * LANES],
                preferred_element_type=jnp.float32,
            )
            for side, j in enumerate(tiles):
                total = jnp.zeros((HEAD_DIM, LANES), jnp.float32)
                for h, lo, hi in tile_heads(j, lanes):
                    part = product[
                        (h - begin) * HEAD_DIM : (h - begin + 1) * HEAD_DIM,
                        side * LANES : (side + 1) * LANES,
                    ]
                    total = jnp.where((lane >= lo) & (lane < hi), part, total)
                row = pl.multiple_of((step * TILES + j) * HEAD_DIM, 16)
                whole[pl.ds(row, HEAD_DIM), :] = total.astype(jnp.bfloat16)

    by_group(dim, groups, body)

    @pl.when(step == pl.num_programs(0) - 1)
    def _():
        used = state_rows(dim, groups)
        if used < whole.shape[0]:
            whole[used:, :] = jnp.zeros((whole.shape[0] - used, LANES), jnp.bfloat16)
        for k, part in enumerate(parts):
            size = part.shape[0]
            row = pl.multiple_of(lax.rem(spot_ref[0] + k, len(parts)) * size, 16)
            part[...] = whole[pl.ds(row, size), :]
        if with_edge:
            for copy in copies:
                copy.wait()


def frame_states(groups, spot, keys, values, parts, edged=()):
    tokens, dim = keys.shape
    rows = cdiv(state_rows(dim, groups), 64) * 64
    part = (rows // parts, LANES)
    block = pl.BlockSpec((tokens, GROUP), lambda g: (0, g + groups[0]))
    return pl.pallas_call(
        functools.partial(state_kernel, dim, groups, bool(edged)),
        out_shape=[pltpu.VMEM(part, jnp.bfloat16)] * parts
        + [pltpu.VMEM((len(edged), 1, *edged[0].shape[1:]), jnp.bfloat16) for _ in edged[:1]],
        grid=(len(groups),),
        in_specs=[pl.BlockSpec(memory_space=pltpu.SMEM), block, block]
        + [pl.BlockSpec(memory_space=pl.ANY)] * len(edged),
        out_specs=[pl.BlockSpec(part, lambda g: (0, 0))] * parts
        + [pl.BlockSpec(memory_space=pl.ANY) for _ in edged[:1]],
        scratch_shapes=[
            pltpu.VMEM((GROUP, tokens), jnp.bfloat16),
            pltpu.VMEM((rows, LANES), jnp.bfloat16),
            pltpu.SemaphoreType.DMA((2,)),
        ],
        compiler_params=pltpu.CompilerParams(vmem_limit_bytes=60 * 2**20),
        cost_estimate=pl.CostEstimate(
            flops=2 * tokens * len(groups) * GROUP * HEAD_DIM,
            bytes_accessed=4 * tokens * len(groups) * GROUP,
            transcendentals=0,
        ),
        name="frame_states",
    )(spot, in_hbm(keys), in_hbm(values), *[in_hbm(array) for array in edged])


def mix_kernel(
    dim, groups, rows, width, edges, earlier,
    place_ref, spots_ref, queries_ref, residual_ref, edge_ref, gain_ref, vtaps_ref, gtaps_ref, *refs,
):
    *pieces, out_ref, states, features, weights, same, numer, squares, shifted = refs
    pieces = pieces[: len(pieces) - earlier]
    step = pl.program_id(0)
    tokens = rows * width
    total = tokens + edges * width

    @pl.when(pl.program_id(0) == 0)
    def _():
        weights[...] = jnp.zeros_like(weights)
        same[...] = jnp.zeros_like(same)
        lane = lane_iota((HEAD_DIM, LANES))
        for number, (tiles, first, _) in enumerate(spans(min(GROUP, dim))):
            for side, j in enumerate(tiles):
                for h, lo, hi in tile_heads(j, GROUP):
                    start = h * HEAD_DIM - first * LANES
                    block = jnp.where((lane >= lo) & (lane < hi), 1.0, 0.0)
                    same[
                        number, start : start + HEAD_DIM, side * LANES : (side + 1) * LANES
                    ] = block.astype(jnp.bfloat16)
        for row in (0, rows + 1):
            shifted[:, row] = jnp.zeros((3, width, LANES), jnp.float32)
        for k, piece in enumerate(pieces):
            size = piece.shape[0]
            states[pl.ds(pl.multiple_of(spots_ref[k] * size, 16), size), :] = piece[...]

    zero = jnp.zeros((), jnp.bfloat16)
    column = lax.broadcasted_iota(jnp.int32, (width, LANES), 0)
    lane = lane_iota((HEAD_DIM, LANES))

    def store_shifted(mixed, row):
        mixed = mixed.astype(jnp.bfloat16).astype(jnp.float32)
        shifted[1, row] = mixed
        shifted[0, row] = jnp.where(column == 0, 0.0, pltpu.roll(mixed, 1, 0))
        shifted[2, row] = jnp.where(column == width - 1, 0.0, pltpu.roll(mixed, width - 1, 0))

    def body(lanes):
        count = cdiv(lanes, LANES)
        end = count * LANES
        inside = lane_iota((1, end)) < lanes

        def feature(queries):
            queries = jnp.maximum(queries, zero)
            return queries if lanes == end else jnp.where(inside, queries, zero)

        features[:tokens, :end] = feature(queries_ref[:, :end])
        for e in range(edges):
            features[tokens + e * width : tokens + (e + 1) * width, :end] = feature(
                edge_ref[0, e, :, :end]
            )
        for number, (tiles, first, last) in enumerate(spans(lanes)):
            for side, j in enumerate(tiles):
                row = pl.multiple_of((step * TILES + j) * HEAD_DIM, 16)
                state = states[pl.ds(row, HEAD_DIM), :].astype(jnp.float32)
                for h, lo, hi in tile_heads(j, lanes):
                    start = h * HEAD_DIM - first * LANES
                    block = jnp.where((lane >= lo) & (lane < hi), state, 0.0)
                    weights[
                        number, start : start + HEAD_DIM, side * LANES : (side + 1) * LANES
                    ] = block.astype(jnp.bfloat16)
            depth, wide = (last - first) * LANES, len(tiles) * LANES
            product = jnp.dot(
                features[:, first * LANES : last * LANES],
                weights[number, :depth, :wide],
                preferred_element_type=jnp.float32,
            )
            here = slice(tiles[0] * LANES, tiles[0] * LANES + wide)
            numer[:, here] = product
            squares[:, here] = (product * product).astype(jnp.bfloat16)

        for number, (tiles, first, last) in enumerate(spans(lanes)):
            depth, wide = (last - first) * LANES, len(tiles) * LANES
            sums = jnp.dot(
                squares[:, first * LANES : last * LANES],
                same[number, :depth, :wide],
                preferred_element_type=jnp.float32,
            )
            here = slice(tiles[0] * LANES, tiles[0] * LANES + wide)
            scale = lax.rsqrt(sums * (1.0 / HEAD_DIM) + 1e-06)
            numer[:, here] = numer[:, here] * scale * gain_ref[:, here]

        for j in range(count):
            here = slice(j * LANES, (j + 1) * LANES)
            for row in range(rows):
                source = slice(row * width, (row + 1) * width)
                store_shifted(
                    residual_ref[source, here].astype(jnp.float32) + numer[source, here], row + 1
                )
            for e in range(edges):
                source = slice(tokens + e * width, tokens + (e + 1) * width)
                store_shifted(
                    edge_ref[1, e, :, here].astype(jnp.float32) + numer[source, here], place_ref[e]
                )

            def convolve(row, carry, here=here):
                conv_v = jnp.zeros((width, LANES), jnp.float32)
                half_g = jnp.zeros((width, LANES), jnp.float32)
                for tap_row in range(3):
                    for tap_col in range(3):
                        window = shifted[tap_col, row + tap_row]
                        tap = 3 * tap_row + tap_col
                        conv_v = conv_v + vtaps_ref[tap : tap + 1, here] * window
                        half_g = half_g + (0.5 * gtaps_ref[tap : tap + 1, here]) * window
                gate = half_g + half_g * jnp.tanh(half_g)
                result = shifted[1, row + 1] + conv_v * gate
                out_ref[pl.ds(pl.multiple_of(row * width, width), width), here] = result.astype(
                    jnp.bfloat16
                )
                return carry

            lax.fori_loop(0, rows, convolve, 0)

    by_group(dim, groups, body)


def mix(groups, out, place, spots, queries, residual, edge, gain, value_taps, gate_taps, pieces, rows, width):
    tokens, dim = queries.shape
    edges = edge.shape[1]
    total = tokens + edges * width
    pairs = spans(min(GROUP, dim))
    depth = max(last - first for _, first, last in pairs) * LANES
    block = pl.BlockSpec((tokens, GROUP), lambda g: (0, g + groups[0]))
    taps = pl.BlockSpec((value_taps.shape[0], GROUP), lambda g: (0, g + groups[0]))
    here = tokens * len(groups) * GROUP
    first = [] if out is None else [out]
    return pl.pallas_call(
        functools.partial(mix_kernel, dim, groups, rows, width, edges, len(first)),
        out_shape=jax.ShapeDtypeStruct((tokens, dim), jnp.bfloat16),
        grid=(len(groups),),
        in_specs=[
            pl.BlockSpec(memory_space=pltpu.SMEM),
            pl.BlockSpec(memory_space=pltpu.SMEM),
            block,
            block,
            pl.BlockSpec((2, edges, width, GROUP), lambda g: (0, 0, 0, g + groups[0])),
            pl.BlockSpec((1, GROUP), lambda g: (0, g + groups[0])),
            taps,
            taps,
        ]
        + [pl.BlockSpec(piece.shape, lambda g: (0, 0)) for piece in pieces]
        + [pl.BlockSpec(memory_space=pl.ANY)] * len(first),
        input_output_aliases={8 + len(pieces): 0} if first else {},
        out_specs=block,
        scratch_shapes=[
            pltpu.VMEM((sum(piece.shape[0] for piece in pieces), LANES), jnp.bfloat16),
            pltpu.VMEM((total, GROUP), jnp.bfloat16),
            pltpu.VMEM((len(pairs), depth, 2 * LANES), jnp.bfloat16),
            pltpu.VMEM((len(pairs), depth, 2 * LANES), jnp.bfloat16),
            pltpu.VMEM((total, GROUP), jnp.float32),
            pltpu.VMEM((total, GROUP), jnp.bfloat16),
            pltpu.VMEM((3, rows + 2, width, LANES), jnp.float32),
        ],
        compiler_params=pltpu.CompilerParams(vmem_limit_bytes=36 * 2**20),
        cost_estimate=pl.CostEstimate(
            flops=1000 * here, bytes_accessed=6 * here, transcendentals=2 * here
        ),
        name="mix",
    )(place, spots, in_hbm(queries), in_hbm(residual), edge, gain, value_taps, gate_taps, *pieces, *first)


def edge_rows(queries, residual):
    devices, rows = lax.axis_size("space"), queries.shape[0]
    up = [(i, i + 1) for i in range(devices - 1)]
    down = [(j, i) for i, j in up]
    both = jnp.stack([queries, residual])
    before = lax.ppermute(both[:, rows - 1 :], "space", up)
    after = lax.ppermute(both[:, :1], "space", down)
    return jnp.concatenate([before, after], axis=1), jnp.array([0, rows + 1], jnp.int32)


def small_kernel(body, name, outs, scalars, *arrays):
    return pl.pallas_call(
        body,
        out_shape=[pltpu.VMEM(shape, jnp.bfloat16) for shape in outs],
        in_specs=[pl.BlockSpec(memory_space=pltpu.SMEM)]
        + [pl.BlockSpec(memory_space=pltpu.VMEM)] * len(arrays),
        out_specs=[pl.BlockSpec(memory_space=pltpu.VMEM)] * len(outs),
        compiler_params=pltpu.CompilerParams(vmem_limit_bytes=4 * 2**20),
        name=name,
    )(scalars, *arrays)


def add(*values):
    total = values[0].astype(jnp.float32)
    for value in values[1:]:
        total = total + value.astype(jnp.float32)
    return total


def split_sum_body(spot_ref, kept_ref, got_ref, mine_ref, theirs_ref):
    size = mine_ref.shape[0]
    for ref, side in ((theirs_ref, 1 - spot_ref[0]), (mine_ref, spot_ref[0])):
        rows = pl.ds(pl.multiple_of(side * size, 16), size)
        ref[...] = add(kept_ref[rows, :], got_ref[rows, :]).astype(jnp.bfloat16)


def sum_body(_, *refs):
    *terms, out_ref = refs
    out_ref[...] = add(*[term[...] for term in terms]).astype(jnp.bfloat16)


def pair_sums_body(spot_ref, own_ref, partner_ref, *refs):
    *earlier, mine_ref, theirs_ref = refs
    before = jnp.zeros(own_ref.shape, jnp.float32)
    for k, ref in enumerate(earlier):
        from_before = lax.rem(spot_ref[1] // (2 << k), 2) == 1
        before = before + jnp.where(from_before, add(ref[...]), 0.0)
    own, partner = add(own_ref[...]), add(partner_ref[...])
    first = spot_ref[0] == 0
    both = before + (own + partner)
    mine_ref[...] = jnp.where(first, before + own, both).astype(jnp.bfloat16)
    theirs_ref[...] = jnp.where(first, both, before + partner).astype(jnp.bfloat16)


def running_states(keys, values, queries, residual):
    devices, frames = lax.axis_size("space"), lax.axis_size("frame")
    core, frame = lax.axis_index("space"), lax.axis_index("frame")
    ranges = chunks(keys.shape[-1])
    if devices != 2 or frames < 2 or frames & (frames - 1):
        reached = (jnp.arange(frames) <= frame)[:, None, None]
        results = []
        for groups in ranges:
            (state,) = frame_states(groups, jnp.zeros((1,), jnp.int32), keys, values, 1)
            state = lax.psum(state.astype(jnp.float32), "space").astype(jnp.bfloat16)
            every = lax.all_gather(state, "frame").astype(jnp.float32)
            total = jnp.sum(jnp.where(reached, every, 0.0), axis=0).astype(jnp.bfloat16)
            results.append([total])
        return results, jnp.zeros((1,), jnp.int32), edge_rows(queries, residual)
    swap = [(0, 1), (1, 0)]
    exchange = lambda array, stride: lax.ppermute(
        array, "frame", [(f, f ^ stride) for f in range(frames)]
    )
    spot = jnp.stack([lax.rem(frame, 2), frame]).astype(jnp.int32)
    kept, own, partner, total, earlier, results = {}, {}, {}, {}, {}, []
    for c, groups in enumerate(ranges):
        kept[c], sent, *edge = frame_states(
            groups, core.astype(jnp.int32)[None], keys, values, 2, (queries, residual) if c == 0 else ()
        )
        if c == 0:
            (edges,) = edge
        got = lax.ppermute(sent, "space", swap)
        quarter = (got.shape[0] // 2, LANES)
        own[c], sent = small_kernel(
            split_sum_body, "split_sum", [quarter] * 2, spot, kept[c], got
        )
        if c == 0:
            edges, sent = lax.optimization_barrier((edges, sent))
            edges = lax.ppermute(edges, "space", swap)
        partner[c] = exchange(sent, 1)
        earlier[c] = []
    for c in own:
        (total[c],) = small_kernel(sum_body, "pair_sum", [own[c].shape], spot, own[c], partner[c])
    stride = 2
    while stride < frames:
        for c in own:
            got = exchange(total[c], stride)
            earlier[c].append(got)
            if stride * 2 < frames:
                (total[c],) = small_kernel(
                    sum_body, "stride_sum", [got.shape], spot, total[c], got
                )
        stride *= 2
    across = [
        (2 * f + c, 2 * (f ^ 1) + (1 - c)) for f in range(frames) for c in range(2)
    ]
    for c in own:
        mine, theirs = small_kernel(
            pair_sums_body, "pair_sums", [own[c].shape] * 2, spot, own[c], partner[c], *earlier[c]
        )
        results.append(
            [
                mine,
                lax.ppermute(mine, "space", swap),
                exchange(theirs, 1),
                lax.ppermute(theirs, ("frame", "space"), across),
            ]
        )
    parity = spot[0]
    spots = [2 * core + parity, 2 * (1 - core) + parity, 2 * core + 1 - parity, 3 - 2 * core - parity]
    place = jnp.where(core == 0, queries.shape[0] + 1, 0).astype(jnp.int32)[None]
    return results, jnp.stack(spots).astype(jnp.int32), (edges, place)


def on_device(queries, keys, values, residual, attn_gain, value_taps, gate_taps):
    frames, rows, width, dim = queries.shape
    tokens = frames * rows * width
    flat = lambda a: a.reshape(tokens, dim)
    results, spots, (edge, place) = running_states(
        flat(keys), flat(values), queries.reshape(rows, width, dim), residual.reshape(rows, width, dim)
    )
    out = None
    for groups, pieces in zip(chunks(dim), results):
        out = mix(
            groups, out, place, spots, flat(queries), flat(residual), edge, attn_gain[None],
            value_taps, gate_taps, pieces, rows, width,
        )
    return out.reshape(frames, rows, width, dim)


def solution(mesh):
    placed = P(("groups", "frame"), "space", None, None)
    return jax.shard_map(
        on_device,
        mesh=mesh,
        in_specs=(placed, placed, placed, placed, P(), P(), P()),
        out_specs=placed,
        check_vma=False,
    )
```

```python
import functools
import math

import jax
import jax.numpy as jnp
from jax import lax
from jax.experimental import pallas as pl
from jax.experimental.pallas import tpu as pltpu
from jax.sharding import PartitionSpec as P

HEAD_DIM = 112
LANES = 128
GROUP = math.lcm(HEAD_DIM, LANES)
TILES = GROUP // LANES


def cdiv(a, b):
    return -(-a // b)


def in_hbm(array):
    return pltpu.with_memory_space_constraint(array, pltpu.HBM)


def lane_iota(shape):
    return lax.broadcasted_iota(jnp.int32, shape, len(shape) - 1)


def tile_heads(j, lanes):
    lo, hi = j * LANES, min((j + 1) * LANES, lanes)
    heads = range(lo // HEAD_DIM, cdiv(hi, HEAD_DIM))
    return [(h, max(h * HEAD_DIM - lo, 0), min((h + 1) * HEAD_DIM - lo, LANES)) for h in heads]


def spans(lanes):
    count = cdiv(lanes, LANES)
    result = []
    for j in range(0, count, 2):
        tiles = list(range(j, min(j + 2, count)))
        first = tile_heads(tiles[0], lanes)[0][0] * HEAD_DIM // LANES
        last = cdiv((tile_heads(tiles[-1], lanes)[-1][0] + 1) * HEAD_DIM, LANES)
        result.append((tiles, first, last))
    return result


def by_group(dim, body):
    full, rest = divmod(dim, GROUP)
    if full:
        pl.when(pl.program_id(0) < full)(lambda: body(GROUP))
    if rest:
        pl.when(pl.program_id(0) >= full)(lambda: body(rest))


def state_kernel(dim, with_edge, spot_ref, keys_ref, values_ref, *refs):
    step = pl.program_id(0)
    *refs, turned, whole, semaphores = refs
    if with_edge:
        *sources, edge_ref = refs[:2] + refs[-1:]
        parts = refs[2:-1]
        row = (sources[0].shape[0] - 1) * (1 - lax.axis_index("space"))
        copies = [
            pltpu.make_async_copy(source.at[row], edge_ref.at[k, 0], semaphores.at[k])
            for k, source in enumerate(sources)
        ]

        @pl.when(step == 0)
        def _():
            for copy in copies:
                copy.start()

    else:
        parts = refs

    def body(lanes):
        turned[...] = jnp.maximum(keys_ref[...], 0).T
        lane = lane_iota((HEAD_DIM, LANES))
        for tiles, _, _ in spans(lanes):
            begin = tile_heads(tiles[0], lanes)[0][0]
            end = tile_heads(tiles[-1], lanes)[-1][0] + 1
            product = jnp.dot(
                turned[begin * HEAD_DIM : end * HEAD_DIM, :],
                values_ref[:, tiles[0] * LANES : (tiles[-1] + 1) * LANES],
                preferred_element_type=jnp.float32,
            )
            for side, j in enumerate(tiles):
                total = jnp.zeros((HEAD_DIM, LANES), jnp.float32)
                for h, lo, hi in tile_heads(j, lanes):
                    part = product[
                        (h - begin) * HEAD_DIM : (h - begin + 1) * HEAD_DIM,
                        side * LANES : (side + 1) * LANES,
                    ]
                    total = jnp.where((lane >= lo) & (lane < hi), part, total)
                row = pl.multiple_of((step * TILES + j) * HEAD_DIM, 16)
                whole[pl.ds(row, HEAD_DIM), :] = total.astype(jnp.bfloat16)

    by_group(dim, body)

    @pl.when(step == pl.num_programs(0) - 1)
    def _():
        used = cdiv(dim, LANES) * HEAD_DIM
        if used < whole.shape[0]:
            whole[used:, :] = jnp.zeros((whole.shape[0] - used, LANES), jnp.bfloat16)
        for k, part in enumerate(parts):
            size = part.shape[0]
            row = pl.multiple_of(lax.rem(spot_ref[0] + k, len(parts)) * size, 16)
            part[...] = whole[pl.ds(row, size), :]
        if with_edge:
            for copy in copies:
                copy.wait()


def frame_states(spot, keys, values, rows, parts, edged=()):
    tokens, dim = keys.shape
    part = (rows // parts, LANES)
    block = pl.BlockSpec((tokens, GROUP), lambda g: (0, g))
    return pl.pallas_call(
        functools.partial(state_kernel, dim, bool(edged)),
        out_shape=[pltpu.VMEM(part, jnp.bfloat16)] * parts
        + [pltpu.VMEM((len(edged), 1, *edged[0].shape[1:]), jnp.bfloat16) for _ in edged[:1]],
        grid=(cdiv(dim, GROUP),),
        in_specs=[pl.BlockSpec(memory_space=pltpu.SMEM), block, block]
        + [pl.BlockSpec(memory_space=pl.ANY)] * len(edged),
        out_specs=[pl.BlockSpec(part, lambda g: (0, 0))] * parts
        + [pl.BlockSpec(memory_space=pl.ANY) for _ in edged[:1]],
        scratch_shapes=[
            pltpu.VMEM((GROUP, tokens), jnp.bfloat16),
            pltpu.VMEM((rows, LANES), jnp.bfloat16),
            pltpu.SemaphoreType.DMA((2,)),
        ],
        compiler_params=pltpu.CompilerParams(vmem_limit_bytes=60 * 2**20),
        cost_estimate=pl.CostEstimate(
            flops=2 * tokens * dim * HEAD_DIM, bytes_accessed=4 * tokens * dim, transcendentals=0
        ),
        name="frame_states",
    )(spot, in_hbm(keys), in_hbm(values), *[in_hbm(array) for array in edged])


def mix_kernel(
    dim, rows, width, edges,
    place_ref, spots_ref, queries_ref, residual_ref, edge_ref, gain_ref, vtaps_ref, gtaps_ref, *refs,
):
    *pieces, out_ref, states, features, weights, same, numer, squares, windows = refs
    step = pl.program_id(0)
    tokens = rows * width

    @pl.when(step == 0)
    def _():
        weights[...] = jnp.zeros_like(weights)
        same[...] = jnp.zeros_like(same)
        lane = lane_iota((HEAD_DIM, LANES))
        for number, (tiles, first, _) in enumerate(spans(min(GROUP, dim))):
            for side, j in enumerate(tiles):
                for h, lo, hi in tile_heads(j, GROUP):
                    start = h * HEAD_DIM - first * LANES
                    block = jnp.where((lane >= lo) & (lane < hi), 1.0, 0.0)
                    same[
                        number, start : start + HEAD_DIM, side * LANES : (side + 1) * LANES
                    ] = block.astype(jnp.bfloat16)
        for k, piece in enumerate(pieces):
            size = piece.shape[0]
            states[pl.ds(pl.multiple_of(spots_ref[k] * size, 16), size), :] = piece[...]

    zero = jnp.zeros((), jnp.bfloat16)
    lane = lane_iota((HEAD_DIM, LANES))
    sublane = lax.broadcasted_iota(jnp.int32, (8, LANES), 0)

    def store_windows(mixed, row, slot):
        mixed = mixed.astype(jnp.bfloat16).astype(jnp.float32)
        windows[slot, 1, row] = mixed
        before, after = pltpu.roll(mixed, 1, 0), pltpu.roll(mixed, width - 1, 0)
        windows[slot, 0, row, :8] = jnp.where(sublane == 0, 0.0, before[:8])
        windows[slot, 0, row, 8:] = before[8:]
        windows[slot, 2, row, : width - 8] = after[: width - 8]
        windows[slot, 2, row, width - 8 :] = jnp.where(sublane == 7, 0.0, after[width - 8 :])

    def body(lanes):
        count = cdiv(lanes, LANES)
        end = count * LANES
        inside = lane_iota((1, end)) < lanes
        groups = spans(lanes)

        def feature(queries):
            queries = jnp.maximum(queries, zero)
            return queries if lanes == end else jnp.where(inside, queries, zero)

        features[:tokens, :end] = feature(queries_ref[:, :end])
        for e in range(edges):
            features[tokens + e * width : tokens + (e + 1) * width, :end] = feature(
                edge_ref[0, e, :, :end]
            )

        def numerators(number):
            tiles, first, last = groups[number]
            for side, j in enumerate(tiles):
                row = pl.multiple_of((step * TILES + j) * HEAD_DIM, 16)
                state = states[pl.ds(row, HEAD_DIM), :].astype(jnp.float32)
                for h, lo, hi in tile_heads(j, lanes):
                    start = h * HEAD_DIM - first * LANES
                    block = jnp.where((lane >= lo) & (lane < hi), state, 0.0)
                    weights[
                        number, start : start + HEAD_DIM, side * LANES : (side + 1) * LANES
                    ] = block.astype(jnp.bfloat16)
            depth, wide = (last - first) * LANES, len(tiles) * LANES
            product = jnp.dot(
                features[:, first * LANES : last * LANES],
                weights[number, :depth, :wide],
                preferred_element_type=jnp.float32,
            )
            here = slice(tiles[0] * LANES, tiles[0] * LANES + wide)
            numer[:, here] = product
            squares[:, here] = (product * product).astype(jnp.bfloat16)

        def head_sums(number):
            tiles, first, last = groups[number]
            depth, wide = (last - first) * LANES, len(tiles) * LANES
            return jnp.dot(
                squares[:, first * LANES : last * LANES],
                same[number, :depth, :wide],
                preferred_element_type=jnp.float32,
            )

        def mix_tile(j, sums):
            here = slice(j * LANES, (j + 1) * LANES)
            slot = j % 2
            gain = gain_ref[:, here] * math.sqrt(HEAD_DIM)

            def mixed(source, residual):
                normed = numer[source, here] * lax.rsqrt(sums[source] + HEAD_DIM * 1e-06)
                return residual.astype(jnp.float32) + normed * gain

            outside = [None, None]
            for e in range(edges):
                source = slice(tokens + e * width, tokens + (e + 1) * width)
                value = mixed(source, edge_ref[1, e, :, here])
                for k, row in enumerate((0, rows + 1)):
                    part = jnp.where(place_ref[e] == row, value, 0.0)
                    outside[k] = part if outside[k] is None else outside[k] + part
            for k, row in enumerate((0, rows + 1)):
                store_windows(outside[k], row, slot)
            for row in range(rows):
                source = slice(row * width, (row + 1) * width)
                store_windows(mixed(source, residual_ref[source, here]), row + 1, slot)
            for row in range(rows):
                conv_v = half_g = None
                for tap in range(9):
                    window = windows[slot, tap % 3, row + tap // 3]
                    value = vtaps_ref[tap : tap + 1, here] * window
                    gate = (0.5 * gtaps_ref[tap : tap + 1, here]) * window
                    conv_v = value if tap == 0 else conv_v + value
                    half_g = gate if tap == 0 else half_g + gate
                result = windows[slot, 1, row + 1] + conv_v * (half_g + half_g * jnp.tanh(half_g))
                out_ref[row * width : (row + 1) * width, here] = result.astype(jnp.bfloat16)

        numerators(0)
        for number, (tiles, _, _) in enumerate(groups):
            if number + 1 < len(groups):
                numerators(number + 1)
            sums = head_sums(number)
            for side, j in enumerate(tiles):
                mix_tile(j, sums[:, side * LANES : (side + 1) * LANES])

    by_group(dim, body)


def mix(place, spots, queries, residual, edge, gain, value_taps, gate_taps, pieces, rows, width):
    tokens, dim = queries.shape
    edges = edge.shape[1]
    total = tokens + edges * width
    pairs = spans(min(GROUP, dim))
    depth = max(last - first for _, first, last in pairs) * LANES
    block = pl.BlockSpec((tokens, GROUP), lambda g: (0, g))
    taps = pl.BlockSpec((value_taps.shape[0], GROUP), lambda g: (0, g))
    return pl.pallas_call(
        functools.partial(mix_kernel, dim, rows, width, edges),
        out_shape=jax.ShapeDtypeStruct((tokens, dim), jnp.bfloat16),
        grid=(cdiv(dim, GROUP),),
        in_specs=[
            pl.BlockSpec(memory_space=pltpu.SMEM),
            pl.BlockSpec(memory_space=pltpu.SMEM),
            block,
            block,
            pl.BlockSpec((2, edges, width, GROUP), lambda g: (0, 0, 0, g)),
            pl.BlockSpec((1, GROUP), lambda g: (0, g)),
            taps,
            taps,
        ]
        + [pl.BlockSpec(piece.shape, lambda g: (0, 0)) for piece in pieces],
        out_specs=block,
        scratch_shapes=[
            pltpu.VMEM((sum(piece.shape[0] for piece in pieces), LANES), jnp.bfloat16),
            pltpu.VMEM((total, GROUP), jnp.bfloat16),
            pltpu.VMEM((len(pairs), depth, 2 * LANES), jnp.bfloat16),
            pltpu.VMEM((len(pairs), depth, 2 * LANES), jnp.bfloat16),
            pltpu.VMEM((total, GROUP), jnp.float32),
            pltpu.VMEM((total, GROUP), jnp.bfloat16),
            pltpu.VMEM((2, 3, rows + 2, width, LANES), jnp.float32),
        ],
        compiler_params=pltpu.CompilerParams(vmem_limit_bytes=36 * 2**20),
        cost_estimate=pl.CostEstimate(
            flops=60 * tokens * dim, bytes_accessed=6 * tokens * dim, transcendentals=2 * tokens * dim
        ),
        name="mix",
    )(place, spots, in_hbm(queries), in_hbm(residual), edge, gain, value_taps, gate_taps, *pieces)


def edge_rows(queries, residual):
    devices, rows = lax.axis_size("space"), queries.shape[0]
    up = [(i, i + 1) for i in range(devices - 1)]
    down = [(j, i) for i, j in up]
    both = jnp.stack([queries, residual])
    before = lax.ppermute(both[:, rows - 1 :], "space", up)
    after = lax.ppermute(both[:, :1], "space", down)
    return jnp.concatenate([before, after], axis=1), jnp.array([0, rows + 1], jnp.int32)


def small_kernel(body, name, outs, scalars, *arrays):
    return pl.pallas_call(
        body,
        out_shape=[pltpu.VMEM(shape, jnp.bfloat16) for shape in outs],
        in_specs=[pl.BlockSpec(memory_space=pltpu.SMEM)]
        + [pl.BlockSpec(memory_space=pltpu.VMEM)] * len(arrays),
        out_specs=[pl.BlockSpec(memory_space=pltpu.VMEM)] * len(outs),
        compiler_params=pltpu.CompilerParams(vmem_limit_bytes=4 * 2**20),
        name=name,
    )(scalars, *arrays)


def add(*values):
    total = values[0].astype(jnp.float32)
    for value in values[1:]:
        total = total + value.astype(jnp.float32)
    return total


def split_sum_body(spot_ref, kept_ref, got_ref, mine_ref, theirs_ref):
    size = mine_ref.shape[0]
    for ref, side in ((theirs_ref, 1 - spot_ref[0]), (mine_ref, spot_ref[0])):
        rows = pl.ds(pl.multiple_of(side * size, 16), size)
        ref[...] = add(kept_ref[rows, :], got_ref[rows, :]).astype(jnp.bfloat16)


def sum_body(_, *refs):
    *terms, out_ref = refs
    out_ref[...] = add(*[term[...] for term in terms]).astype(jnp.bfloat16)


def pair_sums_body(spot_ref, own_ref, partner_ref, *refs):
    *earlier, mine_ref, theirs_ref = refs
    before = jnp.zeros(own_ref.shape, jnp.float32)
    for k, ref in enumerate(earlier):
        from_before = lax.rem(spot_ref[1] // (2 << k), 2) == 1
        before = before + jnp.where(from_before, add(ref[...]), 0.0)
    own, partner = add(own_ref[...]), add(partner_ref[...])
    first = spot_ref[0] == 0
    both = before + (own + partner)
    mine_ref[...] = jnp.where(first, before + own, both).astype(jnp.bfloat16)
    theirs_ref[...] = jnp.where(first, both, before + partner).astype(jnp.bfloat16)


def running_states(keys, values, queries, residual, rows):
    devices, frames = lax.axis_size("space"), lax.axis_size("frame")
    core, frame = lax.axis_index("space"), lax.axis_index("frame")
    if devices != 2 or frames < 2 or frames & (frames - 1):
        (state,) = frame_states(jnp.zeros((1,), jnp.int32), keys, values, rows, 1)
        state = lax.psum(state.astype(jnp.float32), "space").astype(jnp.bfloat16)
        every = lax.all_gather(state, "frame").astype(jnp.float32)
        reached = (jnp.arange(frames) <= frame)[:, None, None]
        total = jnp.sum(jnp.where(reached, every, 0.0), axis=0).astype(jnp.bfloat16)
        return [total], jnp.zeros((1,), jnp.int32), edge_rows(queries, residual)
    swap = [(0, 1), (1, 0)]
    spot = jnp.stack([lax.rem(frame, 2), frame]).astype(jnp.int32)
    kept, sent, edge = frame_states(
        core.astype(jnp.int32)[None], keys, values, rows, 2, (queries, residual)
    )
    got = lax.ppermute(sent, "space", swap)
    quarter = (rows // 4, LANES)
    own, sent = small_kernel(split_sum_body, "split_sum", [quarter] * 2, spot, kept, got)
    edge, sent = lax.optimization_barrier((edge, sent))
    edge = lax.ppermute(edge, "space", swap)
    place = jnp.where(core == 0, queries.shape[0] + 1, 0).astype(jnp.int32)[None]
    partner = lax.ppermute(sent, "frame", [(f, f ^ 1) for f in range(frames)])
    (total,) = small_kernel(sum_body, "pair_sum", [quarter], spot, own, partner)
    earlier = []
    stride = 2
    while stride < frames:
        got = lax.ppermute(total, "frame", [(f, f ^ stride) for f in range(frames)])
        earlier.append(got)
        stride *= 2
        if stride < frames:
            (total,) = small_kernel(sum_body, "stride_sum", [quarter], spot, total, got)
    mine, theirs = small_kernel(
        pair_sums_body, "pair_sums", [quarter] * 2, spot, own, partner, *earlier
    )
    other = lax.ppermute(theirs, "frame", [(f, f ^ 1) for f in range(frames)])
    pieces = [mine, other, lax.ppermute(mine, "space", swap), lax.ppermute(other, "space", swap)]
    spots = [2 * c + p for c in (core, 1 - core) for p in (spot[0], 1 - spot[0])]
    return pieces, jnp.stack(spots).astype(jnp.int32), (edge, place)


def on_device(queries, keys, values, residual, attn_gain, value_taps, gate_taps):
    frames, rows, width, dim = queries.shape
    tokens = frames * rows * width
    flat = lambda a: a.reshape(tokens, dim)
    state_rows = cdiv(cdiv(dim, LANES) * HEAD_DIM, 64) * 64
    pieces, spots, (edge, place) = running_states(
        flat(keys),
        flat(values),
        queries.reshape(rows, width, dim),
        residual.reshape(rows, width, dim),
        state_rows,
    )
    out = mix(
        place, spots, flat(queries), flat(residual), edge, attn_gain[None], value_taps, gate_taps,
        pieces, rows, width,
    )
    return out.reshape(frames, rows, width, dim)


def solution(mesh):
    placed = P(("groups", "frame"), "space", None, None)
    return jax.shard_map(
        on_device,
        mesh=mesh,
        in_specs=(placed, placed, placed, placed, P(), P(), P()),
        out_specs=placed,
        check_vma=False,
    )
```

```python
import functools
import math

import jax
import jax.numpy as jnp
from jax import lax
from jax.experimental import pallas as pl
from jax.experimental.pallas import tpu as pltpu
from jax.sharding import PartitionSpec as P

HEAD_DIM = 112
LANES = 128
GROUP = math.lcm(HEAD_DIM, LANES)
TILES = GROUP // LANES


def cdiv(a, b):
    return -(-a // b)


def in_hbm(array):
    return pltpu.with_memory_space_constraint(array, pltpu.HBM)


def lane_iota(shape):
    return lax.broadcasted_iota(jnp.int32, shape, len(shape) - 1)


def tile_heads(j, lanes):
    lo, hi = j * LANES, min((j + 1) * LANES, lanes)
    heads = range(lo // HEAD_DIM, cdiv(hi, HEAD_DIM))
    return [(h, max(h * HEAD_DIM - lo, 0), min((h + 1) * HEAD_DIM - lo, LANES)) for h in heads]


def spans(lanes):
    count = cdiv(lanes, LANES)
    result = []
    for j in range(0, count, 2):
        tiles = list(range(j, min(j + 2, count)))
        first = tile_heads(tiles[0], lanes)[0][0] * HEAD_DIM // LANES
        last = cdiv((tile_heads(tiles[-1], lanes)[-1][0] + 1) * HEAD_DIM, LANES)
        result.append((tiles, first, last))
    return result


def by_group(dim, body):
    full, rest = divmod(dim, GROUP)
    if full:
        pl.when(pl.program_id(0) < full)(lambda: body(GROUP))
    if rest:
        pl.when(pl.program_id(0) >= full)(lambda: body(rest))


def state_kernel(dim, with_edge, spot_ref, keys_ref, values_ref, *refs):
    step = pl.program_id(0)
    *refs, turned, whole, semaphores = refs
    if with_edge:
        *sources, edge_ref = refs[:2] + refs[-1:]
        parts = refs[2:-1]
        row = (sources[0].shape[0] - 1) * (1 - lax.axis_index("space"))
        copies = [
            pltpu.make_async_copy(source.at[row], edge_ref.at[k, 0], semaphores.at[k])
            for k, source in enumerate(sources)
        ]

        @pl.when(step == 0)
        def _():
            for copy in copies:
                copy.start()

    else:
        parts = refs

    def body(lanes):
        turned[...] = jnp.maximum(keys_ref[...], 0).T
        lane = lane_iota((HEAD_DIM, LANES))
        for tiles, _, _ in spans(lanes):
            begin = tile_heads(tiles[0], lanes)[0][0]
            end = tile_heads(tiles[-1], lanes)[-1][0] + 1
            product = jnp.dot(
                turned[begin * HEAD_DIM : end * HEAD_DIM, :],
                values_ref[:, tiles[0] * LANES : (tiles[-1] + 1) * LANES],
                preferred_element_type=jnp.float32,
            )
            for side, j in enumerate(tiles):
                total = jnp.zeros((HEAD_DIM, LANES), jnp.float32)
                for h, lo, hi in tile_heads(j, lanes):
                    part = product[
                        (h - begin) * HEAD_DIM : (h - begin + 1) * HEAD_DIM,
                        side * LANES : (side + 1) * LANES,
                    ]
                    total = jnp.where((lane >= lo) & (lane < hi), part, total)
                row = pl.multiple_of((step * TILES + j) * HEAD_DIM, 16)
                whole[pl.ds(row, HEAD_DIM), :] = total.astype(jnp.bfloat16)

    by_group(dim, body)

    @pl.when(step == pl.num_programs(0) - 1)
    def _():
        used = cdiv(dim, LANES) * HEAD_DIM
        if used < whole.shape[0]:
            whole[used:, :] = jnp.zeros((whole.shape[0] - used, LANES), jnp.bfloat16)
        for k, part in enumerate(parts):
            size = part.shape[0]
            row = pl.multiple_of(lax.rem(spot_ref[0] + k, len(parts)) * size, 16)
            part[...] = whole[pl.ds(row, size), :]
        if with_edge:
            for copy in copies:
                copy.wait()


def frame_states(spot, keys, values, rows, parts, edged=()):
    tokens, dim = keys.shape
    part = (rows // parts, LANES)
    block = pl.BlockSpec((tokens, GROUP), lambda g: (0, g))
    return pl.pallas_call(
        functools.partial(state_kernel, dim, bool(edged)),
        out_shape=[pltpu.VMEM(part, jnp.bfloat16)] * parts
        + [pltpu.VMEM((len(edged), 1, *edged[0].shape[1:]), jnp.bfloat16) for _ in edged[:1]],
        grid=(cdiv(dim, GROUP),),
        in_specs=[pl.BlockSpec(memory_space=pltpu.SMEM), block, block]
        + [pl.BlockSpec(memory_space=pl.ANY)] * len(edged),
        out_specs=[pl.BlockSpec(part, lambda g: (0, 0))] * parts
        + [pl.BlockSpec(memory_space=pl.ANY) for _ in edged[:1]],
        scratch_shapes=[
            pltpu.VMEM((GROUP, tokens), jnp.bfloat16),
            pltpu.VMEM((rows, LANES), jnp.bfloat16),
            pltpu.SemaphoreType.DMA((2,)),
        ],
        compiler_params=pltpu.CompilerParams(vmem_limit_bytes=60 * 2**20),
        cost_estimate=pl.CostEstimate(
            flops=2 * tokens * dim * HEAD_DIM, bytes_accessed=4 * tokens * dim, transcendentals=0
        ),
        name="frame_states",
    )(spot, in_hbm(keys), in_hbm(values), *[in_hbm(array) for array in edged])


def group_lanes(dim):
    return [(first, min(GROUP, dim - first)) for first in range(0, dim, GROUP)]


def prepare_kernel(dim, queries_ref, residual_ref, edge_ref, features_ref, inputs_ref, same_ref, *refs):
    held, semaphores = refs
    tokens = queries_ref.shape[0]
    full = dim // LANES * LANES
    parts = [slice(0, full), slice(full, dim)] if full < dim else [slice(0, dim)]
    copies = [
        pltpu.make_async_copy(queries_ref, held.at[:tokens], semaphores.at[0]),
        pltpu.make_async_copy(residual_ref, inputs_ref.at[:tokens], semaphores.at[1]),
    ]
    for copy in copies:
        copy.start()
    edges, width = edge_ref.shape[1:3]
    for e in range(edges):
        here = slice(tokens + e * width, tokens + (e + 1) * width)
        held[here] = edge_ref[0, e]
        inputs_ref[here] = edge_ref[1, e]
    same_ref[...] = jnp.zeros_like(same_ref)
    lane = lane_iota((HEAD_DIM, LANES))
    for number, (tiles, first, _) in enumerate(spans(min(GROUP, dim))):
        for side, j in enumerate(tiles):
            for h, lo, hi in tile_heads(j, GROUP):
                start = h * HEAD_DIM - first * LANES
                block = jnp.where((lane >= lo) & (lane < hi), 1.0, 0.0)
                same_ref[
                    number, start : start + HEAD_DIM, side * LANES : (side + 1) * LANES
                ] = block.astype(jnp.bfloat16)
    if full < dim:
        features_ref[:, full:] = jnp.zeros((features_ref.shape[0], LANES), jnp.bfloat16)
    copies[0].wait()
    for part in parts:
        features_ref[:, part] = jnp.maximum(held[:, part], 0)
    copies[1].wait()


def prepare(queries, residual, edge):
    tokens, dim = queries.shape
    total = tokens + edge.shape[1] * edge.shape[2]
    pairs = spans(min(GROUP, dim))
    depth = max(last - first for _, first, last in pairs) * LANES
    whole = pl.BlockSpec(memory_space=pltpu.VMEM)
    return pl.pallas_call(
        functools.partial(prepare_kernel, dim),
        out_shape=[
            pltpu.VMEM((total, cdiv(dim, LANES) * LANES), jnp.bfloat16),
            pltpu.VMEM((total, dim), jnp.bfloat16),
            pltpu.VMEM((len(pairs), depth, 2 * LANES), jnp.bfloat16),
        ],
        in_specs=[pl.BlockSpec(memory_space=pl.ANY)] * 2 + [whole],
        out_specs=[whole] * 3,
        scratch_shapes=[
            pltpu.VMEM((total, dim), jnp.bfloat16),
            pltpu.SemaphoreType.DMA((2,)),
        ],
        compiler_params=pltpu.CompilerParams(vmem_limit_bytes=24 * 2**20),
        cost_estimate=pl.CostEstimate(
            flops=4 * total * dim, bytes_accessed=8 * total * dim, transcendentals=0
        ),
        name="prepare",
    )(in_hbm(queries), in_hbm(residual), edge)


def mix_kernel(
    dim, rows, width, edges,
    place_ref, spots_ref, features_ref, inputs_ref, same_ref, gain_ref, vtaps_ref, gtaps_ref, *refs,
):
    *pieces, out_ref, states, weights, numer, squares, windows, held, semaphores = refs
    tokens = rows * width
    weights[...] = jnp.zeros_like(weights)
    for k, piece in enumerate(pieces):
        size = piece.shape[0]
        states[pl.ds(pl.multiple_of(spots_ref[k] * size, 16), size), :] = piece[...]
    lane = lane_iota((HEAD_DIM, LANES))
    sublane = lax.broadcasted_iota(jnp.int32, (8, LANES), 0)

    def store_windows(mixed, row, slot, used):
        mixed = mixed.astype(jnp.bfloat16).astype(jnp.float32)
        windows[slot, 1, row, :, :used] = mixed
        before, after = pltpu.roll(mixed, 1, 0), pltpu.roll(mixed, width - 1, 0)
        windows[slot, 0, row, :8, :used] = jnp.where(sublane[:, :used] == 0, 0.0, before[:8])
        windows[slot, 0, row, 8:, :used] = before[8:]
        windows[slot, 2, row, : width - 8, :used] = after[: width - 8]
        windows[slot, 2, row, width - 8 :, :used] = jnp.where(
            sublane[:, :used] == 7, 0.0, after[width - 8 :]
        )

    def group(base, lanes):
        pairs = spans(lanes)

        def numerators(number):
            tiles, first, last = pairs[number]
            for side, j in enumerate(tiles):
                row = (base // LANES + j) * HEAD_DIM
                state = states[row : row + HEAD_DIM, :].astype(jnp.float32)
                for h, lo, hi in tile_heads(j, lanes):
                    start = h * HEAD_DIM - first * LANES
                    block = jnp.where((lane >= lo) & (lane < hi), state, 0.0)
                    weights[
                        number, start : start + HEAD_DIM, side * LANES : (side + 1) * LANES
                    ] = block.astype(jnp.bfloat16)
            depth, wide = (last - first) * LANES, len(tiles) * LANES
            product = jnp.dot(
                features_ref[:, base + first * LANES : base + last * LANES],
                weights[number, :depth, :wide],
                preferred_element_type=jnp.float32,
            )
            here = slice(tiles[0] * LANES, tiles[0] * LANES + wide)
            numer[:, here] = product
            squares[:, here] = (product * product).astype(jnp.bfloat16)

        def head_sums(number):
            tiles, first, last = pairs[number]
            depth, wide = (last - first) * LANES, len(tiles) * LANES
            return jnp.dot(
                squares[:, first * LANES : last * LANES],
                same_ref[number, :depth, :wide],
                preferred_element_type=jnp.float32,
            )

        def mix_tile(j, sums):
            slot = j % 2
            used = min(LANES, lanes - j * LANES)
            near = slice(j * LANES, j * LANES + used)
            here = slice(base + j * LANES, base + j * LANES + used)
            gain = gain_ref[:, here] * math.sqrt(HEAD_DIM)

            def mixed(source):
                normed = numer[source, near] * lax.rsqrt(sums[source, :used] + HEAD_DIM * 1e-06)
                return inputs_ref[source, here].astype(jnp.float32) + normed * gain

            outside = [None, None]
            for e in range(edges):
                value = mixed(slice(tokens + e * width, tokens + (e + 1) * width))
                for k, row in enumerate((0, rows + 1)):
                    part = jnp.where(place_ref[e] == row, value, 0.0)
                    outside[k] = part if outside[k] is None else outside[k] + part
            for k, row in enumerate((0, rows + 1)):
                store_windows(outside[k], row, slot, used)
            for row in range(rows):
                store_windows(mixed(slice(row * width, (row + 1) * width)), row + 1, slot, used)
            for row in range(rows):
                conv_v = half_g = None
                for tap in range(9):
                    window = windows[slot, tap % 3, row + tap // 3, :, :used]
                    value = vtaps_ref[tap : tap + 1, here] * window
                    gate = (0.5 * gtaps_ref[tap : tap + 1, here]) * window
                    conv_v = value if tap == 0 else conv_v + value
                    half_g = gate if tap == 0 else half_g + gate
                center = windows[slot, 1, row + 1, :, :used]
                result = center + conv_v * (half_g + half_g * jnp.tanh(half_g))
                held[row * width : (row + 1) * width, here] = result.astype(jnp.bfloat16)

        numerators(0)
        for number, (tiles, _, _) in enumerate(pairs):
            if number + 1 < len(pairs):
                numerators(number + 1)
            sums = head_sums(number)
            for side, j in enumerate(tiles):
                mix_tile(j, sums[:, side * LANES : (side + 1) * LANES])

    copies = []
    for base, lanes in group_lanes(dim):
        group(base, lanes)
        here = slice(base, base + lanes)
        copies.append(
            pltpu.make_async_copy(held.at[:, here], out_ref.at[:, here], semaphores.at[len(copies)])
        )
        copies[-1].start()
    for copy in copies:
        copy.wait()


def mix(place, spots, prepared, gain, value_taps, gate_taps, pieces, rows, width):
    features, inputs, same = prepared
    total, dim = inputs.shape
    tokens = rows * width
    whole = pl.BlockSpec(memory_space=pltpu.VMEM)
    return pl.pallas_call(
        functools.partial(mix_kernel, dim, rows, width, (total - tokens) // width),
        out_shape=jax.ShapeDtypeStruct((tokens, dim), jnp.bfloat16),
        in_specs=[pl.BlockSpec(memory_space=pltpu.SMEM)] * 2 + [whole] * (6 + len(pieces)),
        out_specs=pl.BlockSpec(memory_space=pl.ANY),
        scratch_shapes=[
            pltpu.VMEM((sum(piece.shape[0] for piece in pieces), LANES), jnp.bfloat16),
            pltpu.VMEM(same.shape, jnp.bfloat16),
            pltpu.VMEM((total, GROUP), jnp.float32),
            pltpu.VMEM((total, GROUP), jnp.bfloat16),
            pltpu.VMEM((2, 3, rows + 2, width, LANES), jnp.float32),
            pltpu.VMEM((tokens, dim), jnp.bfloat16),
            pltpu.SemaphoreType.DMA((len(group_lanes(dim)),)),
        ],
        compiler_params=pltpu.CompilerParams(vmem_limit_bytes=36 * 2**20),
        cost_estimate=pl.CostEstimate(
            flops=60 * tokens * dim, bytes_accessed=6 * tokens * dim, transcendentals=2 * tokens * dim
        ),
        name="mix",
    )(place, spots, features, inputs, same, gain, value_taps, gate_taps, *pieces)


def edge_rows(queries, residual):
    devices, rows = lax.axis_size("space"), queries.shape[0]
    up = [(i, i + 1) for i in range(devices - 1)]
    down = [(j, i) for i, j in up]
    both = jnp.stack([queries, residual])
    before = lax.ppermute(both[:, rows - 1 :], "space", up)
    after = lax.ppermute(both[:, :1], "space", down)
    return jnp.concatenate([before, after], axis=1), jnp.array([0, rows + 1], jnp.int32)


def small_kernel(body, name, outs, scalars, *arrays):
    return pl.pallas_call(
        body,
        out_shape=[pltpu.VMEM(shape, jnp.bfloat16) for shape in outs],
        in_specs=[pl.BlockSpec(memory_space=pltpu.SMEM)]
        + [pl.BlockSpec(memory_space=pltpu.VMEM)] * len(arrays),
        out_specs=[pl.BlockSpec(memory_space=pltpu.VMEM)] * len(outs),
        compiler_params=pltpu.CompilerParams(vmem_limit_bytes=4 * 2**20),
        name=name,
    )(scalars, *arrays)


def add(*values):
    total = values[0].astype(jnp.float32)
    for value in values[1:]:
        total = total + value.astype(jnp.float32)
    return total


def split_sum_body(spot_ref, kept_ref, got_ref, mine_ref, theirs_ref):
    size = mine_ref.shape[0]
    for ref, side in ((theirs_ref, 1 - spot_ref[0]), (mine_ref, spot_ref[0])):
        rows = pl.ds(pl.multiple_of(side * size, 16), size)
        ref[...] = add(kept_ref[rows, :], got_ref[rows, :]).astype(jnp.bfloat16)


def sum_body(_, *refs):
    *terms, out_ref = refs
    out_ref[...] = add(*[term[...] for term in terms]).astype(jnp.bfloat16)


def pair_sums_body(spot_ref, own_ref, partner_ref, *refs):
    *earlier, mine_ref, theirs_ref = refs
    before = jnp.zeros(own_ref.shape, jnp.float32)
    for k, ref in enumerate(earlier):
        from_before = lax.rem(spot_ref[1] // (2 << k), 2) == 1
        before = before + jnp.where(from_before, add(ref[...]), 0.0)
    own, partner = add(own_ref[...]), add(partner_ref[...])
    first = spot_ref[0] == 0
    both = before + (own + partner)
    mine_ref[...] = jnp.where(first, before + own, both).astype(jnp.bfloat16)
    theirs_ref[...] = jnp.where(first, both, before + partner).astype(jnp.bfloat16)


def running_states(keys, values, queries, residual, rows, beside):
    devices, frames = lax.axis_size("space"), lax.axis_size("frame")
    core, frame = lax.axis_index("space"), lax.axis_index("frame")
    if devices != 2 or frames < 2 or frames & (frames - 1):
        (state,) = frame_states(jnp.zeros((1,), jnp.int32), keys, values, rows, 1)
        state = lax.psum(state.astype(jnp.float32), "space").astype(jnp.bfloat16)
        every = lax.all_gather(state, "frame").astype(jnp.float32)
        reached = (jnp.arange(frames) <= frame)[:, None, None]
        total = jnp.sum(jnp.where(reached, every, 0.0), axis=0).astype(jnp.bfloat16)
        edge, place = edge_rows(queries, residual)
        return [total], jnp.zeros((1,), jnp.int32), place, beside(edge)
    swap = [(0, 1), (1, 0)]
    spot = jnp.stack([lax.rem(frame, 2), frame]).astype(jnp.int32)
    kept, sent, edge = frame_states(
        core.astype(jnp.int32)[None], keys, values, rows, 2, (queries, residual)
    )
    got = lax.ppermute(sent, "space", swap)
    quarter = (rows // 4, LANES)
    own, sent = small_kernel(split_sum_body, "split_sum", [quarter] * 2, spot, kept, got)
    edge, sent = lax.optimization_barrier((edge, sent))
    edge = lax.ppermute(edge, "space", swap)
    place = jnp.where(core == 0, queries.shape[0] + 1, 0).astype(jnp.int32)[None]
    partner = lax.ppermute(sent, "frame", [(f, f ^ 1) for f in range(frames)])
    (total,) = small_kernel(sum_body, "pair_sum", [quarter], spot, own, partner)
    earlier = []
    stride = 2
    while stride < frames:
        if stride * 2 >= frames:
            total, edge = lax.optimization_barrier((total, edge))
        got = lax.ppermute(total, "frame", [(f, f ^ stride) for f in range(frames)])
        earlier.append(got)
        stride *= 2
        if stride < frames:
            (total,) = small_kernel(sum_body, "stride_sum", [quarter], spot, total, got)
    last = earlier.pop() if earlier else partner
    prepared = beside(edge)
    last, *prepared = lax.optimization_barrier((last, *prepared))
    if earlier or frames > 2:
        earlier.append(last)
    else:
        partner = last
    mine, theirs = small_kernel(
        pair_sums_body, "pair_sums", [quarter] * 2, spot, own, partner, *earlier
    )
    other = lax.ppermute(theirs, "frame", [(f, f ^ 1) for f in range(frames)])
    pieces = [mine, other, lax.ppermute(mine, "space", swap), lax.ppermute(other, "space", swap)]
    spots = [2 * c + p for c in (core, 1 - core) for p in (spot[0], 1 - spot[0])]
    return pieces, jnp.stack(spots).astype(jnp.int32), place, prepared


def on_device(queries, keys, values, residual, attn_gain, value_taps, gate_taps):
    frames, rows, width, dim = queries.shape
    tokens = frames * rows * width
    flat = lambda a: a.reshape(tokens, dim)
    state_rows = cdiv(cdiv(dim, LANES) * HEAD_DIM, 64) * 64
    pieces, spots, place, prepared = running_states(
        flat(keys),
        flat(values),
        queries.reshape(rows, width, dim),
        residual.reshape(rows, width, dim),
        state_rows,
        lambda edge: prepare(flat(queries), flat(residual), edge),
    )
    out = mix(
        place, spots, prepared, attn_gain[None], value_taps, gate_taps, pieces, rows, width
    )
    return out.reshape(frames, rows, width, dim)


def solution(mesh):
    placed = P(("groups", "frame"), "space", None, None)
    return jax.shard_map(
        on_device,
        mesh=mesh,
        in_specs=(placed, placed, placed, placed, P(), P(), P()),
        out_specs=placed,
        check_vma=False,
    )
```

```python
import functools
import math

import jax
import jax.numpy as jnp
from jax import lax
from jax.experimental import pallas as pl
from jax.experimental.pallas import tpu as pltpu
from jax.sharding import PartitionSpec as P

HEAD_DIM = 112
LANES = 128
GROUP = math.lcm(HEAD_DIM, LANES)
TILES = GROUP // LANES


def cdiv(a, b):
    return -(-a // b)


def in_hbm(array):
    return pltpu.with_memory_space_constraint(array, pltpu.HBM)


def lane_iota(shape):
    return lax.broadcasted_iota(jnp.int32, shape, len(shape) - 1)


def tile_heads(j, lanes):
    lo, hi = j * LANES, min((j + 1) * LANES, lanes)
    heads = range(lo // HEAD_DIM, cdiv(hi, HEAD_DIM))
    return [(h, max(h * HEAD_DIM - lo, 0), min((h + 1) * HEAD_DIM - lo, LANES)) for h in heads]


def spans(lanes):
    count = cdiv(lanes, LANES)
    result = []
    for j in range(0, count, 2):
        tiles = list(range(j, min(j + 2, count)))
        first = tile_heads(tiles[0], lanes)[0][0] * HEAD_DIM // LANES
        last = cdiv((tile_heads(tiles[-1], lanes)[-1][0] + 1) * HEAD_DIM, LANES)
        result.append((tiles, first, last))
    return result


def by_group(dim, body):
    full, rest = divmod(dim, GROUP)
    if full:
        pl.when(pl.program_id(0) < full)(lambda: body(GROUP))
    if rest:
        pl.when(pl.program_id(0) >= full)(lambda: body(rest))


def state_kernel(dim, with_edge, keys_ref, values_ref, *refs):
    step = pl.program_id(0)
    *refs, turned, whole, semaphores = refs
    if with_edge:
        *sources, edge_ref = refs[:2] + refs[-1:]
        parts = refs[2:-1]
        row = (sources[0].shape[0] - 1) * (1 - lax.axis_index("space"))
        copies = [
            pltpu.make_async_copy(source.at[row], edge_ref.at[k, 0], semaphores.at[k])
            for k, source in enumerate(sources)
        ]

        @pl.when(step == 0)
        def _():
            for copy in copies:
                copy.start()

    else:
        parts = refs

    def body(lanes):
        turned[...] = jnp.maximum(keys_ref[...], 0).T
        lane = lane_iota((HEAD_DIM, LANES))
        for tiles, _, _ in spans(lanes):
            begin = tile_heads(tiles[0], lanes)[0][0]
            end = tile_heads(tiles[-1], lanes)[-1][0] + 1
            product = jnp.dot(
                turned[begin * HEAD_DIM : end * HEAD_DIM, :],
                values_ref[:, tiles[0] * LANES : (tiles[-1] + 1) * LANES],
                preferred_element_type=jnp.float32,
            )
            for side, j in enumerate(tiles):
                total = jnp.zeros((HEAD_DIM, LANES), jnp.float32)
                for h, lo, hi in tile_heads(j, lanes):
                    part = product[
                        (h - begin) * HEAD_DIM : (h - begin + 1) * HEAD_DIM,
                        side * LANES : (side + 1) * LANES,
                    ]
                    total = jnp.where((lane >= lo) & (lane < hi), part, total)
                row = pl.multiple_of((step * TILES + j) * HEAD_DIM, 16)
                whole[pl.ds(row, HEAD_DIM), :] = total.astype(jnp.bfloat16)

    by_group(dim, body)

    @pl.when(step == pl.num_programs(0) - 1)
    def _():
        used = cdiv(dim, LANES) * HEAD_DIM
        if used < whole.shape[0]:
            whole[used:, :] = jnp.zeros((whole.shape[0] - used, LANES), jnp.bfloat16)
        for k, part in enumerate(parts):
            size = part.shape[0]
            turn = lax.rem(lax.axis_index("space") + k, 2) if len(parts) == 2 else 0
            part[...] = whole[pl.ds(pl.multiple_of(turn * size, 16), size), :]
        if with_edge:
            for copy in copies:
                copy.wait()


def frame_states(keys, values, rows, parts, edged=()):
    tokens, dim = keys.shape
    part = (rows // parts, LANES)
    block = pl.BlockSpec((tokens, GROUP), lambda g: (0, g))
    return pl.pallas_call(
        functools.partial(state_kernel, dim, bool(edged)),
        out_shape=[pltpu.VMEM(part, jnp.bfloat16)] * parts
        + [pltpu.VMEM((len(edged), 1, *edged[0].shape[1:]), jnp.bfloat16) for _ in edged[:1]],
        grid=(cdiv(dim, GROUP),),
        in_specs=[block, block] + [pl.BlockSpec(memory_space=pl.ANY)] * len(edged),
        out_specs=[pl.BlockSpec(part, lambda g: (0, 0))] * parts
        + [pl.BlockSpec(memory_space=pl.ANY) for _ in edged[:1]],
        scratch_shapes=[
            pltpu.VMEM((GROUP, tokens), jnp.bfloat16),
            pltpu.VMEM((rows, LANES), jnp.bfloat16),
            pltpu.SemaphoreType.DMA((2,)),
        ],
        compiler_params=pltpu.CompilerParams(vmem_limit_bytes=60 * 2**20),
        cost_estimate=pl.CostEstimate(
            flops=2 * tokens * dim * HEAD_DIM, bytes_accessed=4 * tokens * dim, transcendentals=0
        ),
        name="frame_states",
    )(in_hbm(keys), in_hbm(values), *[in_hbm(array) for array in edged])


def group_lanes(dim):
    return [(first, min(GROUP, dim - first)) for first in range(0, dim, GROUP)]


def prepare_kernel(
    dim, queries_ref, residual_ref, edge_ref, gain_ref,
    features_ref, inputs_ref, scaled_ref, held, semaphores,
):
    tokens = queries_ref.shape[0]
    full = dim // LANES * LANES
    parts = [slice(0, full), slice(full, dim)] if full < dim else [slice(0, dim)]
    copies = [
        pltpu.make_async_copy(queries_ref, held.at[:tokens], semaphores.at[0]),
        pltpu.make_async_copy(residual_ref, inputs_ref.at[:tokens], semaphores.at[1]),
    ]
    for copy in copies:
        copy.start()
    edges, width = edge_ref.shape[1:3]
    for e in range(edges):
        here = slice(tokens + e * width, tokens + (e + 1) * width)
        held[here] = edge_ref[0, e]
        inputs_ref[here] = edge_ref[1, e]
    scaled_ref[...] = gain_ref[...] * math.sqrt(HEAD_DIM)
    if full < dim:
        features_ref[:, full:] = jnp.zeros((features_ref.shape[0], LANES), jnp.bfloat16)
    copies[0].wait()
    for part in parts:
        features_ref[:, part] = jnp.maximum(held[:, part], 0)
    copies[1].wait()


def prepare(queries, residual, edge, gain):
    tokens, dim = queries.shape
    total = tokens + edge.shape[1] * edge.shape[2]
    whole = pl.BlockSpec(memory_space=pltpu.VMEM)
    return pl.pallas_call(
        functools.partial(prepare_kernel, dim),
        out_shape=[
            pltpu.VMEM((total, cdiv(dim, LANES) * LANES), jnp.bfloat16),
            pltpu.VMEM((total, dim), jnp.bfloat16),
            pltpu.VMEM((1, dim), jnp.float32),
        ],
        in_specs=[pl.BlockSpec(memory_space=pl.ANY)] * 2 + [whole] * 2,
        out_specs=[whole] * 3,
        scratch_shapes=[
            pltpu.VMEM((total, dim), jnp.bfloat16),
            pltpu.SemaphoreType.DMA((2,)),
        ],
        compiler_params=pltpu.CompilerParams(vmem_limit_bytes=24 * 2**20),
        cost_estimate=pl.CostEstimate(
            flops=4 * total * dim, bytes_accessed=8 * total * dim, transcendentals=0
        ),
        name="prepare",
    )(in_hbm(queries), in_hbm(residual), edge, gain)


def mix_kernel(
    dim, rows, width, edges,
    features_ref, inputs_ref, gain_ref, vtaps_ref, gtaps_ref, *refs,
):
    *pieces, out_ref, states, weights, numer, windows, held, semaphores = refs
    places = edge_places(lax.axis_size("space"), rows) if edges else []
    spots = piece_places() if len(pieces) > 1 else [0]
    tokens = rows * width
    weights[...] = jnp.zeros_like(weights)
    for k, piece in enumerate(pieces):
        size = piece.shape[0]
        states[pl.ds(pl.multiple_of(spots[k] * size, 16), size), :] = piece[...]
    lane = lane_iota((HEAD_DIM, LANES))
    sublane = lax.broadcasted_iota(jnp.int32, (8, LANES), 0)

    def store_windows(mixed, row, slot, used):
        mixed = mixed.astype(jnp.bfloat16).astype(jnp.float32)
        windows[slot, 1, row, :, :used] = mixed
        before, after = pltpu.roll(mixed, 1, 0), pltpu.roll(mixed, width - 1, 0)
        windows[slot, 0, row, :8, :used] = jnp.where(sublane[:, :used] == 0, 0.0, before[:8])
        windows[slot, 0, row, 8:, :used] = before[8:]
        windows[slot, 2, row, : width - 8, :used] = after[: width - 8]
        windows[slot, 2, row, width - 8 :, :used] = jnp.where(
            sublane[:, :used] == 7, 0.0, after[width - 8 :]
        )

    def group(base, lanes):
        pairs = spans(lanes)

        def numerators(number):
            tiles, first, last = pairs[number]
            for side, j in enumerate(tiles):
                row = (base // LANES + j) * HEAD_DIM
                state = states[row : row + HEAD_DIM, :].astype(jnp.float32)
                for h, lo, hi in tile_heads(j, lanes):
                    start = h * HEAD_DIM - first * LANES
                    block = jnp.where((lane >= lo) & (lane < hi), state, 0.0)
                    weights[
                        number, start : start + HEAD_DIM, side * LANES : (side + 1) * LANES
                    ] = block.astype(jnp.bfloat16)
            depth, wide = (last - first) * LANES, len(tiles) * LANES
            product = jnp.dot(
                features_ref[:, base + first * LANES : base + last * LANES],
                weights[number, :depth, :wide],
                preferred_element_type=jnp.float32,
            )
            here = slice(tiles[0] * LANES, tiles[0] * LANES + wide)
            numer[:, here] = product

        def tile_sums(j, source):
            square = numer[source, j * LANES : (j + 1) * LANES]
            square = square * square
            heads = tile_heads(j, lanes)
            if len(heads) == 1:
                return {heads[0][0]: jnp.sum(square, axis=-1, keepdims=True)}
            (one, _, bound), (two, _, _) = heads
            part = jnp.where(lane_iota(square.shape) < bound, square, 0.0)
            rest = square - part
            return {
                one: jnp.sum(part, axis=-1, keepdims=True),
                two: jnp.sum(rest, axis=-1, keepdims=True),
            }

        def mix_tile(j):
            slot = j % 2
            used = min(LANES, lanes - j * LANES)
            near = slice(j * LANES, j * LANES + used)
            here = slice(base + j * LANES, base + j * LANES + used)
            heads = tile_heads(j, lanes)

            def mixed(source):
                sums = [
                    sum(tiles[head] for tiles in parts[source.start] if head in tiles)
                    for head, _, _ in heads
                ]
                scale = jnp.broadcast_to(sums[0], (width, used))
                if len(heads) > 1:
                    scale = jnp.where(lane_iota(scale.shape) < heads[0][2], scale, sums[1])
                normed = numer[source, near] * lax.rsqrt(scale + HEAD_DIM * 1e-06)
                return inputs_ref[source, here].astype(jnp.float32) + normed * gain_ref[:, here]

            outside = [None, None]
            for e in range(edges):
                value = mixed(slice(tokens + e * width, tokens + (e + 1) * width))
                for k, row in enumerate((0, rows + 1)):
                    part = jnp.where(places[e] == row, value, 0.0)
                    outside[k] = part if outside[k] is None else outside[k] + part
            for k, row in enumerate((0, rows + 1)):
                store_windows(outside[k], row, slot, used)
            for row in range(rows):
                store_windows(mixed(slice(row * width, (row + 1) * width)), row + 1, slot, used)
            for row in range(rows):
                conv_v = half_g = None
                for tap in range(9):
                    window = windows[slot, tap % 3, row + tap // 3, :, :used]
                    value = vtaps_ref[tap : tap + 1, here] * window
                    gate = (0.5 * gtaps_ref[tap : tap + 1, here]) * window
                    conv_v = value if tap == 0 else conv_v + value
                    half_g = gate if tap == 0 else half_g + gate
                center = windows[slot, 1, row + 1, :, :used]
                result = center + conv_v * (half_g + half_g * jnp.tanh(half_g))
                held[row * width : (row + 1) * width, here] = result.astype(jnp.bfloat16)

        parts = {}
        for number, (tiles, _, _) in enumerate(pairs):
            numerators(number)
            for j in tiles:
                for row in range(rows + edges):
                    source = slice(row * width, (row + 1) * width)
                    parts.setdefault(source.start, []).append(tile_sums(j, source))
        for j in range(cdiv(lanes, LANES)):
            mix_tile(j)

    copies = []
    for base, lanes in group_lanes(dim):
        group(base, lanes)
        here = slice(base, base + lanes)
        copies.append(
            pltpu.make_async_copy(held.at[:, here], out_ref.at[:, here], semaphores.at[len(copies)])
        )
        copies[-1].start()
    for copy in copies:
        copy.wait()


def mix(prepared, value_taps, gate_taps, pieces, rows, width):
    features, inputs, gain = prepared
    total, dim = inputs.shape
    tokens = rows * width
    pairs = spans(min(GROUP, dim))
    depth = max(last - first for _, first, last in pairs) * LANES
    whole = pl.BlockSpec(memory_space=pltpu.VMEM)
    return pl.pallas_call(
        functools.partial(mix_kernel, dim, rows, width, (total - tokens) // width),
        out_shape=jax.ShapeDtypeStruct((tokens, dim), jnp.bfloat16),
        in_specs=[whole] * (5 + len(pieces)),
        out_specs=pl.BlockSpec(memory_space=pl.ANY),
        scratch_shapes=[
            pltpu.VMEM((sum(piece.shape[0] for piece in pieces), LANES), jnp.bfloat16),
            pltpu.VMEM((len(pairs), depth, 2 * LANES), jnp.bfloat16),
            pltpu.VMEM((total, GROUP), jnp.float32),
            pltpu.VMEM((2, 3, rows + 2, width, LANES), jnp.float32),
            pltpu.VMEM((tokens, dim), jnp.bfloat16),
            pltpu.SemaphoreType.DMA((len(group_lanes(dim)),)),
        ],
        compiler_params=pltpu.CompilerParams(vmem_limit_bytes=36 * 2**20),
        cost_estimate=pl.CostEstimate(
            flops=60 * tokens * dim, bytes_accessed=6 * tokens * dim, transcendentals=2 * tokens * dim
        ),
        name="mix",
    )(features, inputs, gain, value_taps, gate_taps, *pieces)


def edge_rows(queries, residual):
    devices, rows = lax.axis_size("space"), queries.shape[0]
    up = [(i, i + 1) for i in range(devices - 1)]
    down = [(j, i) for i, j in up]
    both = jnp.stack([queries, residual])
    if devices == 2:
        first = lax.axis_index("space") == 0
        return lax.ppermute(jnp.where(first, both[:, rows - 1 :], both[:, :1]), "space", up + down)
    before = lax.ppermute(both[:, rows - 1 :], "space", up)
    after = lax.ppermute(both[:, :1], "space", down)
    return jnp.concatenate([before, after], axis=1)


def small_kernel(body, name, outs, *arrays):
    return pl.pallas_call(
        body,
        out_shape=[pltpu.VMEM(shape, jnp.bfloat16) for shape in outs],
        in_specs=[pl.BlockSpec(memory_space=pltpu.VMEM)] * len(arrays),
        out_specs=[pl.BlockSpec(memory_space=pltpu.VMEM)] * len(outs),
        compiler_params=pltpu.CompilerParams(vmem_limit_bytes=4 * 2**20),
        name=name,
    )(*arrays)


def add(*values):
    total = values[0].astype(jnp.float32)
    for value in values[1:]:
        total = total + value.astype(jnp.float32)
    return total


def parity():
    return lax.rem(lax.axis_index("frame"), 2)


def split_sum_body(kept_ref, got_ref, mine_ref, theirs_ref):
    size = mine_ref.shape[0]
    for ref, side in ((theirs_ref, 1 - parity()), (mine_ref, parity())):
        rows = pl.ds(pl.multiple_of(side * size, 16), size)
        ref[...] = add(kept_ref[rows, :], got_ref[rows, :]).astype(jnp.bfloat16)


def sum_body(*refs):
    *terms, out_ref = refs
    out_ref[...] = add(*[term[...] for term in terms]).astype(jnp.bfloat16)


def pair_sums_body(own_ref, partner_ref, *refs):
    *earlier, mine_ref, theirs_ref = refs
    before = jnp.zeros(own_ref.shape, jnp.float32)
    for k, ref in enumerate(earlier):
        from_before = lax.rem(lax.axis_index("frame") // (2 << k), 2) == 1
        before = before + jnp.where(from_before, add(ref[...]), 0.0)
    own, partner = add(own_ref[...]), add(partner_ref[...])
    first = parity() == 0
    both = before + (own + partner)
    mine_ref[...] = jnp.where(first, before + own, both).astype(jnp.bfloat16)
    theirs_ref[...] = jnp.where(first, both, before + partner).astype(jnp.bfloat16)


def paired(devices, frames):
    return devices == 2 and frames >= 4 and frames & (frames - 1) == 0


def piece_places():
    core = lax.axis_index("space")
    return [2 * c + p for c in (core, 1 - core) for p in (parity(), 1 - parity())]


def edge_places(devices, rows):
    if devices == 2:
        return [jnp.where(lax.axis_index("space") == 0, rows + 1, 0)]
    return [0, rows + 1]


def running_states(keys, values, queries, residual, rows, beside):
    devices, frames = lax.axis_size("space"), lax.axis_size("frame")
    if not paired(devices, frames):
        (state,) = frame_states(keys, values, rows, 1)
        state = lax.psum(state.astype(jnp.float32), "space").astype(jnp.bfloat16)
        every = lax.all_gather(state, "frame").astype(jnp.float32)
        reached = (jnp.arange(frames) <= lax.axis_index("frame"))[:, None, None]
        total = jnp.sum(jnp.where(reached, every, 0.0), axis=0).astype(jnp.bfloat16)
        return [total], beside(edge_rows(queries, residual))
    swap = [(0, 1), (1, 0)]
    exchange = lambda array, stride: lax.ppermute(
        array, "frame", [(f, f ^ stride) for f in range(frames)]
    )
    kept, sent, edge = frame_states(keys, values, rows, 2, (queries, residual))
    got = lax.ppermute(sent, "space", swap)
    quarter = (rows // 4, LANES)
    own, sent = small_kernel(split_sum_body, "split_sum", [quarter] * 2, kept, got)
    edge, sent = lax.optimization_barrier((edge, sent))
    edge = lax.ppermute(edge, "space", swap)
    partner = exchange(sent, 1)
    (total,) = small_kernel(sum_body, "pair_sum", [quarter], own, partner)
    earlier = []
    stride = 2
    while stride < frames:
        if stride * 2 == frames:
            total, edge = lax.optimization_barrier((total, edge))
        earlier.append(exchange(total, stride))
        stride *= 2
        if stride < frames:
            (total,) = small_kernel(sum_body, "stride_sum", [quarter], total, earlier[-1])
    prepared = beside(edge)
    earlier[-1], *prepared = lax.optimization_barrier((earlier[-1], *prepared))
    mine, theirs = small_kernel(
        pair_sums_body, "pair_sums", [quarter] * 2, own, partner, *earlier
    )
    other = exchange(theirs, 1)
    pieces = [mine, other, lax.ppermute(mine, "space", swap), lax.ppermute(other, "space", swap)]
    return pieces, prepared


def on_device(queries, keys, values, residual, attn_gain, value_taps, gate_taps):
    frames, rows, width, dim = queries.shape
    tokens = frames * rows * width
    flat = lambda a: a.reshape(tokens, dim)
    state_rows = cdiv(cdiv(dim, LANES) * HEAD_DIM, 64) * 64
    pieces, prepared = running_states(
        flat(keys),
        flat(values),
        queries.reshape(rows, width, dim),
        residual.reshape(rows, width, dim),
        state_rows,
        lambda edge: prepare(flat(queries), flat(residual), edge, attn_gain[None]),
    )
    out = mix(prepared, value_taps, gate_taps, pieces, rows, width)
    return out.reshape(frames, rows, width, dim)


def solution(mesh):
    placed = P(("groups", "frame"), "space", None, None)
    return jax.shard_map(
        on_device,
        mesh=mesh,
        in_specs=(placed, placed, placed, placed, P(), P(), P()),
        out_specs=placed,
        check_vma=False,
    )
```

```python
import functools
import math

import jax
import jax.numpy as jnp
from jax import lax
from jax.experimental import pallas as pl
from jax.experimental.pallas import tpu as pltpu
from jax.sharding import PartitionSpec as P

HEAD_DIM = 112
LANES = 128
GROUP = math.lcm(HEAD_DIM, LANES)
TILES = GROUP // LANES


def cdiv(a, b):
    return -(-a // b)


def in_hbm(array):
    return pltpu.with_memory_space_constraint(array, pltpu.HBM)


def lane_iota(shape):
    return lax.broadcasted_iota(jnp.int32, shape, len(shape) - 1)


def tile_heads(j, lanes):
    lo, hi = j * LANES, min((j + 1) * LANES, lanes)
    heads = range(lo // HEAD_DIM, cdiv(hi, HEAD_DIM))
    return [(h, max(h * HEAD_DIM - lo, 0), min((h + 1) * HEAD_DIM - lo, LANES)) for h in heads]


def spans(lanes):
    count = cdiv(lanes, LANES)
    result = []
    for j in range(0, count, 2):
        tiles = list(range(j, min(j + 2, count)))
        first = tile_heads(tiles[0], lanes)[0][0] * HEAD_DIM // LANES
        last = cdiv((tile_heads(tiles[-1], lanes)[-1][0] + 1) * HEAD_DIM, LANES)
        result.append((tiles, first, last))
    return result


def regions(dim):
    count = cdiv(dim, GROUP)
    result, place = [], 0
    for groups in [range(0, 1), range(1, count)] if count > 1 else [range(0, 1)]:
        lanes = min(dim, groups.stop * GROUP) - groups.start * GROUP
        rows = cdiv(cdiv(lanes, LANES) * HEAD_DIM, 64) * 64
        result.append((groups, place, rows))
        place += rows
    return result


def by_group(dim, body):
    full, rest = divmod(dim, GROUP)
    if full:
        pl.when(pl.program_id(0) < full)(lambda: body(GROUP))
    if rest:
        pl.when(pl.program_id(0) >= full)(lambda: body(rest))


def state_kernel(dim, with_edge, keys_ref, values_ref, *refs):
    step = pl.program_id(0)
    *refs, turned, whole, semaphores = refs
    if with_edge:
        *sources, edge_ref = refs[:2] + refs[-1:]
        parts = refs[2:-1]
        row = (sources[0].shape[0] - 1) * (1 - lax.axis_index("space"))
        copies = [
            pltpu.make_async_copy(source.at[row], edge_ref.at[k, 0], semaphores.at[k])
            for k, source in enumerate(sources)
        ]

        @pl.when(step == 0)
        def _():
            for copy in copies:
                copy.start()

    else:
        parts = refs

    def body(lanes):
        turned[...] = jnp.maximum(keys_ref[...], 0).T
        lane = lane_iota((HEAD_DIM, LANES))
        for tiles, _, _ in spans(lanes):
            begin = tile_heads(tiles[0], lanes)[0][0]
            end = tile_heads(tiles[-1], lanes)[-1][0] + 1
            product = jnp.dot(
                turned[begin * HEAD_DIM : end * HEAD_DIM, :],
                values_ref[:, tiles[0] * LANES : (tiles[-1] + 1) * LANES],
                preferred_element_type=jnp.float32,
            )
            for side, j in enumerate(tiles):
                total = jnp.zeros((HEAD_DIM, LANES), jnp.float32)
                for h, lo, hi in tile_heads(j, lanes):
                    part = product[
                        (h - begin) * HEAD_DIM : (h - begin + 1) * HEAD_DIM,
                        side * LANES : (side + 1) * LANES,
                    ]
                    total = jnp.where((lane >= lo) & (lane < hi), part, total)
                row = (step * TILES + j) * HEAD_DIM
                for groups, place, _ in regions(dim)[1:]:
                    shift = place - groups.start * TILES * HEAD_DIM
                    row = jnp.where(step >= groups.start, (step * TILES + j) * HEAD_DIM + shift, row)
                row = pl.multiple_of(row, 16)
                whole[pl.ds(row, HEAD_DIM), :] = total.astype(jnp.bfloat16)

    by_group(dim, body)

    @pl.when(step == pl.num_programs(0) - 1)
    def _():
        for groups, place, rows in regions(dim):
            lanes = min(dim, groups.stop * GROUP) - groups.start * GROUP
            used = cdiv(lanes, LANES) * HEAD_DIM
            if used < rows:
                whole[place + used : place + rows, :] = jnp.zeros((rows - used, LANES), jnp.bfloat16)
            size = rows // len(parts)
            for k, part in enumerate(parts):
                turn = lax.rem(lax.axis_index("space") + k, 2) if len(parts) == 2 else 0
                source = pl.ds(pl.multiple_of(place + turn * size, 16), size)
                part[place // len(parts) : place // len(parts) + size, :] = whole[source, :]
        if with_edge:
            for copy in copies:
                copy.wait()


def frame_states(keys, values, parts, edged=()):
    tokens, dim = keys.shape
    rows = sum(rows for _, _, rows in regions(dim))
    part = (rows // parts, LANES)
    block = pl.BlockSpec((tokens, GROUP), lambda g: (0, g))
    return pl.pallas_call(
        functools.partial(state_kernel, dim, bool(edged)),
        out_shape=[pltpu.VMEM(part, jnp.bfloat16)] * parts
        + [pltpu.VMEM((len(edged), 1, *edged[0].shape[1:]), jnp.bfloat16) for _ in edged[:1]],
        grid=(cdiv(dim, GROUP),),
        in_specs=[block, block] + [pl.BlockSpec(memory_space=pl.ANY)] * len(edged),
        out_specs=[pl.BlockSpec(part, lambda g: (0, 0))] * parts
        + [pl.BlockSpec(memory_space=pl.ANY) for _ in edged[:1]],
        scratch_shapes=[
            pltpu.VMEM((GROUP, tokens), jnp.bfloat16),
            pltpu.VMEM((rows, LANES), jnp.bfloat16),
            pltpu.SemaphoreType.DMA((2,)),
        ],
        compiler_params=pltpu.CompilerParams(vmem_limit_bytes=60 * 2**20),
        cost_estimate=pl.CostEstimate(
            flops=2 * tokens * dim * HEAD_DIM, bytes_accessed=4 * tokens * dim, transcendentals=0
        ),
        name="frame_states",
    )(in_hbm(keys), in_hbm(values), *[in_hbm(array) for array in edged])


def group_lanes(dim):
    return [(first, min(GROUP, dim - first)) for first in range(0, dim, GROUP)]


def prepare_kernel(
    dim, queries_ref, residual_ref, edge_ref, gain_ref,
    features_ref, inputs_ref, scaled_ref, held, semaphores,
):
    tokens = queries_ref.shape[0]
    full = dim // LANES * LANES
    parts = [slice(0, full), slice(full, dim)] if full < dim else [slice(0, dim)]
    copies = [
        pltpu.make_async_copy(queries_ref, held.at[:tokens], semaphores.at[0]),
        pltpu.make_async_copy(residual_ref, inputs_ref.at[:tokens], semaphores.at[1]),
    ]
    for copy in copies:
        copy.start()
    edges, width = edge_ref.shape[1:3]
    for e in range(edges):
        here = slice(tokens + e * width, tokens + (e + 1) * width)
        held[here] = edge_ref[0, e]
        inputs_ref[here] = edge_ref[1, e]
    scaled_ref[...] = gain_ref[...] * math.sqrt(HEAD_DIM)
    if full < dim:
        features_ref[:, full:] = jnp.zeros((features_ref.shape[0], LANES), jnp.bfloat16)
    copies[0].wait()
    for part in parts:
        features_ref[:, part] = jnp.maximum(held[:, part], 0)
    copies[1].wait()


def prepare(queries, residual, edge, gain):
    tokens, dim = queries.shape
    total = tokens + edge.shape[1] * edge.shape[2]
    whole = pl.BlockSpec(memory_space=pltpu.VMEM)
    return pl.pallas_call(
        functools.partial(prepare_kernel, dim),
        out_shape=[
            pltpu.VMEM((total, cdiv(dim, LANES) * LANES), jnp.bfloat16),
            pltpu.VMEM((total, dim), jnp.bfloat16),
            pltpu.VMEM((1, dim), jnp.float32),
        ],
        in_specs=[pl.BlockSpec(memory_space=pl.ANY)] * 2 + [whole] * 2,
        out_specs=[whole] * 3,
        scratch_shapes=[
            pltpu.VMEM((total, dim), jnp.bfloat16),
            pltpu.SemaphoreType.DMA((2,)),
        ],
        compiler_params=pltpu.CompilerParams(vmem_limit_bytes=24 * 2**20),
        cost_estimate=pl.CostEstimate(
            flops=4 * total * dim, bytes_accessed=8 * total * dim, transcendentals=0
        ),
        name="prepare",
    )(in_hbm(queries), in_hbm(residual), edge, gain)


def mix_kernel(
    dim, groups, rows, width, edges, count,
    features_ref, inputs_ref, gain_ref, vtaps_ref, gtaps_ref, *refs,
):
    *pieces, out_ref, states, weights, numer, windows, held, semaphores = refs
    pieces = pieces[:count]
    places = edge_places(lax.axis_size("space"), rows) if edges else []
    spots = piece_places() if len(pieces) > 1 else [0]
    tokens = rows * width
    weights[...] = jnp.zeros_like(weights)
    for k, piece in enumerate(pieces):
        size = piece.shape[0]
        states[pl.ds(pl.multiple_of(spots[k] * size, 16), size), :] = piece[...]
    lane = lane_iota((HEAD_DIM, LANES))
    sublane = lax.broadcasted_iota(jnp.int32, (8, LANES), 0)

    def store_windows(mixed, row, slot, used):
        mixed = mixed.astype(jnp.bfloat16).astype(jnp.float32)
        windows[slot, 1, row, :, :used] = mixed
        before, after = pltpu.roll(mixed, 1, 0), pltpu.roll(mixed, width - 1, 0)
        windows[slot, 0, row, :8, :used] = jnp.where(sublane[:, :used] == 0, 0.0, before[:8])
        windows[slot, 0, row, 8:, :used] = before[8:]
        windows[slot, 2, row, : width - 8, :used] = after[: width - 8]
        windows[slot, 2, row, width - 8 :, :used] = jnp.where(
            sublane[:, :used] == 7, 0.0, after[width - 8 :]
        )

    def group(base, lanes):
        pairs = spans(lanes)

        def numerators(number):
            tiles, first, last = pairs[number]
            for side, j in enumerate(tiles):
                row = ((base - groups.start * GROUP) // LANES + j) * HEAD_DIM
                state = states[row : row + HEAD_DIM, :].astype(jnp.float32)
                for h, lo, hi in tile_heads(j, lanes):
                    start = h * HEAD_DIM - first * LANES
                    block = jnp.where((lane >= lo) & (lane < hi), state, 0.0)
                    weights[
                        number, start : start + HEAD_DIM, side * LANES : (side + 1) * LANES
                    ] = block.astype(jnp.bfloat16)
            depth, wide = (last - first) * LANES, len(tiles) * LANES
            product = jnp.dot(
                features_ref[:, base + first * LANES : base + last * LANES],
                weights[number, :depth, :wide],
                preferred_element_type=jnp.float32,
            )
            here = slice(tiles[0] * LANES, tiles[0] * LANES + wide)
            numer[:, here] = product

        def tile_sums(j, source):
            square = numer[source, j * LANES : (j + 1) * LANES]
            square = square * square
            heads = tile_heads(j, lanes)
            if len(heads) == 1:
                return {heads[0][0]: jnp.sum(square, axis=-1, keepdims=True)}
            (one, _, bound), (two, _, _) = heads
            part = jnp.where(lane_iota(square.shape) < bound, square, 0.0)
            rest = square - part
            return {
                one: jnp.sum(part, axis=-1, keepdims=True),
                two: jnp.sum(rest, axis=-1, keepdims=True),
            }

        def mix_tile(j):
            slot = j % 2
            used = min(LANES, lanes - j * LANES)
            near = slice(j * LANES, j * LANES + used)
            here = slice(base + j * LANES, base + j * LANES + used)
            heads = tile_heads(j, lanes)

            def mixed(source):
                sums = [
                    sum(tiles[head] for tiles in parts[source.start] if head in tiles)
                    for head, _, _ in heads
                ]
                scale = jnp.broadcast_to(sums[0], (width, used))
                if len(heads) > 1:
                    scale = jnp.where(lane_iota(scale.shape) < heads[0][2], scale, sums[1])
                normed = numer[source, near] * lax.rsqrt(scale + HEAD_DIM * 1e-06)
                return inputs_ref[source, here].astype(jnp.float32) + normed * gain_ref[:, here]

            outside = [None, None]
            for e in range(edges):
                value = mixed(slice(tokens + e * width, tokens + (e + 1) * width))
                for k, row in enumerate((0, rows + 1)):
                    part = jnp.where(places[e] == row, value, 0.0)
                    outside[k] = part if outside[k] is None else outside[k] + part
            for k, row in enumerate((0, rows + 1)):
                store_windows(outside[k], row, slot, used)
            for row in range(rows):
                store_windows(mixed(slice(row * width, (row + 1) * width)), row + 1, slot, used)
            for row in range(rows):
                conv_v = half_g = None
                for tap in range(9):
                    window = windows[slot, tap % 3, row + tap // 3, :, :used]
                    value = vtaps_ref[tap : tap + 1, here] * window
                    gate = (0.5 * gtaps_ref[tap : tap + 1, here]) * window
                    conv_v = value if tap == 0 else conv_v + value
                    half_g = gate if tap == 0 else half_g + gate
                center = windows[slot, 1, row + 1, :, :used]
                result = center + conv_v * (half_g + half_g * jnp.tanh(half_g))
                held[row * width : (row + 1) * width, here] = result.astype(jnp.bfloat16)

        parts = {}
        for number, (tiles, _, _) in enumerate(pairs):
            numerators(number)
            for j in tiles:
                for row in range(rows + edges):
                    source = slice(row * width, (row + 1) * width)
                    parts.setdefault(source.start, []).append(tile_sums(j, source))
        for j in range(cdiv(lanes, LANES)):
            mix_tile(j)

    copies = []
    for base, lanes in group_lanes(dim)[groups.start : groups.stop]:
        group(base, lanes)
        here = slice(base, base + lanes)
        copies.append(
            pltpu.make_async_copy(held.at[:, here], out_ref.at[:, here], semaphores.at[len(copies)])
        )
        copies[-1].start()
    for copy in copies:
        copy.wait()


def mix(groups, out, prepared, value_taps, gate_taps, pieces, rows, width):
    features, inputs, gain = prepared
    total, dim = inputs.shape
    tokens = rows * width
    pairs = spans(min(GROUP, dim))
    depth = max(last - first for _, first, last in pairs) * LANES
    whole = pl.BlockSpec(memory_space=pltpu.VMEM)
    earlier = [] if out is None else [out]
    lanes = min(dim, groups.stop * GROUP) - groups.start * GROUP
    return pl.pallas_call(
        functools.partial(
            mix_kernel, dim, groups, rows, width, (total - tokens) // width, len(pieces)
        ),
        out_shape=jax.ShapeDtypeStruct((tokens, dim), jnp.bfloat16),
        in_specs=[whole] * (5 + len(pieces)) + [pl.BlockSpec(memory_space=pl.ANY)] * len(earlier),
        out_specs=pl.BlockSpec(memory_space=pl.ANY),
        input_output_aliases={5 + len(pieces): 0} if earlier else {},
        scratch_shapes=[
            pltpu.VMEM((sum(piece.shape[0] for piece in pieces), LANES), jnp.bfloat16),
            pltpu.VMEM((len(pairs), depth, 2 * LANES), jnp.bfloat16),
            pltpu.VMEM((total, GROUP), jnp.float32),
            pltpu.VMEM((2, 3, rows + 2, width, LANES), jnp.float32),
            pltpu.VMEM((tokens, dim), jnp.bfloat16),
            pltpu.SemaphoreType.DMA((len(groups),)),
        ],
        compiler_params=pltpu.CompilerParams(vmem_limit_bytes=36 * 2**20),
        cost_estimate=pl.CostEstimate(
            flops=1000 * tokens * lanes, bytes_accessed=6 * tokens * lanes, transcendentals=0
        ),
        name="mix",
    )(features, inputs, gain, value_taps, gate_taps, *pieces, *earlier)


def edge_rows(queries, residual):
    devices, rows = lax.axis_size("space"), queries.shape[0]
    up = [(i, i + 1) for i in range(devices - 1)]
    down = [(j, i) for i, j in up]
    both = jnp.stack([queries, residual])
    if devices == 2:
        first = lax.axis_index("space") == 0
        return lax.ppermute(jnp.where(first, both[:, rows - 1 :], both[:, :1]), "space", up + down)
    before = lax.ppermute(both[:, rows - 1 :], "space", up)
    after = lax.ppermute(both[:, :1], "space", down)
    return jnp.concatenate([before, after], axis=1)


def small_kernel(body, name, outs, *arrays):
    return pl.pallas_call(
        body,
        out_shape=[pltpu.VMEM(shape, jnp.bfloat16) for shape in outs],
        in_specs=[pl.BlockSpec(memory_space=pltpu.VMEM)] * len(arrays),
        out_specs=[pl.BlockSpec(memory_space=pltpu.VMEM)] * len(outs),
        compiler_params=pltpu.CompilerParams(vmem_limit_bytes=4 * 2**20),
        name=name,
    )(*arrays)


def add(*values):
    total = values[0].astype(jnp.float32)
    for value in values[1:]:
        total = total + value.astype(jnp.float32)
    return total


def parity():
    return lax.rem(lax.axis_index("frame"), 2)


def split_sum_body(dim, kept_ref, got_ref, mine_ref, theirs_ref):
    for _, place, rows in regions(dim):
        size = rows // 4
        for ref, side in ((theirs_ref, 1 - parity()), (mine_ref, parity())):
            source = pl.ds(pl.multiple_of(place // 2 + side * size, 16), size)
            ref[place // 4 : place // 4 + size, :] = add(
                kept_ref[source, :], got_ref[source, :]
            ).astype(jnp.bfloat16)


def sum_body(*refs):
    *terms, out_ref = refs
    out_ref[...] = add(*[term[...] for term in terms]).astype(jnp.bfloat16)


def region_sum_body(dim, one_ref, other_ref, *out_refs):
    for (_, place, rows), out_ref in zip(regions(dim), out_refs):
        here = slice(place // 4, (place + rows) // 4)
        out_ref[...] = add(one_ref[here, :], other_ref[here, :]).astype(jnp.bfloat16)


def pair_sums_body(here, own_ref, partner_ref, *refs):
    *earlier, mine_ref, theirs_ref = refs
    before = jnp.zeros(mine_ref.shape, jnp.float32)
    for k, ref in enumerate(earlier):
        from_before = lax.rem(lax.axis_index("frame") // (2 << k), 2) == 1
        part = ref[...] if ref.shape == mine_ref.shape else ref[here, :]
        before = before + jnp.where(from_before, add(part), 0.0)
    own, partner = add(own_ref[here, :]), add(partner_ref[here, :])
    first = parity() == 0
    both = before + (own + partner)
    mine_ref[...] = jnp.where(first, before + own, both).astype(jnp.bfloat16)
    theirs_ref[...] = jnp.where(first, both, before + partner).astype(jnp.bfloat16)


def paired(devices, frames):
    return devices == 2 and frames >= 4 and frames & (frames - 1) == 0


def piece_places():
    core = lax.axis_index("space")
    return [2 * c + p for c in (core, 1 - core) for p in (parity(), 1 - parity())]


def edge_places(devices, rows):
    if devices == 2:
        return [jnp.where(lax.axis_index("space") == 0, rows + 1, 0)]
    return [0, rows + 1]


def running_states(keys, values, queries, residual, beside):
    devices, frames = lax.axis_size("space"), lax.axis_size("frame")
    dim = keys.shape[-1]
    if not paired(devices, frames):
        (state,) = frame_states(keys, values, 1)
        state = lax.psum(state.astype(jnp.float32), "space").astype(jnp.bfloat16)
        every = lax.all_gather(state, "frame").astype(jnp.float32)
        reached = (jnp.arange(frames) <= lax.axis_index("frame"))[:, None, None]
        total = jnp.sum(jnp.where(reached, every, 0.0), axis=0).astype(jnp.bfloat16)
        pieces = [[total[place : place + rows]] for _, place, rows in regions(dim)]
        return pieces, beside(edge_rows(queries, residual))
    swap = [(0, 1), (1, 0)]
    exchange = lambda array, stride: lax.ppermute(
        array, "frame", [(f, f ^ stride) for f in range(frames)]
    )
    kept, sent, edge = frame_states(keys, values, 2, (queries, residual))
    got = lax.ppermute(sent, "space", swap)
    quarter = (got.shape[0] // 2, LANES)
    own, sent = small_kernel(
        functools.partial(split_sum_body, dim), "split_sum", [quarter] * 2, kept, got
    )
    partner = exchange(sent, 1)
    partner, edge = lax.optimization_barrier((partner, edge))
    edge = lax.ppermute(edge, "space", swap)
    total, other = own, partner
    earlier = []
    stride = 2
    while stride * 2 < frames:
        (total,) = small_kernel(sum_body, "sum", [quarter], total, other)
        other = exchange(total, stride)
        earlier.append(other)
        stride *= 2
    shapes = [(rows // 4, LANES) for _, _, rows in regions(dim)]
    totals = small_kernel(
        functools.partial(region_sum_body, dim), "region_sum", shapes, total, other
    )
    *totals, edge = lax.optimization_barrier((*totals, edge))
    last = [exchange(total, stride) for total in totals]
    prepared = beside(edge)
    last[0], *prepared = lax.optimization_barrier((last[0], *prepared))
    across = [(2 * f + c, 2 * (f ^ 1) + 1 - c) for f in range(frames) for c in range(2)]
    results = []
    for k, (_, place, rows) in enumerate(regions(dim)):
        here = slice(place // 4, (place + rows) // 4)
        mine, theirs = small_kernel(
            functools.partial(pair_sums_body, here), "pair_sums", [shapes[k]] * 2,
            own, partner, *earlier, last[k],
        )
        theirs_here = exchange(theirs, 1)
        mine_there = lax.ppermute(mine, "space", swap)
        if k == 0:
            theirs_there = lax.ppermute(theirs_here, "space", swap)
        else:
            theirs_there = lax.ppermute(theirs, ("frame", "space"), across)
        results.append([mine, theirs_here, mine_there, theirs_there])
    return results, prepared


def on_device(queries, keys, values, residual, attn_gain, value_taps, gate_taps):
    frames, rows, width, dim = queries.shape
    tokens = frames * rows * width
    flat = lambda a: a.reshape(tokens, dim)
    results, prepared = running_states(
        flat(keys),
        flat(values),
        queries.reshape(rows, width, dim),
        residual.reshape(rows, width, dim),
        lambda edge: prepare(flat(queries), flat(residual), edge, attn_gain[None]),
    )
    out = None
    for (groups, _, _), pieces in zip(regions(dim), results):
        out = mix(groups, out, prepared, value_taps, gate_taps, pieces, rows, width)
    return out.reshape(frames, rows, width, dim)


def solution(mesh):
    placed = P(("groups", "frame"), "space", None, None)
    return jax.shard_map(
        on_device,
        mesh=mesh,
        in_specs=(placed, placed, placed, placed, P(), P(), P()),
        out_specs=placed,
        check_vma=False,
    )
```

```python
import functools
import math

import jax
import jax.numpy as jnp
from jax import lax
from jax.experimental import pallas as pl
from jax.experimental.pallas import tpu as pltpu
from jax.sharding import PartitionSpec as P

HEAD_DIM = 112
LANES = 128
GROUP = math.lcm(HEAD_DIM, LANES)
TILES = GROUP // LANES


def cdiv(a, b):
    return -(-a // b)


def in_hbm(array):
    return pltpu.with_memory_space_constraint(array, pltpu.HBM)


def lane_iota(shape):
    return lax.broadcasted_iota(jnp.int32, shape, len(shape) - 1)


def tile_heads(j, lanes):
    lo, hi = j * LANES, min((j + 1) * LANES, lanes)
    heads = range(lo // HEAD_DIM, cdiv(hi, HEAD_DIM))
    return [(h, max(h * HEAD_DIM - lo, 0), min((h + 1) * HEAD_DIM - lo, LANES)) for h in heads]


def spans(lanes):
    count = cdiv(lanes, LANES)
    result = []
    for j in range(0, count, 2):
        tiles = list(range(j, min(j + 2, count)))
        first = tile_heads(tiles[0], lanes)[0][0] * HEAD_DIM // LANES
        last = cdiv((tile_heads(tiles[-1], lanes)[-1][0] + 1) * HEAD_DIM, LANES)
        result.append((tiles, first, last))
    return result


def by_group(dim, body):
    full, rest = divmod(dim, GROUP)
    if full:
        pl.when(pl.program_id(0) < full)(lambda: body(GROUP))
    if rest:
        pl.when(pl.program_id(0) >= full)(lambda: body(rest))


def state_kernel(dim, with_edge, keys_refs, values_refs, refs):
    step = pl.program_id(0)
    *refs, turned, whole, semaphores = refs
    if with_edge:
        *sources, edge_ref = refs[:2] + refs[-1:]
        parts = refs[2:-1]
        row = (sources[0].shape[0] - 1) * (1 - lax.axis_index("space"))
        copies = [
            pltpu.make_async_copy(source.at[row], edge_ref.at[k, 0], semaphores.at[k])
            for k, source in enumerate(sources)
        ]

        @pl.when(step == 0)
        def _():
            for copy in copies:
                copy.start()

    else:
        parts = refs

    def body(lanes):
        for k, keys_ref in enumerate(keys_refs):
            turned[k] = jnp.maximum(keys_ref[...], 0).T
        lane = lane_iota((HEAD_DIM, LANES))
        for tiles, _, _ in spans(lanes):
            begin = tile_heads(tiles[0], lanes)[0][0]
            end = tile_heads(tiles[-1], lanes)[-1][0] + 1
            product = sum(
                jnp.dot(
                    turned[k, begin * HEAD_DIM : end * HEAD_DIM, :],
                    values_ref[:, tiles[0] * LANES : (tiles[-1] + 1) * LANES],
                    preferred_element_type=jnp.float32,
                )
                for k, values_ref in enumerate(values_refs)
            )
            for side, j in enumerate(tiles):
                total = jnp.zeros((HEAD_DIM, LANES), jnp.float32)
                for h, lo, hi in tile_heads(j, lanes):
                    part = product[
                        (h - begin) * HEAD_DIM : (h - begin + 1) * HEAD_DIM,
                        side * LANES : (side + 1) * LANES,
                    ]
                    total = jnp.where((lane >= lo) & (lane < hi), part, total)
                row = pl.multiple_of((step * TILES + j) * HEAD_DIM, 16)
                whole[pl.ds(row, HEAD_DIM), :] = total.astype(jnp.bfloat16)

    by_group(dim, body)

    @pl.when(step == pl.num_programs(0) - 1)
    def _():
        used = cdiv(dim, LANES) * HEAD_DIM
        if used < whole.shape[0]:
            whole[used:, :] = jnp.zeros((whole.shape[0] - used, LANES), jnp.bfloat16)
        for k, part in enumerate(parts):
            size = part.shape[0]
            turn = lax.rem(lax.axis_index("space") + k, 2) if len(parts) == 2 else 0
            part[...] = whole[pl.ds(pl.multiple_of(turn * size, 16), size), :]
        if with_edge:
            for copy in copies:
                copy.wait()


def frame_states(keys, values, rows, parts, edged=()):
    tokens, dim = keys.shape
    part = (rows // parts, LANES)
    slabs = 2 if tokens % 32 == 0 else 1
    blocks = [
        pl.BlockSpec((tokens // slabs, GROUP), functools.partial(lambda k, g: (k, g), k))
        for k in range(slabs)
    ]

    def body(*refs):
        state_kernel(dim, bool(edged), refs[:slabs], refs[slabs : 2 * slabs], refs[2 * slabs :])

    return pl.pallas_call(
        body,
        out_shape=[pltpu.VMEM(part, jnp.bfloat16)] * parts
        + [pltpu.VMEM((len(edged), 1, *edged[0].shape[1:]), jnp.bfloat16) for _ in edged[:1]],
        grid=(cdiv(dim, GROUP),),
        in_specs=blocks + blocks + [pl.BlockSpec(memory_space=pl.ANY)] * len(edged),
        out_specs=[pl.BlockSpec(part, lambda g: (0, 0))] * parts
        + [pl.BlockSpec(memory_space=pl.ANY) for _ in edged[:1]],
        scratch_shapes=[
            pltpu.VMEM((slabs, GROUP, tokens // slabs), jnp.bfloat16),
            pltpu.VMEM((rows, LANES), jnp.bfloat16),
            pltpu.SemaphoreType.DMA((2,)),
        ],
        compiler_params=pltpu.CompilerParams(vmem_limit_bytes=60 * 2**20),
        cost_estimate=pl.CostEstimate(
            flops=2 * tokens * dim * HEAD_DIM, bytes_accessed=4 * tokens * dim, transcendentals=0
        ),
        name="frame_states",
    )(*[in_hbm(keys)] * slabs, *[in_hbm(values)] * slabs, *[in_hbm(array) for array in edged])


def group_lanes(dim):
    return [(first, min(GROUP, dim - first)) for first in range(0, dim, GROUP)]


def prepare_kernel(
    dim, queries_ref, residual_ref, edge_ref, gain_ref,
    features_ref, inputs_ref, scaled_ref, held, semaphores,
):
    tokens = queries_ref.shape[0]
    full = dim // LANES * LANES
    parts = [slice(0, full), slice(full, dim)] if full < dim else [slice(0, dim)]
    copies = [
        pltpu.make_async_copy(queries_ref, held.at[:tokens], semaphores.at[0]),
        pltpu.make_async_copy(residual_ref, inputs_ref.at[:tokens], semaphores.at[1]),
    ]
    for copy in copies:
        copy.start()
    edges, width = edge_ref.shape[1:3]
    for e in range(edges):
        here = slice(tokens + e * width, tokens + (e + 1) * width)
        held[here] = edge_ref[0, e]
        inputs_ref[here] = edge_ref[1, e]
    scaled_ref[...] = gain_ref[...] * math.sqrt(HEAD_DIM)
    if full < dim:
        features_ref[:, full:] = jnp.zeros((features_ref.shape[0], LANES), jnp.bfloat16)
    copies[0].wait()
    for part in parts:
        features_ref[:, part] = jnp.maximum(held[:, part], 0)
    copies[1].wait()


def prepare(queries, residual, edge, gain):
    tokens, dim = queries.shape
    total = tokens + edge.shape[1] * edge.shape[2]
    whole = pl.BlockSpec(memory_space=pltpu.VMEM)
    return pl.pallas_call(
        functools.partial(prepare_kernel, dim),
        out_shape=[
            pltpu.VMEM((total, cdiv(dim, LANES) * LANES), jnp.bfloat16),
            pltpu.VMEM((total, dim), jnp.bfloat16),
            pltpu.VMEM((1, dim), jnp.float32),
        ],
        in_specs=[pl.BlockSpec(memory_space=pl.ANY)] * 2 + [whole] * 2,
        out_specs=[whole] * 3,
        scratch_shapes=[
            pltpu.VMEM((total, dim), jnp.bfloat16),
            pltpu.SemaphoreType.DMA((2,)),
        ],
        compiler_params=pltpu.CompilerParams(vmem_limit_bytes=24 * 2**20),
        cost_estimate=pl.CostEstimate(
            flops=4 * total * dim, bytes_accessed=8 * total * dim, transcendentals=0
        ),
        name="prepare",
    )(in_hbm(queries), in_hbm(residual), edge, gain)


def mix_kernel(
    dim, rows, width, edges,
    features_ref, inputs_ref, gain_ref, vtaps_ref, gtaps_ref, *refs,
):
    *pieces, out_ref, states, weights, numer, rounded, windows, results, held, semaphores = refs
    places = edge_places(lax.axis_size("space"), rows) if edges else []
    spots = piece_places() if len(pieces) > 1 else [0]
    tokens = rows * width
    weights[...] = jnp.zeros_like(weights)
    for k, piece in enumerate(pieces):
        size = piece.shape[0]
        states[pl.ds(pl.multiple_of(spots[k] * size, 16), size), :] = piece[...]
    lane = lane_iota((HEAD_DIM, LANES))
    sublane = lax.broadcasted_iota(jnp.int32, (8, LANES), 0)

    half = width // 2
    even, odd = pl.ds(0, half, stride=2), pl.ds(1, half, stride=2)

    def store_windows(mixed, row, slot, used):
        rounded[slot, row, :, :used] = mixed.astype(jnp.bfloat16).astype(jnp.float32)
        left, right = rounded[slot, row, even, :used], rounded[slot, row, odd, :used]
        sub = sublane[:, :used]
        before, after = pltpu.roll(right, 1, 0), pltpu.roll(left, half - 1, 0)
        before = jnp.concatenate([jnp.where(sub == 0, 0.0, before[:8]), before[8:]], axis=0)
        after = jnp.concatenate([after[: half - 8], jnp.where(sub == 7, 0.0, after[half - 8 :])], axis=0)
        for k, window in enumerate((before - right, left + right, right - left, left - after)):
            windows[slot, k, row, :, :used] = window

    def group(base, lanes):
        pairs = spans(lanes)

        def numerators(number):
            tiles, first, last = pairs[number]
            for side, j in enumerate(tiles):
                row = (base // LANES + j) * HEAD_DIM
                state = states[row : row + HEAD_DIM, :].astype(jnp.float32)
                for h, lo, hi in tile_heads(j, lanes):
                    start = h * HEAD_DIM - first * LANES
                    block = jnp.where((lane >= lo) & (lane < hi), state, 0.0)
                    weights[
                        number, start : start + HEAD_DIM, side * LANES : (side + 1) * LANES
                    ] = block.astype(jnp.bfloat16)
            depth, wide = (last - first) * LANES, len(tiles) * LANES
            product = jnp.dot(
                features_ref[:, base + first * LANES : base + last * LANES],
                weights[number, :depth, :wide],
                preferred_element_type=jnp.float32,
            )
            here = slice(tiles[0] * LANES, tiles[0] * LANES + wide)
            numer[:, here] = product

        def tile_sums(j, source):
            square = numer[source, j * LANES : (j + 1) * LANES]
            square = square * square
            heads = tile_heads(j, lanes)
            if len(heads) == 1:
                return {heads[0][0]: jnp.sum(square, axis=-1, keepdims=True)}
            (one, _, bound), (two, _, _) = heads
            part = jnp.where(lane_iota(square.shape) < bound, square, 0.0)
            rest = square - part
            return {
                one: jnp.sum(part, axis=-1, keepdims=True),
                two: jnp.sum(rest, axis=-1, keepdims=True),
            }

        def mix_tile(j):
            slot = j % 2
            used = min(LANES, lanes - j * LANES)
            near = slice(j * LANES, j * LANES + used)
            here = slice(base + j * LANES, base + j * LANES + used)
            heads = tile_heads(j, lanes)

            def mixed(source):
                sums = [
                    sum(tiles[head] for tiles in parts[source.start] if head in tiles)
                    for head, _, _ in heads
                ]
                scale = jnp.broadcast_to(sums[0], (width, used))
                if len(heads) > 1:
                    scale = jnp.where(lane_iota(scale.shape) < heads[0][2], scale, sums[1])
                normed = numer[source, near] * lax.rsqrt(scale + HEAD_DIM * 1e-06)
                return inputs_ref[source, here].astype(jnp.float32) + normed * gain_ref[:, here]

            outside = [None, None]
            for e in range(edges):
                value = mixed(slice(tokens + e * width, tokens + (e + 1) * width))
                for k, row in enumerate((0, rows + 1)):
                    part = jnp.where(places[e] == row, value, 0.0)
                    outside[k] = part if outside[k] is None else outside[k] + part
            for k, row in enumerate((0, rows + 1)):
                store_windows(outside[k], row, slot, used)
            for row in range(rows):
                store_windows(mixed(slice(row * width, (row + 1) * width)), row + 1, slot, used)
            taps = []
            for ref, factor in ((vtaps_ref, 1.0), (gtaps_ref, 0.5)):
                for tap_row in range(3):
                    one, two, three = [
                        ref[3 * tap_row + i : 3 * tap_row + i + 1, here] * factor for i in range(3)
                    ]
                    outer = 0.5 * (one + three)
                    taps.append((one, outer + 0.5 * two, outer - 0.5 * two, three))
            for row in range(rows):
                columns = []
                for f in range(2):
                    products = []
                    for k in range(4):
                        total = None
                        for tap_row in range(3):
                            term = taps[3 * f + tap_row][k] * windows[slot, k, row + tap_row, :, :used]
                            total = term if total is None else total + term
                        products.append(total)
                    columns.append(
                        (
                            products[0] + products[1] + products[2],
                            products[1] - products[2] - products[3],
                        )
                    )
                for side, (conv_v, half_g) in zip((even, odd), zip(*columns)):
                    center = rounded[slot, row + 1, side, :used]
                    results[slot, row, side, :used] = center + conv_v * (
                        half_g + half_g * jnp.tanh(half_g)
                    )
                held[row * width : (row + 1) * width, here] = results[slot, row, :, :used].astype(
                    jnp.bfloat16
                )

        parts = {}
        for number, (tiles, _, _) in enumerate(pairs):
            numerators(number)
            for j in tiles:
                for row in range(rows + edges):
                    source = slice(row * width, (row + 1) * width)
                    parts.setdefault(source.start, []).append(tile_sums(j, source))
        for j in range(cdiv(lanes, LANES)):
            mix_tile(j)

    copies = []
    for base, lanes in group_lanes(dim):
        group(base, lanes)
        here = slice(base, base + lanes)
        copies.append(
            pltpu.make_async_copy(held.at[:, here], out_ref.at[:, here], semaphores.at[len(copies)])
        )
        copies[-1].start()
    for copy in copies:
        copy.wait()


def mix(prepared, value_taps, gate_taps, pieces, rows, width):
    features, inputs, gain = prepared
    total, dim = inputs.shape
    tokens = rows * width
    pairs = spans(min(GROUP, dim))
    depth = max(last - first for _, first, last in pairs) * LANES
    whole = pl.BlockSpec(memory_space=pltpu.VMEM)
    return pl.pallas_call(
        functools.partial(mix_kernel, dim, rows, width, (total - tokens) // width),
        out_shape=jax.ShapeDtypeStruct((tokens, dim), jnp.bfloat16),
        in_specs=[whole] * (5 + len(pieces)),
        out_specs=pl.BlockSpec(memory_space=pl.ANY),
        scratch_shapes=[
            pltpu.VMEM((sum(piece.shape[0] for piece in pieces), LANES), jnp.bfloat16),
            pltpu.VMEM((len(pairs), depth, 2 * LANES), jnp.bfloat16),
            pltpu.VMEM((total, GROUP), jnp.float32),
            pltpu.VMEM((2, rows + 2, width, LANES), jnp.float32),
            pltpu.VMEM((2, 4, rows + 2, width // 2, LANES), jnp.float32),
            pltpu.VMEM((2, rows, width, LANES), jnp.float32),
            pltpu.VMEM((tokens, dim), jnp.bfloat16),
            pltpu.SemaphoreType.DMA((len(group_lanes(dim)),)),
        ],
        compiler_params=pltpu.CompilerParams(vmem_limit_bytes=36 * 2**20),
        cost_estimate=pl.CostEstimate(
            flops=60 * tokens * dim, bytes_accessed=6 * tokens * dim, transcendentals=2 * tokens * dim
        ),
        name="mix",
    )(features, inputs, gain, value_taps, gate_taps, *pieces)


def edge_rows(queries, residual):
    devices, rows = lax.axis_size("space"), queries.shape[0]
    up = [(i, i + 1) for i in range(devices - 1)]
    down = [(j, i) for i, j in up]
    both = jnp.stack([queries, residual])
    if devices == 2:
        first = lax.axis_index("space") == 0
        return lax.ppermute(jnp.where(first, both[:, rows - 1 :], both[:, :1]), "space", up + down)
    before = lax.ppermute(both[:, rows - 1 :], "space", up)
    after = lax.ppermute(both[:, :1], "space", down)
    return jnp.concatenate([before, after], axis=1)


def small_kernel(body, name, outs, *arrays):
    return pl.pallas_call(
        body,
        out_shape=[pltpu.VMEM(shape, jnp.bfloat16) for shape in outs],
        in_specs=[pl.BlockSpec(memory_space=pltpu.VMEM)] * len(arrays),
        out_specs=[pl.BlockSpec(memory_space=pltpu.VMEM)] * len(outs),
        compiler_params=pltpu.CompilerParams(vmem_limit_bytes=4 * 2**20),
        name=name,
    )(*arrays)


def add(*values):
    total = values[0].astype(jnp.float32)
    for value in values[1:]:
        total = total + value.astype(jnp.float32)
    return total


def parity():
    return lax.rem(lax.axis_index("frame"), 2)


def split_sum_body(kept_ref, got_ref, mine_ref, theirs_ref):
    size = mine_ref.shape[0]
    for ref, side in ((theirs_ref, 1 - parity()), (mine_ref, parity())):
        rows = pl.ds(pl.multiple_of(side * size, 16), size)
        ref[...] = add(kept_ref[rows, :], got_ref[rows, :]).astype(jnp.bfloat16)


def sum_body(*refs):
    *terms, out_ref = refs
    out_ref[...] = add(*[term[...] for term in terms]).astype(jnp.bfloat16)


def pair_sums_body(own_ref, partner_ref, *refs):
    *earlier, mine_ref, theirs_ref = refs
    before = jnp.zeros(own_ref.shape, jnp.float32)
    for k, ref in enumerate(earlier):
        from_before = lax.rem(lax.axis_index("frame") // (2 << k), 2) == 1
        before = before + jnp.where(from_before, add(ref[...]), 0.0)
    own, partner = add(own_ref[...]), add(partner_ref[...])
    first = parity() == 0
    both = before + (own + partner)
    mine_ref[...] = jnp.where(first, before + own, both).astype(jnp.bfloat16)
    theirs_ref[...] = jnp.where(first, both, before + partner).astype(jnp.bfloat16)


def paired(devices, frames):
    return devices == 2 and frames >= 4 and frames & (frames - 1) == 0


def piece_places():
    core = lax.axis_index("space")
    return [2 * c + p for c in (core, 1 - core) for p in (parity(), 1 - parity())]


def edge_places(devices, rows):
    if devices == 2:
        return [jnp.where(lax.axis_index("space") == 0, rows + 1, 0)]
    return [0, rows + 1]


def running_states(keys, values, queries, residual, rows, beside):
    devices, frames = lax.axis_size("space"), lax.axis_size("frame")
    if not paired(devices, frames):
        (state,) = frame_states(keys, values, rows, 1)
        state = lax.psum(state.astype(jnp.float32), "space").astype(jnp.bfloat16)
        every = lax.all_gather(state, "frame").astype(jnp.float32)
        reached = (jnp.arange(frames) <= lax.axis_index("frame"))[:, None, None]
        total = jnp.sum(jnp.where(reached, every, 0.0), axis=0).astype(jnp.bfloat16)
        return [total], beside(edge_rows(queries, residual))
    swap = [(0, 1), (1, 0)]
    exchange = lambda array, stride: lax.ppermute(
        array, "frame", [(f, f ^ stride) for f in range(frames)]
    )
    kept, sent, edge = frame_states(keys, values, rows, 2, (queries, residual))
    got = lax.ppermute(sent, "space", swap)
    quarter = (rows // 4, LANES)
    own, sent = small_kernel(split_sum_body, "split_sum", [quarter] * 2, kept, got)
    edge, sent = lax.optimization_barrier((edge, sent))
    edge = lax.ppermute(edge, "space", swap)
    partner = exchange(sent, 1)
    (total,) = small_kernel(sum_body, "pair_sum", [quarter], own, partner)
    earlier = []
    stride = 2
    while stride < frames:
        if stride * 2 == frames:
            total, edge = lax.optimization_barrier((total, edge))
        earlier.append(exchange(total, stride))
        stride *= 2
        if stride < frames:
            (total,) = small_kernel(sum_body, "stride_sum", [quarter], total, earlier[-1])
    prepared = beside(edge)
    earlier[-1], *prepared = lax.optimization_barrier((earlier[-1], *prepared))
    mine, theirs = small_kernel(
        pair_sums_body, "pair_sums", [quarter] * 2, own, partner, *earlier
    )
    other = exchange(theirs, 1)
    pieces = [mine, other, lax.ppermute(mine, "space", swap), lax.ppermute(other, "space", swap)]
    return pieces, prepared


def on_device(queries, keys, values, residual, attn_gain, value_taps, gate_taps):
    frames, rows, width, dim = queries.shape
    tokens = frames * rows * width
    flat = lambda a: a.reshape(tokens, dim)
    state_rows = cdiv(cdiv(dim, LANES) * HEAD_DIM, 64) * 64
    pieces, prepared = running_states(
        flat(keys),
        flat(values),
        queries.reshape(rows, width, dim),
        residual.reshape(rows, width, dim),
        state_rows,
        lambda edge: prepare(flat(queries), flat(residual), edge, attn_gain[None]),
    )
    out = mix(prepared, value_taps, gate_taps, pieces, rows, width)
    return out.reshape(frames, rows, width, dim)


def solution(mesh):
    placed = P(("groups", "frame"), "space", None, None)
    return jax.shard_map(
        on_device,
        mesh=mesh,
        in_specs=(placed, placed, placed, placed, P(), P(), P()),
        out_specs=placed,
        check_vma=False,
    )
```

```python
import functools
import math

import jax
import jax.numpy as jnp
from jax import lax
from jax.experimental import pallas as pl
from jax.experimental.pallas import tpu as pltpu
from jax.sharding import PartitionSpec as P

HEAD_DIM = 112
LANES = 128
GROUP = math.lcm(HEAD_DIM, LANES)
TILES = GROUP // LANES
HEADS = GROUP // HEAD_DIM


def cdiv(a, b):
    return -(-a // b)


def in_hbm(array):
    return pltpu.with_memory_space_constraint(array, pltpu.HBM)


def lane_iota(shape):
    return lax.broadcasted_iota(jnp.int32, shape, len(shape) - 1)


def tile_heads(j, lanes):
    lo, hi = j * LANES, min((j + 1) * LANES, lanes)
    heads = range(lo // HEAD_DIM, cdiv(hi, HEAD_DIM))
    return [(h, max(h * HEAD_DIM - lo, 0), min((h + 1) * HEAD_DIM - lo, LANES)) for h in heads]


def spans(lanes):
    count = cdiv(lanes, LANES)
    result = []
    for j in range(0, count, 2):
        tiles = list(range(j, min(j + 2, count)))
        first = tile_heads(tiles[0], lanes)[0][0] * HEAD_DIM // LANES
        last = cdiv((tile_heads(tiles[-1], lanes)[-1][0] + 1) * HEAD_DIM, LANES)
        result.append((tiles, first, last))
    return result


def by_group(dim, body):
    full, rest = divmod(dim, GROUP)
    if full:
        pl.when(pl.program_id(0) < full)(lambda: body(GROUP))
    if rest:
        pl.when(pl.program_id(0) >= full)(lambda: body(rest))


def state_kernel(dim, with_edge, keys_refs, values_refs, refs):
    step = pl.program_id(0)
    *refs, turned, whole, semaphores = refs
    if with_edge:
        *sources, edge_ref = refs[:2] + refs[-1:]
        parts = refs[2:-1]
        row = (sources[0].shape[0] - 1) * (1 - lax.axis_index("space"))
        copies = [
            pltpu.make_async_copy(source.at[row], edge_ref.at[k, 0], semaphores.at[k])
            for k, source in enumerate(sources)
        ]

        @pl.when(step == 0)
        def _():
            for copy in copies:
                copy.start()

    else:
        parts = refs

    def body(lanes):
        for k, keys_ref in enumerate(keys_refs):
            turned[k] = jnp.maximum(keys_ref[...], 0).T
        lane = lane_iota((HEAD_DIM, LANES))
        for tiles, _, _ in spans(lanes):
            begin = tile_heads(tiles[0], lanes)[0][0]
            end = tile_heads(tiles[-1], lanes)[-1][0] + 1
            product = sum(
                jnp.dot(
                    turned[k, begin * HEAD_DIM : end * HEAD_DIM, :],
                    values_ref[:, tiles[0] * LANES : (tiles[-1] + 1) * LANES],
                    preferred_element_type=jnp.float32,
                )
                for k, values_ref in enumerate(values_refs)
            )
            for side, j in enumerate(tiles):
                total = jnp.zeros((HEAD_DIM, LANES), jnp.float32)
                for h, lo, hi in tile_heads(j, lanes):
                    part = product[
                        (h - begin) * HEAD_DIM : (h - begin + 1) * HEAD_DIM,
                        side * LANES : (side + 1) * LANES,
                    ]
                    total = jnp.where((lane >= lo) & (lane < hi), part, total)
                row = pl.multiple_of((step * TILES + j) * HEAD_DIM, 16)
                whole[pl.ds(row, HEAD_DIM), :] = total.astype(jnp.bfloat16)

    by_group(dim, body)

    @pl.when(step == pl.num_programs(0) - 1)
    def _():
        used = cdiv(dim, LANES) * HEAD_DIM
        if used < whole.shape[0]:
            whole[used:, :] = jnp.zeros((whole.shape[0] - used, LANES), jnp.bfloat16)
        for k, part in enumerate(parts):
            size = part.shape[0]
            turn = lax.rem(lax.axis_index("space") + k, 2) if len(parts) == 2 else 0
            part[...] = whole[pl.ds(pl.multiple_of(turn * size, 16), size), :]
        if with_edge:
            for copy in copies:
                copy.wait()


def frame_states(keys, values, rows, parts, edged=()):
    tokens, dim = keys.shape
    part = (rows // parts, LANES)
    slabs = 2 if tokens % 32 == 0 else 1
    blocks = [
        pl.BlockSpec((tokens // slabs, GROUP), functools.partial(lambda k, g: (k, g), k))
        for k in range(slabs)
    ]

    def body(*refs):
        state_kernel(dim, bool(edged), refs[:slabs], refs[slabs : 2 * slabs], refs[2 * slabs :])

    return pl.pallas_call(
        body,
        out_shape=[pltpu.VMEM(part, jnp.bfloat16)] * parts
        + [pltpu.VMEM((len(edged), 1, *edged[0].shape[1:]), jnp.bfloat16) for _ in edged[:1]],
        grid=(cdiv(dim, GROUP),),
        in_specs=blocks + blocks + [pl.BlockSpec(memory_space=pl.ANY)] * len(edged),
        out_specs=[pl.BlockSpec(part, lambda g: (0, 0))] * parts
        + [pl.BlockSpec(memory_space=pl.ANY) for _ in edged[:1]],
        scratch_shapes=[
            pltpu.VMEM((slabs, GROUP, tokens // slabs), jnp.bfloat16),
            pltpu.VMEM((rows, LANES), jnp.bfloat16),
            pltpu.SemaphoreType.DMA((2,)),
        ],
        compiler_params=pltpu.CompilerParams(vmem_limit_bytes=60 * 2**20),
        cost_estimate=pl.CostEstimate(
            flops=2 * tokens * dim * HEAD_DIM, bytes_accessed=4 * tokens * dim, transcendentals=0
        ),
        name="frame_states",
    )(*[in_hbm(keys)] * slabs, *[in_hbm(values)] * slabs, *[in_hbm(array) for array in edged])


def group_lanes(dim):
    return [(first, min(GROUP, dim - first)) for first in range(0, dim, GROUP)]


def prepare_kernel(
    dim, queries_ref, residual_ref, edge_ref, gain_ref,
    features_ref, inputs_ref, heads_ref, spread_ref, held, semaphores,
):
    tokens = queries_ref.shape[0]
    full = dim // LANES * LANES
    parts = [slice(0, full), slice(full, dim)] if full < dim else [slice(0, dim)]
    copies = [
        pltpu.make_async_copy(source, held.at[k, :tokens], semaphores.at[k])
        for k, source in enumerate((queries_ref, residual_ref))
    ]
    for copy in copies:
        copy.start()
    edges, width = edge_ref.shape[1:3]
    for e in range(edges):
        here = slice(tokens + e * width, tokens + (e + 1) * width)
        held[0, here] = edge_ref[0, e]
        held[1, here] = edge_ref[1, e]
    head = lax.rem(lane_iota((GROUP, LANES)), HEADS)
    lane = lax.broadcasted_iota(jnp.int32, (GROUP, LANES), 0) - head * HEAD_DIM
    inside = (lane >= 0) & (lane < HEAD_DIM) & (lane_iota((GROUP, LANES)) < 3 * HEADS)
    heads_ref[...] = jnp.where(inside, 1.0, 0.0).astype(jnp.bfloat16)
    spread_ref[...] = jnp.zeros_like(spread_ref)
    used = cdiv(3 * HEADS, 16) * 16
    for group, (base, lanes) in enumerate(group_lanes(dim)):
        row = lax.broadcasted_iota(jnp.int32, (used, lanes), 0)
        lane = lane_iota((used, lanes)) - lax.rem(row, HEADS) * HEAD_DIM
        inside = (lane >= 0) & (lane < HEAD_DIM) & (row < 3 * HEADS)
        scaled = gain_ref[:, base : base + lanes] * math.sqrt(HEAD_DIM)
        coarse = scaled.astype(jnp.bfloat16).astype(jnp.float32)
        value = jnp.where((row >= HEADS) & (row < 2 * HEADS), scaled - coarse, coarse)
        spread_ref[group, :used, :lanes] = jnp.where(inside, value, 0.0).astype(jnp.bfloat16)
    if full < dim:
        features_ref[:, full:] = jnp.zeros((features_ref.shape[0], LANES), jnp.bfloat16)
    copies[0].wait()
    for part in parts:
        features_ref[:, part] = jnp.maximum(held[0, :, part], 0)
    copies[1].wait()
    for part in parts:
        inputs_ref[:, part] = held[1, :, part].astype(jnp.float32)


def prepare(queries, residual, edge, gain):
    tokens, dim = queries.shape
    total = tokens + edge.shape[1] * edge.shape[2]
    whole = pl.BlockSpec(memory_space=pltpu.VMEM)
    return pl.pallas_call(
        functools.partial(prepare_kernel, dim),
        out_shape=[
            pltpu.VMEM((total, cdiv(dim, LANES) * LANES), jnp.bfloat16),
            pltpu.VMEM((total, dim), jnp.float32),
            pltpu.VMEM((GROUP, LANES), jnp.bfloat16),
            pltpu.VMEM((len(group_lanes(dim)), LANES, GROUP), jnp.bfloat16),
        ],
        in_specs=[pl.BlockSpec(memory_space=pl.ANY)] * 2 + [whole] * 2,
        out_specs=[whole] * 4,
        scratch_shapes=[
            pltpu.VMEM((2, total, dim), jnp.bfloat16),
            pltpu.SemaphoreType.DMA((2,)),
        ],
        compiler_params=pltpu.CompilerParams(vmem_limit_bytes=24 * 2**20),
        cost_estimate=pl.CostEstimate(
            flops=4 * total * dim, bytes_accessed=8 * total * dim, transcendentals=0
        ),
        name="prepare",
    )(in_hbm(queries), in_hbm(residual), edge, gain)


def mix_kernel(
    dim, rows, width, edges,
    features_ref, inputs_ref, heads_ref, spread_ref, vtaps_ref, gtaps_ref, *refs,
):
    *pieces, out_ref, states, weights, numer, squares, mixed, windows, results, held, semaphores = refs
    places = edge_places(lax.axis_size("space"), rows) if edges else []
    spots = piece_places() if len(pieces) > 1 else [0]
    tokens = rows * width
    weights[...] = jnp.zeros_like(weights)
    for row in (0, rows + 1):
        windows[:, :, row] = jnp.zeros((2, 4, width // 2, LANES), jnp.float32)
    for k, piece in enumerate(pieces):
        size = piece.shape[0]
        states[pl.ds(pl.multiple_of(spots[k] * size, 16), size), :] = piece[...]
    lane = lane_iota((HEAD_DIM, LANES))
    sublane = lax.broadcasted_iota(jnp.int32, (8, LANES), 0)

    half = width // 2
    even, odd = pl.ds(0, half, stride=2), pl.ds(1, half, stride=2)

    def store_windows(value, slot, used, row, place):
        mixed[slot, row, :, :used] = value
        left, right = mixed[slot, row, even, :used], mixed[slot, row, odd, :used]
        sub = sublane[:, :used]
        before, after = pltpu.roll(right, 1, 0), pltpu.roll(left, half - 1, 0)
        before = jnp.concatenate([jnp.where(sub == 0, 0.0, before[:8]), before[8:]], axis=0)
        after = jnp.concatenate([after[: half - 8], jnp.where(sub == 7, 0.0, after[half - 8 :])], axis=0)
        for k, window in enumerate((before - right, left + right, right - left, left - after)):
            windows[slot, k, place, :, :used] = window

    def group(base, lanes):
        pairs = spans(lanes)

        def numerators(number):
            tiles, first, last = pairs[number]
            for side, j in enumerate(tiles):
                row = (base // LANES + j) * HEAD_DIM
                state = states[row : row + HEAD_DIM, :].astype(jnp.float32)
                for h, lo, hi in tile_heads(j, lanes):
                    start = h * HEAD_DIM - first * LANES
                    block = jnp.where((lane >= lo) & (lane < hi), state, 0.0)
                    weights[
                        number, start : start + HEAD_DIM, side * LANES : (side + 1) * LANES
                    ] = block.astype(jnp.bfloat16)
            depth, wide = (last - first) * LANES, len(tiles) * LANES
            product = jnp.dot(
                features_ref[:, base + first * LANES : base + last * LANES],
                weights[number, :depth, :wide],
                preferred_element_type=jnp.float32,
            )
            here = slice(tiles[0] * LANES, tiles[0] * LANES + wide)
            numer[:, here] = product
            squares[:, here] = (product * product).astype(jnp.bfloat16)

        def mix_tile(j, scale):
            slot = j % 2
            used = min(LANES, lanes - j * LANES)
            near = slice(j * LANES, j * LANES + used)
            here = slice(base + j * LANES, base + j * LANES + used)
            for row in range(rows + edges):
                source = slice(row * width, (row + 1) * width)
                value = inputs_ref[source, here] + numer[source, near] * scale[source, :used]
                if row < rows:
                    store_windows(value, slot, used, row + 1, row + 1)
                else:
                    edge = row - rows
                    store_windows(value, slot, used, edge * (rows + 1), places[edge])
            taps = []
            for ref, factor in ((vtaps_ref, 1.0), (gtaps_ref, 0.5)):
                for tap_row in range(3):
                    one, two, three = [
                        ref[3 * tap_row + i : 3 * tap_row + i + 1, here] * factor for i in range(3)
                    ]
                    outer = 0.5 * (one + three)
                    taps.append((one, outer + 0.5 * two, outer - 0.5 * two, three))
            for row in range(rows):
                columns = []
                for f in range(2):
                    products = []
                    for k in range(4):
                        total = None
                        for tap_row in range(3):
                            term = taps[3 * f + tap_row][k] * windows[slot, k, row + tap_row, :, :used]
                            total = term if total is None else total + term
                        products.append(total)
                    columns.append(
                        (
                            products[0] + products[1] + products[2],
                            products[1] - products[2] - products[3],
                        )
                    )
                for side, (conv_v, half_g) in zip((even, odd), zip(*columns)):
                    center = mixed[slot, row + 1, side, :used]
                    results[slot, row, side, :used] = center + conv_v * (
                        half_g + half_g * jnp.tanh(half_g)
                    )
                held[row * width : (row + 1) * width, here] = results[slot, row, :, :used].astype(
                    jnp.bfloat16
                )

        for number in range(len(pairs)):
            numerators(number)
        depth = cdiv(lanes, LANES) * LANES
        sums = jnp.dot(
            squares[:, :depth], heads_ref[:depth, :], preferred_element_type=jnp.float32
        )
        scale = lax.rsqrt(sums + HEAD_DIM * 1e-06)
        coarse = scale.astype(jnp.bfloat16).astype(jnp.float32)
        terms = jnp.where(lane_iota(scale.shape) < 2 * HEADS, coarse, scale - coarse)
        terms = terms.astype(jnp.bfloat16)
        for tiles, _, _ in pairs:
            here = slice(tiles[0] * LANES, (tiles[-1] + 1) * LANES)
            spread = jnp.dot(
                terms,
                spread_ref[base // GROUP, :, here],
                preferred_element_type=jnp.float32,
            )
            for side, j in enumerate(tiles):
                mix_tile(j, spread[:, side * LANES : (side + 1) * LANES])

    copies = []
    for base, lanes in group_lanes(dim):
        group(base, lanes)
        here = slice(base, base + lanes)
        copies.append(
            pltpu.make_async_copy(held.at[:, here], out_ref.at[:, here], semaphores.at[len(copies)])
        )
        copies[-1].start()
    for copy in copies:
        copy.wait()


def mix(prepared, value_taps, gate_taps, pieces, rows, width):
    features, inputs, heads, spread = prepared
    total, dim = inputs.shape
    tokens = rows * width
    pairs = spans(min(GROUP, dim))
    depth = max(last - first for _, first, last in pairs) * LANES
    whole = pl.BlockSpec(memory_space=pltpu.VMEM)
    return pl.pallas_call(
        functools.partial(mix_kernel, dim, rows, width, (total - tokens) // width),
        out_shape=jax.ShapeDtypeStruct((tokens, dim), jnp.bfloat16),
        in_specs=[whole] * (6 + len(pieces)),
        out_specs=pl.BlockSpec(memory_space=pl.ANY),
        scratch_shapes=[
            pltpu.VMEM((sum(piece.shape[0] for piece in pieces), LANES), jnp.bfloat16),
            pltpu.VMEM((len(pairs), depth, 2 * LANES), jnp.bfloat16),
            pltpu.VMEM((total, GROUP), jnp.float32),
            pltpu.VMEM((total, GROUP), jnp.bfloat16),
            pltpu.VMEM((2, rows + 2, width, LANES), jnp.float32),
            pltpu.VMEM((2, 4, rows + 2, width // 2, LANES), jnp.float32),
            pltpu.VMEM((2, rows, width, LANES), jnp.float32),
            pltpu.VMEM((tokens, dim), jnp.bfloat16),
            pltpu.SemaphoreType.DMA((len(group_lanes(dim)),)),
        ],
        compiler_params=pltpu.CompilerParams(vmem_limit_bytes=28 * 2**20),
        cost_estimate=pl.CostEstimate(
            flops=60 * tokens * dim, bytes_accessed=6 * tokens * dim, transcendentals=2 * tokens * dim
        ),
        name="mix",
    )(features, inputs, heads, spread, value_taps, gate_taps, *pieces)


def edge_rows(queries, residual):
    devices, rows = lax.axis_size("space"), queries.shape[0]
    up = [(i, i + 1) for i in range(devices - 1)]
    down = [(j, i) for i, j in up]
    both = jnp.stack([queries, residual])
    if devices == 2:
        first = lax.axis_index("space") == 0
        return lax.ppermute(jnp.where(first, both[:, rows - 1 :], both[:, :1]), "space", up + down)
    before = lax.ppermute(both[:, rows - 1 :], "space", up)
    after = lax.ppermute(both[:, :1], "space", down)
    return jnp.concatenate([before, after], axis=1)


def small_kernel(body, name, outs, *arrays):
    return pl.pallas_call(
        body,
        out_shape=[pltpu.VMEM(shape, jnp.bfloat16) for shape in outs],
        in_specs=[pl.BlockSpec(memory_space=pltpu.VMEM)] * len(arrays),
        out_specs=[pl.BlockSpec(memory_space=pltpu.VMEM)] * len(outs),
        compiler_params=pltpu.CompilerParams(vmem_limit_bytes=4 * 2**20),
        name=name,
    )(*arrays)


def add(*values):
    total = values[0].astype(jnp.float32)
    for value in values[1:]:
        total = total + value.astype(jnp.float32)
    return total


def parity():
    return lax.rem(lax.axis_index("frame"), 2)


def split_sum_body(kept_ref, got_ref, mine_ref, theirs_ref):
    size = mine_ref.shape[0]
    for ref, side in ((theirs_ref, 1 - parity()), (mine_ref, parity())):
        rows = pl.ds(pl.multiple_of(side * size, 16), size)
        ref[...] = add(kept_ref[rows, :], got_ref[rows, :]).astype(jnp.bfloat16)


def sum_body(*refs):
    *terms, out_ref = refs
    out_ref[...] = add(*[term[...] for term in terms]).astype(jnp.bfloat16)


def pair_sums_body(own_ref, partner_ref, *refs):
    *earlier, mine_ref, theirs_ref = refs
    before = jnp.zeros(own_ref.shape, jnp.float32)
    for k, ref in enumerate(earlier):
        from_before = lax.rem(lax.axis_index("frame") // (2 << k), 2) == 1
        before = before + jnp.where(from_before, add(ref[...]), 0.0)
    own, partner = add(own_ref[...]), add(partner_ref[...])
    first = parity() == 0
    both = before + (own + partner)
    mine_ref[...] = jnp.where(first, before + own, both).astype(jnp.bfloat16)
    theirs_ref[...] = jnp.where(first, both, before + partner).astype(jnp.bfloat16)


def paired(devices, frames):
    return devices == 2 and frames >= 4 and frames & (frames - 1) == 0


def piece_places():
    core = lax.axis_index("space")
    return [2 * c + p for c in (core, 1 - core) for p in (parity(), 1 - parity())]


def edge_places(devices, rows):
    if devices == 2:
        return [jnp.where(lax.axis_index("space") == 0, rows + 1, 0)]
    return [0, rows + 1]


def running_states(keys, values, queries, residual, rows, beside):
    devices, frames = lax.axis_size("space"), lax.axis_size("frame")
    if not paired(devices, frames):
        (state,) = frame_states(keys, values, rows, 1)
        state = lax.psum(state.astype(jnp.float32), "space").astype(jnp.bfloat16)
        every = lax.all_gather(state, "frame").astype(jnp.float32)
        reached = (jnp.arange(frames) <= lax.axis_index("frame"))[:, None, None]
        total = jnp.sum(jnp.where(reached, every, 0.0), axis=0).astype(jnp.bfloat16)
        return [total], beside(edge_rows(queries, residual))
    swap = [(0, 1), (1, 0)]
    exchange = lambda array, stride: lax.ppermute(
        array, "frame", [(f, f ^ stride) for f in range(frames)]
    )
    kept, sent, edge = frame_states(keys, values, rows, 2, (queries, residual))
    got = lax.ppermute(sent, "space", swap)
    quarter = (rows // 4, LANES)
    own, sent = small_kernel(split_sum_body, "split_sum", [quarter] * 2, kept, got)
    edge, sent = lax.optimization_barrier((edge, sent))
    edge = lax.ppermute(edge, "space", swap)
    partner = exchange(sent, 1)
    (total,) = small_kernel(sum_body, "pair_sum", [quarter], own, partner)
    earlier = []
    stride = 2
    while stride < frames:
        if stride * 2 == frames:
            total, edge = lax.optimization_barrier((total, edge))
        earlier.append(exchange(total, stride))
        stride *= 2
        if stride < frames:
            (total,) = small_kernel(sum_body, "stride_sum", [quarter], total, earlier[-1])
    prepared = beside(edge)
    earlier[-1], *prepared = lax.optimization_barrier((earlier[-1], *prepared))
    mine, theirs = small_kernel(
        pair_sums_body, "pair_sums", [quarter] * 2, own, partner, *earlier
    )
    other = exchange(theirs, 1)
    pieces = [mine, other, lax.ppermute(mine, "space", swap), lax.ppermute(other, "space", swap)]
    return pieces, prepared


def on_device(queries, keys, values, residual, attn_gain, value_taps, gate_taps):
    frames, rows, width, dim = queries.shape
    tokens = frames * rows * width
    flat = lambda a: a.reshape(tokens, dim)
    state_rows = cdiv(cdiv(dim, LANES) * HEAD_DIM, 64) * 64
    pieces, prepared = running_states(
        flat(keys),
        flat(values),
        queries.reshape(rows, width, dim),
        residual.reshape(rows, width, dim),
        state_rows,
        lambda edge: prepare(flat(queries), flat(residual), edge, attn_gain[None]),
    )
    out = mix(prepared, value_taps, gate_taps, pieces, rows, width)
    return out.reshape(frames, rows, width, dim)


def solution(mesh):
    placed = P(("groups", "frame"), "space", None, None)
    return jax.shard_map(
        on_device,
        mesh=mesh,
        in_specs=(placed, placed, placed, placed, P(), P(), P()),
        out_specs=placed,
        check_vma=False,
    )
```

```python
import functools
import math

import jax
import jax.numpy as jnp
from jax import lax
from jax.experimental import pallas as pl
from jax.experimental.pallas import tpu as pltpu
from jax.sharding import PartitionSpec as P

HEAD_DIM = 112
LANES = 128
GROUP = math.lcm(HEAD_DIM, LANES)
TILES = GROUP // LANES
HEADS = GROUP // HEAD_DIM


def cdiv(a, b):
    return -(-a // b)


def in_hbm(array):
    return pltpu.with_memory_space_constraint(array, pltpu.HBM)


def lane_iota(shape):
    return lax.broadcasted_iota(jnp.int32, shape, len(shape) - 1)


def tile_heads(j, lanes):
    lo, hi = j * LANES, min((j + 1) * LANES, lanes)
    heads = range(lo // HEAD_DIM, cdiv(hi, HEAD_DIM))
    return [(h, max(h * HEAD_DIM - lo, 0), min((h + 1) * HEAD_DIM - lo, LANES)) for h in heads]


def spans(lanes):
    count = cdiv(lanes, LANES)
    result = []
    for j in range(0, count, 2):
        tiles = list(range(j, min(j + 2, count)))
        first = tile_heads(tiles[0], lanes)[0][0] * HEAD_DIM // LANES
        last = cdiv((tile_heads(tiles[-1], lanes)[-1][0] + 1) * HEAD_DIM, LANES)
        result.append((tiles, first, last))
    return result


def by_group(dim, body):
    full, rest = divmod(dim, GROUP)
    if full:
        pl.when(pl.program_id(0) < full)(lambda: body(GROUP))
    if rest:
        pl.when(pl.program_id(0) >= full)(lambda: body(rest))


def state_kernel(dim, with_edge, keys_refs, values_refs, refs):
    step = pl.program_id(0)
    *refs, turned, whole, semaphores = refs
    if with_edge:
        *sources, edge_ref = refs[:2] + refs[-1:]
        parts = refs[2:-1]
        row = (sources[0].shape[0] - 1) * (1 - lax.axis_index("space"))
        copies = [
            pltpu.make_async_copy(source.at[row], edge_ref.at[k, 0], semaphores.at[k])
            for k, source in enumerate(sources)
        ]

        @pl.when(step == 0)
        def _():
            for copy in copies:
                copy.start()

    else:
        parts = refs

    def body(lanes):
        for k, keys_ref in enumerate(keys_refs):
            turned[k] = jnp.maximum(keys_ref[...], 0).T
        lane = lane_iota((HEAD_DIM, LANES))
        for tiles, _, _ in spans(lanes):
            begin = tile_heads(tiles[0], lanes)[0][0]
            end = tile_heads(tiles[-1], lanes)[-1][0] + 1
            product = sum(
                jnp.dot(
                    turned[k, begin * HEAD_DIM : end * HEAD_DIM, :],
                    values_ref[:, tiles[0] * LANES : (tiles[-1] + 1) * LANES],
                    preferred_element_type=jnp.float32,
                )
                for k, values_ref in enumerate(values_refs)
            )
            for side, j in enumerate(tiles):
                total = jnp.zeros((HEAD_DIM, LANES), jnp.float32)
                for h, lo, hi in tile_heads(j, lanes):
                    part = product[
                        (h - begin) * HEAD_DIM : (h - begin + 1) * HEAD_DIM,
                        side * LANES : (side + 1) * LANES,
                    ]
                    total = jnp.where((lane >= lo) & (lane < hi), part, total)
                row = pl.multiple_of((step * TILES + j) * HEAD_DIM, 16)
                whole[pl.ds(row, HEAD_DIM), :] = total.astype(jnp.bfloat16)

    by_group(dim, body)

    @pl.when(step == pl.num_programs(0) - 1)
    def _():
        used = cdiv(dim, LANES) * HEAD_DIM
        if used < whole.shape[0]:
            whole[used:, :] = jnp.zeros((whole.shape[0] - used, LANES), jnp.bfloat16)
        for k, part in enumerate(parts):
            size = part.shape[0]
            turn = lax.rem(lax.axis_index("space") + k, 2) if len(parts) == 2 else 0
            part[...] = whole[pl.ds(pl.multiple_of(turn * size, 16), size), :]
        if with_edge:
            for copy in copies:
                copy.wait()


def frame_states(keys, values, rows, parts, edged=()):
    tokens, dim = keys.shape
    part = (rows // parts, LANES)
    slabs = 2 if tokens % 32 == 0 else 1
    blocks = [
        pl.BlockSpec((tokens // slabs, GROUP), functools.partial(lambda k, g: (k, g), k))
        for k in range(slabs)
    ]

    def body(*refs):
        state_kernel(dim, bool(edged), refs[:slabs], refs[slabs : 2 * slabs], refs[2 * slabs :])

    return pl.pallas_call(
        body,
        out_shape=[pltpu.VMEM(part, jnp.bfloat16)] * parts
        + [pltpu.VMEM((len(edged), 1, *edged[0].shape[1:]), jnp.bfloat16) for _ in edged[:1]],
        grid=(cdiv(dim, GROUP),),
        in_specs=blocks + blocks + [pl.BlockSpec(memory_space=pl.ANY)] * len(edged),
        out_specs=[pl.BlockSpec(part, lambda g: (0, 0))] * parts
        + [pl.BlockSpec(memory_space=pl.ANY) for _ in edged[:1]],
        scratch_shapes=[
            pltpu.VMEM((slabs, GROUP, tokens // slabs), jnp.bfloat16),
            pltpu.VMEM((rows, LANES), jnp.bfloat16),
            pltpu.SemaphoreType.DMA((2,)),
        ],
        compiler_params=pltpu.CompilerParams(vmem_limit_bytes=60 * 2**20),
        cost_estimate=pl.CostEstimate(
            flops=2 * tokens * dim * HEAD_DIM, bytes_accessed=4 * tokens * dim, transcendentals=0
        ),
        name="frame_states",
    )(*[in_hbm(keys)] * slabs, *[in_hbm(values)] * slabs, *[in_hbm(array) for array in edged])


def group_lanes(dim):
    return [(first, min(GROUP, dim - first)) for first in range(0, dim, GROUP)]


def prepare_kernel(
    dim, queries_ref, residual_ref, edge_ref, gain_ref,
    features_ref, inputs_ref, heads_ref, spread_ref, held, semaphores,
):
    tokens = queries_ref.shape[0]
    full = dim // LANES * LANES
    parts = [slice(0, full), slice(full, dim)] if full < dim else [slice(0, dim)]
    copies = [
        pltpu.make_async_copy(source, held.at[k, :tokens], semaphores.at[k])
        for k, source in enumerate((queries_ref, residual_ref))
    ]
    for copy in copies:
        copy.start()
    edges, width = edge_ref.shape[1:3]
    for e in range(edges):
        here = slice(tokens + e * width, tokens + (e + 1) * width)
        held[0, here] = edge_ref[0, e]
        held[1, here] = edge_ref[1, e]
    head = lax.rem(lane_iota((GROUP, LANES)), HEADS)
    lane = lax.broadcasted_iota(jnp.int32, (GROUP, LANES), 0) - head * HEAD_DIM
    inside = (lane >= 0) & (lane < HEAD_DIM) & (lane_iota((GROUP, LANES)) < 3 * HEADS)
    heads_ref[...] = jnp.where(inside, 1.0, 0.0).astype(jnp.bfloat16)
    spread_ref[...] = jnp.zeros_like(spread_ref)
    used = cdiv(3 * HEADS, 16) * 16
    for group, (base, lanes) in enumerate(group_lanes(dim)):
        row = lax.broadcasted_iota(jnp.int32, (used, lanes), 0)
        lane = lane_iota((used, lanes)) - lax.rem(row, HEADS) * HEAD_DIM
        inside = (lane >= 0) & (lane < HEAD_DIM) & (row < 3 * HEADS)
        scaled = gain_ref[:, base : base + lanes] * math.sqrt(HEAD_DIM)
        coarse = scaled.astype(jnp.bfloat16).astype(jnp.float32)
        value = jnp.where((row >= HEADS) & (row < 2 * HEADS), scaled - coarse, coarse)
        spread_ref[group, :used, :lanes] = jnp.where(inside, value, 0.0).astype(jnp.bfloat16)
    if full < dim:
        features_ref[:, full:] = jnp.zeros((features_ref.shape[0], LANES), jnp.bfloat16)
    copies[0].wait()
    for part in parts:
        features_ref[:, part] = jnp.maximum(held[0, :, part], 0)
    copies[1].wait()
    for part in parts:
        inputs_ref[:, part] = held[1, :, part].astype(jnp.float32)


def prepare(queries, residual, edge, gain):
    tokens, dim = queries.shape
    total = tokens + edge.shape[1] * edge.shape[2]
    whole = pl.BlockSpec(memory_space=pltpu.VMEM)
    return pl.pallas_call(
        functools.partial(prepare_kernel, dim),
        out_shape=[
            pltpu.VMEM((total, cdiv(dim, LANES) * LANES), jnp.bfloat16),
            pltpu.VMEM((total, dim), jnp.float32),
            pltpu.VMEM((GROUP, LANES), jnp.bfloat16),
            pltpu.VMEM((len(group_lanes(dim)), LANES, GROUP), jnp.bfloat16),
        ],
        in_specs=[pl.BlockSpec(memory_space=pl.ANY)] * 2 + [whole] * 2,
        out_specs=[whole] * 4,
        scratch_shapes=[
            pltpu.VMEM((2, total, dim), jnp.bfloat16),
            pltpu.SemaphoreType.DMA((2,)),
        ],
        compiler_params=pltpu.CompilerParams(vmem_limit_bytes=24 * 2**20),
        cost_estimate=pl.CostEstimate(
            flops=4 * total * dim, bytes_accessed=8 * total * dim, transcendentals=0
        ),
        name="prepare",
    )(in_hbm(queries), in_hbm(residual), edge, gain)


def mix_kernel(
    dim, rows, width, edges,
    features_ref, inputs_ref, heads_ref, spread_ref, vtaps_ref, gtaps_ref, *refs,
):
    *pieces, out_ref, states, weights, numer, squares, spreads, mixed, windows, results, held = refs[:-1]
    semaphores = refs[-1]
    places = edge_places(lax.axis_size("space"), rows) if edges else []
    spots = piece_places() if len(pieces) > 1 else [0]
    tokens = rows * width
    for row in (0, rows + 1):
        windows[:, :, row] = jnp.zeros((2, 4, width // 2, LANES), jnp.float32)
    for k, piece in enumerate(pieces):
        size = piece.shape[0]
        states[pl.ds(pl.multiple_of(spots[k] * size, 16), size), :] = piece[...]
    lane = lane_iota((HEAD_DIM, LANES))
    sublane = lax.broadcasted_iota(jnp.int32, (8, LANES), 0)

    half = width // 2
    even, odd = pl.ds(0, half, stride=2), pl.ds(1, half, stride=2)

    def store_windows(value, slot, used, row, place):
        mixed[slot, row, :, :used] = value
        left, right = mixed[slot, row, even, :used], mixed[slot, row, odd, :used]
        sub = sublane[:, :used]
        before, after = pltpu.roll(right, 1, 0), pltpu.roll(left, half - 1, 0)
        before = jnp.concatenate([jnp.where(sub == 0, 0.0, before[:8]), before[8:]], axis=0)
        after = jnp.concatenate([after[: half - 8], jnp.where(sub == 7, 0.0, after[half - 8 :])], axis=0)
        for k, window in enumerate((before - right, left + right, right - left, left - after)):
            windows[slot, k, place, :, :used] = window

    def group(base, lanes, turn):
        pairs = spans(lanes)

        def numerators(number):
            tiles, first, last = pairs[number]
            depth, wide = (last - first) * LANES, len(tiles) * LANES
            for side, j in enumerate(tiles):
                row = (base // LANES + j) * HEAD_DIM
                state = states[row : row + HEAD_DIM, :].astype(jnp.float32)
                heads = tile_heads(j, lanes)
                start = heads[0][0] * HEAD_DIM - first * LANES
                blocks = [jnp.where((lane >= lo) & (lane < hi), state, 0.0) for _, lo, hi in heads]
                rest = depth - start - len(heads) * HEAD_DIM
                if start:
                    blocks.insert(0, jnp.zeros((start, LANES), jnp.float32))
                if rest:
                    blocks.append(jnp.zeros((rest, LANES), jnp.float32))
                weights[turn, number, :depth, side * LANES : (side + 1) * LANES] = jnp.concatenate(
                    blocks, axis=0
                ).astype(jnp.bfloat16)
            product = jnp.dot(
                features_ref[:, base + first * LANES : base + last * LANES],
                weights[turn, number, :depth, :wide],
                preferred_element_type=jnp.float32,
            )
            here = slice(tiles[0] * LANES, tiles[0] * LANES + wide)
            numer[turn, :, here] = product
            squares[turn, :, here] = (product * product).astype(jnp.bfloat16)

        terms = []

        def scales():
            depth = cdiv(lanes, LANES) * LANES
            sums = jnp.dot(
                squares[turn, :, :depth], heads_ref[:depth, :], preferred_element_type=jnp.float32
            )
            scale = lax.rsqrt(sums + HEAD_DIM * 1e-06)
            coarse = scale.astype(jnp.bfloat16).astype(jnp.float32)
            fine = jnp.where(lane_iota(scale.shape) < 2 * HEADS, coarse, scale - coarse)
            terms.append(fine.astype(jnp.bfloat16))

        def spread(number):
            tiles, _, _ = pairs[number]
            here = slice(tiles[0] * LANES, (tiles[-1] + 1) * LANES)
            spreads[turn, :, here] = jnp.dot(
                terms[0], spread_ref[base // GROUP, :, here], preferred_element_type=jnp.float32
            )

        def mix_tile(j):
            slot = j % 2
            used = min(LANES, lanes - j * LANES)
            near = slice(j * LANES, j * LANES + used)
            here = slice(base + j * LANES, base + j * LANES + used)
            for row in range(rows + edges):
                source = slice(row * width, (row + 1) * width)
                value = inputs_ref[source, here] + numer[turn, source, near] * spreads[turn, source, near]
                if row < rows:
                    store_windows(value, slot, used, row + 1, row + 1)
                else:
                    edge = row - rows
                    store_windows(value, slot, used, edge * (rows + 1), places[edge])
            taps = []
            for ref, factor in ((vtaps_ref, 1.0), (gtaps_ref, 0.5)):
                for tap_row in range(3):
                    one, two, three = [
                        ref[3 * tap_row + i : 3 * tap_row + i + 1, here] * factor for i in range(3)
                    ]
                    outer = 0.5 * (one + three)
                    taps.append((one, outer + 0.5 * two, outer - 0.5 * two, three))
            for row in range(rows):
                columns = []
                for f in range(2):
                    products = []
                    for k in range(4):
                        total = None
                        for tap_row in range(3):
                            term = taps[3 * f + tap_row][k] * windows[slot, k, row + tap_row, :, :used]
                            total = term if total is None else total + term
                        products.append(total)
                    columns.append(
                        (
                            products[0] + products[1] + products[2],
                            products[1] - products[2] - products[3],
                        )
                    )
                for side, (conv_v, half_g) in zip((even, odd), zip(*columns)):
                    center = mixed[slot, row + 1, side, :used]
                    results[slot, row, side, :used] = center + conv_v * (
                        half_g + half_g * jnp.tanh(half_g)
                    )
                held[row * width : (row + 1) * width, here] = results[slot, row, :, :used].astype(
                    jnp.bfloat16
                )

        numbers = range(len(pairs))
        ahead = [functools.partial(numerators, n) for n in numbers]
        ahead += [scales] + [functools.partial(spread, n) for n in numbers]
        return ahead, [functools.partial(mix_tile, j) for j in range(cdiv(lanes, LANES))]

    order = sorted(group_lanes(dim), key=lambda item: item[1])
    steps = [group(base, lanes, k % 2) for k, (base, lanes) in enumerate(order)]
    for step in steps[0][0]:
        step()
    copies = []
    for k, (base, lanes) in enumerate(order):
        tiles = steps[k][1]
        ahead = steps[k + 1][0] if k + 1 < len(steps) else []
        for n, tile in enumerate(tiles):
            for step in ahead[len(ahead) * n // len(tiles) : len(ahead) * (n + 1) // len(tiles)]:
                step()
            tile()
        here = slice(base, base + lanes)
        copies.append(
            pltpu.make_async_copy(held.at[:, here], out_ref.at[:, here], semaphores.at[k])
        )
        copies[-1].start()
    for copy in copies:
        copy.wait()


def mix(prepared, value_taps, gate_taps, pieces, rows, width):
    features, inputs, heads, spread = prepared
    total, dim = inputs.shape
    tokens = rows * width
    pairs = spans(min(GROUP, dim))
    depth = max(last - first for _, first, last in pairs) * LANES
    whole = pl.BlockSpec(memory_space=pltpu.VMEM)
    return pl.pallas_call(
        functools.partial(mix_kernel, dim, rows, width, (total - tokens) // width),
        out_shape=jax.ShapeDtypeStruct((tokens, dim), jnp.bfloat16),
        in_specs=[whole] * (6 + len(pieces)),
        out_specs=pl.BlockSpec(memory_space=pl.ANY),
        scratch_shapes=[
            pltpu.VMEM((sum(piece.shape[0] for piece in pieces), LANES), jnp.bfloat16),
            pltpu.VMEM((2, len(pairs), depth, 2 * LANES), jnp.bfloat16),
            pltpu.VMEM((2, total, GROUP), jnp.float32),
            pltpu.VMEM((2, total, GROUP), jnp.bfloat16),
            pltpu.VMEM((2, total, GROUP), jnp.float32),
            pltpu.VMEM((2, rows + 2, width, LANES), jnp.float32),
            pltpu.VMEM((2, 4, rows + 2, width // 2, LANES), jnp.float32),
            pltpu.VMEM((2, rows, width, LANES), jnp.float32),
            pltpu.VMEM((tokens, dim), jnp.bfloat16),
            pltpu.SemaphoreType.DMA((len(group_lanes(dim)),)),
        ],
        compiler_params=pltpu.CompilerParams(vmem_limit_bytes=36 * 2**20),
        cost_estimate=pl.CostEstimate(
            flops=60 * tokens * dim, bytes_accessed=6 * tokens * dim, transcendentals=2 * tokens * dim
        ),
        name="mix",
    )(features, inputs, heads, spread, value_taps, gate_taps, *pieces)


def edge_rows(queries, residual):
    devices, rows = lax.axis_size("space"), queries.shape[0]
    up = [(i, i + 1) for i in range(devices - 1)]
    down = [(j, i) for i, j in up]
    both = jnp.stack([queries, residual])
    if devices == 2:
        first = lax.axis_index("space") == 0
        return lax.ppermute(jnp.where(first, both[:, rows - 1 :], both[:, :1]), "space", up + down)
    before = lax.ppermute(both[:, rows - 1 :], "space", up)
    after = lax.ppermute(both[:, :1], "space", down)
    return jnp.concatenate([before, after], axis=1)


def small_kernel(body, name, outs, *arrays):
    return pl.pallas_call(
        body,
        out_shape=[pltpu.VMEM(shape, jnp.bfloat16) for shape in outs],
        in_specs=[pl.BlockSpec(memory_space=pltpu.VMEM)] * len(arrays),
        out_specs=[pl.BlockSpec(memory_space=pltpu.VMEM)] * len(outs),
        compiler_params=pltpu.CompilerParams(vmem_limit_bytes=4 * 2**20),
        name=name,
    )(*arrays)


def add(*values):
    total = values[0].astype(jnp.float32)
    for value in values[1:]:
        total = total + value.astype(jnp.float32)
    return total


def parity():
    return lax.rem(lax.axis_index("frame"), 2)


def split_sum_body(kept_ref, got_ref, mine_ref, theirs_ref):
    size = mine_ref.shape[0]
    for ref, side in ((theirs_ref, 1 - parity()), (mine_ref, parity())):
        rows = pl.ds(pl.multiple_of(side * size, 16), size)
        ref[...] = add(kept_ref[rows, :], got_ref[rows, :]).astype(jnp.bfloat16)


def sum_body(*refs):
    *terms, out_ref = refs
    out_ref[...] = add(*[term[...] for term in terms]).astype(jnp.bfloat16)


def pair_sums_body(own_ref, partner_ref, *refs):
    *earlier, mine_ref, theirs_ref = refs
    before = jnp.zeros(own_ref.shape, jnp.float32)
    for k, ref in enumerate(earlier):
        from_before = lax.rem(lax.axis_index("frame") // (2 << k), 2) == 1
        before = before + jnp.where(from_before, add(ref[...]), 0.0)
    own, partner = add(own_ref[...]), add(partner_ref[...])
    first = parity() == 0
    both = before + (own + partner)
    mine_ref[...] = jnp.where(first, before + own, both).astype(jnp.bfloat16)
    theirs_ref[...] = jnp.where(first, both, before + partner).astype(jnp.bfloat16)


def paired(devices, frames):
    return devices == 2 and frames >= 4 and frames & (frames - 1) == 0


def piece_places():
    core = lax.axis_index("space")
    return [2 * c + p for c in (core, 1 - core) for p in (parity(), 1 - parity())]


def edge_places(devices, rows):
    if devices == 2:
        return [jnp.where(lax.axis_index("space") == 0, rows + 1, 0)]
    return [0, rows + 1]


def running_states(keys, values, queries, residual, rows, beside):
    devices, frames = lax.axis_size("space"), lax.axis_size("frame")
    if not paired(devices, frames):
        (state,) = frame_states(keys, values, rows, 1)
        state = lax.psum(state.astype(jnp.float32), "space").astype(jnp.bfloat16)
        every = lax.all_gather(state, "frame").astype(jnp.float32)
        reached = (jnp.arange(frames) <= lax.axis_index("frame"))[:, None, None]
        total = jnp.sum(jnp.where(reached, every, 0.0), axis=0).astype(jnp.bfloat16)
        return [total], beside(edge_rows(queries, residual))
    swap = [(0, 1), (1, 0)]
    exchange = lambda array, stride: lax.ppermute(
        array, "frame", [(f, f ^ stride) for f in range(frames)]
    )
    kept, sent, edge = frame_states(keys, values, rows, 2, (queries, residual))
    got = lax.ppermute(sent, "space", swap)
    quarter = (rows // 4, LANES)
    own, sent = small_kernel(split_sum_body, "split_sum", [quarter] * 2, kept, got)
    edge, sent = lax.optimization_barrier((edge, sent))
    edge = lax.ppermute(edge, "space", swap)
    partner = exchange(sent, 1)
    (total,) = small_kernel(sum_body, "pair_sum", [quarter], own, partner)
    earlier = []
    stride = 2
    while stride < frames:
        if stride * 2 == frames:
            total, edge = lax.optimization_barrier((total, edge))
        earlier.append(exchange(total, stride))
        stride *= 2
        if stride < frames:
            (total,) = small_kernel(sum_body, "stride_sum", [quarter], total, earlier[-1])
    prepared = beside(edge)
    earlier[-1], *prepared = lax.optimization_barrier((earlier[-1], *prepared))
    mine, theirs = small_kernel(
        pair_sums_body, "pair_sums", [quarter] * 2, own, partner, *earlier
    )
    other = exchange(theirs, 1)
    pieces = [mine, other, lax.ppermute(mine, "space", swap), lax.ppermute(other, "space", swap)]
    return pieces, prepared


def on_device(queries, keys, values, residual, attn_gain, value_taps, gate_taps):
    frames, rows, width, dim = queries.shape
    tokens = frames * rows * width
    flat = lambda a: a.reshape(tokens, dim)
    state_rows = cdiv(cdiv(dim, LANES) * HEAD_DIM, 64) * 64
    pieces, prepared = running_states(
        flat(keys),
        flat(values),
        queries.reshape(rows, width, dim),
        residual.reshape(rows, width, dim),
        state_rows,
        lambda edge: prepare(flat(queries), flat(residual), edge, attn_gain[None]),
    )
    out = mix(prepared, value_taps, gate_taps, pieces, rows, width)
    return out.reshape(frames, rows, width, dim)


def solution(mesh):
    placed = P(("groups", "frame"), "space", None, None)
    return jax.shard_map(
        on_device,
        mesh=mesh,
        in_specs=(placed, placed, placed, placed, P(), P(), P()),
        out_specs=placed,
        check_vma=False,
    )
```

```python
import functools
import math

import jax
import jax.numpy as jnp
from jax import lax
from jax.experimental import pallas as pl
from jax.experimental.pallas import tpu as pltpu
from jax.sharding import PartitionSpec as P

HEAD_DIM = 112
LANES = 128
GROUP = math.lcm(HEAD_DIM, LANES)
TILES = GROUP // LANES
HEADS = GROUP // HEAD_DIM


def cdiv(a, b):
    return -(-a // b)


def in_hbm(array):
    return pltpu.with_memory_space_constraint(array, pltpu.HBM)


def lane_iota(shape):
    return lax.broadcasted_iota(jnp.int32, shape, len(shape) - 1)


def tile_heads(j, lanes):
    lo, hi = j * LANES, min((j + 1) * LANES, lanes)
    heads = range(lo // HEAD_DIM, cdiv(hi, HEAD_DIM))
    return [(h, max(h * HEAD_DIM - lo, 0), min((h + 1) * HEAD_DIM - lo, LANES)) for h in heads]


def spans(lanes):
    count = cdiv(lanes, LANES)
    result = []
    for j in range(0, count, 2):
        tiles = list(range(j, min(j + 2, count)))
        first = tile_heads(tiles[0], lanes)[0][0] * HEAD_DIM // LANES
        last = cdiv((tile_heads(tiles[-1], lanes)[-1][0] + 1) * HEAD_DIM, LANES)
        result.append((tiles, first, last))
    return result


def by_group(dim, body):
    full, rest = divmod(dim, GROUP)
    if full:
        pl.when(pl.program_id(0) < full)(lambda: body(GROUP))
    if rest:
        pl.when(pl.program_id(0) >= full)(lambda: body(rest))


def state_kernel(dim, with_edge, keys_refs, values_refs, refs):
    step = pl.program_id(0)
    *refs, turned, whole, semaphores = refs
    if with_edge:
        *sources, edge_ref = refs[:2] + refs[-1:]
        parts = refs[2:-1]
        row = (sources[0].shape[0] - 1) * (1 - lax.axis_index("space"))
        copies = [
            pltpu.make_async_copy(source.at[row], edge_ref.at[k, 0], semaphores.at[k])
            for k, source in enumerate(sources)
        ]

        @pl.when(step == 0)
        def _():
            for copy in copies:
                copy.start()

    else:
        parts = refs

    def body(lanes):
        for k, keys_ref in enumerate(keys_refs):
            turned[k] = jnp.maximum(keys_ref[...], 0).T
        lane = lane_iota((HEAD_DIM, LANES))
        for tiles, _, _ in spans(lanes):
            begin = tile_heads(tiles[0], lanes)[0][0]
            end = tile_heads(tiles[-1], lanes)[-1][0] + 1
            product = sum(
                jnp.dot(
                    turned[k, begin * HEAD_DIM : end * HEAD_DIM, :],
                    values_ref[:, tiles[0] * LANES : (tiles[-1] + 1) * LANES],
                    preferred_element_type=jnp.float32,
                )
                for k, values_ref in enumerate(values_refs)
            )
            for side, j in enumerate(tiles):
                total = jnp.zeros((HEAD_DIM, LANES), jnp.float32)
                for h, lo, hi in tile_heads(j, lanes):
                    part = product[
                        (h - begin) * HEAD_DIM : (h - begin + 1) * HEAD_DIM,
                        side * LANES : (side + 1) * LANES,
                    ]
                    total = jnp.where((lane >= lo) & (lane < hi), part, total)
                row = pl.multiple_of((step * TILES + j) * HEAD_DIM, 16)
                whole[pl.ds(row, HEAD_DIM), :] = total.astype(jnp.bfloat16)

    by_group(dim, body)

    @pl.when(step == pl.num_programs(0) - 1)
    def _():
        used = cdiv(dim, LANES) * HEAD_DIM
        if used < whole.shape[0]:
            whole[used:, :] = jnp.zeros((whole.shape[0] - used, LANES), jnp.bfloat16)
        for k, part in enumerate(parts):
            size = part.shape[0]
            turn = lax.rem(lax.axis_index("space") + k, 2) if len(parts) == 2 else 0
            part[...] = whole[pl.ds(pl.multiple_of(turn * size, 16), size), :]
        if with_edge:
            for copy in copies:
                copy.wait()


def frame_states(keys, values, rows, parts, edged=()):
    tokens, dim = keys.shape
    part = (rows // parts, LANES)
    slabs = 2 if tokens % 32 == 0 else 1
    blocks = [
        pl.BlockSpec((tokens // slabs, GROUP), functools.partial(lambda k, g: (k, g), k))
        for k in range(slabs)
    ]

    def body(*refs):
        state_kernel(dim, bool(edged), refs[:slabs], refs[slabs : 2 * slabs], refs[2 * slabs :])

    return pl.pallas_call(
        body,
        out_shape=[pltpu.VMEM(part, jnp.bfloat16)] * parts
        + [pltpu.VMEM((len(edged), 1, *edged[0].shape[1:]), jnp.bfloat16) for _ in edged[:1]],
        grid=(cdiv(dim, GROUP),),
        in_specs=blocks + blocks + [pl.BlockSpec(memory_space=pl.ANY)] * len(edged),
        out_specs=[pl.BlockSpec(part, lambda g: (0, 0))] * parts
        + [pl.BlockSpec(memory_space=pl.ANY) for _ in edged[:1]],
        scratch_shapes=[
            pltpu.VMEM((slabs, GROUP, tokens // slabs), jnp.bfloat16),
            pltpu.VMEM((rows, LANES), jnp.bfloat16),
            pltpu.SemaphoreType.DMA((2,)),
        ],
        compiler_params=pltpu.CompilerParams(vmem_limit_bytes=60 * 2**20),
        cost_estimate=pl.CostEstimate(
            flops=2 * tokens * dim * HEAD_DIM, bytes_accessed=4 * tokens * dim, transcendentals=0
        ),
        name="frame_states",
    )(*[in_hbm(keys)] * slabs, *[in_hbm(values)] * slabs, *[in_hbm(array) for array in edged])


def group_lanes(dim):
    return [(first, min(GROUP, dim - first)) for first in range(0, dim, GROUP)]


def prepare_kernel(
    dim, queries_ref, residual_ref, edge_ref, gain_ref,
    features_ref, inputs_ref, heads_ref, spread_ref, held, semaphores,
):
    tokens = queries_ref.shape[0]
    full = dim // LANES * LANES
    parts = [slice(0, full), slice(full, dim)] if full < dim else [slice(0, dim)]
    copies = [
        pltpu.make_async_copy(source, held.at[k, :tokens], semaphores.at[k])
        for k, source in enumerate((queries_ref, residual_ref))
    ]
    for copy in copies:
        copy.start()
    edges, width = edge_ref.shape[1:3]
    for e in range(edges):
        here = slice(tokens + e * width, tokens + (e + 1) * width)
        held[0, here] = edge_ref[0, e]
        held[1, here] = edge_ref[1, e]
    head = lax.rem(lane_iota((GROUP, LANES)), HEADS)
    lane = lax.broadcasted_iota(jnp.int32, (GROUP, LANES), 0) - head * HEAD_DIM
    inside = (lane >= 0) & (lane < HEAD_DIM) & (lane_iota((GROUP, LANES)) < 3 * HEADS)
    heads_ref[...] = jnp.where(inside, 1.0, 0.0).astype(jnp.bfloat16)
    spread_ref[...] = jnp.zeros_like(spread_ref)
    used = cdiv(3 * HEADS, 16) * 16
    for group, (base, lanes) in enumerate(group_lanes(dim)):
        row = lax.broadcasted_iota(jnp.int32, (used, lanes), 0)
        lane = lane_iota((used, lanes)) - lax.rem(row, HEADS) * HEAD_DIM
        inside = (lane >= 0) & (lane < HEAD_DIM) & (row < 3 * HEADS)
        scaled = gain_ref[:, base : base + lanes] * math.sqrt(HEAD_DIM)
        coarse = scaled.astype(jnp.bfloat16).astype(jnp.float32)
        value = jnp.where((row >= HEADS) & (row < 2 * HEADS), scaled - coarse, coarse)
        spread_ref[group, :used, :lanes] = jnp.where(inside, value, 0.0).astype(jnp.bfloat16)
    if full < dim:
        features_ref[:, full:] = jnp.zeros((features_ref.shape[0], LANES), jnp.bfloat16)
    copies[0].wait()
    for part in parts:
        features_ref[:, part] = jnp.maximum(held[0, :, part], 0)
    copies[1].wait()
    for part in parts:
        inputs_ref[:, part] = held[1, :, part].astype(jnp.float32)


def prepare(queries, residual, edge, gain):
    tokens, dim = queries.shape
    total = tokens + edge.shape[1] * edge.shape[2]
    whole = pl.BlockSpec(memory_space=pltpu.VMEM)
    return pl.pallas_call(
        functools.partial(prepare_kernel, dim),
        out_shape=[
            pltpu.VMEM((total, cdiv(dim, LANES) * LANES), jnp.bfloat16),
            pltpu.VMEM((total, dim), jnp.float32),
            pltpu.VMEM((GROUP, LANES), jnp.bfloat16),
            pltpu.VMEM((len(group_lanes(dim)), LANES, GROUP), jnp.bfloat16),
        ],
        in_specs=[pl.BlockSpec(memory_space=pl.ANY)] * 2 + [whole] * 2,
        out_specs=[whole] * 4,
        scratch_shapes=[
            pltpu.VMEM((2, total, dim), jnp.bfloat16),
            pltpu.SemaphoreType.DMA((2,)),
        ],
        compiler_params=pltpu.CompilerParams(vmem_limit_bytes=24 * 2**20),
        cost_estimate=pl.CostEstimate(
            flops=4 * total * dim, bytes_accessed=8 * total * dim, transcendentals=0
        ),
        name="prepare",
    )(in_hbm(queries), in_hbm(residual), edge, gain)


def mix_kernel(
    dim, rows, width, edges,
    features_ref, inputs_ref, heads_ref, spread_ref, vtaps_ref, gtaps_ref, *refs,
):
    *pieces, out_ref, states, weights, numer, squares, spreads, mixed, windows, results, held = refs[:-1]
    semaphores = refs[-1]
    places = edge_places(lax.axis_size("space"), rows) if edges else []
    spots = piece_places() if len(pieces) > 1 else [0]
    tokens = rows * width
    for k, piece in enumerate(pieces):
        size = piece.shape[0]
        states[pl.ds(pl.multiple_of(spots[k] * size, 16), size), :] = piece[...]
    lane = lane_iota((HEAD_DIM, LANES))
    sublane = lax.broadcasted_iota(jnp.int32, (8, LANES), 0)

    half = width // 2
    even, odd = pl.ds(0, half, stride=2), pl.ds(1, half, stride=2)

    def store_windows(value, slot, used, row):
        mixed[slot, row, :, :used] = value
        left, right = mixed[slot, row, even, :used], mixed[slot, row, odd, :used]
        sub = sublane[:, :used]
        before, after = pltpu.roll(right, 1, 0), pltpu.roll(left, half - 1, 0)
        before = jnp.concatenate([jnp.where(sub == 0, 0.0, before[:8]), before[8:]], axis=0)
        after = jnp.concatenate([after[: half - 8], jnp.where(sub == 7, 0.0, after[half - 8 :])], axis=0)
        for k, window in enumerate((before - right, left + right, right - left, left - after)):
            windows[slot, k, row, :, :used] = window

    def group(base, lanes, turn):
        pairs = spans(lanes)

        def numerators(number):
            tiles, first, last = pairs[number]
            depth, wide = (last - first) * LANES, len(tiles) * LANES
            for side, j in enumerate(tiles):
                row = (base // LANES + j) * HEAD_DIM
                state = states[row : row + HEAD_DIM, :].astype(jnp.float32)
                heads = tile_heads(j, lanes)
                start = heads[0][0] * HEAD_DIM - first * LANES
                blocks = [jnp.where((lane >= lo) & (lane < hi), state, 0.0) for _, lo, hi in heads]
                rest = depth - start - len(heads) * HEAD_DIM
                if start:
                    blocks.insert(0, jnp.zeros((start, LANES), jnp.float32))
                if rest:
                    blocks.append(jnp.zeros((rest, LANES), jnp.float32))
                weights[turn, number, :depth, side * LANES : (side + 1) * LANES] = jnp.concatenate(
                    blocks, axis=0
                ).astype(jnp.bfloat16)
            product = jnp.dot(
                features_ref[:, base + first * LANES : base + last * LANES],
                weights[turn, number, :depth, :wide],
                preferred_element_type=jnp.float32,
            )
            here = slice(tiles[0] * LANES, tiles[0] * LANES + wide)
            numer[turn, :, here] = product
            squares[turn, :, here] = (product * product).astype(jnp.bfloat16)

        terms = []

        def scales():
            depth = cdiv(lanes, LANES) * LANES
            sums = jnp.dot(
                squares[turn, :, :depth], heads_ref[:depth, :], preferred_element_type=jnp.float32
            )
            scale = lax.rsqrt(sums + HEAD_DIM * 1e-06)
            coarse = scale.astype(jnp.bfloat16).astype(jnp.float32)
            fine = jnp.where(lane_iota(scale.shape) < 2 * HEADS, coarse, scale - coarse)
            terms.append(fine.astype(jnp.bfloat16))

        def spread(number):
            tiles, _, _ = pairs[number]
            here = slice(tiles[0] * LANES, (tiles[-1] + 1) * LANES)
            spreads[turn, :, here] = jnp.dot(
                terms[0], spread_ref[base // GROUP, :, here], preferred_element_type=jnp.float32
            )

        def mix_tile(j):
            slot = j % 2
            used = min(LANES, lanes - j * LANES)
            near = slice(j * LANES, j * LANES + used)
            here = slice(base + j * LANES, base + j * LANES + used)
            outside = [None, None]
            for row in range(rows + edges):
                source = slice(row * width, (row + 1) * width)
                value = inputs_ref[source, here] + numer[turn, source, near] * spreads[turn, source, near]
                if row < rows:
                    store_windows(value, slot, used, row + 1)
                    continue
                for k, place in enumerate((0, rows + 1)):
                    part = jnp.where(places[row - rows] == place, value, 0.0)
                    outside[k] = part if outside[k] is None else outside[k] + part
            for k, place in enumerate((0, rows + 1)):
                store_windows(outside[k], slot, used, place)
            taps = []
            for ref, factor in ((vtaps_ref, 1.0), (gtaps_ref, 0.5)):
                for tap_row in range(3):
                    one, two, three = [
                        ref[3 * tap_row + i : 3 * tap_row + i + 1, here] * factor for i in range(3)
                    ]
                    outer = 0.5 * (one + three)
                    taps.append((one, outer + 0.5 * two, outer - 0.5 * two, three))
            for row in range(rows):
                columns = []
                for f in range(2):
                    products = []
                    for k in range(4):
                        total = None
                        for tap_row in range(3):
                            term = taps[3 * f + tap_row][k] * windows[slot, k, row + tap_row, :, :used]
                            total = term if total is None else total + term
                        products.append(total)
                    columns.append(
                        (
                            products[0] + products[1] + products[2],
                            products[1] - products[2] - products[3],
                        )
                    )
                for side, (conv_v, half_g) in zip((even, odd), zip(*columns)):
                    center = mixed[slot, row + 1, side, :used]
                    results[slot, row, side, :used] = center + conv_v * (
                        half_g + half_g * jnp.tanh(half_g)
                    )
                held[row * width : (row + 1) * width, here] = results[slot, row, :, :used].astype(
                    jnp.bfloat16
                )

        numbers = range(len(pairs))
        ahead = [functools.partial(numerators, n) for n in numbers]
        ahead += [scales] + [functools.partial(spread, n) for n in numbers]
        return ahead, [functools.partial(mix_tile, j) for j in range(cdiv(lanes, LANES))]

    order = sorted(group_lanes(dim), key=lambda item: item[1])
    steps = [group(base, lanes, k % 2) for k, (base, lanes) in enumerate(order)]
    for step in steps[0][0]:
        step()
    copies = []
    for k, (base, lanes) in enumerate(order):
        tiles = steps[k][1]
        ahead = steps[k + 1][0] if k + 1 < len(steps) else []
        for n, tile in enumerate(tiles):
            for step in ahead[len(ahead) * n // len(tiles) : len(ahead) * (n + 1) // len(tiles)]:
                step()
            tile()
        here = slice(base, base + lanes)
        copies.append(
            pltpu.make_async_copy(held.at[:, here], out_ref.at[:, here], semaphores.at[k])
        )
        copies[-1].start()
    for copy in copies:
        copy.wait()


def mix(prepared, value_taps, gate_taps, pieces, rows, width):
    features, inputs, heads, spread = prepared
    total, dim = inputs.shape
    tokens = rows * width
    pairs = spans(min(GROUP, dim))
    depth = max(last - first for _, first, last in pairs) * LANES
    whole = pl.BlockSpec(memory_space=pltpu.VMEM)
    return pl.pallas_call(
        functools.partial(mix_kernel, dim, rows, width, (total - tokens) // width),
        out_shape=jax.ShapeDtypeStruct((tokens, dim), jnp.bfloat16),
        in_specs=[whole] * (6 + len(pieces)),
        out_specs=pl.BlockSpec(memory_space=pl.ANY),
        scratch_shapes=[
            pltpu.VMEM((sum(piece.shape[0] for piece in pieces), LANES), jnp.bfloat16),
            pltpu.VMEM((2, len(pairs), depth, 2 * LANES), jnp.bfloat16),
            pltpu.VMEM((2, total, GROUP), jnp.float32),
            pltpu.VMEM((2, total, GROUP), jnp.bfloat16),
            pltpu.VMEM((2, total, GROUP), jnp.float32),
            pltpu.VMEM((2, rows + 2, width, LANES), jnp.float32),
            pltpu.VMEM((2, 4, rows + 2, width // 2, LANES), jnp.float32),
            pltpu.VMEM((2, rows, width, LANES), jnp.float32),
            pltpu.VMEM((tokens, dim), jnp.bfloat16),
            pltpu.SemaphoreType.DMA((len(group_lanes(dim)),)),
        ],
        compiler_params=pltpu.CompilerParams(vmem_limit_bytes=36 * 2**20),
        cost_estimate=pl.CostEstimate(
            flops=60 * tokens * dim, bytes_accessed=6 * tokens * dim, transcendentals=2 * tokens * dim
        ),
        name="mix",
    )(features, inputs, heads, spread, value_taps, gate_taps, *pieces)


def edge_rows(queries, residual):
    devices, rows = lax.axis_size("space"), queries.shape[0]
    up = [(i, i + 1) for i in range(devices - 1)]
    down = [(j, i) for i, j in up]
    both = jnp.stack([queries, residual])
    if devices == 2:
        first = lax.axis_index("space") == 0
        return lax.ppermute(jnp.where(first, both[:, rows - 1 :], both[:, :1]), "space", up + down)
    before = lax.ppermute(both[:, rows - 1 :], "space", up)
    after = lax.ppermute(both[:, :1], "space", down)
    return jnp.concatenate([before, after], axis=1)


def small_kernel(body, name, outs, *arrays):
    return pl.pallas_call(
        body,
        out_shape=[pltpu.VMEM(shape, jnp.bfloat16) for shape in outs],
        in_specs=[pl.BlockSpec(memory_space=pltpu.VMEM)] * len(arrays),
        out_specs=[pl.BlockSpec(memory_space=pltpu.VMEM)] * len(outs),
        compiler_params=pltpu.CompilerParams(vmem_limit_bytes=4 * 2**20),
        name=name,
    )(*arrays)


def add(*values):
    total = values[0].astype(jnp.float32)
    for value in values[1:]:
        total = total + value.astype(jnp.float32)
    return total


def parity():
    return lax.rem(lax.axis_index("frame"), 2)


def split_sum_body(kept_ref, got_ref, mine_ref, theirs_ref):
    size = mine_ref.shape[0]
    for ref, side in ((theirs_ref, 1 - parity()), (mine_ref, parity())):
        rows = pl.ds(pl.multiple_of(side * size, 16), size)
        ref[...] = add(kept_ref[rows, :], got_ref[rows, :]).astype(jnp.bfloat16)


def sum_body(*refs):
    *terms, out_ref = refs
    out_ref[...] = add(*[term[...] for term in terms]).astype(jnp.bfloat16)


def pair_sums_body(own_ref, partner_ref, *refs):
    *earlier, mine_ref, theirs_ref = refs
    before = jnp.zeros(own_ref.shape, jnp.float32)
    for k, ref in enumerate(earlier):
        from_before = lax.rem(lax.axis_index("frame") // (2 << k), 2) == 1
        before = before + jnp.where(from_before, add(ref[...]), 0.0)
    own, partner = add(own_ref[...]), add(partner_ref[...])
    first = parity() == 0
    both = before + (own + partner)
    mine_ref[...] = jnp.where(first, before + own, both).astype(jnp.bfloat16)
    theirs_ref[...] = jnp.where(first, both, before + partner).astype(jnp.bfloat16)


def paired(devices, frames):
    return devices == 2 and frames >= 4 and frames & (frames - 1) == 0


def piece_places():
    core = lax.axis_index("space")
    return [2 * c + p for c in (core, 1 - core) for p in (parity(), 1 - parity())]


def edge_places(devices, rows):
    if devices == 2:
        return [jnp.where(lax.axis_index("space") == 0, rows + 1, 0)]
    return [0, rows + 1]


def running_states(keys, values, queries, residual, rows, beside):
    devices, frames = lax.axis_size("space"), lax.axis_size("frame")
    if not paired(devices, frames):
        (state,) = frame_states(keys, values, rows, 1)
        state = lax.psum(state.astype(jnp.float32), "space").astype(jnp.bfloat16)
        every = lax.all_gather(state, "frame").astype(jnp.float32)
        reached = (jnp.arange(frames) <= lax.axis_index("frame"))[:, None, None]
        total = jnp.sum(jnp.where(reached, every, 0.0), axis=0).astype(jnp.bfloat16)
        return [total], beside(edge_rows(queries, residual))
    swap = [(0, 1), (1, 0)]
    exchange = lambda array, stride: lax.ppermute(
        array, "frame", [(f, f ^ stride) for f in range(frames)]
    )
    kept, sent, edge = frame_states(keys, values, rows, 2, (queries, residual))
    got = lax.ppermute(sent, "space", swap)
    quarter = (rows // 4, LANES)
    own, sent = small_kernel(split_sum_body, "split_sum", [quarter] * 2, kept, got)
    edge, sent = lax.optimization_barrier((edge, sent))
    edge = lax.ppermute(edge, "space", swap)
    partner = exchange(sent, 1)
    (total,) = small_kernel(sum_body, "pair_sum", [quarter], own, partner)
    earlier = []
    stride = 2
    while stride < frames:
        if stride * 2 == frames:
            total, edge = lax.optimization_barrier((total, edge))
        earlier.append(exchange(total, stride))
        stride *= 2
        if stride < frames:
            (total,) = small_kernel(sum_body, "stride_sum", [quarter], total, earlier[-1])
    prepared = beside(edge)
    earlier[-1], *prepared = lax.optimization_barrier((earlier[-1], *prepared))
    mine, theirs = small_kernel(
        pair_sums_body, "pair_sums", [quarter] * 2, own, partner, *earlier
    )
    other = exchange(theirs, 1)
    pieces = [mine, other, lax.ppermute(mine, "space", swap), lax.ppermute(other, "space", swap)]
    return pieces, prepared


def on_device(queries, keys, values, residual, attn_gain, value_taps, gate_taps):
    frames, rows, width, dim = queries.shape
    tokens = frames * rows * width
    flat = lambda a: a.reshape(tokens, dim)
    state_rows = cdiv(cdiv(dim, LANES) * HEAD_DIM, 64) * 64
    pieces, prepared = running_states(
        flat(keys),
        flat(values),
        queries.reshape(rows, width, dim),
        residual.reshape(rows, width, dim),
        state_rows,
        lambda edge: prepare(flat(queries), flat(residual), edge, attn_gain[None]),
    )
    out = mix(prepared, value_taps, gate_taps, pieces, rows, width)
    return out.reshape(frames, rows, width, dim)


def solution(mesh):
    placed = P(("groups", "frame"), "space", None, None)
    return jax.shard_map(
        on_device,
        mesh=mesh,
        in_specs=(placed, placed, placed, placed, P(), P(), P()),
        out_specs=placed,
        check_vma=False,
    )
```

```python
import functools
import math

import jax
import jax.numpy as jnp
from jax import lax
from jax.experimental import pallas as pl
from jax.experimental.pallas import tpu as pltpu
from jax.sharding import PartitionSpec as P

HEAD_DIM = 112
LANES = 128
GROUP = math.lcm(HEAD_DIM, LANES)
TILES = GROUP // LANES


def cdiv(a, b):
    return -(-a // b)


def in_hbm(array):
    return pltpu.with_memory_space_constraint(array, pltpu.HBM)


def lane_iota(shape):
    return lax.broadcasted_iota(jnp.int32, shape, len(shape) - 1)


def tile_heads(j, lanes):
    lo, hi = j * LANES, min((j + 1) * LANES, lanes)
    heads = range(lo // HEAD_DIM, cdiv(hi, HEAD_DIM))
    return [(h, max(h * HEAD_DIM - lo, 0), min((h + 1) * HEAD_DIM - lo, LANES)) for h in heads]


def spans(lanes):
    count = cdiv(lanes, LANES)
    result = []
    for j in range(0, count, 2):
        tiles = list(range(j, min(j + 2, count)))
        first = tile_heads(tiles[0], lanes)[0][0] * HEAD_DIM // LANES
        last = cdiv((tile_heads(tiles[-1], lanes)[-1][0] + 1) * HEAD_DIM, LANES)
        result.append((tiles, first, last))
    return result


def by_group(dim, body):
    full, rest = divmod(dim, GROUP)
    if full:
        pl.when(pl.program_id(0) < full)(lambda: body(GROUP))
    if rest:
        pl.when(pl.program_id(0) >= full)(lambda: body(rest))


def state_kernel(dim, with_edge, keys_refs, values_refs, refs):
    step = pl.program_id(0)
    *refs, turned, whole, semaphores = refs
    if with_edge:
        *sources, edge_ref = refs[:2] + refs[-1:]
        parts = refs[2:-1]
        row = (sources[0].shape[0] - 1) * (1 - lax.axis_index("space"))
        copies = [
            pltpu.make_async_copy(source.at[row], edge_ref.at[k, 0], semaphores.at[k])
            for k, source in enumerate(sources)
        ]

        @pl.when(step == 0)
        def _():
            for copy in copies:
                copy.start()

    else:
        parts = refs

    def body(lanes):
        for k, keys_ref in enumerate(keys_refs):
            turned[k] = jnp.maximum(keys_ref[...], 0).T
        lane = lane_iota((HEAD_DIM, LANES))
        for tiles, _, _ in spans(lanes):
            begin = tile_heads(tiles[0], lanes)[0][0]
            end = tile_heads(tiles[-1], lanes)[-1][0] + 1
            product = sum(
                jnp.dot(
                    turned[k, begin * HEAD_DIM : end * HEAD_DIM, :],
                    values_ref[:, tiles[0] * LANES : (tiles[-1] + 1) * LANES],
                    preferred_element_type=jnp.float32,
                )
                for k, values_ref in enumerate(values_refs)
            )
            for side, j in enumerate(tiles):
                total = jnp.zeros((HEAD_DIM, LANES), jnp.float32)
                for h, lo, hi in tile_heads(j, lanes):
                    part = product[
                        (h - begin) * HEAD_DIM : (h - begin + 1) * HEAD_DIM,
                        side * LANES : (side + 1) * LANES,
                    ]
                    total = jnp.where((lane >= lo) & (lane < hi), part, total)
                row = pl.multiple_of((step * TILES + j) * HEAD_DIM, 16)
                whole[pl.ds(row, HEAD_DIM), :] = total.astype(jnp.bfloat16)

    by_group(dim, body)

    @pl.when(step == pl.num_programs(0) - 1)
    def _():
        used = cdiv(dim, LANES) * HEAD_DIM
        if used < whole.shape[0]:
            whole[used:, :] = jnp.zeros((whole.shape[0] - used, LANES), jnp.bfloat16)
        for k, part in enumerate(parts):
            size = part.shape[0]
            turn = lax.rem(lax.axis_index("space") + k, 2) if len(parts) == 2 else 0
            part[...] = whole[pl.ds(pl.multiple_of(turn * size, 16), size), :]
        if with_edge:
            for copy in copies:
                copy.wait()


def frame_states(keys, values, rows, parts, edged=()):
    tokens, dim = keys.shape
    part = (rows // parts, LANES)
    slabs = 2 if tokens % 32 == 0 else 1
    blocks = [
        pl.BlockSpec((tokens // slabs, GROUP), functools.partial(lambda k, g: (k, g), k))
        for k in range(slabs)
    ]

    def body(*refs):
        state_kernel(dim, bool(edged), refs[:slabs], refs[slabs : 2 * slabs], refs[2 * slabs :])

    return pl.pallas_call(
        body,
        out_shape=[pltpu.VMEM(part, jnp.bfloat16)] * parts
        + [pltpu.VMEM((len(edged), 1, *edged[0].shape[1:]), jnp.bfloat16) for _ in edged[:1]],
        grid=(cdiv(dim, GROUP),),
        in_specs=blocks + blocks + [pl.BlockSpec(memory_space=pl.ANY)] * len(edged),
        out_specs=[pl.BlockSpec(part, lambda g: (0, 0))] * parts
        + [pl.BlockSpec(memory_space=pl.ANY) for _ in edged[:1]],
        scratch_shapes=[
            pltpu.VMEM((slabs, GROUP, tokens // slabs), jnp.bfloat16),
            pltpu.VMEM((rows, LANES), jnp.bfloat16),
            pltpu.SemaphoreType.DMA((2,)),
        ],
        compiler_params=pltpu.CompilerParams(vmem_limit_bytes=60 * 2**20),
        cost_estimate=pl.CostEstimate(
            flops=2 * tokens * dim * HEAD_DIM, bytes_accessed=4 * tokens * dim, transcendentals=0
        ),
        name="frame_states",
    )(*[in_hbm(keys)] * slabs, *[in_hbm(values)] * slabs, *[in_hbm(array) for array in edged])


def group_lanes(dim):
    return [(first, min(GROUP, dim - first)) for first in range(0, dim, GROUP)]


def prepare_kernel(
    dim, queries_ref, residual_ref, edge_ref, gain_ref,
    features_ref, inputs_ref, scaled_ref, held, wide, semaphores,
):
    tokens = queries_ref.shape[0]
    copies = [
        pltpu.make_async_copy(source, held.at[k, :tokens], semaphores.at[k])
        for k, source in enumerate((queries_ref, residual_ref))
    ]
    for copy in copies:
        copy.start()
    edges, width = edge_ref.shape[1:3]
    for e in range(edges):
        here = slice(tokens + e * width, tokens + (e + 1) * width)
        held[0, here] = edge_ref[0, e]
        held[1, here] = edge_ref[1, e]
    scaled_ref[...] = gain_ref[...] * math.sqrt(HEAD_DIM)
    half = width // 2
    for k, copy in enumerate(copies):
        copy.wait()
        for j in range(cdiv(dim, LANES)):
            here = slice(j * LANES, min((j + 1) * LANES, dim))
            used = here.stop - here.start
            slot = j % 2
            if k == 0 and used < LANES:
                features_ref[:, here.stop :] = jnp.zeros(
                    (features_ref.shape[0], LANES - used), jnp.bfloat16
                )
            wide[slot, :, :used] = held[k, :, here].astype(jnp.float32)
            for row in range(wide.shape[1] // width):
                value = jnp.concatenate(
                    [
                        wide[slot, pl.ds(row * width + side, half, stride=2), :used]
                        for side in range(2)
                    ],
                    axis=0,
                )
                source = slice(row * width, (row + 1) * width)
                if k == 0:
                    features_ref[source, here] = jnp.maximum(value, 0.0).astype(jnp.bfloat16)
                else:
                    inputs_ref[source, here] = value


def prepare(queries, residual, edge, gain):
    tokens, dim = queries.shape
    total = tokens + edge.shape[1] * edge.shape[2]
    whole = pl.BlockSpec(memory_space=pltpu.VMEM)
    return pl.pallas_call(
        functools.partial(prepare_kernel, dim),
        out_shape=[
            pltpu.VMEM((total, cdiv(dim, LANES) * LANES), jnp.bfloat16),
            pltpu.VMEM((total, dim), jnp.float32),
            pltpu.VMEM((1, dim), jnp.float32),
        ],
        in_specs=[pl.BlockSpec(memory_space=pl.ANY)] * 2 + [whole] * 2,
        out_specs=[whole] * 3,
        scratch_shapes=[
            pltpu.VMEM((2, total, dim), jnp.bfloat16),
            pltpu.VMEM((2, total, LANES), jnp.float32),
            pltpu.SemaphoreType.DMA((2,)),
        ],
        compiler_params=pltpu.CompilerParams(vmem_limit_bytes=24 * 2**20),
        cost_estimate=pl.CostEstimate(
            flops=4 * total * dim, bytes_accessed=8 * total * dim, transcendentals=0
        ),
        name="prepare",
    )(in_hbm(queries), in_hbm(residual), edge, gain)


def mix_kernel(
    dim, rows, width, edges,
    features_ref, inputs_ref, gain_ref, vtaps_ref, gtaps_ref, *refs,
):
    *pieces, out_ref, states, weights, numer, mixed_rows, windows, results, held, semaphores = refs
    places = edge_places(lax.axis_size("space"), rows) if edges else []
    spots = piece_places() if len(pieces) > 1 else [0]
    tokens = rows * width
    weights[...] = jnp.zeros_like(weights)
    for row in (0, rows + 1):
        windows[:, :, row] = jnp.zeros((2, 4, width // 2, LANES), jnp.float32)
    for k, piece in enumerate(pieces):
        size = piece.shape[0]
        states[pl.ds(pl.multiple_of(spots[k] * size, 16), size), :] = piece[...]
    lane = lane_iota((HEAD_DIM, LANES))
    sublane = lax.broadcasted_iota(jnp.int32, (8, LANES), 0)

    half = width // 2
    even, odd = pl.ds(0, half, stride=2), pl.ds(1, half, stride=2)

    def store_windows(value, slot, used, row, place):
        left, right = value[:half], value[half:]
        if 0 < row <= rows:
            mixed_rows[slot, row, :, :used] = value
        sub = sublane[:, :used]
        before, after = pltpu.roll(right, 1, 0), pltpu.roll(left, half - 1, 0)
        before = jnp.concatenate([jnp.where(sub == 0, 0.0, before[:8]), before[8:]], axis=0)
        after = jnp.concatenate([after[: half - 8], jnp.where(sub == 7, 0.0, after[half - 8 :])], axis=0)
        for k, window in enumerate((before - right, left + right, right - left, left - after)):
            windows[slot, k, place, :, :used] = window

    def group(base, lanes):
        pairs = spans(lanes)

        def numerators(number):
            tiles, first, last = pairs[number]
            for side, j in enumerate(tiles):
                row = (base // LANES + j) * HEAD_DIM
                state = states[row : row + HEAD_DIM, :].astype(jnp.float32)
                for h, lo, hi in tile_heads(j, lanes):
                    start = h * HEAD_DIM - first * LANES
                    block = jnp.where((lane >= lo) & (lane < hi), state, 0.0)
                    weights[
                        number, start : start + HEAD_DIM, side * LANES : (side + 1) * LANES
                    ] = block.astype(jnp.bfloat16)
            depth, wide = (last - first) * LANES, len(tiles) * LANES
            product = jnp.dot(
                features_ref[:, base + first * LANES : base + last * LANES],
                weights[number, :depth, :wide],
                preferred_element_type=jnp.float32,
            )
            here = slice(tiles[0] * LANES, tiles[0] * LANES + wide)
            numer[:, here] = product

        def tile_sums(j, source):
            square = numer[source, j * LANES : (j + 1) * LANES]
            square = square * square
            heads = tile_heads(j, lanes)
            if len(heads) == 1:
                return {heads[0][0]: jnp.sum(square, axis=-1, keepdims=True)}
            (one, _, bound), (two, _, _) = heads
            part = jnp.where(lane_iota(square.shape) < bound, square, 0.0)
            rest = square - part
            return {
                one: jnp.sum(part, axis=-1, keepdims=True),
                two: jnp.sum(rest, axis=-1, keepdims=True),
            }

        def mix_tile(j):
            slot = j % 2
            used = min(LANES, lanes - j * LANES)
            near = slice(j * LANES, j * LANES + used)
            here = slice(base + j * LANES, base + j * LANES + used)
            heads = tile_heads(j, lanes)

            def mixed(source):
                sums = [
                    sum(tiles[head] for tiles in parts[source.start] if head in tiles)
                    for head, _, _ in heads
                ]
                scale = jnp.broadcast_to(sums[0], (width, used))
                if len(heads) > 1:
                    scale = jnp.where(lane_iota(scale.shape) < heads[0][2], scale, sums[1])
                normed = numer[source, near] * lax.rsqrt(scale + HEAD_DIM * 1e-06)
                return inputs_ref[source, here] + normed * gain_ref[:, here]

            for row in range(rows):
                value = mixed(slice(row * width, (row + 1) * width))
                store_windows(value, slot, used, row + 1, row + 1)
            for e in range(edges):
                value = mixed(slice(tokens + e * width, tokens + (e + 1) * width))
                store_windows(value, slot, used, 0, places[e])
            taps = []
            for ref, factor in ((vtaps_ref, 1.0), (gtaps_ref, 0.5)):
                for tap_row in range(3):
                    one, two, three = [
                        ref[3 * tap_row + i : 3 * tap_row + i + 1, here] * factor for i in range(3)
                    ]
                    outer = 0.5 * (one + three)
                    taps.append((one, outer + 0.5 * two, outer - 0.5 * two, three))
            for row in range(rows):
                columns = []
                for f in range(2):
                    products = []
                    for k in range(4):
                        total = None
                        for tap_row in range(3):
                            term = taps[3 * f + tap_row][k] * windows[slot, k, row + tap_row, :, :used]
                            total = term if total is None else total + term
                        products.append(total)
                    columns.append(
                        (
                            products[0] + products[1] + products[2],
                            products[1] - products[2] - products[3],
                        )
                    )
                for k, (side, (conv_v, half_g)) in enumerate(zip((even, odd), zip(*columns))):
                    center = mixed_rows[slot, row + 1, k * half : (k + 1) * half, :used]
                    results[slot, row, side, :used] = center + conv_v * (
                        half_g + half_g * jnp.tanh(half_g)
                    )
                held[row * width : (row + 1) * width, here] = results[slot, row, :, :used].astype(
                    jnp.bfloat16
                )

        parts = {}
        for number, (tiles, _, _) in enumerate(pairs):
            numerators(number)
            for j in tiles:
                for row in range(rows + edges):
                    source = slice(row * width, (row + 1) * width)
                    parts.setdefault(source.start, []).append(tile_sums(j, source))
        for j in range(cdiv(lanes, LANES)):
            mix_tile(j)

    copies = []
    for base, lanes in group_lanes(dim):
        group(base, lanes)
        here = slice(base, base + lanes)
        copies.append(
            pltpu.make_async_copy(held.at[:, here], out_ref.at[:, here], semaphores.at[len(copies)])
        )
        copies[-1].start()
    for copy in copies:
        copy.wait()


def mix(prepared, value_taps, gate_taps, pieces, rows, width):
    features, inputs, gain = prepared
    total, dim = inputs.shape
    tokens = rows * width
    pairs = spans(min(GROUP, dim))
    depth = max(last - first for _, first, last in pairs) * LANES
    whole = pl.BlockSpec(memory_space=pltpu.VMEM)
    return pl.pallas_call(
        functools.partial(mix_kernel, dim, rows, width, (total - tokens) // width),
        out_shape=jax.ShapeDtypeStruct((tokens, dim), jnp.bfloat16),
        in_specs=[whole] * (5 + len(pieces)),
        out_specs=pl.BlockSpec(memory_space=pl.ANY),
        scratch_shapes=[
            pltpu.VMEM((sum(piece.shape[0] for piece in pieces), LANES), jnp.bfloat16),
            pltpu.VMEM((len(pairs), depth, 2 * LANES), jnp.bfloat16),
            pltpu.VMEM((total, GROUP), jnp.float32),
            pltpu.VMEM((2, rows + 2, width, LANES), jnp.float32),
            pltpu.VMEM((2, 4, rows + 2, width // 2, LANES), jnp.float32),
            pltpu.VMEM((2, rows, width, LANES), jnp.float32),
            pltpu.VMEM((tokens, dim), jnp.bfloat16),
            pltpu.SemaphoreType.DMA((len(group_lanes(dim)),)),
        ],
        compiler_params=pltpu.CompilerParams(vmem_limit_bytes=36 * 2**20),
        cost_estimate=pl.CostEstimate(
            flops=60 * tokens * dim, bytes_accessed=6 * tokens * dim, transcendentals=2 * tokens * dim
        ),
        name="mix",
    )(features, inputs, gain, value_taps, gate_taps, *pieces)


def edge_rows(queries, residual):
    devices, rows = lax.axis_size("space"), queries.shape[0]
    up = [(i, i + 1) for i in range(devices - 1)]
    down = [(j, i) for i, j in up]
    both = jnp.stack([queries, residual])
    if devices == 2:
        first = lax.axis_index("space") == 0
        return lax.ppermute(jnp.where(first, both[:, rows - 1 :], both[:, :1]), "space", up + down)
    before = lax.ppermute(both[:, rows - 1 :], "space", up)
    after = lax.ppermute(both[:, :1], "space", down)
    return jnp.concatenate([before, after], axis=1)


def small_kernel(body, name, outs, *arrays):
    return pl.pallas_call(
        body,
        out_shape=[pltpu.VMEM(shape, jnp.bfloat16) for shape in outs],
        in_specs=[pl.BlockSpec(memory_space=pltpu.VMEM)] * len(arrays),
        out_specs=[pl.BlockSpec(memory_space=pltpu.VMEM)] * len(outs),
        compiler_params=pltpu.CompilerParams(vmem_limit_bytes=4 * 2**20),
        name=name,
    )(*arrays)


def add(*values):
    total = values[0].astype(jnp.float32)
    for value in values[1:]:
        total = total + value.astype(jnp.float32)
    return total


def parity():
    return lax.rem(lax.axis_index("frame"), 2)


def split_sum_body(kept_ref, got_ref, mine_ref, theirs_ref):
    size = mine_ref.shape[0]
    for ref, side in ((theirs_ref, 1 - parity()), (mine_ref, parity())):
        rows = pl.ds(pl.multiple_of(side * size, 16), size)
        ref[...] = add(kept_ref[rows, :], got_ref[rows, :]).astype(jnp.bfloat16)


def sum_body(*refs):
    *terms, out_ref = refs
    out_ref[...] = add(*[term[...] for term in terms]).astype(jnp.bfloat16)


def pair_sums_body(own_ref, partner_ref, *refs):
    *earlier, mine_ref, theirs_ref = refs
    before = jnp.zeros(own_ref.shape, jnp.float32)
    for k, ref in enumerate(earlier):
        from_before = lax.rem(lax.axis_index("frame") // (2 << k), 2) == 1
        before = before + jnp.where(from_before, add(ref[...]), 0.0)
    own, partner = add(own_ref[...]), add(partner_ref[...])
    first = parity() == 0
    both = before + (own + partner)
    mine_ref[...] = jnp.where(first, before + own, both).astype(jnp.bfloat16)
    theirs_ref[...] = jnp.where(first, both, before + partner).astype(jnp.bfloat16)


def paired(devices, frames):
    return devices == 2 and frames >= 4 and frames & (frames - 1) == 0


def piece_places():
    core = lax.axis_index("space")
    return [2 * c + p for c in (core, 1 - core) for p in (parity(), 1 - parity())]


def edge_places(devices, rows):
    if devices == 2:
        return [jnp.where(lax.axis_index("space") == 0, rows + 1, 0)]
    return [0, rows + 1]


def running_states(keys, values, queries, residual, rows, beside):
    devices, frames = lax.axis_size("space"), lax.axis_size("frame")
    if not paired(devices, frames):
        (state,) = frame_states(keys, values, rows, 1)
        state = lax.psum(state.astype(jnp.float32), "space").astype(jnp.bfloat16)
        every = lax.all_gather(state, "frame").astype(jnp.float32)
        reached = (jnp.arange(frames) <= lax.axis_index("frame"))[:, None, None]
        total = jnp.sum(jnp.where(reached, every, 0.0), axis=0).astype(jnp.bfloat16)
        return [total], beside(edge_rows(queries, residual))
    swap = [(0, 1), (1, 0)]
    exchange = lambda array, stride: lax.ppermute(
        array, "frame", [(f, f ^ stride) for f in range(frames)]
    )
    kept, sent, edge = frame_states(keys, values, rows, 2, (queries, residual))
    got = lax.ppermute(sent, "space", swap)
    quarter = (rows // 4, LANES)
    own, sent = small_kernel(split_sum_body, "split_sum", [quarter] * 2, kept, got)
    edge, sent = lax.optimization_barrier((edge, sent))
    edge = lax.ppermute(edge, "space", swap)
    partner = exchange(sent, 1)
    (total,) = small_kernel(sum_body, "pair_sum", [quarter], own, partner)
    earlier = []
    stride = 2
    while stride < frames:
        if stride * 2 == frames:
            total, edge = lax.optimization_barrier((total, edge))
        earlier.append(exchange(total, stride))
        stride *= 2
        if stride < frames:
            (total,) = small_kernel(sum_body, "stride_sum", [quarter], total, earlier[-1])
    prepared = beside(edge)
    earlier[-1], *prepared = lax.optimization_barrier((earlier[-1], *prepared))
    mine, theirs = small_kernel(
        pair_sums_body, "pair_sums", [quarter] * 2, own, partner, *earlier
    )
    other = exchange(theirs, 1)
    pieces = [mine, other, lax.ppermute(mine, "space", swap), lax.ppermute(other, "space", swap)]
    return pieces, prepared


def on_device(queries, keys, values, residual, attn_gain, value_taps, gate_taps):
    frames, rows, width, dim = queries.shape
    tokens = frames * rows * width
    flat = lambda a: a.reshape(tokens, dim)
    state_rows = cdiv(cdiv(dim, LANES) * HEAD_DIM, 64) * 64
    pieces, prepared = running_states(
        flat(keys),
        flat(values),
        queries.reshape(rows, width, dim),
        residual.reshape(rows, width, dim),
        state_rows,
        lambda edge: prepare(flat(queries), flat(residual), edge, attn_gain[None]),
    )
    out = mix(prepared, value_taps, gate_taps, pieces, rows, width)
    return out.reshape(frames, rows, width, dim)


def solution(mesh):
    placed = P(("groups", "frame"), "space", None, None)
    return jax.shard_map(
        on_device,
        mesh=mesh,
        in_specs=(placed, placed, placed, placed, P(), P(), P()),
        out_specs=placed,
        check_vma=False,
    )
```

```python
import functools
import math

import jax
import jax.numpy as jnp
from jax import lax
from jax.experimental import pallas as pl
from jax.experimental.pallas import tpu as pltpu
from jax.sharding import PartitionSpec as P

HEAD_DIM = 112
LANES = 128
GROUP = math.lcm(HEAD_DIM, LANES)
TILES = GROUP // LANES


def cdiv(a, b):
    return -(-a // b)


def in_hbm(array):
    return pltpu.with_memory_space_constraint(array, pltpu.HBM)


def lane_iota(shape):
    return lax.broadcasted_iota(jnp.int32, shape, len(shape) - 1)


def tile_heads(j, lanes):
    lo, hi = j * LANES, min((j + 1) * LANES, lanes)
    heads = range(lo // HEAD_DIM, cdiv(hi, HEAD_DIM))
    return [(h, max(h * HEAD_DIM - lo, 0), min((h + 1) * HEAD_DIM - lo, LANES)) for h in heads]


def spans(lanes):
    count = cdiv(lanes, LANES)
    result = []
    for j in range(0, count, 2):
        tiles = list(range(j, min(j + 2, count)))
        first = tile_heads(tiles[0], lanes)[0][0] * HEAD_DIM // LANES
        last = cdiv((tile_heads(tiles[-1], lanes)[-1][0] + 1) * HEAD_DIM, LANES)
        result.append((tiles, first, last))
    return result


def by_group(dim, body):
    full, rest = divmod(dim, GROUP)
    if full:
        pl.when(pl.program_id(0) < full)(lambda: body(GROUP))
    if rest:
        pl.when(pl.program_id(0) >= full)(lambda: body(rest))


def state_kernel(dim, with_edge, keys_refs, values_refs, refs):
    step = pl.program_id(0)
    *refs, turned, whole, semaphores = refs
    if with_edge:
        *sources, edge_ref = refs[:2] + refs[-1:]
        parts = refs[2:-1]
        row = (sources[0].shape[0] - 1) * (1 - lax.axis_index("space"))
        copies = [
            pltpu.make_async_copy(source.at[row], edge_ref.at[k, 0], semaphores.at[k])
            for k, source in enumerate(sources)
        ]

        @pl.when(step == 0)
        def _():
            for copy in copies:
                copy.start()

    else:
        parts = refs

    def body(lanes):
        for k, keys_ref in enumerate(keys_refs):
            turned[k] = jnp.maximum(keys_ref[...], 0).T
        lane = lane_iota((HEAD_DIM, LANES))
        for tiles, _, _ in spans(lanes):
            begin = tile_heads(tiles[0], lanes)[0][0]
            end = tile_heads(tiles[-1], lanes)[-1][0] + 1
            product = sum(
                jnp.dot(
                    turned[k, begin * HEAD_DIM : end * HEAD_DIM, :],
                    values_ref[:, tiles[0] * LANES : (tiles[-1] + 1) * LANES],
                    preferred_element_type=jnp.float32,
                )
                for k, values_ref in enumerate(values_refs)
            )
            for side, j in enumerate(tiles):
                total = jnp.zeros((HEAD_DIM, LANES), jnp.float32)
                for h, lo, hi in tile_heads(j, lanes):
                    part = product[
                        (h - begin) * HEAD_DIM : (h - begin + 1) * HEAD_DIM,
                        side * LANES : (side + 1) * LANES,
                    ]
                    total = jnp.where((lane >= lo) & (lane < hi), part, total)
                row = pl.multiple_of((step * TILES + j) * HEAD_DIM, 16)
                whole[pl.ds(row, HEAD_DIM), :] = total.astype(jnp.bfloat16)

    by_group(dim, body)

    @pl.when(step == pl.num_programs(0) - 1)
    def _():
        used = cdiv(dim, LANES) * HEAD_DIM
        if used < whole.shape[0]:
            whole[used:, :] = jnp.zeros((whole.shape[0] - used, LANES), jnp.bfloat16)
        for k, part in enumerate(parts):
            size = part.shape[0]
            turn = lax.rem(lax.axis_index("space") + k, 2) if len(parts) == 2 else 0
            part[...] = whole[pl.ds(pl.multiple_of(turn * size, 16), size), :]
        if with_edge:
            for copy in copies:
                copy.wait()


def frame_states(keys, values, rows, parts, edged=()):
    tokens, dim = keys.shape
    part = (rows // parts, LANES)
    slabs = 2 if tokens % 32 == 0 else 1
    blocks = [
        pl.BlockSpec((tokens // slabs, GROUP), functools.partial(lambda k, g: (k, g), k))
        for k in range(slabs)
    ]

    def body(*refs):
        state_kernel(dim, bool(edged), refs[:slabs], refs[slabs : 2 * slabs], refs[2 * slabs :])

    return pl.pallas_call(
        body,
        out_shape=[pltpu.VMEM(part, jnp.bfloat16)] * parts
        + [pltpu.VMEM((len(edged), 1, *edged[0].shape[1:]), jnp.bfloat16) for _ in edged[:1]],
        grid=(cdiv(dim, GROUP),),
        in_specs=blocks + blocks + [pl.BlockSpec(memory_space=pl.ANY)] * len(edged),
        out_specs=[pl.BlockSpec(part, lambda g: (0, 0))] * parts
        + [pl.BlockSpec(memory_space=pl.ANY) for _ in edged[:1]],
        scratch_shapes=[
            pltpu.VMEM((slabs, GROUP, tokens // slabs), jnp.bfloat16),
            pltpu.VMEM((rows, LANES), jnp.bfloat16),
            pltpu.SemaphoreType.DMA((2,)),
        ],
        compiler_params=pltpu.CompilerParams(vmem_limit_bytes=60 * 2**20),
        cost_estimate=pl.CostEstimate(
            flops=2 * tokens * dim * HEAD_DIM, bytes_accessed=4 * tokens * dim, transcendentals=0
        ),
        name="frame_states",
    )(*[in_hbm(keys)] * slabs, *[in_hbm(values)] * slabs, *[in_hbm(array) for array in edged])


def group_lanes(dim):
    return [(first, min(GROUP, dim - first)) for first in range(0, dim, GROUP)]


def prepare_kernel(
    dim, queries_ref, residual_ref, edge_ref, gain_ref, vtaps_ref, gtaps_ref,
    features_ref, inputs_ref, scaled_ref, taps_ref, held, wide, semaphores,
):
    tokens = queries_ref.shape[0]
    copies = [
        pltpu.make_async_copy(source, held.at[k, :tokens], semaphores.at[k])
        for k, source in enumerate((queries_ref, residual_ref))
    ]
    for copy in copies:
        copy.start()
    edges, width = edge_ref.shape[1:3]
    for e in range(edges):
        here = slice(tokens + e * width, tokens + (e + 1) * width)
        held[0, here] = edge_ref[0, e]
        held[1, here] = edge_ref[1, e]
    scaled_ref[...] = gain_ref[...] * math.sqrt(HEAD_DIM)
    half = width // 2
    for j in range(cdiv(dim, LANES)):
        here = slice(j * LANES, min((j + 1) * LANES, dim))
        used = here.stop - here.start
        number = 0
        for ref, factor in ((vtaps_ref, 1.0), (gtaps_ref, 0.5)):
            for tap in (0, 3, 6):
                one, two, three = [ref[tap + i : tap + i + 1, here] * factor for i in range(3)]
                outer = 0.5 * (one + three)
                for row in (one, outer + 0.5 * two, outer - 0.5 * two, three):
                    taps_ref[j, number, :, :used] = jnp.broadcast_to(row, (8, used))
                    number += 1
    for k, copy in enumerate(copies):
        copy.wait()
        for j in range(cdiv(dim, LANES)):
            here = slice(j * LANES, min((j + 1) * LANES, dim))
            used = here.stop - here.start
            slot = j % 2
            if k == 0 and used < LANES:
                features_ref[:, here.stop :] = jnp.zeros(
                    (features_ref.shape[0], LANES - used), jnp.bfloat16
                )
            wide[slot, :, :used] = held[k, :, here].astype(jnp.float32)
            for row in range(wide.shape[1] // width):
                value = jnp.concatenate(
                    [
                        wide[slot, pl.ds(row * width + side, half, stride=2), :used]
                        for side in range(2)
                    ],
                    axis=0,
                )
                source = slice(row * width, (row + 1) * width)
                if k == 0:
                    features_ref[source, here] = jnp.maximum(value, 0.0).astype(jnp.bfloat16)
                else:
                    inputs_ref[source, here] = value


def prepare(queries, residual, edge, gain, value_taps, gate_taps):
    tokens, dim = queries.shape
    total = tokens + edge.shape[1] * edge.shape[2]
    whole = pl.BlockSpec(memory_space=pltpu.VMEM)
    return pl.pallas_call(
        functools.partial(prepare_kernel, dim),
        out_shape=[
            pltpu.VMEM((total, cdiv(dim, LANES) * LANES), jnp.bfloat16),
            pltpu.VMEM((total, dim), jnp.float32),
            pltpu.VMEM((1, dim), jnp.float32),
            pltpu.VMEM((cdiv(dim, LANES), 24, 8, LANES), jnp.float32),
        ],
        in_specs=[pl.BlockSpec(memory_space=pl.ANY)] * 2 + [whole] * 4,
        out_specs=[whole] * 4,
        scratch_shapes=[
            pltpu.VMEM((2, total, dim), jnp.bfloat16),
            pltpu.VMEM((2, total, LANES), jnp.float32),
            pltpu.SemaphoreType.DMA((2,)),
        ],
        compiler_params=pltpu.CompilerParams(vmem_limit_bytes=24 * 2**20),
        cost_estimate=pl.CostEstimate(
            flops=4 * total * dim, bytes_accessed=8 * total * dim, transcendentals=0
        ),
        name="prepare",
    )(in_hbm(queries), in_hbm(residual), edge, gain, value_taps, gate_taps)


def mix_kernel(
    dim, rows, width, edges,
    features_ref, inputs_ref, gain_ref, taps_ref, *refs,
):
    *pieces, out_ref, states, weights, numer, mixed_rows, windows, results, held, semaphores = refs
    places = edge_places(lax.axis_size("space"), rows) if edges else []
    spots = piece_places() if len(pieces) > 1 else [0]
    tokens = rows * width
    weights[...] = jnp.zeros_like(weights)
    for row in (0, rows + 1):
        windows[:, :, row] = jnp.zeros((2, 4, width // 16, 8, LANES), jnp.float32)
    for k, piece in enumerate(pieces):
        size = piece.shape[0]
        states[pl.ds(pl.multiple_of(spots[k] * size, 16), size), :] = piece[...]
    lane = lane_iota((HEAD_DIM, LANES))
    sublane = lax.broadcasted_iota(jnp.int32, (8, LANES), 0)

    half = width // 2
    even, odd = pl.ds(0, half, stride=2), pl.ds(1, half, stride=2)

    def store_windows(value, slot, used, row, place):
        left, right = value[:half], value[half:]
        if 0 < row <= rows:
            mixed_rows[slot, row, :, :used] = value
        sub = sublane[:, :used]
        before, after = pltpu.roll(right, 1, 0), pltpu.roll(left, half - 1, 0)
        before = jnp.concatenate([jnp.where(sub == 0, 0.0, before[:8]), before[8:]], axis=0)
        after = jnp.concatenate([after[: half - 8], jnp.where(sub == 7, 0.0, after[half - 8 :])], axis=0)
        for k, window in enumerate((before - right, left + right, right - left, left - after)):
            windows[slot, k, place, :, :, :used] = window.reshape(half // 8, 8, used)

    def group(base, lanes):
        pairs = spans(lanes)

        def numerators(number):
            tiles, first, last = pairs[number]
            for side, j in enumerate(tiles):
                row = (base // LANES + j) * HEAD_DIM
                state = states[row : row + HEAD_DIM, :].astype(jnp.float32)
                for h, lo, hi in tile_heads(j, lanes):
                    start = h * HEAD_DIM - first * LANES
                    block = jnp.where((lane >= lo) & (lane < hi), state, 0.0)
                    weights[
                        number, start : start + HEAD_DIM, side * LANES : (side + 1) * LANES
                    ] = block.astype(jnp.bfloat16)
            depth, wide = (last - first) * LANES, len(tiles) * LANES
            product = jnp.dot(
                features_ref[:, base + first * LANES : base + last * LANES],
                weights[number, :depth, :wide],
                preferred_element_type=jnp.float32,
            )
            here = slice(tiles[0] * LANES, tiles[0] * LANES + wide)
            numer[:, here] = product

        def tile_sums(j, source):
            square = numer[source, j * LANES : (j + 1) * LANES]
            square = square * square
            position = lane_iota(square.shape)
            sums = {}
            for head, lo, hi in tile_heads(j, lanes):
                ends = (head + 1) * HEAD_DIM <= (j + 1) * LANES
                fill = HEAD_DIM * 1e-06 / (LANES - (hi - lo)) if ends else 0.0
                mine = position < hi if lo == 0 else position >= lo
                sums[head] = jnp.sum(jnp.where(mine, square, fill), axis=-1, keepdims=True)
            return sums

        def mix_tile(j):
            slot = j % 2
            used = min(LANES, lanes - j * LANES)
            near = slice(j * LANES, j * LANES + used)
            here = slice(base + j * LANES, base + j * LANES + used)
            heads = tile_heads(j, lanes)

            def mixed(source):
                sums = [
                    sum(tiles[head] for tiles in parts[source.start] if head in tiles)
                    for head, _, _ in heads
                ]
                scale = jnp.broadcast_to(sums[0], (width, used))
                if len(heads) > 1:
                    scale = jnp.where(lane_iota(scale.shape) < heads[0][2], scale, sums[1])
                normed = numer[source, near] * lax.rsqrt(scale)
                return inputs_ref[source, here] + normed * gain_ref[:, here]

            for row in range(rows):
                value = mixed(slice(row * width, (row + 1) * width))
                store_windows(value, slot, used, row + 1, row + 1)
            for e in range(edges):
                value = mixed(slice(tokens + e * width, tokens + (e + 1) * width))
                store_windows(value, slot, used, 0, places[e])
            for row in range(rows):
                columns = []
                for f in range(2):
                    products = []
                    for k in range(4):
                        total = None
                        for tap_row in range(3):
                            tap = taps_ref[base // LANES + j, 12 * f + 4 * tap_row + k, :, :used]
                            term = tap * windows[slot, k, row + tap_row, :, :, :used]
                            total = term if total is None else total + term
                        products.append(total)
                    columns.append(
                        (
                            products[0] + products[1] + products[2],
                            products[1] - products[2] - products[3],
                        )
                    )
                for k, (side, (conv_v, half_g)) in enumerate(zip((even, odd), zip(*columns))):
                    center = mixed_rows[slot, row + 1, k * half : (k + 1) * half, :used]
                    gated = conv_v * (half_g + half_g * jnp.tanh(half_g))
                    results[slot, row, side, :used] = center + gated.reshape(half, used)
                held[row * width : (row + 1) * width, here] = results[slot, row, :, :used].astype(
                    jnp.bfloat16
                )

        parts = {}
        for number, (tiles, _, _) in enumerate(pairs):
            numerators(number)
            for j in tiles:
                for row in range(rows + edges):
                    source = slice(row * width, (row + 1) * width)
                    parts.setdefault(source.start, []).append(tile_sums(j, source))
        for j in range(cdiv(lanes, LANES)):
            mix_tile(j)

    copies = []
    for base, lanes in group_lanes(dim):
        group(base, lanes)
        here = slice(base, base + lanes)
        copies.append(
            pltpu.make_async_copy(held.at[:, here], out_ref.at[:, here], semaphores.at[len(copies)])
        )
        copies[-1].start()
    for copy in copies:
        copy.wait()


def mix(prepared, pieces, rows, width):
    features, inputs, gain, taps = prepared
    total, dim = inputs.shape
    tokens = rows * width
    pairs = spans(min(GROUP, dim))
    depth = max(last - first for _, first, last in pairs) * LANES
    whole = pl.BlockSpec(memory_space=pltpu.VMEM)
    return pl.pallas_call(
        functools.partial(mix_kernel, dim, rows, width, (total - tokens) // width),
        out_shape=jax.ShapeDtypeStruct((tokens, dim), jnp.bfloat16),
        in_specs=[whole] * (4 + len(pieces)),
        out_specs=pl.BlockSpec(memory_space=pl.ANY),
        scratch_shapes=[
            pltpu.VMEM((sum(piece.shape[0] for piece in pieces), LANES), jnp.bfloat16),
            pltpu.VMEM((len(pairs), depth, 2 * LANES), jnp.bfloat16),
            pltpu.VMEM((total, GROUP), jnp.float32),
            pltpu.VMEM((2, rows + 2, width, LANES), jnp.float32),
            pltpu.VMEM((2, 4, rows + 2, width // 16, 8, LANES), jnp.float32),
            pltpu.VMEM((2, rows, width, LANES), jnp.float32),
            pltpu.VMEM((tokens, dim), jnp.bfloat16),
            pltpu.SemaphoreType.DMA((len(group_lanes(dim)),)),
        ],
        compiler_params=pltpu.CompilerParams(vmem_limit_bytes=36 * 2**20),
        cost_estimate=pl.CostEstimate(
            flops=60 * tokens * dim, bytes_accessed=6 * tokens * dim, transcendentals=2 * tokens * dim
        ),
        name="mix",
    )(features, inputs, gain, taps, *pieces)


def edge_rows(queries, residual):
    devices, rows = lax.axis_size("space"), queries.shape[0]
    up = [(i, i + 1) for i in range(devices - 1)]
    down = [(j, i) for i, j in up]
    both = jnp.stack([queries, residual])
    if devices == 2:
        first = lax.axis_index("space") == 0
        return lax.ppermute(jnp.where(first, both[:, rows - 1 :], both[:, :1]), "space", up + down)
    before = lax.ppermute(both[:, rows - 1 :], "space", up)
    after = lax.ppermute(both[:, :1], "space", down)
    return jnp.concatenate([before, after], axis=1)


def small_kernel(body, name, outs, *arrays):
    return pl.pallas_call(
        body,
        out_shape=[pltpu.VMEM(shape, jnp.bfloat16) for shape in outs],
        in_specs=[pl.BlockSpec(memory_space=pltpu.VMEM)] * len(arrays),
        out_specs=[pl.BlockSpec(memory_space=pltpu.VMEM)] * len(outs),
        compiler_params=pltpu.CompilerParams(vmem_limit_bytes=4 * 2**20),
        name=name,
    )(*arrays)


def add(*values):
    total = values[0].astype(jnp.float32)
    for value in values[1:]:
        total = total + value.astype(jnp.float32)
    return total


def parity():
    return lax.rem(lax.axis_index("frame"), 2)


def split_sum_body(kept_ref, got_ref, mine_ref, theirs_ref):
    size = mine_ref.shape[0]
    for ref, side in ((theirs_ref, 1 - parity()), (mine_ref, parity())):
        rows = pl.ds(pl.multiple_of(side * size, 16), size)
        ref[...] = add(kept_ref[rows, :], got_ref[rows, :]).astype(jnp.bfloat16)


def sum_body(*refs):
    *terms, out_ref = refs
    out_ref[...] = add(*[term[...] for term in terms]).astype(jnp.bfloat16)


def pair_sums_body(own_ref, partner_ref, *refs):
    *earlier, mine_ref, theirs_ref = refs
    before = jnp.zeros(own_ref.shape, jnp.float32)
    for k, ref in enumerate(earlier):
        from_before = lax.rem(lax.axis_index("frame") // (2 << k), 2) == 1
        before = before + jnp.where(from_before, add(ref[...]), 0.0)
    own, partner = add(own_ref[...]), add(partner_ref[...])
    first = parity() == 0
    both = before + (own + partner)
    mine_ref[...] = jnp.where(first, before + own, both).astype(jnp.bfloat16)
    theirs_ref[...] = jnp.where(first, both, before + partner).astype(jnp.bfloat16)


def paired(devices, frames):
    return devices == 2 and frames >= 4 and frames & (frames - 1) == 0


def piece_places():
    core = lax.axis_index("space")
    return [2 * c + p for c in (core, 1 - core) for p in (parity(), 1 - parity())]


def edge_places(devices, rows):
    if devices == 2:
        return [jnp.where(lax.axis_index("space") == 0, rows + 1, 0)]
    return [0, rows + 1]


def running_states(keys, values, queries, residual, rows, beside):
    devices, frames = lax.axis_size("space"), lax.axis_size("frame")
    if not paired(devices, frames):
        (state,) = frame_states(keys, values, rows, 1)
        state = lax.psum(state.astype(jnp.float32), "space").astype(jnp.bfloat16)
        every = lax.all_gather(state, "frame").astype(jnp.float32)
        reached = (jnp.arange(frames) <= lax.axis_index("frame"))[:, None, None]
        total = jnp.sum(jnp.where(reached, every, 0.0), axis=0).astype(jnp.bfloat16)
        return [total], beside(edge_rows(queries, residual))
    swap = [(0, 1), (1, 0)]
    exchange = lambda array, stride: lax.ppermute(
        array, "frame", [(f, f ^ stride) for f in range(frames)]
    )
    kept, sent, edge = frame_states(keys, values, rows, 2, (queries, residual))
    got = lax.ppermute(sent, "space", swap)
    quarter = (rows // 4, LANES)
    own, sent = small_kernel(split_sum_body, "split_sum", [quarter] * 2, kept, got)
    edge, sent = lax.optimization_barrier((edge, sent))
    edge = lax.ppermute(edge, "space", swap)
    partner = exchange(sent, 1)
    (total,) = small_kernel(sum_body, "pair_sum", [quarter], own, partner)
    earlier = []
    stride = 2
    while stride < frames:
        if stride * 2 == frames:
            total, edge = lax.optimization_barrier((total, edge))
        earlier.append(exchange(total, stride))
        stride *= 2
        if stride < frames:
            (total,) = small_kernel(sum_body, "stride_sum", [quarter], total, earlier[-1])
    prepared = beside(edge)
    earlier[-1], *prepared = lax.optimization_barrier((earlier[-1], *prepared))
    mine, theirs = small_kernel(
        pair_sums_body, "pair_sums", [quarter] * 2, own, partner, *earlier
    )
    other = exchange(theirs, 1)
    pieces = [mine, other, lax.ppermute(mine, "space", swap), lax.ppermute(other, "space", swap)]
    return pieces, prepared


def on_device(queries, keys, values, residual, attn_gain, value_taps, gate_taps):
    frames, rows, width, dim = queries.shape
    tokens = frames * rows * width
    flat = lambda a: a.reshape(tokens, dim)
    state_rows = cdiv(cdiv(dim, LANES) * HEAD_DIM, 64) * 64
    pieces, prepared = running_states(
        flat(keys),
        flat(values),
        queries.reshape(rows, width, dim),
        residual.reshape(rows, width, dim),
        state_rows,
        lambda edge: prepare(
            flat(queries), flat(residual), edge, attn_gain[None], value_taps, gate_taps
        ),
    )
    out = mix(prepared, pieces, rows, width)
    return out.reshape(frames, rows, width, dim)


def solution(mesh):
    placed = P(("groups", "frame"), "space", None, None)
    return jax.shard_map(
        on_device,
        mesh=mesh,
        in_specs=(placed, placed, placed, placed, P(), P(), P()),
        out_specs=placed,
        check_vma=False,
    )
```

```python
import functools
import math

import jax
import jax.numpy as jnp
from jax import lax
from jax.experimental import pallas as pl
from jax.experimental.pallas import tpu as pltpu
from jax.sharding import PartitionSpec as P

HEAD_DIM = 112
LANES = 128
GROUP = math.lcm(HEAD_DIM, LANES)
TILES = GROUP // LANES


def cdiv(a, b):
    return -(-a // b)


def in_hbm(array):
    return pltpu.with_memory_space_constraint(array, pltpu.HBM)


def lane_iota(shape):
    return lax.broadcasted_iota(jnp.int32, shape, len(shape) - 1)


def tile_heads(j, lanes):
    lo, hi = j * LANES, min((j + 1) * LANES, lanes)
    heads = range(lo // HEAD_DIM, cdiv(hi, HEAD_DIM))
    return [(h, max(h * HEAD_DIM - lo, 0), min((h + 1) * HEAD_DIM - lo, LANES)) for h in heads]


def spans(lanes):
    count = cdiv(lanes, LANES)
    result = []
    for j in range(0, count, 2):
        tiles = list(range(j, min(j + 2, count)))
        first = tile_heads(tiles[0], lanes)[0][0] * HEAD_DIM // LANES
        last = cdiv((tile_heads(tiles[-1], lanes)[-1][0] + 1) * HEAD_DIM, LANES)
        result.append((tiles, first, last))
    return result


def by_group(dim, body):
    full, rest = divmod(dim, GROUP)
    if full:
        pl.when(pl.program_id(0) < full)(lambda: body(GROUP))
    if rest:
        pl.when(pl.program_id(0) >= full)(lambda: body(rest))


def state_kernel(dim, with_edge, keys_refs, values_refs, refs):
    step = pl.program_id(0)
    *refs, turned, whole, semaphores = refs
    if with_edge:
        *sources, edge_ref = refs[:2] + refs[-1:]
        parts = refs[2:-1]
        row = (sources[0].shape[0] - 1) * (1 - lax.axis_index("space"))
        copies = [
            pltpu.make_async_copy(source.at[row], edge_ref.at[k, 0], semaphores.at[k])
            for k, source in enumerate(sources)
        ]

        @pl.when(step == 0)
        def _():
            for copy in copies:
                copy.start()

    else:
        parts = refs

    def body(lanes):
        for k, keys_ref in enumerate(keys_refs):
            turned[k] = jnp.maximum(keys_ref[...], 0).T
        lane = lane_iota((HEAD_DIM, LANES))
        for tiles, _, _ in spans(lanes):
            begin = tile_heads(tiles[0], lanes)[0][0]
            end = tile_heads(tiles[-1], lanes)[-1][0] + 1
            product = sum(
                jnp.dot(
                    turned[k, begin * HEAD_DIM : end * HEAD_DIM, :],
                    values_ref[:, tiles[0] * LANES : (tiles[-1] + 1) * LANES],
                    preferred_element_type=jnp.float32,
                )
                for k, values_ref in enumerate(values_refs)
            )
            for side, j in enumerate(tiles):
                total = jnp.zeros((HEAD_DIM, LANES), jnp.float32)
                for h, lo, hi in tile_heads(j, lanes):
                    part = product[
                        (h - begin) * HEAD_DIM : (h - begin + 1) * HEAD_DIM,
                        side * LANES : (side + 1) * LANES,
                    ]
                    total = jnp.where((lane >= lo) & (lane < hi), part, total)
                row = pl.multiple_of((step * TILES + j) * HEAD_DIM, 16)
                whole[pl.ds(row, HEAD_DIM), :] = total.astype(jnp.bfloat16)

    by_group(dim, body)

    @pl.when(step == pl.num_programs(0) - 1)
    def _():
        used = cdiv(dim, LANES) * HEAD_DIM
        if used < whole.shape[0]:
            whole[used:, :] = jnp.zeros((whole.shape[0] - used, LANES), jnp.bfloat16)
        for k, part in enumerate(parts):
            size = part.shape[0]
            turn = lax.rem(lax.axis_index("space") + k, 2) if len(parts) == 2 else 0
            part[...] = whole[pl.ds(pl.multiple_of(turn * size, 16), size), :]
        if with_edge:
            for copy in copies:
                copy.wait()


def frame_states(keys, values, rows, parts, edged=()):
    tokens, dim = keys.shape
    part = (rows // parts, LANES)
    slabs = 2 if tokens % 32 == 0 else 1
    blocks = [
        pl.BlockSpec((tokens // slabs, GROUP), functools.partial(lambda k, g: (k, g), k))
        for k in range(slabs)
    ]

    def body(*refs):
        state_kernel(dim, bool(edged), refs[:slabs], refs[slabs : 2 * slabs], refs[2 * slabs :])

    return pl.pallas_call(
        body,
        out_shape=[pltpu.VMEM(part, jnp.bfloat16)] * parts
        + [pltpu.VMEM((len(edged), 1, *edged[0].shape[1:]), jnp.bfloat16) for _ in edged[:1]],
        grid=(cdiv(dim, GROUP),),
        in_specs=blocks + blocks + [pl.BlockSpec(memory_space=pl.ANY)] * len(edged),
        out_specs=[pl.BlockSpec(part, lambda g: (0, 0))] * parts
        + [pl.BlockSpec(memory_space=pl.ANY) for _ in edged[:1]],
        scratch_shapes=[
            pltpu.VMEM((slabs, GROUP, tokens // slabs), jnp.bfloat16),
            pltpu.VMEM((rows, LANES), jnp.bfloat16),
            pltpu.SemaphoreType.DMA((2,)),
        ],
        compiler_params=pltpu.CompilerParams(vmem_limit_bytes=60 * 2**20),
        cost_estimate=pl.CostEstimate(
            flops=2 * tokens * dim * HEAD_DIM, bytes_accessed=4 * tokens * dim, transcendentals=0
        ),
        name="frame_states",
    )(*[in_hbm(keys)] * slabs, *[in_hbm(values)] * slabs, *[in_hbm(array) for array in edged])


def group_lanes(dim):
    return [(first, min(GROUP, dim - first)) for first in range(0, dim, GROUP)]


def prepare_kernel(
    dim, queries_ref, residual_ref, edge_ref, gain_ref, vtaps_ref, gtaps_ref,
    features_ref, inputs_ref, scaled_ref, taps_ref, held, wide, semaphores,
):
    tokens = queries_ref.shape[0]
    copies = [
        pltpu.make_async_copy(source, held.at[k, :tokens], semaphores.at[k])
        for k, source in enumerate((queries_ref, residual_ref))
    ]
    for copy in copies:
        copy.start()
    edges, width = edge_ref.shape[1:3]
    for e in range(edges):
        here = slice(tokens + e * width, tokens + (e + 1) * width)
        held[0, here] = edge_ref[0, e]
        held[1, here] = edge_ref[1, e]
    scaled_ref[...] = gain_ref[...] * math.sqrt(HEAD_DIM)
    half = width // 2
    for j in range(cdiv(dim, LANES)):
        here = slice(j * LANES, min((j + 1) * LANES, dim))
        used = here.stop - here.start
        number = 0
        for ref, factor in ((vtaps_ref, 1.0), (gtaps_ref, 0.5)):
            for tap in (0, 3, 6):
                one, two, three = [ref[tap + i : tap + i + 1, here] * factor for i in range(3)]
                outer = 0.5 * (one + three)
                for row in (one, outer + 0.5 * two, outer - 0.5 * two, three):
                    taps_ref[j, number, :, :used] = jnp.broadcast_to(row, (8, used))
                    number += 1
    for k, copy in enumerate(copies):
        copy.wait()
        for j in range(cdiv(dim, LANES)):
            here = slice(j * LANES, min((j + 1) * LANES, dim))
            used = here.stop - here.start
            slot = j % 2
            if k == 0 and used < LANES:
                features_ref[:, here.stop :] = jnp.zeros(
                    (features_ref.shape[0], LANES - used), jnp.bfloat16
                )
            wide[slot, :, :used] = held[k, :, here].astype(jnp.float32)
            for row in range(wide.shape[1] // width):
                value = jnp.concatenate(
                    [
                        wide[slot, pl.ds(row * width + side, half, stride=2), :used]
                        for side in range(2)
                    ],
                    axis=0,
                )
                source = slice(row * width, (row + 1) * width)
                if k == 0:
                    features_ref[source, here] = jnp.maximum(value, 0.0).astype(jnp.bfloat16)
                else:
                    inputs_ref[source, here] = value


def prepare(queries, residual, edge, gain, value_taps, gate_taps):
    tokens, dim = queries.shape
    total = tokens + edge.shape[1] * edge.shape[2]
    whole = pl.BlockSpec(memory_space=pltpu.VMEM)
    return pl.pallas_call(
        functools.partial(prepare_kernel, dim),
        out_shape=[
            pltpu.VMEM((total, cdiv(dim, LANES) * LANES), jnp.bfloat16),
            pltpu.VMEM((total, dim), jnp.float32),
            pltpu.VMEM((1, dim), jnp.float32),
            pltpu.VMEM((cdiv(dim, LANES), 24, 8, LANES), jnp.float32),
        ],
        in_specs=[pl.BlockSpec(memory_space=pl.ANY)] * 2 + [whole] * 4,
        out_specs=[whole] * 4,
        scratch_shapes=[
            pltpu.VMEM((2, total, dim), jnp.bfloat16),
            pltpu.VMEM((2, total, LANES), jnp.float32),
            pltpu.SemaphoreType.DMA((2,)),
        ],
        compiler_params=pltpu.CompilerParams(vmem_limit_bytes=24 * 2**20),
        cost_estimate=pl.CostEstimate(
            flops=4 * total * dim, bytes_accessed=8 * total * dim, transcendentals=0
        ),
        name="prepare",
    )(in_hbm(queries), in_hbm(residual), edge, gain, value_taps, gate_taps)


def mix_kernel(
    dim, rows, width, edges,
    features_ref, inputs_ref, gain_ref, taps_ref, *refs,
):
    *pieces, out_ref, states, weights, numer, mixed_rows, windows, results, held, semaphores = refs
    places = edge_places(lax.axis_size("space"), rows) if edges else []
    spots = piece_places() if len(pieces) > 1 else [0]
    tokens = rows * width
    weights[...] = jnp.zeros_like(weights)
    for row in (0, rows + 1):
        windows[:, :, row] = jnp.zeros((2, 4, width // 16, 8, LANES), jnp.float32)
    for k, piece in enumerate(pieces):
        size = piece.shape[0]
        states[pl.ds(pl.multiple_of(spots[k] * size, 16), size), :] = piece[...]
    lane = lane_iota((HEAD_DIM, LANES))
    sublane = lax.broadcasted_iota(jnp.int32, (8, LANES), 0)

    half = width // 2
    even, odd = pl.ds(0, half, stride=2), pl.ds(1, half, stride=2)

    def store_windows(value, slot, used, row, place):
        left, right = value[:half], value[half:]
        if 0 < row <= rows:
            mixed_rows[slot, row, :, :used] = value
        sub = sublane[:, :used]
        before, after = pltpu.roll(right, 1, 0), pltpu.roll(left, half - 1, 0)
        before = jnp.concatenate([jnp.where(sub == 0, 0.0, before[:8]), before[8:]], axis=0)
        after = jnp.concatenate([after[: half - 8], jnp.where(sub == 7, 0.0, after[half - 8 :])], axis=0)
        for k, window in enumerate((before - right, left + right, right - left, left - after)):
            windows[slot, k, place, :, :, :used] = window.reshape(half // 8, 8, used)

    def group(base, lanes):
        pairs = spans(lanes)

        def numerators(number):
            tiles, first, last = pairs[number]
            for side, j in enumerate(tiles):
                row = (base // LANES + j) * HEAD_DIM
                state = states[row : row + HEAD_DIM, :].astype(jnp.float32)
                for h, lo, hi in tile_heads(j, lanes):
                    start = h * HEAD_DIM - first * LANES
                    block = jnp.where((lane >= lo) & (lane < hi), state, 0.0)
                    weights[
                        number, start : start + HEAD_DIM, side * LANES : (side + 1) * LANES
                    ] = block.astype(jnp.bfloat16)
            depth, wide = (last - first) * LANES, len(tiles) * LANES
            product = jnp.dot(
                features_ref[:, base + first * LANES : base + last * LANES],
                weights[number, :depth, :wide],
                preferred_element_type=jnp.float32,
            )
            here = slice(tiles[0] * LANES, tiles[0] * LANES + wide)
            numer[:, here] = product
            for side, j in enumerate(tiles):
                for row in range(rows + edges):
                    source = slice(row * width, (row + 1) * width)
                    square = product[source, side * LANES : (side + 1) * LANES]
                    parts.setdefault(source.start, []).append(tile_sums(j, square * square))

        parts = {}

        def tile_sums(j, square):
            position = lane_iota(square.shape)
            sums = {}
            for head, lo, hi in tile_heads(j, lanes):
                ends = (head + 1) * HEAD_DIM <= (j + 1) * LANES
                fill = HEAD_DIM * 1e-06 / (LANES - (hi - lo)) if ends else 0.0
                mine = position < hi if lo == 0 else position >= lo
                sums[head] = jnp.sum(jnp.where(mine, square, fill), axis=-1, keepdims=True)
            return sums

        def mix_tile(j):
            slot = j % 2
            used = min(LANES, lanes - j * LANES)
            near = slice(j * LANES, j * LANES + used)
            here = slice(base + j * LANES, base + j * LANES + used)
            heads = tile_heads(j, lanes)

            def mixed(source):
                sums = [
                    sum(tiles[head] for tiles in parts[source.start] if head in tiles)
                    for head, _, _ in heads
                ]
                scale = jnp.broadcast_to(sums[0], (width, used))
                if len(heads) > 1:
                    scale = jnp.where(lane_iota(scale.shape) < heads[0][2], scale, sums[1])
                normed = numer[source, near] * lax.rsqrt(scale)
                return inputs_ref[source, here] + normed * gain_ref[:, here]

            for row in range(rows):
                value = mixed(slice(row * width, (row + 1) * width))
                store_windows(value, slot, used, row + 1, row + 1)
            for e in range(edges):
                value = mixed(slice(tokens + e * width, tokens + (e + 1) * width))
                store_windows(value, slot, used, 0, places[e])
            for row in range(rows):
                lefts, rights = [], []
                for k in range(4):
                    products = [None, None]
                    for tap_row in range(3):
                        window = windows[slot, k, row + tap_row, :, :, :used]
                        for f in range(2):
                            tap = taps_ref[base // LANES + j, 12 * f + 4 * tap_row + k, :, :used]
                            term = tap * window
                            products[f] = term if tap_row == 0 else products[f] + term
                    if k == 0:
                        lefts = products
                    elif k == 1:
                        lefts = [one + two for one, two in zip(lefts, products)]
                        rights = products
                    elif k == 2:
                        lefts = [one + two for one, two in zip(lefts, products)]
                        rights = [one - two for one, two in zip(rights, products)]
                    else:
                        rights = [one - two for one, two in zip(rights, products)]
                for k, (side, (conv_v, half_g)) in enumerate(zip((even, odd), (lefts, rights))):
                    center = mixed_rows[slot, row + 1, k * half : (k + 1) * half, :used]
                    gated = conv_v * (half_g + half_g * jnp.tanh(half_g))
                    results[slot, row, side, :used] = center + gated.reshape(half, used)
                held[row * width : (row + 1) * width, here] = results[slot, row, :, :used].astype(
                    jnp.bfloat16
                )

        for number in range(len(pairs)):
            numerators(number)
        for j in range(cdiv(lanes, LANES)):
            mix_tile(j)

    copies = []
    for base, lanes in group_lanes(dim):
        group(base, lanes)
        here = slice(base, base + lanes)
        copies.append(
            pltpu.make_async_copy(held.at[:, here], out_ref.at[:, here], semaphores.at[len(copies)])
        )
        copies[-1].start()
    for copy in copies:
        copy.wait()


def mix(prepared, pieces, rows, width):
    features, inputs, gain, taps = prepared
    total, dim = inputs.shape
    tokens = rows * width
    pairs = spans(min(GROUP, dim))
    depth = max(last - first for _, first, last in pairs) * LANES
    whole = pl.BlockSpec(memory_space=pltpu.VMEM)
    return pl.pallas_call(
        functools.partial(mix_kernel, dim, rows, width, (total - tokens) // width),
        out_shape=jax.ShapeDtypeStruct((tokens, dim), jnp.bfloat16),
        in_specs=[whole] * (4 + len(pieces)),
        out_specs=pl.BlockSpec(memory_space=pl.ANY),
        scratch_shapes=[
            pltpu.VMEM((sum(piece.shape[0] for piece in pieces), LANES), jnp.bfloat16),
            pltpu.VMEM((len(pairs), depth, 2 * LANES), jnp.bfloat16),
            pltpu.VMEM((total, GROUP), jnp.float32),
            pltpu.VMEM((2, rows + 2, width, LANES), jnp.float32),
            pltpu.VMEM((2, 4, rows + 2, width // 16, 8, LANES), jnp.float32),
            pltpu.VMEM((2, rows, width, LANES), jnp.float32),
            pltpu.VMEM((tokens, dim), jnp.bfloat16),
            pltpu.SemaphoreType.DMA((len(group_lanes(dim)),)),
        ],
        compiler_params=pltpu.CompilerParams(vmem_limit_bytes=36 * 2**20),
        cost_estimate=pl.CostEstimate(
            flops=60 * tokens * dim, bytes_accessed=6 * tokens * dim, transcendentals=2 * tokens * dim
        ),
        name="mix",
    )(features, inputs, gain, taps, *pieces)


def edge_rows(queries, residual):
    devices, rows = lax.axis_size("space"), queries.shape[0]
    up = [(i, i + 1) for i in range(devices - 1)]
    down = [(j, i) for i, j in up]
    both = jnp.stack([queries, residual])
    if devices == 2:
        first = lax.axis_index("space") == 0
        return lax.ppermute(jnp.where(first, both[:, rows - 1 :], both[:, :1]), "space", up + down)
    before = lax.ppermute(both[:, rows - 1 :], "space", up)
    after = lax.ppermute(both[:, :1], "space", down)
    return jnp.concatenate([before, after], axis=1)


def small_kernel(body, name, outs, *arrays):
    return pl.pallas_call(
        body,
        out_shape=[pltpu.VMEM(shape, jnp.bfloat16) for shape in outs],
        in_specs=[pl.BlockSpec(memory_space=pltpu.VMEM)] * len(arrays),
        out_specs=[pl.BlockSpec(memory_space=pltpu.VMEM)] * len(outs),
        compiler_params=pltpu.CompilerParams(vmem_limit_bytes=4 * 2**20),
        name=name,
    )(*arrays)


def add(*values):
    total = values[0].astype(jnp.float32)
    for value in values[1:]:
        total = total + value.astype(jnp.float32)
    return total


def parity():
    return lax.rem(lax.axis_index("frame"), 2)


def split_sum_body(kept_ref, got_ref, mine_ref, theirs_ref):
    size = mine_ref.shape[0]
    for ref, side in ((theirs_ref, 1 - parity()), (mine_ref, parity())):
        rows = pl.ds(pl.multiple_of(side * size, 16), size)
        ref[...] = add(kept_ref[rows, :], got_ref[rows, :]).astype(jnp.bfloat16)


def sum_body(*refs):
    *terms, out_ref = refs
    out_ref[...] = add(*[term[...] for term in terms]).astype(jnp.bfloat16)


def pair_sums_body(own_ref, partner_ref, *refs):
    *earlier, mine_ref, theirs_ref = refs
    before = jnp.zeros(own_ref.shape, jnp.float32)
    for k, ref in enumerate(earlier):
        from_before = lax.rem(lax.axis_index("frame") // (2 << k), 2) == 1
        before = before + jnp.where(from_before, add(ref[...]), 0.0)
    own, partner = add(own_ref[...]), add(partner_ref[...])
    first = parity() == 0
    both = before + (own + partner)
    mine_ref[...] = jnp.where(first, before + own, both).astype(jnp.bfloat16)
    theirs_ref[...] = jnp.where(first, both, before + partner).astype(jnp.bfloat16)


def paired(devices, frames):
    return devices == 2 and frames >= 4 and frames & (frames - 1) == 0


def piece_places():
    core = lax.axis_index("space")
    return [2 * c + p for c in (core, 1 - core) for p in (parity(), 1 - parity())]


def edge_places(devices, rows):
    if devices == 2:
        return [jnp.where(lax.axis_index("space") == 0, rows + 1, 0)]
    return [0, rows + 1]


def running_states(keys, values, queries, residual, rows, beside):
    devices, frames = lax.axis_size("space"), lax.axis_size("frame")
    if not paired(devices, frames):
        (state,) = frame_states(keys, values, rows, 1)
        state = lax.psum(state.astype(jnp.float32), "space").astype(jnp.bfloat16)
        every = lax.all_gather(state, "frame").astype(jnp.float32)
        reached = (jnp.arange(frames) <= lax.axis_index("frame"))[:, None, None]
        total = jnp.sum(jnp.where(reached, every, 0.0), axis=0).astype(jnp.bfloat16)
        return [total], beside(edge_rows(queries, residual))
    swap = [(0, 1), (1, 0)]
    exchange = lambda array, stride: lax.ppermute(
        array, "frame", [(f, f ^ stride) for f in range(frames)]
    )
    kept, sent, edge = frame_states(keys, values, rows, 2, (queries, residual))
    got = lax.ppermute(sent, "space", swap)
    quarter = (rows // 4, LANES)
    own, sent = small_kernel(split_sum_body, "split_sum", [quarter] * 2, kept, got)
    edge, sent = lax.optimization_barrier((edge, sent))
    edge = lax.ppermute(edge, "space", swap)
    partner = exchange(sent, 1)
    (total,) = small_kernel(sum_body, "pair_sum", [quarter], own, partner)
    earlier = []
    stride = 2
    while stride < frames:
        if stride * 2 == frames:
            total, edge = lax.optimization_barrier((total, edge))
        earlier.append(exchange(total, stride))
        stride *= 2
        if stride < frames:
            (total,) = small_kernel(sum_body, "stride_sum", [quarter], total, earlier[-1])
    prepared = beside(edge)
    earlier[-1], *prepared = lax.optimization_barrier((earlier[-1], *prepared))
    mine, theirs = small_kernel(
        pair_sums_body, "pair_sums", [quarter] * 2, own, partner, *earlier
    )
    other = exchange(theirs, 1)
    pieces = [mine, other, lax.ppermute(mine, "space", swap), lax.ppermute(other, "space", swap)]
    return pieces, prepared


def on_device(queries, keys, values, residual, attn_gain, value_taps, gate_taps):
    frames, rows, width, dim = queries.shape
    tokens = frames * rows * width
    flat = lambda a: a.reshape(tokens, dim)
    state_rows = cdiv(cdiv(dim, LANES) * HEAD_DIM, 64) * 64
    pieces, prepared = running_states(
        flat(keys),
        flat(values),
        queries.reshape(rows, width, dim),
        residual.reshape(rows, width, dim),
        state_rows,
        lambda edge: prepare(
            flat(queries), flat(residual), edge, attn_gain[None], value_taps, gate_taps
        ),
    )
    out = mix(prepared, pieces, rows, width)
    return out.reshape(frames, rows, width, dim)


def solution(mesh):
    placed = P(("groups", "frame"), "space", None, None)
    return jax.shard_map(
        on_device,
        mesh=mesh,
        in_specs=(placed, placed, placed, placed, P(), P(), P()),
        out_specs=placed,
        check_vma=False,
    )
```

```python
import functools
import math

import jax
import jax.numpy as jnp
from jax import lax
from jax.experimental import pallas as pl
from jax.experimental.pallas import tpu as pltpu
from jax.sharding import PartitionSpec as P

HEAD_DIM = 112
LANES = 128
GROUP = math.lcm(HEAD_DIM, LANES)
TILES = GROUP // LANES


def cdiv(a, b):
    return -(-a // b)


def in_hbm(array):
    return pltpu.with_memory_space_constraint(array, pltpu.HBM)


def lane_iota(shape):
    return lax.broadcasted_iota(jnp.int32, shape, len(shape) - 1)


def tile_heads(j, lanes):
    lo, hi = j * LANES, min((j + 1) * LANES, lanes)
    heads = range(lo // HEAD_DIM, cdiv(hi, HEAD_DIM))
    return [(h, max(h * HEAD_DIM - lo, 0), min((h + 1) * HEAD_DIM - lo, LANES)) for h in heads]


def spans(lanes):
    count = cdiv(lanes, LANES)
    result = []
    for j in range(0, count, 2):
        tiles = list(range(j, min(j + 2, count)))
        first = tile_heads(tiles[0], lanes)[0][0] * HEAD_DIM // LANES
        last = cdiv((tile_heads(tiles[-1], lanes)[-1][0] + 1) * HEAD_DIM, LANES)
        result.append((tiles, first, last))
    return result


def state_kernel(dim, parts, keys_ref, values_ref, *refs):
    *refs, keys, values, turned, whole, semaphores = refs
    sources, part_refs, edge_refs = refs[: -parts - 1], refs[-parts - 1 : -1], refs[-1:]
    if not sources:
        part_refs, edge_refs = refs, ()
    order = sorted(group_lanes(dim), key=lambda item: item[1])
    copies = []
    for k, (base, lanes) in enumerate(order):
        here = slice(base, base + lanes)
        copies += [
            pltpu.make_async_copy(ref.at[:, here], held.at[:, here], semaphores.at[2 * k + i])
            for i, (ref, held) in enumerate(((keys_ref, keys), (values_ref, values)))
        ]
    for k, source in enumerate(sources):
        row = (source.shape[0] - 1) * (1 - lax.axis_index("space"))
        copies.append(
            pltpu.make_async_copy(
                source.at[row], edge_refs[0].at[k, 0], semaphores.at[2 * len(order) + k]
            )
        )
    for copy in copies:
        copy.start()
    used = cdiv(dim, LANES) * HEAD_DIM
    if used < whole.shape[0]:
        whole[used:, :] = jnp.zeros((whole.shape[0] - used, LANES), jnp.bfloat16)
    lane = lane_iota((HEAD_DIM, LANES))
    for k, (base, lanes) in enumerate(order):
        for copy in copies[2 * k : 2 * k + 2]:
            copy.wait()
        turn = turned.at[k % 2]
        turn[:lanes, :] = jnp.maximum(keys[:, base : base + lanes], 0).T
        for tiles, _, _ in spans(lanes):
            begin = tile_heads(tiles[0], lanes)[0][0]
            end = tile_heads(tiles[-1], lanes)[-1][0] + 1
            first, last = tiles[0] * LANES, min((tiles[-1] + 1) * LANES, lanes)
            product = jnp.dot(
                turn[begin * HEAD_DIM : end * HEAD_DIM, :],
                values[:, base + first : base + last],
                preferred_element_type=jnp.float32,
            )
            for j in tiles:
                wide = min(LANES, lanes - j * LANES)
                blocks = [
                    product[
                        (h - begin) * HEAD_DIM : (h - begin + 1) * HEAD_DIM,
                        j * LANES - first : j * LANES - first + wide,
                    ]
                    for h, _, _ in tile_heads(j, lanes)
                ]
                total = blocks[0]
                if len(blocks) > 1:
                    total = jnp.where(lane < tile_heads(j, lanes)[0][2], blocks[0], blocks[1])
                if wide < LANES:
                    total = jnp.concatenate(
                        [total, jnp.zeros((HEAD_DIM, LANES - wide), jnp.float32)], axis=1
                    )
                row = (base // LANES + j) * HEAD_DIM
                whole[row : row + HEAD_DIM, :] = total.astype(jnp.bfloat16)
    for k, part in enumerate(part_refs):
        size = part.shape[0]
        place = lax.rem(lax.axis_index("space") + k, 2) if parts == 2 else 0
        part[...] = whole[pl.ds(pl.multiple_of(place * size, 16), size), :]
    for copy in copies[2 * len(order) :]:
        copy.wait()


def frame_states(keys, values, rows, parts, edged=()):
    tokens, dim = keys.shape
    part = (rows // parts, LANES)
    outside = pl.BlockSpec(memory_space=pl.ANY)
    return pl.pallas_call(
        functools.partial(state_kernel, dim, parts),
        out_shape=[pltpu.VMEM(part, jnp.bfloat16)] * parts
        + [pltpu.VMEM((len(edged), 1, *edged[0].shape[1:]), jnp.bfloat16) for _ in edged[:1]],
        in_specs=[outside] * (2 + len(edged)),
        out_specs=[pl.BlockSpec(memory_space=pltpu.VMEM)] * parts + [outside for _ in edged[:1]],
        scratch_shapes=[
            pltpu.VMEM((tokens, dim), jnp.bfloat16),
            pltpu.VMEM((tokens, dim), jnp.bfloat16),
            pltpu.VMEM((2, GROUP, tokens), jnp.bfloat16),
            pltpu.VMEM((rows, LANES), jnp.bfloat16),
            pltpu.SemaphoreType.DMA((2 * len(group_lanes(dim)) + len(edged),)),
        ],
        compiler_params=pltpu.CompilerParams(vmem_limit_bytes=32 * 2**20),
        cost_estimate=pl.CostEstimate(
            flops=2 * tokens * dim * HEAD_DIM, bytes_accessed=4 * tokens * dim, transcendentals=0
        ),
        name="frame_states",
    )(in_hbm(keys), in_hbm(values), *[in_hbm(array) for array in edged])


def group_lanes(dim):
    return [(first, min(GROUP, dim - first)) for first in range(0, dim, GROUP)]


def prepare_kernel(
    dim, queries_ref, residual_ref, edge_ref, gain_ref, vtaps_ref, gtaps_ref,
    features_ref, inputs_ref, scaled_ref, taps_ref, held, wide, semaphores,
):
    tokens = queries_ref.shape[0]
    copies = [
        pltpu.make_async_copy(source, held.at[k, :tokens], semaphores.at[k])
        for k, source in enumerate((queries_ref, residual_ref))
    ]
    for copy in copies:
        copy.start()
    edges, width = edge_ref.shape[1:3]
    for e in range(edges):
        here = slice(tokens + e * width, tokens + (e + 1) * width)
        held[0, here] = edge_ref[0, e]
        held[1, here] = edge_ref[1, e]
    scaled_ref[...] = gain_ref[...] * math.sqrt(HEAD_DIM)
    half = width // 2
    for j in range(cdiv(dim, LANES)):
        here = slice(j * LANES, min((j + 1) * LANES, dim))
        used = here.stop - here.start
        number = 0
        for ref, factor in ((vtaps_ref, 1.0), (gtaps_ref, 0.5)):
            for tap in (0, 3, 6):
                one, two, three = [ref[tap + i : tap + i + 1, here] * factor for i in range(3)]
                outer = 0.5 * (one + three)
                for row in (one, outer + 0.5 * two, outer - 0.5 * two, three):
                    taps_ref[j, number, :, :used] = jnp.broadcast_to(row, (8, used))
                    number += 1
    for k, copy in enumerate(copies):
        copy.wait()
        for j in range(cdiv(dim, LANES)):
            here = slice(j * LANES, min((j + 1) * LANES, dim))
            used = here.stop - here.start
            slot = j % 2
            if k == 0 and used < LANES:
                features_ref[:, here.stop :] = jnp.zeros(
                    (features_ref.shape[0], LANES - used), jnp.bfloat16
                )
            wide[slot, :, :used] = held[k, :, here].astype(jnp.float32)
            for row in range(wide.shape[1] // width):
                value = jnp.concatenate(
                    [
                        wide[slot, pl.ds(row * width + side, half, stride=2), :used]
                        for side in range(2)
                    ],
                    axis=0,
                )
                source = slice(row * width, (row + 1) * width)
                if k == 0:
                    features_ref[source, here] = jnp.maximum(value, 0.0).astype(jnp.bfloat16)
                else:
                    inputs_ref[source, here] = value


def prepare(queries, residual, edge, gain, value_taps, gate_taps):
    tokens, dim = queries.shape
    total = tokens + edge.shape[1] * edge.shape[2]
    whole = pl.BlockSpec(memory_space=pltpu.VMEM)
    return pl.pallas_call(
        functools.partial(prepare_kernel, dim),
        out_shape=[
            pltpu.VMEM((total, cdiv(dim, LANES) * LANES), jnp.bfloat16),
            pltpu.VMEM((total, dim), jnp.float32),
            pltpu.VMEM((1, dim), jnp.float32),
            pltpu.VMEM((cdiv(dim, LANES), 24, 8, LANES), jnp.float32),
        ],
        in_specs=[pl.BlockSpec(memory_space=pl.ANY)] * 2 + [whole] * 4,
        out_specs=[whole] * 4,
        scratch_shapes=[
            pltpu.VMEM((2, total, dim), jnp.bfloat16),
            pltpu.VMEM((2, total, LANES), jnp.float32),
            pltpu.SemaphoreType.DMA((2,)),
        ],
        compiler_params=pltpu.CompilerParams(vmem_limit_bytes=24 * 2**20),
        cost_estimate=pl.CostEstimate(
            flops=4 * total * dim, bytes_accessed=8 * total * dim, transcendentals=0
        ),
        name="prepare",
    )(in_hbm(queries), in_hbm(residual), edge, gain, value_taps, gate_taps)


def mix_kernel(
    dim, rows, width, edges,
    features_ref, inputs_ref, gain_ref, taps_ref, *refs,
):
    *pieces, out_ref, states, weights, numer, mixed_rows, windows, results, held, semaphores = refs
    places = edge_places(lax.axis_size("space"), rows) if edges else []
    spots = piece_places() if len(pieces) > 1 else [0]
    tokens = rows * width
    weights[...] = jnp.zeros_like(weights)
    for row in (0, rows + 1):
        windows[:, :, row] = jnp.zeros((2, 4, width // 16, 8, LANES), jnp.float32)
    for k, piece in enumerate(pieces):
        size = piece.shape[0]
        states[pl.ds(pl.multiple_of(spots[k] * size, 16), size), :] = piece[...]
    lane = lane_iota((HEAD_DIM, LANES))
    sublane = lax.broadcasted_iota(jnp.int32, (8, LANES), 0)

    half = width // 2
    even, odd = pl.ds(0, half, stride=2), pl.ds(1, half, stride=2)

    def store_windows(value, slot, used, row, place):
        left, right = value[:half], value[half:]
        if 0 < row <= rows:
            mixed_rows[slot, row, :, :used] = value
        sub = sublane[:, :used]
        before, after = pltpu.roll(right, 1, 0), pltpu.roll(left, half - 1, 0)
        before = jnp.concatenate([jnp.where(sub == 0, 0.0, before[:8]), before[8:]], axis=0)
        after = jnp.concatenate([after[: half - 8], jnp.where(sub == 7, 0.0, after[half - 8 :])], axis=0)
        for k, window in enumerate((before - right, left + right, right - left, left - after)):
            windows[slot, k, place, :, :, :used] = window.reshape(half // 8, 8, used)

    def group(base, lanes):
        pairs = spans(lanes)

        def numerators(number):
            tiles, first, last = pairs[number]
            for side, j in enumerate(tiles):
                row = (base // LANES + j) * HEAD_DIM
                state = states[row : row + HEAD_DIM, :].astype(jnp.float32)
                for h, lo, hi in tile_heads(j, lanes):
                    start = h * HEAD_DIM - first * LANES
                    block = jnp.where((lane >= lo) & (lane < hi), state, 0.0)
                    weights[
                        number, start : start + HEAD_DIM, side * LANES : (side + 1) * LANES
                    ] = block.astype(jnp.bfloat16)
            depth, wide = (last - first) * LANES, len(tiles) * LANES
            product = jnp.dot(
                features_ref[:, base + first * LANES : base + last * LANES],
                weights[number, :depth, :wide],
                preferred_element_type=jnp.float32,
            )
            here = slice(tiles[0] * LANES, tiles[0] * LANES + wide)
            numer[:, here] = product
            for side, j in enumerate(tiles):
                for row in range(rows + edges):
                    source = slice(row * width, (row + 1) * width)
                    square = product[source, side * LANES : (side + 1) * LANES]
                    parts.setdefault(source.start, []).append(tile_sums(j, square * square))

        parts = {}

        def tile_sums(j, square):
            position = lane_iota(square.shape)
            sums = {}
            for head, lo, hi in tile_heads(j, lanes):
                ends = (head + 1) * HEAD_DIM <= (j + 1) * LANES
                fill = HEAD_DIM * 1e-06 / (LANES - (hi - lo)) if ends else 0.0
                mine = position < hi if lo == 0 else position >= lo
                sums[head] = jnp.sum(jnp.where(mine, square, fill), axis=-1, keepdims=True)
            return sums

        def mix_tile(j):
            slot = j % 2
            used = min(LANES, lanes - j * LANES)
            near = slice(j * LANES, j * LANES + used)
            here = slice(base + j * LANES, base + j * LANES + used)
            heads = tile_heads(j, lanes)

            def mixed(source):
                sums = [
                    sum(tiles[head] for tiles in parts[source.start] if head in tiles)
                    for head, _, _ in heads
                ]
                scale = jnp.broadcast_to(sums[0], (width, used))
                if len(heads) > 1:
                    scale = jnp.where(lane_iota(scale.shape) < heads[0][2], scale, sums[1])
                normed = numer[source, near] * lax.rsqrt(scale)
                return inputs_ref[source, here] + normed * gain_ref[:, here]

            for row in range(rows):
                value = mixed(slice(row * width, (row + 1) * width))
                store_windows(value, slot, used, row + 1, row + 1)
            for e in range(edges):
                value = mixed(slice(tokens + e * width, tokens + (e + 1) * width))
                store_windows(value, slot, used, 0, places[e])
            for row in range(rows):
                lefts, rights = [], []
                for k in range(4):
                    products = [None, None]
                    for tap_row in range(3):
                        window = windows[slot, k, row + tap_row, :, :, :used]
                        for f in range(2):
                            tap = taps_ref[base // LANES + j, 12 * f + 4 * tap_row + k, :, :used]
                            term = tap * window
                            products[f] = term if tap_row == 0 else products[f] + term
                    if k == 0:
                        lefts = products
                    elif k == 1:
                        lefts = [one + two for one, two in zip(lefts, products)]
                        rights = products
                    elif k == 2:
                        lefts = [one + two for one, two in zip(lefts, products)]
                        rights = [one - two for one, two in zip(rights, products)]
                    else:
                        rights = [one - two for one, two in zip(rights, products)]
                for k, (side, (conv_v, half_g)) in enumerate(zip((even, odd), (lefts, rights))):
                    center = mixed_rows[slot, row + 1, k * half : (k + 1) * half, :used]
                    gated = conv_v * (half_g + half_g * jnp.tanh(half_g))
                    results[slot, row, side, :used] = center + gated.reshape(half, used)
                held[row * width : (row + 1) * width, here] = results[slot, row, :, :used].astype(
                    jnp.bfloat16
                )

        for number in range(len(pairs)):
            numerators(number)
        for j in range(cdiv(lanes, LANES)):
            mix_tile(j)

    copies = []
    for base, lanes in group_lanes(dim):
        group(base, lanes)
        here = slice(base, base + lanes)
        copies.append(
            pltpu.make_async_copy(held.at[:, here], out_ref.at[:, here], semaphores.at[len(copies)])
        )
        copies[-1].start()
    for copy in copies:
        copy.wait()


def mix(prepared, pieces, rows, width):
    features, inputs, gain, taps = prepared
    total, dim = inputs.shape
    tokens = rows * width
    pairs = spans(min(GROUP, dim))
    depth = max(last - first for _, first, last in pairs) * LANES
    whole = pl.BlockSpec(memory_space=pltpu.VMEM)
    return pl.pallas_call(
        functools.partial(mix_kernel, dim, rows, width, (total - tokens) // width),
        out_shape=jax.ShapeDtypeStruct((tokens, dim), jnp.bfloat16),
        in_specs=[whole] * (4 + len(pieces)),
        out_specs=pl.BlockSpec(memory_space=pl.ANY),
        scratch_shapes=[
            pltpu.VMEM((sum(piece.shape[0] for piece in pieces), LANES), jnp.bfloat16),
            pltpu.VMEM((len(pairs), depth, 2 * LANES), jnp.bfloat16),
            pltpu.VMEM((total, GROUP), jnp.float32),
            pltpu.VMEM((2, rows + 2, width, LANES), jnp.float32),
            pltpu.VMEM((2, 4, rows + 2, width // 16, 8, LANES), jnp.float32),
            pltpu.VMEM((2, rows, width, LANES), jnp.float32),
            pltpu.VMEM((tokens, dim), jnp.bfloat16),
            pltpu.SemaphoreType.DMA((len(group_lanes(dim)),)),
        ],
        compiler_params=pltpu.CompilerParams(vmem_limit_bytes=36 * 2**20),
        cost_estimate=pl.CostEstimate(
            flops=60 * tokens * dim, bytes_accessed=6 * tokens * dim, transcendentals=2 * tokens * dim
        ),
        name="mix",
    )(features, inputs, gain, taps, *pieces)


def edge_rows(queries, residual):
    devices, rows = lax.axis_size("space"), queries.shape[0]
    up = [(i, i + 1) for i in range(devices - 1)]
    down = [(j, i) for i, j in up]
    both = jnp.stack([queries, residual])
    if devices == 2:
        first = lax.axis_index("space") == 0
        return lax.ppermute(jnp.where(first, both[:, rows - 1 :], both[:, :1]), "space", up + down)
    before = lax.ppermute(both[:, rows - 1 :], "space", up)
    after = lax.ppermute(both[:, :1], "space", down)
    return jnp.concatenate([before, after], axis=1)


def small_kernel(body, name, outs, *arrays):
    return pl.pallas_call(
        body,
        out_shape=[pltpu.VMEM(shape, jnp.bfloat16) for shape in outs],
        in_specs=[pl.BlockSpec(memory_space=pltpu.VMEM)] * len(arrays),
        out_specs=[pl.BlockSpec(memory_space=pltpu.VMEM)] * len(outs),
        compiler_params=pltpu.CompilerParams(vmem_limit_bytes=4 * 2**20),
        name=name,
    )(*arrays)


def add(*values):
    total = values[0].astype(jnp.float32)
    for value in values[1:]:
        total = total + value.astype(jnp.float32)
    return total


def parity():
    return lax.rem(lax.axis_index("frame"), 2)


def split_sum_body(kept_ref, got_ref, mine_ref, theirs_ref):
    size = mine_ref.shape[0]
    for ref, side in ((theirs_ref, 1 - parity()), (mine_ref, parity())):
        rows = pl.ds(pl.multiple_of(side * size, 16), size)
        ref[...] = add(kept_ref[rows, :], got_ref[rows, :]).astype(jnp.bfloat16)


def sum_body(*refs):
    *terms, out_ref = refs
    out_ref[...] = add(*[term[...] for term in terms]).astype(jnp.bfloat16)


def pair_sums_body(own_ref, partner_ref, *refs):
    *earlier, mine_ref, theirs_ref = refs
    before = jnp.zeros(own_ref.shape, jnp.float32)
    for k, ref in enumerate(earlier):
        from_before = lax.rem(lax.axis_index("frame") // (2 << k), 2) == 1
        before = before + jnp.where(from_before, add(ref[...]), 0.0)
    own, partner = add(own_ref[...]), add(partner_ref[...])
    first = parity() == 0
    both = before + (own + partner)
    mine_ref[...] = jnp.where(first, before + own, both).astype(jnp.bfloat16)
    theirs_ref[...] = jnp.where(first, both, before + partner).astype(jnp.bfloat16)


def paired(devices, frames):
    return devices == 2 and frames >= 4 and frames & (frames - 1) == 0


def piece_places():
    core = lax.axis_index("space")
    return [2 * c + p for c in (core, 1 - core) for p in (parity(), 1 - parity())]


def edge_places(devices, rows):
    if devices == 2:
        return [jnp.where(lax.axis_index("space") == 0, rows + 1, 0)]
    return [0, rows + 1]


def running_states(keys, values, queries, residual, rows, beside):
    devices, frames = lax.axis_size("space"), lax.axis_size("frame")
    if not paired(devices, frames):
        (state,) = frame_states(keys, values, rows, 1)
        state = lax.psum(state.astype(jnp.float32), "space").astype(jnp.bfloat16)
        every = lax.all_gather(state, "frame").astype(jnp.float32)
        reached = (jnp.arange(frames) <= lax.axis_index("frame"))[:, None, None]
        total = jnp.sum(jnp.where(reached, every, 0.0), axis=0).astype(jnp.bfloat16)
        return [total], beside(edge_rows(queries, residual))
    swap = [(0, 1), (1, 0)]
    exchange = lambda array, stride: lax.ppermute(
        array, "frame", [(f, f ^ stride) for f in range(frames)]
    )
    kept, sent, edge = frame_states(keys, values, rows, 2, (queries, residual))
    got = lax.ppermute(sent, "space", swap)
    quarter = (rows // 4, LANES)
    own, sent = small_kernel(split_sum_body, "split_sum", [quarter] * 2, kept, got)
    edge, sent = lax.optimization_barrier((edge, sent))
    edge = lax.ppermute(edge, "space", swap)
    partner = exchange(sent, 1)
    (total,) = small_kernel(sum_body, "pair_sum", [quarter], own, partner)
    earlier = []
    stride = 2
    while stride < frames:
        if stride * 2 == frames:
            total, edge = lax.optimization_barrier((total, edge))
        earlier.append(exchange(total, stride))
        stride *= 2
        if stride < frames:
            (total,) = small_kernel(sum_body, "stride_sum", [quarter], total, earlier[-1])
    prepared = beside(edge)
    earlier[-1], *prepared = lax.optimization_barrier((earlier[-1], *prepared))
    mine, theirs = small_kernel(
        pair_sums_body, "pair_sums", [quarter] * 2, own, partner, *earlier
    )
    other = exchange(theirs, 1)
    pieces = [mine, other, lax.ppermute(mine, "space", swap), lax.ppermute(other, "space", swap)]
    return pieces, prepared


def on_device(queries, keys, values, residual, attn_gain, value_taps, gate_taps):
    frames, rows, width, dim = queries.shape
    tokens = frames * rows * width
    flat = lambda a: a.reshape(tokens, dim)
    state_rows = cdiv(cdiv(dim, LANES) * HEAD_DIM, 64) * 64
    pieces, prepared = running_states(
        flat(keys),
        flat(values),
        queries.reshape(rows, width, dim),
        residual.reshape(rows, width, dim),
        state_rows,
        lambda edge: prepare(
            flat(queries), flat(residual), edge, attn_gain[None], value_taps, gate_taps
        ),
    )
    out = mix(prepared, pieces, rows, width)
    return out.reshape(frames, rows, width, dim)


def solution(mesh):
    placed = P(("groups", "frame"), "space", None, None)
    return jax.shard_map(
        on_device,
        mesh=mesh,
        in_specs=(placed, placed, placed, placed, P(), P(), P()),
        out_specs=placed,
        check_vma=False,
    )
```

```python
import functools
import math

import jax
import jax.numpy as jnp
from jax import lax
from jax.experimental import pallas as pl
from jax.experimental.pallas import tpu as pltpu
from jax.sharding import PartitionSpec as P

HEAD_DIM = 112
LANES = 128
GROUP = math.lcm(HEAD_DIM, LANES)
TILES = GROUP // LANES


def cdiv(a, b):
    return -(-a // b)


def in_hbm(array):
    return pltpu.with_memory_space_constraint(array, pltpu.HBM)


def lane_iota(shape):
    return lax.broadcasted_iota(jnp.int32, shape, len(shape) - 1)


def tile_heads(j, lanes):
    lo, hi = j * LANES, min((j + 1) * LANES, lanes)
    heads = range(lo // HEAD_DIM, cdiv(hi, HEAD_DIM))
    return [(h, max(h * HEAD_DIM - lo, 0), min((h + 1) * HEAD_DIM - lo, LANES)) for h in heads]


def spans(lanes):
    count = cdiv(lanes, LANES)
    result = []
    for j in range(0, count, 2):
        tiles = list(range(j, min(j + 2, count)))
        first = tile_heads(tiles[0], lanes)[0][0] * HEAD_DIM // LANES
        last = cdiv((tile_heads(tiles[-1], lanes)[-1][0] + 1) * HEAD_DIM, LANES)
        result.append((tiles, first, last))
    return result


def state_kernel(dim, parts, keys_ref, values_ref, *refs):
    *refs, keys, values, turned, whole, semaphores = refs
    sources, part_refs, edge_refs = refs[: -parts - 1], refs[-parts - 1 : -1], refs[-1:]
    if not sources:
        part_refs, edge_refs = refs, ()
    order = sorted(group_lanes(dim), key=lambda item: item[1])
    copies = []
    for k, (base, lanes) in enumerate(order):
        here = slice(base, base + lanes)
        copies += [
            pltpu.make_async_copy(ref.at[:, here], held.at[:, here], semaphores.at[2 * k + i])
            for i, (ref, held) in enumerate(((keys_ref, keys), (values_ref, values)))
        ]
    for k, source in enumerate(sources):
        row = (source.shape[0] - 1) * (1 - lax.axis_index("space"))
        copies.append(
            pltpu.make_async_copy(
                source.at[row], edge_refs[0].at[k, 0], semaphores.at[2 * len(order) + k]
            )
        )
    for copy in copies:
        copy.start()
    used = cdiv(dim, LANES) * HEAD_DIM
    if used < whole.shape[0]:
        whole[used:, :] = jnp.zeros((whole.shape[0] - used, LANES), jnp.bfloat16)
    lane = lane_iota((HEAD_DIM, LANES))
    for k, (base, lanes) in enumerate(order):
        for copy in copies[2 * k : 2 * k + 2]:
            copy.wait()
        turn = turned.at[k % 2]
        turn[:lanes, :] = jnp.maximum(keys[:, base : base + lanes], 0).T
        for tiles, _, _ in spans(lanes):
            begin = tile_heads(tiles[0], lanes)[0][0]
            end = tile_heads(tiles[-1], lanes)[-1][0] + 1
            first, last = tiles[0] * LANES, min((tiles[-1] + 1) * LANES, lanes)
            product = jnp.dot(
                turn[begin * HEAD_DIM : end * HEAD_DIM, :],
                values[:, base + first : base + last],
                preferred_element_type=jnp.float32,
            )
            for j in tiles:
                wide = min(LANES, lanes - j * LANES)
                blocks = [
                    product[
                        (h - begin) * HEAD_DIM : (h - begin + 1) * HEAD_DIM,
                        j * LANES - first : j * LANES - first + wide,
                    ]
                    for h, _, _ in tile_heads(j, lanes)
                ]
                total = blocks[0]
                if len(blocks) > 1:
                    total = jnp.where(lane < tile_heads(j, lanes)[0][2], blocks[0], blocks[1])
                if wide < LANES:
                    total = jnp.concatenate(
                        [total, jnp.zeros((HEAD_DIM, LANES - wide), jnp.float32)], axis=1
                    )
                row = (base // LANES + j) * HEAD_DIM
                whole[row : row + HEAD_DIM, :] = total.astype(jnp.bfloat16)
    for k, part in enumerate(part_refs):
        size = part.shape[0]
        place = lax.rem(lax.axis_index("space") + k, 2) if parts == 2 else 0
        part[...] = whole[pl.ds(pl.multiple_of(place * size, 16), size), :]
    for copy in copies[2 * len(order) :]:
        copy.wait()


def frame_states(keys, values, rows, parts, edged=()):
    tokens, dim = keys.shape
    part = (rows // parts, LANES)
    outside = pl.BlockSpec(memory_space=pl.ANY)
    return pl.pallas_call(
        functools.partial(state_kernel, dim, parts),
        out_shape=[pltpu.VMEM(part, jnp.bfloat16)] * parts
        + [pltpu.VMEM((len(edged), 1, *edged[0].shape[1:]), jnp.bfloat16) for _ in edged[:1]],
        in_specs=[outside] * (2 + len(edged)),
        out_specs=[pl.BlockSpec(memory_space=pltpu.VMEM)] * parts + [outside for _ in edged[:1]],
        scratch_shapes=[
            pltpu.VMEM((tokens, dim), jnp.bfloat16),
            pltpu.VMEM((tokens, dim), jnp.bfloat16),
            pltpu.VMEM((2, GROUP, tokens), jnp.bfloat16),
            pltpu.VMEM((rows, LANES), jnp.bfloat16),
            pltpu.SemaphoreType.DMA((2 * len(group_lanes(dim)) + len(edged),)),
        ],
        compiler_params=pltpu.CompilerParams(vmem_limit_bytes=32 * 2**20),
        cost_estimate=pl.CostEstimate(
            flops=2 * tokens * dim * HEAD_DIM, bytes_accessed=4 * tokens * dim, transcendentals=0
        ),
        name="frame_states",
    )(in_hbm(keys), in_hbm(values), *[in_hbm(array) for array in edged])


def group_lanes(dim):
    return [(first, min(GROUP, dim - first)) for first in range(0, dim, GROUP)]


def prepare_kernel(
    dim, queries_ref, residual_ref, edge_ref, gain_ref, vtaps_ref, gtaps_ref,
    features_ref, inputs_ref, scaled_ref, taps_ref, held, wide, semaphores,
):
    tokens = queries_ref.shape[0]
    copies = [
        pltpu.make_async_copy(source, held.at[k, :tokens], semaphores.at[k])
        for k, source in enumerate((queries_ref, residual_ref))
    ]
    for copy in copies:
        copy.start()
    edges, width = edge_ref.shape[1:3]
    for e in range(edges):
        here = slice(tokens + e * width, tokens + (e + 1) * width)
        held[0, here] = edge_ref[0, e]
        held[1, here] = edge_ref[1, e]
    scaled_ref[...] = gain_ref[...] * math.sqrt(HEAD_DIM)
    half = width // 2
    for j in range(cdiv(dim, LANES)):
        here = slice(j * LANES, min((j + 1) * LANES, dim))
        used = here.stop - here.start
        number = 0
        for ref, factor in ((vtaps_ref, 1.0), (gtaps_ref, 0.5)):
            for tap in (0, 3, 6):
                one, two, three = [ref[tap + i : tap + i + 1, here] * factor for i in range(3)]
                outer = 0.5 * (one + three)
                for row in (one, outer + 0.5 * two, outer - 0.5 * two, three):
                    taps_ref[j, number, :, :used] = jnp.broadcast_to(row, (8, used))
                    number += 1
    for k, copy in enumerate(copies):
        copy.wait()
        for j in range(cdiv(dim, LANES)):
            here = slice(j * LANES, min((j + 1) * LANES, dim))
            used = here.stop - here.start
            slot = j % 2
            if k == 0 and used < LANES:
                features_ref[:, here.stop :] = jnp.zeros(
                    (features_ref.shape[0], LANES - used), jnp.bfloat16
                )
            total = held.shape[1]
            wide[slot, :total, :used] = held[k, :, here].astype(jnp.float32)
            for row in range(total // width):
                value = jnp.concatenate(
                    [
                        wide[slot, pl.ds(row * width + side, half, stride=2), :used]
                        for side in range(2)
                    ],
                    axis=0,
                )
                source = slice(row * width, (row + 1) * width)
                if k == 0:
                    features_ref[source, here] = jnp.maximum(value, 0.0).astype(jnp.bfloat16)
                else:
                    inputs_ref[source, here] = value


def prepare(queries, residual, edge, gain, value_taps, gate_taps):
    tokens, dim = queries.shape
    total = tokens + edge.shape[1] * edge.shape[2]
    whole = pl.BlockSpec(memory_space=pltpu.VMEM)
    return pl.pallas_call(
        functools.partial(prepare_kernel, dim),
        out_shape=[
            pltpu.VMEM((total, cdiv(dim, LANES) * LANES), jnp.bfloat16),
            pltpu.VMEM((total, dim), jnp.float32),
            pltpu.VMEM((1, dim), jnp.float32),
            pltpu.VMEM((cdiv(dim, LANES), 24, 8, LANES), jnp.float32),
        ],
        in_specs=[pl.BlockSpec(memory_space=pl.ANY)] * 2 + [whole] * 4,
        out_specs=[whole] * 4,
        scratch_shapes=[
            pltpu.VMEM((2, total, dim), jnp.bfloat16),
            pltpu.VMEM((2, total + 8, LANES), jnp.float32),
            pltpu.SemaphoreType.DMA((2,)),
        ],
        compiler_params=pltpu.CompilerParams(vmem_limit_bytes=24 * 2**20),
        cost_estimate=pl.CostEstimate(
            flops=4 * total * dim, bytes_accessed=8 * total * dim, transcendentals=0
        ),
        name="prepare",
    )(in_hbm(queries), in_hbm(residual), edge, gain, value_taps, gate_taps)


def mix_kernel(
    dim, rows, width, edges,
    features_ref, inputs_ref, gain_ref, taps_ref, *refs,
):
    *pieces, out_ref, states, weights, numer, mixed_rows, windows, results, held, semaphores = refs
    places = edge_places(lax.axis_size("space"), rows) if edges else []
    spots = piece_places() if len(pieces) > 1 else [0]
    tokens = rows * width
    weights[...] = jnp.zeros_like(weights)
    for row in (0, rows + 1):
        windows[:, :, row] = jnp.zeros((2, 4, width // 16, 8, LANES), jnp.float32)
    for k, piece in enumerate(pieces):
        size = piece.shape[0]
        states[pl.ds(pl.multiple_of(spots[k] * size, 16), size), :] = piece[...]
    lane = lane_iota((HEAD_DIM, LANES))
    sublane = lax.broadcasted_iota(jnp.int32, (8, LANES), 0)

    half = width // 2
    even, odd = pl.ds(0, half, stride=2), pl.ds(1, half, stride=2)

    def store_windows(value, slot, used, row, place):
        left, right = value[:half], value[half:]
        if 0 < row <= rows:
            mixed_rows[slot, row, :, :used] = value
        sub = sublane[:, :used]
        before, after = pltpu.roll(right, 1, 0), pltpu.roll(left, half - 1, 0)
        before = jnp.concatenate([jnp.where(sub == 0, 0.0, before[:8]), before[8:]], axis=0)
        after = jnp.concatenate([after[: half - 8], jnp.where(sub == 7, 0.0, after[half - 8 :])], axis=0)
        for k, window in enumerate((before - right, left + right, right - left, left - after)):
            windows[slot, k, place, :, :, :used] = window.reshape(half // 8, 8, used)

    def group(base, lanes):
        pairs = spans(lanes)

        def numerators(number):
            tiles, first, last = pairs[number]
            for side, j in enumerate(tiles):
                row = (base // LANES + j) * HEAD_DIM
                state = states[row : row + HEAD_DIM, :].astype(jnp.float32)
                for h, lo, hi in tile_heads(j, lanes):
                    start = h * HEAD_DIM - first * LANES
                    block = jnp.where((lane >= lo) & (lane < hi), state, 0.0)
                    weights[
                        number, start : start + HEAD_DIM, side * LANES : (side + 1) * LANES
                    ] = block.astype(jnp.bfloat16)
            depth, wide = (last - first) * LANES, len(tiles) * LANES
            product = jnp.dot(
                features_ref[:, base + first * LANES : base + last * LANES],
                weights[number, :depth, :wide],
                preferred_element_type=jnp.float32,
            )
            here = slice(tiles[0] * LANES, tiles[0] * LANES + wide)
            numer[:, here] = product
            for side, j in enumerate(tiles):
                for row in range(rows + edges):
                    source = slice(row * width, (row + 1) * width)
                    square = product[source, side * LANES : (side + 1) * LANES]
                    parts.setdefault(source.start, []).append(tile_sums(j, square * square))

        parts = {}

        def tile_sums(j, square):
            position = lane_iota(square.shape)
            sums = {}
            for head, lo, hi in tile_heads(j, lanes):
                ends = (head + 1) * HEAD_DIM <= (j + 1) * LANES
                fill = HEAD_DIM * 1e-06 / (LANES - (hi - lo)) if ends else 0.0
                mine = position < hi if lo == 0 else position >= lo
                sums[head] = jnp.sum(jnp.where(mine, square, fill), axis=-1, keepdims=True)
            return sums

        def mix_tile(j):
            slot = j % 2
            used = min(LANES, lanes - j * LANES)
            near = slice(j * LANES, j * LANES + used)
            here = slice(base + j * LANES, base + j * LANES + used)
            heads = tile_heads(j, lanes)

            def mixed(source):
                sums = [
                    sum(tiles[head] for tiles in parts[source.start] if head in tiles)
                    for head, _, _ in heads
                ]
                scale = jnp.broadcast_to(sums[0], (width, used))
                if len(heads) > 1:
                    scale = jnp.where(lane_iota(scale.shape) < heads[0][2], scale, sums[1])
                normed = numer[source, near] * lax.rsqrt(scale)
                return inputs_ref[source, here] + normed * gain_ref[:, here]

            for row in range(rows):
                value = mixed(slice(row * width, (row + 1) * width))
                store_windows(value, slot, used, row + 1, row + 1)
            for e in range(edges):
                value = mixed(slice(tokens + e * width, tokens + (e + 1) * width))
                store_windows(value, slot, used, 0, places[e])
            for row in range(rows):
                lefts, rights = [], []
                for k in range(4):
                    products = [None, None]
                    for tap_row in range(3):
                        window = windows[slot, k, row + tap_row, :, :, :used]
                        for f in range(2):
                            tap = taps_ref[base // LANES + j, 12 * f + 4 * tap_row + k, :, :used]
                            term = tap * window
                            products[f] = term if tap_row == 0 else products[f] + term
                    if k == 0:
                        lefts = products
                    elif k == 1:
                        lefts = [one + two for one, two in zip(lefts, products)]
                        rights = products
                    elif k == 2:
                        lefts = [one + two for one, two in zip(lefts, products)]
                        rights = [one - two for one, two in zip(rights, products)]
                    else:
                        rights = [one - two for one, two in zip(rights, products)]
                for k, (side, (conv_v, half_g)) in enumerate(zip((even, odd), (lefts, rights))):
                    center = mixed_rows[slot, row + 1, k * half : (k + 1) * half, :used]
                    gated = conv_v * (half_g + half_g * jnp.tanh(half_g))
                    results[slot, row, side, :used] = center + gated.reshape(half, used)
                held[row * width : (row + 1) * width, here] = results[slot, row, :width, :used].astype(
                    jnp.bfloat16
                )

        for number in range(len(pairs)):
            numerators(number)
        for j in range(cdiv(lanes, LANES)):
            mix_tile(j)

    copies = []
    for base, lanes in group_lanes(dim):
        group(base, lanes)
        here = slice(base, base + lanes)
        copies.append(
            pltpu.make_async_copy(held.at[:, here], out_ref.at[:, here], semaphores.at[len(copies)])
        )
        copies[-1].start()
    for copy in copies:
        copy.wait()


def mix(prepared, pieces, rows, width):
    features, inputs, gain, taps = prepared
    total, dim = inputs.shape
    tokens = rows * width
    pairs = spans(min(GROUP, dim))
    depth = max(last - first for _, first, last in pairs) * LANES
    whole = pl.BlockSpec(memory_space=pltpu.VMEM)
    return pl.pallas_call(
        functools.partial(mix_kernel, dim, rows, width, (total - tokens) // width),
        out_shape=jax.ShapeDtypeStruct((tokens, dim), jnp.bfloat16),
        in_specs=[whole] * (4 + len(pieces)),
        out_specs=pl.BlockSpec(memory_space=pl.ANY),
        scratch_shapes=[
            pltpu.VMEM((sum(piece.shape[0] for piece in pieces), LANES), jnp.bfloat16),
            pltpu.VMEM((len(pairs), depth, 2 * LANES), jnp.bfloat16),
            pltpu.VMEM((total, GROUP), jnp.float32),
            pltpu.VMEM((2, rows + 2, width, LANES), jnp.float32),
            pltpu.VMEM((2, 4, rows + 2, width // 16, 8, LANES), jnp.float32),
            pltpu.VMEM((2, rows, width + 8, LANES), jnp.float32),
            pltpu.VMEM((tokens, dim), jnp.bfloat16),
            pltpu.SemaphoreType.DMA((len(group_lanes(dim)),)),
        ],
        compiler_params=pltpu.CompilerParams(vmem_limit_bytes=36 * 2**20),
        cost_estimate=pl.CostEstimate(
            flops=60 * tokens * dim, bytes_accessed=6 * tokens * dim, transcendentals=2 * tokens * dim
        ),
        name="mix",
    )(features, inputs, gain, taps, *pieces)


def edge_rows(queries, residual):
    devices, rows = lax.axis_size("space"), queries.shape[0]
    up = [(i, i + 1) for i in range(devices - 1)]
    down = [(j, i) for i, j in up]
    both = jnp.stack([queries, residual])
    if devices == 2:
        first = lax.axis_index("space") == 0
        return lax.ppermute(jnp.where(first, both[:, rows - 1 :], both[:, :1]), "space", up + down)
    before = lax.ppermute(both[:, rows - 1 :], "space", up)
    after = lax.ppermute(both[:, :1], "space", down)
    return jnp.concatenate([before, after], axis=1)


def small_kernel(body, name, outs, *arrays):
    return pl.pallas_call(
        body,
        out_shape=[pltpu.VMEM(shape, jnp.bfloat16) for shape in outs],
        in_specs=[pl.BlockSpec(memory_space=pltpu.VMEM)] * len(arrays),
        out_specs=[pl.BlockSpec(memory_space=pltpu.VMEM)] * len(outs),
        compiler_params=pltpu.CompilerParams(vmem_limit_bytes=4 * 2**20),
        name=name,
    )(*arrays)


def add(*values):
    total = values[0].astype(jnp.float32)
    for value in values[1:]:
        total = total + value.astype(jnp.float32)
    return total


def parity():
    return lax.rem(lax.axis_index("frame"), 2)


def split_sum_body(kept_ref, got_ref, mine_ref, theirs_ref):
    size = mine_ref.shape[0]
    for ref, side in ((theirs_ref, 1 - parity()), (mine_ref, parity())):
        rows = pl.ds(pl.multiple_of(side * size, 16), size)
        ref[...] = add(kept_ref[rows, :], got_ref[rows, :]).astype(jnp.bfloat16)


def sum_body(*refs):
    *terms, out_ref = refs
    out_ref[...] = add(*[term[...] for term in terms]).astype(jnp.bfloat16)


def pair_sums_body(own_ref, partner_ref, *refs):
    *earlier, mine_ref, theirs_ref = refs
    before = jnp.zeros(own_ref.shape, jnp.float32)
    for k, ref in enumerate(earlier):
        from_before = lax.rem(lax.axis_index("frame") // (2 << k), 2) == 1
        before = before + jnp.where(from_before, add(ref[...]), 0.0)
    own, partner = add(own_ref[...]), add(partner_ref[...])
    first = parity() == 0
    both = before + (own + partner)
    mine_ref[...] = jnp.where(first, before + own, both).astype(jnp.bfloat16)
    theirs_ref[...] = jnp.where(first, both, before + partner).astype(jnp.bfloat16)


def paired(devices, frames):
    return devices == 2 and frames >= 4 and frames & (frames - 1) == 0


def piece_places():
    core = lax.axis_index("space")
    return [2 * c + p for c in (core, 1 - core) for p in (parity(), 1 - parity())]


def edge_places(devices, rows):
    if devices == 2:
        return [jnp.where(lax.axis_index("space") == 0, rows + 1, 0)]
    return [0, rows + 1]


def running_states(keys, values, queries, residual, rows, beside):
    devices, frames = lax.axis_size("space"), lax.axis_size("frame")
    if not paired(devices, frames):
        (state,) = frame_states(keys, values, rows, 1)
        state = lax.psum(state.astype(jnp.float32), "space").astype(jnp.bfloat16)
        every = lax.all_gather(state, "frame").astype(jnp.float32)
        reached = (jnp.arange(frames) <= lax.axis_index("frame"))[:, None, None]
        total = jnp.sum(jnp.where(reached, every, 0.0), axis=0).astype(jnp.bfloat16)
        return [total], beside(edge_rows(queries, residual))
    swap = [(0, 1), (1, 0)]
    exchange = lambda array, stride: lax.ppermute(
        array, "frame", [(f, f ^ stride) for f in range(frames)]
    )
    kept, sent, edge = frame_states(keys, values, rows, 2, (queries, residual))
    got = lax.ppermute(sent, "space", swap)
    quarter = (rows // 4, LANES)
    own, sent = small_kernel(split_sum_body, "split_sum", [quarter] * 2, kept, got)
    edge, sent = lax.optimization_barrier((edge, sent))
    edge = lax.ppermute(edge, "space", swap)
    partner = exchange(sent, 1)
    (total,) = small_kernel(sum_body, "pair_sum", [quarter], own, partner)
    earlier = []
    stride = 2
    while stride < frames:
        if stride * 2 == frames:
            total, edge = lax.optimization_barrier((total, edge))
        earlier.append(exchange(total, stride))
        stride *= 2
        if stride < frames:
            (total,) = small_kernel(sum_body, "stride_sum", [quarter], total, earlier[-1])
    prepared = beside(edge)
    earlier[-1], *prepared = lax.optimization_barrier((earlier[-1], *prepared))
    mine, theirs = small_kernel(
        pair_sums_body, "pair_sums", [quarter] * 2, own, partner, *earlier
    )
    other = exchange(theirs, 1)
    pieces = [mine, other, lax.ppermute(mine, "space", swap), lax.ppermute(other, "space", swap)]
    return pieces, prepared


def on_device(queries, keys, values, residual, attn_gain, value_taps, gate_taps):
    frames, rows, width, dim = queries.shape
    tokens = frames * rows * width
    flat = lambda a: a.reshape(tokens, dim)
    state_rows = cdiv(cdiv(dim, LANES) * HEAD_DIM, 64) * 64
    pieces, prepared = running_states(
        flat(keys),
        flat(values),
        queries.reshape(rows, width, dim),
        residual.reshape(rows, width, dim),
        state_rows,
        lambda edge: prepare(
            flat(queries), flat(residual), edge, attn_gain[None], value_taps, gate_taps
        ),
    )
    out = mix(prepared, pieces, rows, width)
    return out.reshape(frames, rows, width, dim)


def solution(mesh):
    placed = P(("groups", "frame"), "space", None, None)
    return jax.shard_map(
        on_device,
        mesh=mesh,
        in_specs=(placed, placed, placed, placed, P(), P(), P()),
        out_specs=placed,
        check_vma=False,
    )
```

```python
import functools
import math

import jax
import jax.numpy as jnp
from jax import lax
from jax.experimental import pallas as pl
from jax.experimental.pallas import tpu as pltpu
from jax.sharding import PartitionSpec as P

HEAD_DIM = 112
LANES = 128
GROUP = math.lcm(HEAD_DIM, LANES)
TILES = GROUP // LANES


def cdiv(a, b):
    return -(-a // b)


def in_hbm(array):
    return pltpu.with_memory_space_constraint(array, pltpu.HBM)


def lane_iota(shape):
    return lax.broadcasted_iota(jnp.int32, shape, len(shape) - 1)


def tile_heads(j, lanes):
    lo, hi = j * LANES, min((j + 1) * LANES, lanes)
    heads = range(lo // HEAD_DIM, cdiv(hi, HEAD_DIM))
    return [(h, max(h * HEAD_DIM - lo, 0), min((h + 1) * HEAD_DIM - lo, LANES)) for h in heads]


def spans(lanes):
    count = cdiv(lanes, LANES)
    result = []
    for j in range(0, count, 2):
        tiles = list(range(j, min(j + 2, count)))
        first = tile_heads(tiles[0], lanes)[0][0] * HEAD_DIM // LANES
        last = cdiv((tile_heads(tiles[-1], lanes)[-1][0] + 1) * HEAD_DIM, LANES)
        result.append((tiles, first, last))
    return result


def state_kernel(dim, parts, keys_ref, values_ref, *refs):
    *refs, keys, values, turned, whole, semaphores = refs
    sources, part_refs, edge_refs = refs[: -parts - 1], refs[-parts - 1 : -1], refs[-1:]
    if not sources:
        part_refs, edge_refs = refs, ()
    order = sorted(group_lanes(dim), key=lambda item: item[1])
    copies = []
    for k, (base, lanes) in enumerate(order):
        here = slice(base, base + lanes)
        copies += [
            pltpu.make_async_copy(ref.at[:, here], held.at[:, here], semaphores.at[2 * k + i])
            for i, (ref, held) in enumerate(((keys_ref, keys), (values_ref, values)))
        ]
    for k, source in enumerate(sources):
        row = (source.shape[0] - 1) * (1 - lax.axis_index("space"))
        copies.append(
            pltpu.make_async_copy(
                source.at[row], edge_refs[0].at[k, 0], semaphores.at[2 * len(order) + k]
            )
        )
    for copy in copies:
        copy.start()
    used = cdiv(dim, LANES) * HEAD_DIM
    if used < whole.shape[0]:
        whole[used:, :] = jnp.zeros((whole.shape[0] - used, LANES), jnp.bfloat16)
    lane = lane_iota((HEAD_DIM, LANES))
    for k, (base, lanes) in enumerate(order):
        for copy in copies[2 * k : 2 * k + 2]:
            copy.wait()
        turn = turned.at[k % 2]
        turn[:lanes, :] = jnp.maximum(keys[:, base : base + lanes], 0).T
        for tiles, _, _ in spans(lanes):
            begin = tile_heads(tiles[0], lanes)[0][0]
            end = tile_heads(tiles[-1], lanes)[-1][0] + 1
            first, last = tiles[0] * LANES, min((tiles[-1] + 1) * LANES, lanes)
            product = jnp.dot(
                turn[begin * HEAD_DIM : end * HEAD_DIM, :],
                values[:, base + first : base + last],
                preferred_element_type=jnp.float32,
            )
            for j in tiles:
                wide = min(LANES, lanes - j * LANES)
                blocks = [
                    product[
                        (h - begin) * HEAD_DIM : (h - begin + 1) * HEAD_DIM,
                        j * LANES - first : j * LANES - first + wide,
                    ]
                    for h, _, _ in tile_heads(j, lanes)
                ]
                total = blocks[0]
                if len(blocks) > 1:
                    total = jnp.where(lane < tile_heads(j, lanes)[0][2], blocks[0], blocks[1])
                if wide < LANES:
                    total = jnp.concatenate(
                        [total, jnp.zeros((HEAD_DIM, LANES - wide), jnp.float32)], axis=1
                    )
                row = (base // LANES + j) * HEAD_DIM
                whole[row : row + HEAD_DIM, :] = total.astype(jnp.bfloat16)
    for k, part in enumerate(part_refs):
        size = part.shape[0]
        place = lax.rem(lax.axis_index("space") + k, 2) if parts == 2 else 0
        part[...] = whole[pl.ds(pl.multiple_of(place * size, 16), size), :]
    for copy in copies[2 * len(order) :]:
        copy.wait()


def frame_states(keys, values, rows, parts, edged=()):
    tokens, dim = keys.shape
    part = (rows // parts, LANES)
    outside = pl.BlockSpec(memory_space=pl.ANY)
    return pl.pallas_call(
        functools.partial(state_kernel, dim, parts),
        out_shape=[pltpu.VMEM(part, jnp.bfloat16)] * parts
        + [pltpu.VMEM((len(edged), 1, *edged[0].shape[1:]), jnp.bfloat16) for _ in edged[:1]],
        in_specs=[outside] * (2 + len(edged)),
        out_specs=[pl.BlockSpec(memory_space=pltpu.VMEM)] * parts + [outside for _ in edged[:1]],
        scratch_shapes=[
            pltpu.VMEM((tokens, dim), jnp.bfloat16),
            pltpu.VMEM((tokens, dim), jnp.bfloat16),
            pltpu.VMEM((2, GROUP, tokens), jnp.bfloat16),
            pltpu.VMEM((rows, LANES), jnp.bfloat16),
            pltpu.SemaphoreType.DMA((2 * len(group_lanes(dim)) + len(edged),)),
        ],
        compiler_params=pltpu.CompilerParams(vmem_limit_bytes=32 * 2**20),
        cost_estimate=pl.CostEstimate(
            flops=2 * tokens * dim * HEAD_DIM, bytes_accessed=4 * tokens * dim, transcendentals=0
        ),
        name="frame_states",
    )(in_hbm(keys), in_hbm(values), *[in_hbm(array) for array in edged])


def group_lanes(dim):
    return [(first, min(GROUP, dim - first)) for first in range(0, dim, GROUP)]


def prepare_kernel(
    dim, queries_ref, residual_ref, edge_ref, gain_ref, vtaps_ref, gtaps_ref,
    features_ref, inputs_ref, scaled_ref, taps_ref, held, wide, semaphores,
):
    tokens = queries_ref.shape[0]
    copies = [
        pltpu.make_async_copy(source, held.at[k, :tokens], semaphores.at[k])
        for k, source in enumerate((queries_ref, residual_ref))
    ]
    for copy in copies:
        copy.start()
    edges, width = edge_ref.shape[1:3]
    for e in range(edges):
        here = slice(tokens + e * width, tokens + (e + 1) * width)
        held[0, here] = edge_ref[0, e]
        held[1, here] = edge_ref[1, e]
    scaled_ref[...] = gain_ref[...] * math.sqrt(HEAD_DIM)
    half = width // 2
    for j in range(cdiv(dim, LANES)):
        here = slice(j * LANES, min((j + 1) * LANES, dim))
        used = here.stop - here.start
        number = 0
        for ref, factor in ((vtaps_ref, 1.0), (gtaps_ref, 0.5)):
            for tap in (0, 3, 6):
                one, two, three = [ref[tap + i : tap + i + 1, here] * factor for i in range(3)]
                outer = 0.5 * (one + three)
                for row in (one, outer + 0.5 * two, outer - 0.5 * two, three):
                    taps_ref[j, number, :, :used] = jnp.broadcast_to(row, (8, used))
                    number += 1
    for k, copy in enumerate(copies):
        copy.wait()
        for j in range(cdiv(dim, LANES)):
            here = slice(j * LANES, min((j + 1) * LANES, dim))
            used = here.stop - here.start
            slot = j % 2
            if k == 0 and used < LANES:
                features_ref[:, here.stop :] = jnp.zeros(
                    (features_ref.shape[0], LANES - used), jnp.bfloat16
                )
            total = held.shape[1]
            wide[slot, :total, :used] = held[k, :, here].astype(jnp.float32)
            for row in range(total // width):
                value = jnp.concatenate(
                    [
                        wide[slot, pl.ds(row * width + side, half, stride=2), :used]
                        for side in range(2)
                    ],
                    axis=0,
                )
                source = slice(row * width, (row + 1) * width)
                if k == 0:
                    features_ref[source, here] = jnp.maximum(value, 0.0).astype(jnp.bfloat16)
                else:
                    inputs_ref[source, here] = value


def prepare(queries, residual, edge, gain, value_taps, gate_taps):
    tokens, dim = queries.shape
    total = tokens + edge.shape[1] * edge.shape[2]
    whole = pl.BlockSpec(memory_space=pltpu.VMEM)
    return pl.pallas_call(
        functools.partial(prepare_kernel, dim),
        out_shape=[
            pltpu.VMEM((total, cdiv(dim, LANES) * LANES), jnp.bfloat16),
            pltpu.VMEM((total, dim), jnp.float32),
            pltpu.VMEM((1, dim), jnp.float32),
            pltpu.VMEM((cdiv(dim, LANES), 24, 8, LANES), jnp.float32),
        ],
        in_specs=[pl.BlockSpec(memory_space=pl.ANY)] * 2 + [whole] * 4,
        out_specs=[whole] * 4,
        scratch_shapes=[
            pltpu.VMEM((2, total, dim), jnp.bfloat16),
            pltpu.VMEM((2, total + 8, LANES), jnp.float32),
            pltpu.SemaphoreType.DMA((2,)),
        ],
        compiler_params=pltpu.CompilerParams(vmem_limit_bytes=24 * 2**20),
        cost_estimate=pl.CostEstimate(
            flops=4 * total * dim, bytes_accessed=8 * total * dim, transcendentals=0
        ),
        name="prepare",
    )(in_hbm(queries), in_hbm(residual), edge, gain, value_taps, gate_taps)


def mix_kernel(
    dim, rows, width, edges,
    features_ref, inputs_ref, gain_ref, taps_ref, *refs,
):
    *pieces, out_ref, states, weights, numer, mixed_rows, windows, results, held, semaphores = refs
    places = edge_places(lax.axis_size("space"), rows) if edges else []
    spots = piece_places() if len(pieces) > 1 else [0]
    tokens = rows * width
    weights[...] = jnp.zeros_like(weights)
    for row in (0, rows + 1):
        windows[:, :, row] = jnp.zeros((2, 4, width // 16, 8, LANES), jnp.float32)
    for k, piece in enumerate(pieces):
        size = piece.shape[0]
        states[pl.ds(pl.multiple_of(spots[k] * size, 16), size), :] = piece[...]
    lane = lane_iota((HEAD_DIM, LANES))
    sublane = lax.broadcasted_iota(jnp.int32, (8, LANES), 0)

    half = width // 2
    even, odd = pl.ds(0, half, stride=2), pl.ds(1, half, stride=2)

    def store_windows(value, slot, used, row, place):
        left, right = value[:half], value[half:]
        if 0 < row <= rows:
            mixed_rows[slot, row, :, :used] = value
        sub = sublane[:, :used]
        before, after = pltpu.roll(right, 1, 0), pltpu.roll(left, half - 1, 0)
        before = jnp.concatenate([jnp.where(sub == 0, 0.0, before[:8]), before[8:]], axis=0)
        after = jnp.concatenate([after[: half - 8], jnp.where(sub == 7, 0.0, after[half - 8 :])], axis=0)
        for k, window in enumerate((before - right, left + right, right - left, left - after)):
            windows[slot, k, place, :, :, :used] = window.reshape(half // 8, 8, used)

    def group(base, lanes):
        pairs = spans(lanes)

        def numerators(number):
            tiles, first, last = pairs[number]
            for side, j in enumerate(tiles):
                row = (base // LANES + j) * HEAD_DIM
                state = states[row : row + HEAD_DIM, :].astype(jnp.float32)
                for h, lo, hi in tile_heads(j, lanes):
                    start = h * HEAD_DIM - first * LANES
                    block = jnp.where((lane >= lo) & (lane < hi), state, 0.0)
                    weights[
                        number, start : start + HEAD_DIM, side * LANES : (side + 1) * LANES
                    ] = block.astype(jnp.bfloat16)
            depth, wide = (last - first) * LANES, len(tiles) * LANES
            product = jnp.dot(
                features_ref[:, base + first * LANES : base + last * LANES],
                weights[number, :depth, :wide],
                preferred_element_type=jnp.float32,
            )
            here = slice(tiles[0] * LANES, tiles[0] * LANES + wide)
            numer[:, here] = product
            for side, j in enumerate(tiles):
                for row in range(rows + edges):
                    source = slice(row * width, (row + 1) * width)
                    square = product[source, side * LANES : (side + 1) * LANES]
                    parts.setdefault(source.start, []).append(tile_sums(j, square * square))

        parts = {}

        def tile_sums(j, square):
            position = lane_iota(square.shape)
            sums = {}
            for head, lo, hi in tile_heads(j, lanes):
                ends = (head + 1) * HEAD_DIM <= (j + 1) * LANES
                fill = HEAD_DIM * 1e-06 / (LANES - (hi - lo)) if ends else 0.0
                mine = position < hi if lo == 0 else position >= lo
                sums[head] = jnp.sum(jnp.where(mine, square, fill), axis=-1, keepdims=True)
            return sums

        def mix_tile(j):
            slot = j % 2
            used = min(LANES, lanes - j * LANES)
            near = slice(j * LANES, j * LANES + used)
            here = slice(base + j * LANES, base + j * LANES + used)
            heads = tile_heads(j, lanes)

            def mixed(source):
                sums = [
                    sum(tiles[head] for tiles in parts[source.start] if head in tiles)
                    for head, _, _ in heads
                ]
                scale = jnp.broadcast_to(sums[0], (width, used))
                if len(heads) > 1:
                    scale = jnp.where(lane_iota(scale.shape) < heads[0][2], scale, sums[1])
                normed = numer[source, near] * lax.rsqrt(scale)
                return inputs_ref[source, here] + normed * gain_ref[:, here]

            for row in range(rows):
                value = mixed(slice(row * width, (row + 1) * width))
                store_windows(value, slot, used, row + 1, row + 1)
            for e in range(edges):
                value = mixed(slice(tokens + e * width, tokens + (e + 1) * width))
                store_windows(value, slot, used, 0, places[e])
            for row in range(rows):
                lefts, rights = [], []
                for k in range(4):
                    products = [None, None]
                    for tap_row in range(3):
                        window = windows[slot, k, row + tap_row, :, :, :used]
                        for f in range(2):
                            tap = taps_ref[base // LANES + j, 12 * f + 4 * tap_row + k, :, :used]
                            term = tap * window
                            products[f] = term if tap_row == 0 else products[f] + term
                    if k == 0:
                        lefts = products
                    elif k == 1:
                        lefts = [one + two for one, two in zip(lefts, products)]
                        rights = products
                    elif k == 2:
                        lefts = [one + two for one, two in zip(lefts, products)]
                        rights = [one - two for one, two in zip(rights, products)]
                    else:
                        rights = [one - two for one, two in zip(rights, products)]
                for k, (side, (conv_v, half_g)) in enumerate(zip((even, odd), (lefts, rights))):
                    center = mixed_rows[slot, row + 1, k * half : (k + 1) * half, :used]
                    gated = conv_v * (half_g + half_g * jnp.tanh(half_g))
                    results[slot, row, side, :used] = center + gated.reshape(half, used)
                held[row * width : (row + 1) * width, here] = results[slot, row, :width, :used].astype(
                    jnp.bfloat16
                )

        numerators(0)
        for number, (tiles, _, _) in enumerate(pairs):
            if number + 1 < len(pairs):
                numerators(number + 1)
            for j in tiles:
                mix_tile(j)

    copies = []
    for base, lanes in group_lanes(dim):
        group(base, lanes)
        here = slice(base, base + lanes)
        copies.append(
            pltpu.make_async_copy(held.at[:, here], out_ref.at[:, here], semaphores.at[len(copies)])
        )
        copies[-1].start()
    for copy in copies:
        copy.wait()


def mix(prepared, pieces, rows, width):
    features, inputs, gain, taps = prepared
    total, dim = inputs.shape
    tokens = rows * width
    pairs = spans(min(GROUP, dim))
    depth = max(last - first for _, first, last in pairs) * LANES
    whole = pl.BlockSpec(memory_space=pltpu.VMEM)
    return pl.pallas_call(
        functools.partial(mix_kernel, dim, rows, width, (total - tokens) // width),
        out_shape=jax.ShapeDtypeStruct((tokens, dim), jnp.bfloat16),
        in_specs=[whole] * (4 + len(pieces)),
        out_specs=pl.BlockSpec(memory_space=pl.ANY),
        scratch_shapes=[
            pltpu.VMEM((sum(piece.shape[0] for piece in pieces), LANES), jnp.bfloat16),
            pltpu.VMEM((len(pairs), depth, 2 * LANES), jnp.bfloat16),
            pltpu.VMEM((total, GROUP), jnp.float32),
            pltpu.VMEM((2, rows + 2, width, LANES), jnp.float32),
            pltpu.VMEM((2, 4, rows + 2, width // 16, 8, LANES), jnp.float32),
            pltpu.VMEM((2, rows, width + 8, LANES), jnp.float32),
            pltpu.VMEM((tokens, dim), jnp.bfloat16),
            pltpu.SemaphoreType.DMA((len(group_lanes(dim)),)),
        ],
        compiler_params=pltpu.CompilerParams(vmem_limit_bytes=36 * 2**20),
        cost_estimate=pl.CostEstimate(
            flops=60 * tokens * dim, bytes_accessed=6 * tokens * dim, transcendentals=2 * tokens * dim
        ),
        name="mix",
    )(features, inputs, gain, taps, *pieces)


def edge_rows(queries, residual):
    devices, rows = lax.axis_size("space"), queries.shape[0]
    up = [(i, i + 1) for i in range(devices - 1)]
    down = [(j, i) for i, j in up]
    both = jnp.stack([queries, residual])
    if devices == 2:
        first = lax.axis_index("space") == 0
        return lax.ppermute(jnp.where(first, both[:, rows - 1 :], both[:, :1]), "space", up + down)
    before = lax.ppermute(both[:, rows - 1 :], "space", up)
    after = lax.ppermute(both[:, :1], "space", down)
    return jnp.concatenate([before, after], axis=1)


def small_kernel(body, name, outs, *arrays):
    return pl.pallas_call(
        body,
        out_shape=[pltpu.VMEM(shape, jnp.bfloat16) for shape in outs],
        in_specs=[pl.BlockSpec(memory_space=pltpu.VMEM)] * len(arrays),
        out_specs=[pl.BlockSpec(memory_space=pltpu.VMEM)] * len(outs),
        compiler_params=pltpu.CompilerParams(vmem_limit_bytes=4 * 2**20),
        name=name,
    )(*arrays)


def add(*values):
    total = values[0].astype(jnp.float32)
    for value in values[1:]:
        total = total + value.astype(jnp.float32)
    return total


def parity():
    return lax.rem(lax.axis_index("frame"), 2)


def split_sum_body(kept_ref, got_ref, mine_ref, theirs_ref):
    size = mine_ref.shape[0]
    for ref, side in ((theirs_ref, 1 - parity()), (mine_ref, parity())):
        rows = pl.ds(pl.multiple_of(side * size, 16), size)
        ref[...] = add(kept_ref[rows, :], got_ref[rows, :]).astype(jnp.bfloat16)


def sum_body(*refs):
    *terms, out_ref = refs
    out_ref[...] = add(*[term[...] for term in terms]).astype(jnp.bfloat16)


def pair_sums_body(own_ref, partner_ref, *refs):
    *earlier, mine_ref, theirs_ref = refs
    before = jnp.zeros(own_ref.shape, jnp.float32)
    for k, ref in enumerate(earlier):
        from_before = lax.rem(lax.axis_index("frame") // (2 << k), 2) == 1
        before = before + jnp.where(from_before, add(ref[...]), 0.0)
    own, partner = add(own_ref[...]), add(partner_ref[...])
    first = parity() == 0
    both = before + (own + partner)
    mine_ref[...] = jnp.where(first, before + own, both).astype(jnp.bfloat16)
    theirs_ref[...] = jnp.where(first, both, before + partner).astype(jnp.bfloat16)


def paired(devices, frames):
    return devices == 2 and frames >= 4 and frames & (frames - 1) == 0


def piece_places():
    core = lax.axis_index("space")
    return [2 * c + p for c in (core, 1 - core) for p in (parity(), 1 - parity())]


def edge_places(devices, rows):
    if devices == 2:
        return [jnp.where(lax.axis_index("space") == 0, rows + 1, 0)]
    return [0, rows + 1]


def running_states(keys, values, queries, residual, rows, beside):
    devices, frames = lax.axis_size("space"), lax.axis_size("frame")
    if not paired(devices, frames):
        (state,) = frame_states(keys, values, rows, 1)
        state = lax.psum(state.astype(jnp.float32), "space").astype(jnp.bfloat16)
        every = lax.all_gather(state, "frame").astype(jnp.float32)
        reached = (jnp.arange(frames) <= lax.axis_index("frame"))[:, None, None]
        total = jnp.sum(jnp.where(reached, every, 0.0), axis=0).astype(jnp.bfloat16)
        return [total], beside(edge_rows(queries, residual))
    swap = [(0, 1), (1, 0)]
    exchange = lambda array, stride: lax.ppermute(
        array, "frame", [(f, f ^ stride) for f in range(frames)]
    )
    kept, sent, edge = frame_states(keys, values, rows, 2, (queries, residual))
    got = lax.ppermute(sent, "space", swap)
    quarter = (rows // 4, LANES)
    own, sent = small_kernel(split_sum_body, "split_sum", [quarter] * 2, kept, got)
    edge, sent = lax.optimization_barrier((edge, sent))
    edge = lax.ppermute(edge, "space", swap)
    partner = exchange(sent, 1)
    (total,) = small_kernel(sum_body, "pair_sum", [quarter], own, partner)
    earlier = []
    stride = 2
    while stride < frames:
        if stride * 2 == frames:
            total, edge = lax.optimization_barrier((total, edge))
        earlier.append(exchange(total, stride))
        stride *= 2
        if stride < frames:
            (total,) = small_kernel(sum_body, "stride_sum", [quarter], total, earlier[-1])
    prepared = beside(edge)
    earlier[-1], *prepared = lax.optimization_barrier((earlier[-1], *prepared))
    mine, theirs = small_kernel(
        pair_sums_body, "pair_sums", [quarter] * 2, own, partner, *earlier
    )
    other = exchange(theirs, 1)
    pieces = [mine, other, lax.ppermute(mine, "space", swap), lax.ppermute(other, "space", swap)]
    return pieces, prepared


def on_device(queries, keys, values, residual, attn_gain, value_taps, gate_taps):
    frames, rows, width, dim = queries.shape
    tokens = frames * rows * width
    flat = lambda a: a.reshape(tokens, dim)
    state_rows = cdiv(cdiv(dim, LANES) * HEAD_DIM, 64) * 64
    pieces, prepared = running_states(
        flat(keys),
        flat(values),
        queries.reshape(rows, width, dim),
        residual.reshape(rows, width, dim),
        state_rows,
        lambda edge: prepare(
            flat(queries), flat(residual), edge, attn_gain[None], value_taps, gate_taps
        ),
    )
    out = mix(prepared, pieces, rows, width)
    return out.reshape(frames, rows, width, dim)


def solution(mesh):
    placed = P(("groups", "frame"), "space", None, None)
    return jax.shard_map(
        on_device,
        mesh=mesh,
        in_specs=(placed, placed, placed, placed, P(), P(), P()),
        out_specs=placed,
        check_vma=False,
    )
```

```python
import functools
import math

import jax
import jax.numpy as jnp
from jax import lax
from jax.experimental import pallas as pl
from jax.experimental.pallas import tpu as pltpu
from jax.sharding import PartitionSpec as P

HEAD_DIM = 112
LANES = 128
GROUP = math.lcm(HEAD_DIM, LANES)
TILES = GROUP // LANES


def cdiv(a, b):
    return -(-a // b)


def in_hbm(array):
    return pltpu.with_memory_space_constraint(array, pltpu.HBM)


def lane_iota(shape):
    return lax.broadcasted_iota(jnp.int32, shape, len(shape) - 1)


def tile_heads(j, lanes):
    lo, hi = j * LANES, min((j + 1) * LANES, lanes)
    heads = range(lo // HEAD_DIM, cdiv(hi, HEAD_DIM))
    return [(h, max(h * HEAD_DIM - lo, 0), min((h + 1) * HEAD_DIM - lo, LANES)) for h in heads]


def spans(lanes):
    count = cdiv(lanes, LANES)
    result = []
    for j in range(0, count, 2):
        tiles = list(range(j, min(j + 2, count)))
        first = tile_heads(tiles[0], lanes)[0][0] * HEAD_DIM // LANES
        last = cdiv((tile_heads(tiles[-1], lanes)[-1][0] + 1) * HEAD_DIM, LANES)
        result.append((tiles, first, last))
    return result


def state_kernel(dim, parts, keys_ref, values_ref, *refs):
    *refs, keys, values, turned, whole, semaphores = refs
    sources, part_refs, edge_refs = refs[: -parts - 1], refs[-parts - 1 : -1], refs[-1:]
    if not sources:
        part_refs, edge_refs = refs, ()
    order = sorted(group_lanes(dim), key=lambda item: item[1])
    copies = []
    for k, (base, lanes) in enumerate(order):
        here = slice(base, base + lanes)
        copies += [
            pltpu.make_async_copy(ref.at[:, here], held.at[:, here], semaphores.at[2 * k + i])
            for i, (ref, held) in enumerate(((keys_ref, keys), (values_ref, values)))
        ]
    for k, source in enumerate(sources):
        row = (source.shape[0] - 1) * (1 - lax.axis_index("space"))
        copies.append(
            pltpu.make_async_copy(
                source.at[row], edge_refs[0].at[k, 0], semaphores.at[2 * len(order) + k]
            )
        )
    for copy in copies:
        copy.start()
    used = cdiv(dim, LANES) * HEAD_DIM
    if used < whole.shape[0]:
        whole[used:, :] = jnp.zeros((whole.shape[0] - used, LANES), jnp.bfloat16)
    lane = lane_iota((HEAD_DIM, LANES))
    for k, (base, lanes) in enumerate(order):
        turn = turned.at[k % 2]
        copies[2 * k].wait()
        turn[:lanes, :] = jnp.maximum(keys[:, base : base + lanes], 0).T
        copies[2 * k + 1].wait()
        for tiles, _, _ in spans(lanes):
            begin = tile_heads(tiles[0], lanes)[0][0]
            end = tile_heads(tiles[-1], lanes)[-1][0] + 1
            first, last = tiles[0] * LANES, min((tiles[-1] + 1) * LANES, lanes)
            product = jnp.dot(
                turn[begin * HEAD_DIM : end * HEAD_DIM, :],
                values[:, base + first : base + last],
                preferred_element_type=jnp.float32,
            )
            for j in tiles:
                wide = min(LANES, lanes - j * LANES)
                blocks = [
                    product[
                        (h - begin) * HEAD_DIM : (h - begin + 1) * HEAD_DIM,
                        j * LANES - first : j * LANES - first + wide,
                    ]
                    for h, _, _ in tile_heads(j, lanes)
                ]
                total = blocks[0]
                if len(blocks) > 1:
                    total = jnp.where(lane < tile_heads(j, lanes)[0][2], blocks[0], blocks[1])
                if wide < LANES:
                    total = jnp.concatenate(
                        [total, jnp.zeros((HEAD_DIM, LANES - wide), jnp.float32)], axis=1
                    )
                row = (base // LANES + j) * HEAD_DIM
                whole[row : row + HEAD_DIM, :] = total.astype(jnp.bfloat16)
    for k, part in enumerate(part_refs):
        size = part.shape[0]
        place = lax.rem(lax.axis_index("space") + k, 2) if parts == 2 else 0
        part[...] = whole[pl.ds(pl.multiple_of(place * size, 16), size), :]
    for copy in copies[2 * len(order) :]:
        copy.wait()


def frame_states(keys, values, rows, parts, edged=()):
    tokens, dim = keys.shape
    part = (rows // parts, LANES)
    outside = pl.BlockSpec(memory_space=pl.ANY)
    return pl.pallas_call(
        functools.partial(state_kernel, dim, parts),
        out_shape=[pltpu.VMEM(part, jnp.bfloat16)] * parts
        + [pltpu.VMEM((len(edged), 1, *edged[0].shape[1:]), jnp.bfloat16) for _ in edged[:1]],
        in_specs=[outside] * (2 + len(edged)),
        out_specs=[pl.BlockSpec(memory_space=pltpu.VMEM)] * parts + [outside for _ in edged[:1]],
        scratch_shapes=[
            pltpu.VMEM((tokens, dim), jnp.bfloat16),
            pltpu.VMEM((tokens, dim), jnp.bfloat16),
            pltpu.VMEM((2, GROUP, tokens), jnp.bfloat16),
            pltpu.VMEM((rows, LANES), jnp.bfloat16),
            pltpu.SemaphoreType.DMA((2 * len(group_lanes(dim)) + len(edged),)),
        ],
        compiler_params=pltpu.CompilerParams(vmem_limit_bytes=32 * 2**20),
        cost_estimate=pl.CostEstimate(
            flops=2 * tokens * dim * HEAD_DIM, bytes_accessed=4 * tokens * dim, transcendentals=0
        ),
        name="frame_states",
    )(in_hbm(keys), in_hbm(values), *[in_hbm(array) for array in edged])


def group_lanes(dim):
    return [(first, min(GROUP, dim - first)) for first in range(0, dim, GROUP)]


def prepare_kernel(
    dim, queries_ref, residual_ref, edge_ref, gain_ref, vtaps_ref, gtaps_ref,
    features_ref, inputs_ref, scaled_ref, taps_ref, held, wide, semaphores,
):
    tokens = queries_ref.shape[0]
    copies = [
        pltpu.make_async_copy(source, held.at[k, :tokens], semaphores.at[k])
        for k, source in enumerate((queries_ref, residual_ref))
    ]
    for copy in copies:
        copy.start()
    edges, width = edge_ref.shape[1:3]
    for e in range(edges):
        here = slice(tokens + e * width, tokens + (e + 1) * width)
        held[0, here] = edge_ref[0, e]
        held[1, here] = edge_ref[1, e]
    scaled_ref[...] = gain_ref[...] * math.sqrt(HEAD_DIM)
    half = width // 2
    for j in range(cdiv(dim, LANES)):
        here = slice(j * LANES, min((j + 1) * LANES, dim))
        used = here.stop - here.start
        number = 0
        for ref, factor in ((vtaps_ref, 1.0), (gtaps_ref, 0.5)):
            for tap in (0, 3, 6):
                one, two, three = [ref[tap + i : tap + i + 1, here] * factor for i in range(3)]
                outer = 0.5 * (one + three)
                for row in (one, outer + 0.5 * two, outer - 0.5 * two, three):
                    taps_ref[j, number, :, :used] = jnp.broadcast_to(row, (8, used))
                    number += 1
    for k, copy in enumerate(copies):
        copy.wait()
        for j in range(cdiv(dim, LANES)):
            here = slice(j * LANES, min((j + 1) * LANES, dim))
            used = here.stop - here.start
            slot = j % 2
            if k == 0 and used < LANES:
                features_ref[:, here.stop :] = jnp.zeros(
                    (features_ref.shape[0], LANES - used), jnp.bfloat16
                )
            total = held.shape[1]
            wide[slot, :total, :used] = held[k, :, here].astype(jnp.float32)
            for row in range(total // width):
                value = jnp.concatenate(
                    [
                        wide[slot, pl.ds(row * width + side, half, stride=2), :used]
                        for side in range(2)
                    ],
                    axis=0,
                )
                source = slice(row * width, (row + 1) * width)
                if k == 0:
                    features_ref[source, here] = jnp.maximum(value, 0.0).astype(jnp.bfloat16)
                else:
                    inputs_ref[source, here] = value


def prepare(queries, residual, edge, gain, value_taps, gate_taps):
    tokens, dim = queries.shape
    total = tokens + edge.shape[1] * edge.shape[2]
    whole = pl.BlockSpec(memory_space=pltpu.VMEM)
    return pl.pallas_call(
        functools.partial(prepare_kernel, dim),
        out_shape=[
            pltpu.VMEM((total, cdiv(dim, LANES) * LANES), jnp.bfloat16),
            pltpu.VMEM((total, dim), jnp.float32),
            pltpu.VMEM((1, dim), jnp.float32),
            pltpu.VMEM((cdiv(dim, LANES), 24, 8, LANES), jnp.float32),
        ],
        in_specs=[pl.BlockSpec(memory_space=pl.ANY)] * 2 + [whole] * 4,
        out_specs=[whole] * 4,
        scratch_shapes=[
            pltpu.VMEM((2, total, dim), jnp.bfloat16),
            pltpu.VMEM((2, total + 8, LANES), jnp.float32),
            pltpu.SemaphoreType.DMA((2,)),
        ],
        compiler_params=pltpu.CompilerParams(vmem_limit_bytes=24 * 2**20),
        cost_estimate=pl.CostEstimate(
            flops=4 * total * dim, bytes_accessed=8 * total * dim, transcendentals=0
        ),
        name="prepare",
    )(in_hbm(queries), in_hbm(residual), edge, gain, value_taps, gate_taps)


def mix_kernel(
    dim, rows, width, edges,
    features_ref, inputs_ref, gain_ref, taps_ref, *refs,
):
    *pieces, out_ref, states, weights, numer, mixed_rows, windows, results, held, semaphores = refs
    places = edge_places(lax.axis_size("space"), rows) if edges else []
    spots = piece_places() if len(pieces) > 1 else [0]
    tokens = rows * width
    weights[...] = jnp.zeros_like(weights)
    for row in (0, rows + 1):
        windows[:, :, row] = jnp.zeros((2, 4, width // 16, 8, LANES), jnp.float32)
    for k, piece in enumerate(pieces):
        size = piece.shape[0]
        states[pl.ds(pl.multiple_of(spots[k] * size, 16), size), :] = piece[...]
    lane = lane_iota((HEAD_DIM, LANES))
    sublane = lax.broadcasted_iota(jnp.int32, (8, LANES), 0)

    half = width // 2
    even, odd = pl.ds(0, half, stride=2), pl.ds(1, half, stride=2)

    def store_windows(value, slot, used, row, place):
        left, right = value[:half], value[half:]
        if 0 < row <= rows:
            mixed_rows[slot, row, :, :used] = value
        sub = sublane[:, :used]
        before, after = pltpu.roll(right, 1, 0), pltpu.roll(left, half - 1, 0)
        before = jnp.concatenate([jnp.where(sub == 0, 0.0, before[:8]), before[8:]], axis=0)
        after = jnp.concatenate([after[: half - 8], jnp.where(sub == 7, 0.0, after[half - 8 :])], axis=0)
        for k, window in enumerate((before - right, left + right, right - left, left - after)):
            windows[slot, k, place, :, :, :used] = window.reshape(half // 8, 8, used)

    def group(base, lanes):
        pairs = spans(lanes)

        def numerators(number):
            tiles, first, last = pairs[number]
            for side, j in enumerate(tiles):
                row = (base // LANES + j) * HEAD_DIM
                state = states[row : row + HEAD_DIM, :].astype(jnp.float32)
                for h, lo, hi in tile_heads(j, lanes):
                    start = h * HEAD_DIM - first * LANES
                    block = jnp.where((lane >= lo) & (lane < hi), state, 0.0)
                    weights[
                        number, start : start + HEAD_DIM, side * LANES : (side + 1) * LANES
                    ] = block.astype(jnp.bfloat16)
            depth, wide = (last - first) * LANES, len(tiles) * LANES
            product = jnp.dot(
                features_ref[:, base + first * LANES : base + last * LANES],
                weights[number, :depth, :wide],
                preferred_element_type=jnp.float32,
            )
            here = slice(tiles[0] * LANES, tiles[0] * LANES + wide)
            numer[:, here] = product
            for side, j in enumerate(tiles):
                for row in range(rows + edges):
                    source = slice(row * width, (row + 1) * width)
                    square = product[source, side * LANES : (side + 1) * LANES]
                    parts.setdefault(source.start, []).append(tile_sums(j, square * square))

        parts = {}

        def tile_sums(j, square):
            position = lane_iota(square.shape)
            sums = {}
            for head, lo, hi in tile_heads(j, lanes):
                ends = (head + 1) * HEAD_DIM <= (j + 1) * LANES
                fill = HEAD_DIM * 1e-06 / (LANES - (hi - lo)) if ends else 0.0
                mine = position < hi if lo == 0 else position >= lo
                sums[head] = jnp.sum(jnp.where(mine, square, fill), axis=-1, keepdims=True)
            return sums

        def mix_tile(j):
            slot = j % 2
            used = min(LANES, lanes - j * LANES)
            near = slice(j * LANES, j * LANES + used)
            here = slice(base + j * LANES, base + j * LANES + used)
            heads = tile_heads(j, lanes)

            def mixed(source):
                sums = [
                    sum(tiles[head] for tiles in parts[source.start] if head in tiles)
                    for head, _, _ in heads
                ]
                scale = jnp.broadcast_to(sums[0], (width, used))
                if len(heads) > 1:
                    scale = jnp.where(lane_iota(scale.shape) < heads[0][2], scale, sums[1])
                normed = numer[source, near] * lax.rsqrt(scale)
                return inputs_ref[source, here] + normed * gain_ref[:, here]

            for row in range(rows):
                value = mixed(slice(row * width, (row + 1) * width))
                store_windows(value, slot, used, row + 1, row + 1)
            for e in range(edges):
                value = mixed(slice(tokens + e * width, tokens + (e + 1) * width))
                store_windows(value, slot, used, 0, places[e])
            for row in range(rows):
                lefts, rights = [], []
                for k in range(4):
                    products = [None, None]
                    for tap_row in range(3):
                        window = windows[slot, k, row + tap_row, :, :, :used]
                        for f in range(2):
                            tap = taps_ref[base // LANES + j, 12 * f + 4 * tap_row + k, :, :used]
                            term = tap * window
                            products[f] = term if tap_row == 0 else products[f] + term
                    if k == 0:
                        lefts = products
                    elif k == 1:
                        lefts = [one + two for one, two in zip(lefts, products)]
                        rights = products
                    elif k == 2:
                        lefts = [one + two for one, two in zip(lefts, products)]
                        rights = [one - two for one, two in zip(rights, products)]
                    else:
                        rights = [one - two for one, two in zip(rights, products)]
                for k, (side, (conv_v, half_g)) in enumerate(zip((even, odd), (lefts, rights))):
                    center = mixed_rows[slot, row + 1, k * half : (k + 1) * half, :used]
                    gated = conv_v * (half_g + half_g * jnp.tanh(half_g))
                    results[slot, row, side, :used] = center + gated.reshape(half, used)
                held[row * width : (row + 1) * width, here] = results[slot, row, :width, :used].astype(
                    jnp.bfloat16
                )

        numerators(0)
        for number, (tiles, _, _) in enumerate(pairs):
            if number + 1 < len(pairs):
                numerators(number + 1)
            for j in tiles:
                mix_tile(j)

    copies = []
    for base, lanes in group_lanes(dim):
        group(base, lanes)
        here = slice(base, base + lanes)
        copies.append(
            pltpu.make_async_copy(held.at[:, here], out_ref.at[:, here], semaphores.at[len(copies)])
        )
        copies[-1].start()
    for copy in copies:
        copy.wait()


def mix(prepared, pieces, rows, width):
    features, inputs, gain, taps = prepared
    total, dim = inputs.shape
    tokens = rows * width
    pairs = spans(min(GROUP, dim))
    depth = max(last - first for _, first, last in pairs) * LANES
    whole = pl.BlockSpec(memory_space=pltpu.VMEM)
    return pl.pallas_call(
        functools.partial(mix_kernel, dim, rows, width, (total - tokens) // width),
        out_shape=jax.ShapeDtypeStruct((tokens, dim), jnp.bfloat16),
        in_specs=[whole] * (4 + len(pieces)),
        out_specs=pl.BlockSpec(memory_space=pl.ANY),
        scratch_shapes=[
            pltpu.VMEM((sum(piece.shape[0] for piece in pieces), LANES), jnp.bfloat16),
            pltpu.VMEM((len(pairs), depth, 2 * LANES), jnp.bfloat16),
            pltpu.VMEM((total, GROUP), jnp.float32),
            pltpu.VMEM((2, rows + 2, width, LANES), jnp.float32),
            pltpu.VMEM((2, 4, rows + 2, width // 16, 8, LANES), jnp.float32),
            pltpu.VMEM((2, rows, width + 8, LANES), jnp.float32),
            pltpu.VMEM((tokens, dim), jnp.bfloat16),
            pltpu.SemaphoreType.DMA((len(group_lanes(dim)),)),
        ],
        compiler_params=pltpu.CompilerParams(vmem_limit_bytes=36 * 2**20),
        cost_estimate=pl.CostEstimate(
            flops=60 * tokens * dim, bytes_accessed=6 * tokens * dim, transcendentals=2 * tokens * dim
        ),
        name="mix",
    )(features, inputs, gain, taps, *pieces)


def edge_rows(queries, residual):
    devices, rows = lax.axis_size("space"), queries.shape[0]
    up = [(i, i + 1) for i in range(devices - 1)]
    down = [(j, i) for i, j in up]
    both = jnp.stack([queries, residual])
    if devices == 2:
        first = lax.axis_index("space") == 0
        return lax.ppermute(jnp.where(first, both[:, rows - 1 :], both[:, :1]), "space", up + down)
    before = lax.ppermute(both[:, rows - 1 :], "space", up)
    after = lax.ppermute(both[:, :1], "space", down)
    return jnp.concatenate([before, after], axis=1)


def small_kernel(body, name, outs, *arrays):
    return pl.pallas_call(
        body,
        out_shape=[pltpu.VMEM(shape, jnp.bfloat16) for shape in outs],
        in_specs=[pl.BlockSpec(memory_space=pltpu.VMEM)] * len(arrays),
        out_specs=[pl.BlockSpec(memory_space=pltpu.VMEM)] * len(outs),
        compiler_params=pltpu.CompilerParams(vmem_limit_bytes=4 * 2**20),
        name=name,
    )(*arrays)


def add(*values):
    total = values[0].astype(jnp.float32)
    for value in values[1:]:
        total = total + value.astype(jnp.float32)
    return total


def parity():
    return lax.rem(lax.axis_index("frame"), 2)


def split_sum_body(kept_ref, got_ref, mine_ref, theirs_ref):
    size = mine_ref.shape[0]
    for ref, side in ((theirs_ref, 1 - parity()), (mine_ref, parity())):
        rows = pl.ds(pl.multiple_of(side * size, 16), size)
        ref[...] = add(kept_ref[rows, :], got_ref[rows, :]).astype(jnp.bfloat16)


def sum_body(*refs):
    *terms, out_ref = refs
    out_ref[...] = add(*[term[...] for term in terms]).astype(jnp.bfloat16)


def pair_sums_body(own_ref, partner_ref, *refs):
    *earlier, mine_ref, theirs_ref = refs
    before = jnp.zeros(own_ref.shape, jnp.float32)
    for k, ref in enumerate(earlier):
        from_before = lax.rem(lax.axis_index("frame") // (2 << k), 2) == 1
        before = before + jnp.where(from_before, add(ref[...]), 0.0)
    own, partner = add(own_ref[...]), add(partner_ref[...])
    first = parity() == 0
    both = before + (own + partner)
    mine_ref[...] = jnp.where(first, before + own, both).astype(jnp.bfloat16)
    theirs_ref[...] = jnp.where(first, both, before + partner).astype(jnp.bfloat16)


def paired(devices, frames):
    return devices == 2 and frames >= 4 and frames & (frames - 1) == 0


def piece_places():
    core = lax.axis_index("space")
    return [2 * c + p for c in (core, 1 - core) for p in (parity(), 1 - parity())]


def edge_places(devices, rows):
    if devices == 2:
        return [jnp.where(lax.axis_index("space") == 0, rows + 1, 0)]
    return [0, rows + 1]


def running_states(keys, values, queries, residual, rows, beside):
    devices, frames = lax.axis_size("space"), lax.axis_size("frame")
    if not paired(devices, frames):
        (state,) = frame_states(keys, values, rows, 1)
        state = lax.psum(state.astype(jnp.float32), "space").astype(jnp.bfloat16)
        every = lax.all_gather(state, "frame").astype(jnp.float32)
        reached = (jnp.arange(frames) <= lax.axis_index("frame"))[:, None, None]
        total = jnp.sum(jnp.where(reached, every, 0.0), axis=0).astype(jnp.bfloat16)
        return [total], beside(edge_rows(queries, residual))
    swap = [(0, 1), (1, 0)]
    exchange = lambda array, stride: lax.ppermute(
        array, "frame", [(f, f ^ stride) for f in range(frames)]
    )
    kept, sent, edge = frame_states(keys, values, rows, 2, (queries, residual))
    got = lax.ppermute(sent, "space", swap)
    quarter = (rows // 4, LANES)
    own, sent = small_kernel(split_sum_body, "split_sum", [quarter] * 2, kept, got)
    edge, sent = lax.optimization_barrier((edge, sent))
    edge = lax.ppermute(edge, "space", swap)
    partner = exchange(sent, 1)
    (total,) = small_kernel(sum_body, "pair_sum", [quarter], own, partner)
    earlier = []
    stride = 2
    while stride < frames:
        if stride * 2 == frames:
            total, edge = lax.optimization_barrier((total, edge))
        earlier.append(exchange(total, stride))
        stride *= 2
        if stride < frames:
            (total,) = small_kernel(sum_body, "stride_sum", [quarter], total, earlier[-1])
    prepared = beside(edge)
    earlier[-1], *prepared = lax.optimization_barrier((earlier[-1], *prepared))
    mine, theirs = small_kernel(
        pair_sums_body, "pair_sums", [quarter] * 2, own, partner, *earlier
    )
    other = exchange(theirs, 1)
    pieces = [mine, other, lax.ppermute(mine, "space", swap), lax.ppermute(other, "space", swap)]
    return pieces, prepared


def on_device(queries, keys, values, residual, attn_gain, value_taps, gate_taps):
    frames, rows, width, dim = queries.shape
    tokens = frames * rows * width
    flat = lambda a: a.reshape(tokens, dim)
    state_rows = cdiv(cdiv(dim, LANES) * HEAD_DIM, 64) * 64
    pieces, prepared = running_states(
        flat(keys),
        flat(values),
        queries.reshape(rows, width, dim),
        residual.reshape(rows, width, dim),
        state_rows,
        lambda edge: prepare(
            flat(queries), flat(residual), edge, attn_gain[None], value_taps, gate_taps
        ),
    )
    out = mix(prepared, pieces, rows, width)
    return out.reshape(frames, rows, width, dim)


def solution(mesh):
    placed = P(("groups", "frame"), "space", None, None)
    return jax.shard_map(
        on_device,
        mesh=mesh,
        in_specs=(placed, placed, placed, placed, P(), P(), P()),
        out_specs=placed,
        check_vma=False,
    )
```
